32 devices in a mesh: groups: 2 (over y), rows: 8 (over z, x), member: 2 (over core).
Axes of the slice: x: 2, y: 2, z: 4, core: 2. Of those that a mesh axis runs over, the one named last changes fastest.
Arguments:
- features: bfloat16 [16384, 512], P(('groups', 'rows')), parts along dimension 0, may hold values from -6 to 6
- escalated: int32 [16, 256], P(('groups', 'rows')), parts along dimension 0, may hold values from 0 to 1023, as said below
- owner_ids: int32 [16, 256, 1], P(('groups', 'rows')), parts along dimension 0, may hold values from 0 to 7; in each aligned block of 256 rows (0 to 255, 256 to 511, ..., all dimensions but the last counted through in order) at most 64 rows name the same one
- member_in: bfloat16 [4, 512, 1024], P('member'), may hold values from -0.25 to 0.25
- member_bias: float32 [4, 1024], P('member'), may hold values from -3 to 3
- member_out: bfloat16 [4, 1024], P('member'), may hold values from -0.1875 to 0.1875
- feat_weight: bfloat16 [512, 512], P('member'), may hold values from -0.25 to 0.25
- feat_bias: float32 [512], replicated, may hold values from -5 to 5
- pred_scale: float32 [4, 512], replicated, may hold values from -5 to 5
- pred_shift: float32 [4, 512], replicated, may hold values from -5 to 5
- cls_token: float32 [512], replicated, may hold values from -5 to 5
- attn_gain: float32 [512], replicated, may hold values from 0.1 to 1.9
- qkv_weight: bfloat16 [3, 512, 512], P(None, None, 'member'), may hold values from -0.25 to 0.25
- out_weight: bfloat16 [512, 512], P('member'), may hold values from -0.25 to 0.25
- ffn_gain: float32 [512], replicated, may hold values from 0.1 to 1.9
- up_weight: bfloat16 [8, 512, 1024], P('rows', None, 'member'), may hold values from -0.25 to 0.25
- up_bias: float32 [8, 1024], P('rows', 'member'), may hold values from -3 to 3
- down_weight: bfloat16 [8, 1024, 512], P('rows', 'member'), may hold values from -0.1875 to 0.1875
- owner_heads: float32 [8, 512], P('rows'), may hold values from -0.25 to 0.25
Outputs:
- scores: float32 [16384], P(('groups', 'rows')), parts along dimension 0
The draws below stay inside these ranges and needn't reach their ends.
There are 2 independent parts, one for each index of `groups`. The reference program is written for one: setup_inputs(seed, part) draws one part's arguments, and reference() takes and returns one part's arrays. A program takes and returns all parts, laid end to end along the dimension named above; an argument that names none is the same for every part. Nothing has to cross between parts.
Inputs may be any that keep to these rules, and one draw needn't show every extreme that they name: Each row of escalated lists 256 distinct local row indices of its shard. `owner_ids`: within one row shard at most 64 escalated rows have the same segment.
All inputs are finite; a program needn't handle non-finite values.
Results may differ from the reference program's by a relative error of at most 0.0034.
Values may be sent and summed in bfloat16 or wider, within the bound.
No kernel may reach another device: no remote copies, remote signals or barrier semaphores. Data moves between devices by JAX's collectives and lax.ppermute only.
A program may use at most 64 MiB of HBM per device.

```python
import math
import jax
import jax.numpy as jnp
import numpy as np
from jax import lax

R_DEV = 1024
F = 512
H1 = 1024
D2 = 512
NH = 8
FF2 = 1024
HD = 64
MEMBERS = 4
NT = 6
ROWS_ALL = 8192
OWNERS = 8
ESC_DEV = 256
CAP = 64


def draw_escalated(key, part):
    key = jax.random.fold_in(key, 7)
    shard_keys = jax.random.split(key, OWNERS)

    def one_shard(shard_key):
        return jax.random.permutation(shard_key, R_DEV)[:ESC_DEV]
    return jax.vmap(one_shard)(shard_keys).astype(jnp.int32)


def block_scale(own_key, extent, cuts, low, top_value):
    def one(axis_at, shards_of):
        heights = jax.random.uniform(jax.random.fold_in(jax.random.fold_in(own_key, 6), axis_at), (shards_of,), jnp.float32, low / len(cuts), top_value / len(cuts))
        return jnp.repeat(jnp.exp(heights), extent[axis_at] // shards_of).reshape((-1,) + (1,) * (len(extent) - axis_at - 1))

    level = one(*cuts[0])
    for cut in cuts[1:]:
        level = level * one(*cut)
    return level


def shared_out(stream_key, own, number, rows, amount, top, most, slope):
    sequence = jax.random.permutation(stream_key, amount)
    crowded, ordinary = portions_of(amount, rows * top, most, slope, True), portions_of(amount, rows * top, most, slope, False)
    places = jnp.arange(amount)

    def named(sizes, turn):
        used = int((sizes > 0).sum())
        fixed = max(1, used // 4)
        passed = fixed + (places - fixed + turn * (used - fixed)) % max(1, amount - fixed)
        return jnp.zeros((amount,), jnp.int32).at[sequence[jnp.where(places < fixed, places, passed)]].set(jnp.asarray(sizes, jnp.int32))

    sizes = jnp.where(number % 4 == 0, named(crowded, number // 4), named(ordinary, number - number // 4 - 1))
    mixed = jax.random.permutation(jax.random.fold_in(own, 3), amount)
    source_of, taker = mixed[0:amount // 2 * 2:2], mixed[1:amount // 2 * 2:2]
    slack = jnp.minimum(sizes[source_of] - 1, most - sizes[taker]) // 2
    slack = jnp.where((source_of == sequence[0]) | (taker == sequence[0]) | (sizes[taker] == 0), 0, jnp.maximum(slack, 0))
    passed = jax.random.randint(jax.random.fold_in(own, 4), (amount // 2,), 0, 1 << 20) % (slack + 1)
    sizes = sizes.at[source_of].add(-passed).at[taker].add(passed)
    labels = jnp.searchsorted(jnp.cumsum(sizes), jnp.arange(rows * top), side="right").astype(jnp.int32)
    listing = labels.reshape(top, rows).T
    listing = listing[jax.random.permutation(jax.random.fold_in(own, 1), rows)]
    turn = jax.random.randint(jax.random.fold_in(own, 2), (rows, 1), 0, top)
    return jnp.take_along_axis(listing, (jnp.arange(top)[None, :] + turn) % top, axis=1)


def portions_of(count, total, bound, lean, full):
    loads = [(1 << 20) // math.isqrt(grade ** lean) + 1 for grade in range(1, count + 1)]
    largest = bound if full else min(bound, max(-(-total // count), total * loads[0] // sum(loads)))
    least = 1 if total - largest >= count - 1 else 0
    holding, rest = [largest] + [least] * (count - 1), total - largest - least * (count - 1)
    while rest > 0:
        free = [i for i in range(1, count) if holding[i] < largest] or [i for i in range(1, count) if holding[i] < bound]
        whole, left = sum([loads[i] for i in free]), rest
        for i in free:
            addition = min(bound - holding[i], max(1, left * loads[i] // whole), rest)
            holding[i] = holding[i] + addition
            rest = rest - addition
    return np.array(holding)


def gaussian(rng, dims, width, bound, pieces=(), kind=jnp.bfloat16):
    loudness = block_scale(rng, dims, pieces, -0.22, 0.18) if pieces else 1.0
    drawn = jax.random.normal(rng, dims, jnp.float32) * width * loudness
    return jnp.minimum(jnp.maximum(drawn, -bound), bound).astype(kind)


def setup_inputs(seed: int = 0, part: int = 0) -> dict:
    splits = jax.random.split(jax.random.key(seed), 20)
    own_keys = jax.random.split(jax.random.fold_in(splits[19], part), 20)
    features = gaussian(own_keys[0], (ROWS_ALL, F), 1.0, 6.0, ((0, 8),))
    escalated = draw_escalated(jax.random.fold_in(jax.random.fold_in(splits[19], part), 71), part)
    owner_ids_keys = jax.random.split(jax.random.fold_in(own_keys[2], 1), OWNERS * ESC_DEV // ESC_DEV)
    owner_ids_turns = jax.random.permutation(jax.random.fold_in(own_keys[2], 3), OWNERS * ESC_DEV // ESC_DEV)
    owner_ids = jax.vmap(lambda own, number: shared_out(jax.random.fold_in(own_keys[2], 2), own, number, ESC_DEV, OWNERS, 1, CAP, 2))(owner_ids_keys, owner_ids_turns).reshape((OWNERS, ESC_DEV, 1))
    member_in = gaussian(splits[3], (MEMBERS, F, H1), F ** -0.5, 0.25, ((0, 2),))
    member_bias = gaussian(splits[4], (MEMBERS, H1), 0.5, 3.0, ((0, 2),), jnp.float32)
    member_out = gaussian(splits[5], (MEMBERS, H1), H1 ** -0.5, 0.1875, ((0, 2),))
    feat_weight = gaussian(splits[6], (F, D2), F ** -0.5, 0.25, ((0, 2),))
    feat_bias = gaussian(splits[7], (D2,), 1.0, 5.0, (), jnp.float32)
    pred_scale = gaussian(splits[8], (MEMBERS, D2), 1.0, 5.0, (), jnp.float32)
    pred_shift = gaussian(splits[9], (MEMBERS, D2), 1.0, 5.0, (), jnp.float32)
    cls_token = gaussian(splits[10], (D2,), 1.0, 5.0, (), jnp.float32)
    attn_gain = jnp.clip(1.0 + 0.18 * jax.random.normal(splits[11], (D2,), jnp.float32), 0.1, 1.9)
    qkv_weight = gaussian(splits[12], (3, D2, D2), D2 ** -0.5, 0.25, ((2, 2),))
    out_weight = gaussian(splits[13], (D2, D2), D2 ** -0.5, 0.25, ((0, 2),))
    ffn_gain = jnp.clip(1.0 + 0.18 * jax.random.normal(splits[14], (D2,), jnp.float32), 0.1, 1.9)
    up_weight = gaussian(splits[15], (OWNERS, D2, FF2), D2 ** -0.5, 0.25, ((0, 8), (2, 2)))
    up_bias = gaussian(splits[16], (OWNERS, FF2), 0.5, 3.0, ((0, 8), (1, 2)), jnp.float32)
    down_weight = gaussian(splits[17], (OWNERS, FF2, D2), FF2 ** -0.5, 0.1875, ((0, 8), (1, 2)))
    owner_heads = gaussian(splits[18], (OWNERS, D2), D2 ** -0.5, 0.25, ((0, 8),), jnp.float32)
    return {"features": features, "escalated": escalated, "owner_ids": owner_ids, "member_in": member_in, "member_bias": member_bias, "member_out": member_out, "feat_weight": feat_weight, "feat_bias": feat_bias, "pred_scale": pred_scale, "pred_shift": pred_shift, "cls_token": cls_token, "attn_gain": attn_gain, "qkv_weight": qkv_weight, "out_weight": out_weight, "ffn_gain": ffn_gain, "up_weight": up_weight, "up_bias": up_bias, "down_weight": down_weight, "owner_heads": owner_heads}


def normalize(values, gain):
    mean = lax.optimization_barrier(jnp.mean(values, axis=-1, keepdims=True))
    centered = values - mean
    spread = lax.optimization_barrier(jnp.mean(centered * centered, axis=-1, keepdims=True))
    return centered * lax.rsqrt(spread + 1e-05) * gain

def reference(features, escalated, owner_ids, member_in, member_bias, member_out, feat_weight, feat_bias, pred_scale, pred_shift, cls_token, attn_gain, qkv_weight, out_weight, ffn_gain, up_weight, up_bias, down_weight, owner_heads):
    outputs = []
    for member in range(MEMBERS):
        hidden = jax.nn.gelu(jnp.dot(features, member_in[member], preferred_element_type=jnp.float32) + member_bias[member]).astype(jnp.bfloat16)
        outputs.append(jnp.dot(hidden, member_out[member], preferred_element_type=jnp.float32))
    all_preds = jnp.stack(outputs)
    ensemble = lax.optimization_barrier(jnp.mean(all_preds, axis=0))
    offsets = (jnp.arange(OWNERS, dtype=jnp.int32) * R_DEV)[:, None]
    picked = (escalated.astype(jnp.int32) + offsets).reshape(-1).astype(jnp.int32)
    owners = owner_ids.reshape(-1).astype(jnp.int32)
    total = picked.shape[0]
    rows_f = jnp.take(features, picked, axis=0)
    rows_b = jnp.take(all_preds, picked, axis=1).T.astype(jnp.bfloat16)
    rows_p = lax.optimization_barrier(rows_b).astype(jnp.float32)
    feat_tok = jnp.dot(rows_f, feat_weight, preferred_element_type=jnp.float32) + feat_bias
    pred_tok = rows_p[:, :, None] * pred_scale[None] + pred_shift[None]
    cls_rows = jnp.broadcast_to(cls_token, (total, 1, D2))
    tokens = jnp.concatenate([cls_rows, feat_tok[:, None], pred_tok], axis=1)
    normed = normalize(tokens, attn_gain).astype(jnp.bfloat16)
    query = jnp.dot(normed[:, 0], qkv_weight[0], preferred_element_type=jnp.float32).reshape(total, NH, HD)
    flat_n = normed.reshape(total * NT, D2)
    keys = jnp.dot(flat_n, qkv_weight[1], preferred_element_type=jnp.float32).reshape(total, NT, NH, HD)
    values = jnp.dot(flat_n, qkv_weight[2], preferred_element_type=jnp.float32).reshape(total, NT, NH, HD)
    logits = jnp.einsum('shd,sthd->sht', query, keys, precision=lax.Precision.HIGHEST) / math.sqrt(HD)
    expo = jnp.exp(logits)
    weights = expo / lax.optimization_barrier(jnp.sum(expo, axis=-1, keepdims=True))
    mixed = jnp.einsum('sht,sthd->shd', weights, values, precision=lax.Precision.HIGHEST).reshape(total, D2).astype(jnp.bfloat16)
    states = cls_token + jnp.dot(mixed, out_weight, preferred_element_type=jnp.float32)
    normed2 = normalize(states, ffn_gain).astype(jnp.bfloat16)
    slots = OWNERS * CAP

    def one_owner(owner):
        index = jnp.nonzero(owners == owner, size=slots, fill_value=total)[0].astype(jnp.int32)
        rows_n = jnp.take(normed2, index, axis=0, mode='clip')
        upper = jax.nn.relu(jnp.dot(rows_n, up_weight[owner], preferred_element_type=jnp.float32) + up_bias[owner]).astype(jnp.bfloat16)
        ffn_out = jnp.dot(upper, down_weight[owner], preferred_element_type=jnp.float32)
        rows_h = jnp.take(states, index, axis=0, mode='clip')
        return (lax.optimization_barrier(jnp.sum((rows_h + ffn_out) * owner_heads[owner], axis=-1)), index)
    owner_scores, owner_index = lax.map(one_owner, jnp.arange(OWNERS, dtype=jnp.int32))
    stack_score = jnp.zeros((total,), jnp.float32).at[owner_index.reshape(-1)].set(owner_scores.reshape(-1), mode='drop')
    return ensemble.at[picked].set(stack_score)
```

```python
import functools
import math

import jax
import jax.numpy as jnp
from jax import lax
from jax.experimental import pallas as pl
from jax.experimental.pallas import tpu as pltpu
from jax.sharding import PartitionSpec as P

HD = 64
EPS = 1e-05
LANES = 128
SLOT = 16
BF = jnp.bfloat16
F32 = jnp.float32
HIGH = lax.Precision.HIGHEST
VMEM = pl.BlockSpec(memory_space=pltpu.VMEM)
GELU_C = math.sqrt(2.0 / math.pi)


def iota(shape, dim):
    return lax.broadcasted_iota(jnp.int32, shape, dim)


def gelu(x):
    inner = x * (GELU_C + (GELU_C * 0.044715) * (x * x))
    half = 0.5 * x
    return half + half * jnp.tanh(inner)


def dot(a, b, precision=None):
    return lax.dot_general(
        a, b, (((1,), (0,)), ((), ())), precision=precision, preferred_element_type=F32
    )


def dot_t(a, b, precision=None):
    return lax.dot_general(
        a, b, (((1,), (1,)), ((), ())), precision=precision, preferred_element_type=F32
    )


def split(x):
    high = x.astype(BF)
    return high, (x - high.astype(F32)).astype(BF)


def route_kernel(n, half, relative, esc_ref, own_ref, feat_ref, where_ref, *block_refs):
    me = lax.axis_index("rows")
    core = lax.axis_index("member")
    count = esc_ref.shape[1]
    slots = n * half
    esc = esc_ref[...]
    own_col = own_ref[0]
    ii = iota((count, count), 0)
    jj = iota((count, count), 1)
    diag = ii == jj

    def to_row(col):
        return jnp.sum(jnp.where(diag, col, 0).astype(F32), axis=0, keepdims=True)

    def to_col(row):
        return jnp.sum(jnp.where(diag, row, 0).astype(F32), axis=1, keepdims=True)

    own = to_row(own_col).astype(jnp.int32)
    before = jnp.sum((own_col < own).astype(F32), axis=0, keepdims=True).astype(jnp.int32)
    rank = jnp.sum(
        ((own_col == own) & (ii < jj)).astype(F32), axis=0, keepdims=True
    ).astype(jnp.int32)
    side = (before + rank) & 1
    slot = rank >> 1
    if relative:
        hop = jnp.where(own >= me, own - me, own - me + n)
        lane = (hop * LANES + slot) + jnp.where(side == core, 0, n * LANES)
    else:
        hop = own
        lane = (hop * half + slot) + jnp.where(side == core, 0, slots)
    place = hop * half + slot
    where_ref[:, 0:1] = to_col(lane).astype(jnp.int32)
    where_ref[:, 1:2] = to_col(esc).astype(jnp.int32)

    mine = (place == iota((slots, count), 0)) & (side == core)
    source = jnp.sum(jnp.where(mine, esc + 1, 0).astype(F32), axis=1, keepdims=True)
    chosen = source.astype(jnp.int32) == iota((slots, feat_ref.shape[0]), 1) + 1
    rows = dot(chosen.astype(F32).astype(BF), feat_ref[...]).astype(BF)
    per = slots // len(block_refs)
    for k, block in enumerate(block_refs):
        block[...] = rows[k * per : (k + 1) * per]


def constants_kernel(
    cls_ref, gain_ref, qkv_ref, scale_ref, shift_ref, bias_ref, out_ref, up_ref, down_ref, head_ref,
    mine_ref, other_ref, values_ref,
):
    members, width = scale_ref.shape
    local = qkv_ref.shape[2]
    gain = gain_ref[...]
    cls = cls_ref[...]
    centered = cls - jnp.mean(cls, axis=-1, keepdims=True)
    spread = jnp.mean(centered * centered, axis=-1, keepdims=True)
    ncls = (centered * lax.rsqrt(spread + EPS) * gain).astype(BF)
    query = dot(ncls, qkv_ref[0]) * (1.0 / math.sqrt(HD))
    scale = scale_ref[...]
    shift = shift_ref[...]
    cscale = (scale - jnp.mean(scale, axis=-1, keepdims=True)) * gain
    cshift = (shift - jnp.mean(shift, axis=-1, keepdims=True)) * gain
    vectors = jnp.concatenate(
        [ncls.astype(F32), jnp.zeros((7, width), F32), cscale, jnp.zeros((8 - members, width), F32),
         cshift, jnp.zeros((8 - members, width), F32)], axis=0)
    keys = qkv_ref[1].astype(F32)
    values = dot(vectors, qkv_ref[2].astype(F32), HIGH)
    down = dot_t(head_ref[...], down_ref[0].astype(F32), HIGH)
    row = iota((LANES, local), 0)
    col = iota((LANES, local), 1)
    for shifted, ref in ((0, mine_ref), (local // HD, other_ref)):
        mask = (row & (SLOT - 1)) == (col // HD + shifted)
        key_map = dot_t(jnp.where(mask, query, 0.0), keys, HIGH)
        logits = dot_t(vectors, key_map, HIGH)
        token = iota((1, LANES), 1) // SLOT
        on_cls = jnp.where(token == 0, logits[0:1], 0.0)
        on_scale = jnp.zeros((1, LANES), F32)
        on_shift = jnp.zeros((1, LANES), F32)
        for m in range(members):
            on_scale = jnp.where(token == 2 + m, logits[8 + m : 9 + m], on_scale)
            on_shift = jnp.where(token == 2 + m, logits[16 + m : 17 + m], on_shift)
        ref[...] = jnp.zeros_like(ref)
        ref[0:LANES] = key_map
        ref[128:152, :local] = values
        ref[152:153, :LANES] = on_cls
        ref[153:154, :LANES] = on_scale
        ref[154:155, :LANES] = on_shift
        ref[155:156, :] = down
        ref[156:157, :] = up_ref[...]
        hidden = bias_ref.shape[1]
        per = hidden // width
        for m in range(bias_ref.shape[0]):
            for part in range(per):
                at = slice(part * width, (part + 1) * width)
                ref[160 + m * per + part : 161 + m * per + part, :] = bias_ref[m : m + 1, at]
                ref[168 + m * per + part : 169 + m * per + part, :] = out_ref[m : m + 1, at].astype(F32)
    values_ref[...] = qkv_ref[2]


def ensemble_kernel(feat_ref, w_ref, bias_ref, out_ref, pred_ref):
    total = None
    for m in range(w_ref.shape[0]):
        hidden = gelu(dot(feat_ref[...], w_ref[m]) + bias_ref[m : m + 1]).astype(BF)
        weights = jnp.broadcast_to(out_ref[m : m + 1], (8, out_ref.shape[1]))
        pred = dot_t(weights, hidden)[0:1]
        total = pred if total is None else total + pred
    pred_ref[...] = total


def stacker_kernel(
    n, half, blocks,
    *refs,
):
    feat_refs = refs[:blocks]
    (w0_ref, w1_ref, fw0_ref, fw1_ref, wv0_ref, wv1_ref, ow0_ref, ow1_ref, up0_ref, up1_ref,
     pk0_ref, pk1_ref, fbias_ref, scale_ref, shift_ref, cls_ref, gain_ref, fgain_ref, head_ref,
     *out_refs) = refs[blocks:]
    core = lax.axis_index("member")
    feats = jnp.concatenate([ref[...] for ref in feat_refs], axis=0)
    total, fwidth = feats.shape
    fhalf = fwidth // 2
    width = cls_ref.shape[1]
    local = wv0_ref.shape[1]
    here = w0_ref.shape[0]
    members = scale_ref.shape[0]
    hidden = w0_ref.shape[2]
    per = hidden // width
    token = iota((1, LANES), 1) // SLOT
    row_token = iota((LANES, 1), 0) // SLOT

    preds = jnp.zeros((total, LANES), F32)
    for side, w_ref, pk_ref in ((core, w0_ref, pk0_ref), (1 - core, w1_ref, pk1_ref)):
        for m in range(here):
            at = slice(160 + m * per, 160 + (m + 1) * per)
            bias = jnp.concatenate([pk_ref[160 + m * per + i : 161 + m * per + i, :] for i in range(per)], axis=1)
            outs = jnp.concatenate([pk_ref[168 + m * per + i : 169 + m * per + i, :] for i in range(per)], axis=1)
            act = gelu(dot(feats, w_ref[m]) + bias).astype(BF)
            spread = jnp.where(row_token == 2 + side * here + m, outs, 0.0).astype(BF)
            preds = preds + dot_t(act, spread)
    preds = preds.astype(BF).astype(F32)

    low, high = feats[:, :fhalf], feats[:, fhalf:]
    first = jnp.where(core == 0, low.astype(F32), high.astype(F32)).astype(BF)
    second = jnp.where(core == 0, high.astype(F32), low.astype(F32)).astype(BF)
    tok = dot(first, fw0_ref[...]) + dot(second, fw1_ref[...]) + fbias_ref[...]
    gain = gain_ref[...]
    centered = tok - jnp.mean(tok, axis=-1, keepdims=True)
    var = jnp.mean(centered * centered, axis=-1, keepdims=True)
    normed = (centered * lax.rsqrt(var + EPS) * gain).astype(BF)

    scale = scale_ref[...]
    shift = shift_ref[...]
    cscale = scale - jnp.mean(scale, axis=-1, keepdims=True)
    cshift = shift - jnp.mean(shift, axis=-1, keepdims=True)
    square = jnp.mean(cscale * cscale, axis=-1, keepdims=True)
    ratio = jnp.mean(cscale * cshift, axis=-1, keepdims=True) / jnp.maximum(square, 1e-30)
    rest = cshift - ratio * cscale
    rest = jnp.mean(rest * rest, axis=-1, keepdims=True)
    square_l = jnp.zeros((1, LANES), F32)
    ratio_l = jnp.zeros((1, LANES), F32)
    rest_l = jnp.zeros((1, LANES), F32)
    for m in range(members):
        on = token == 2 + m
        square_l = jnp.where(on, square[m : m + 1], square_l)
        ratio_l = jnp.where(on, ratio[m : m + 1], ratio_l)
        rest_l = jnp.where(on, rest[m : m + 1], rest_l)
    moved = preds + ratio_l
    inv = lax.rsqrt(square_l * moved * moved + rest_l + EPS)
    inv = jnp.where((token >= 2) & (token < 2 + members), inv, 0.0)
    times = inv * preds

    pk = pk0_ref[...] + pk1_ref[...]
    kmap = jnp.where(row_token == 1, pk[0:LANES], 0.0)
    khigh, klow = split(kmap)
    logits = dot_t(normed, khigh) + dot_t(normed, klow)
    logits = logits + pk[152:153, :LANES] + times * pk[153:154, :LANES] + inv * pk[154:155, :LANES]
    expo = jnp.where(token < 2 + members, jnp.exp(logits), 0.0)
    norm = expo
    for by in (SLOT, 2 * SLOT, 4 * SLOT):
        norm = norm + pltpu.roll(norm, by, 1)
    weights = expo / norm
    on_scale = jnp.where(token == 0, weights, weights * times)
    on_shift = weights * inv

    row_head = iota((LANES, 2 * local), 0) & (SLOT - 1)
    head_mask = row_head == iota((LANES, 2 * local), 1) // HD
    table = jnp.concatenate([pk0_ref[128:152, :local], pk1_ref[128:152, :local]], axis=1)
    vcls = table[0:1]
    map_scale = jnp.where(row_token == 0, vcls, 0.0)
    map_shift = jnp.zeros((LANES, 2 * local), F32)
    for m in range(members):
        map_scale = jnp.where(row_token == 2 + m, table[8 + m : 9 + m], map_scale)
        map_shift = jnp.where(row_token == 2 + m, table[16 + m : 17 + m], map_shift)
    map_scale = jnp.where(head_mask, map_scale, 0.0)
    map_shift = jnp.where(head_mask, map_shift, 0.0)
    expand = jnp.where(head_mask & (row_token == 1), 1.0, 0.0).astype(BF)
    maps = jnp.concatenate([map_scale, map_shift], axis=0)
    maps_high, maps_low = split(maps)
    coefs_high, coefs_low = split(jnp.concatenate([on_scale, on_shift], axis=1))
    fixed = dot(coefs_high, maps_high) + dot(coefs_low, maps_high) + dot(coefs_high, maps_low)
    w_high, w_low = split(weights)
    by_head = dot(w_high, expand) + dot(w_low, expand)
    value = jnp.concatenate([dot(normed, wv0_ref[...]), dot(normed, wv1_ref[...])], axis=1)
    mixed = (fixed + by_head * value).astype(BF)
    state = cls_ref[...] + dot(mixed[:, :local], ow0_ref[...]) + dot(mixed[:, local:], ow1_ref[...])

    centered = state - jnp.mean(state, axis=-1, keepdims=True)
    var = jnp.mean(centered * centered, axis=-1, keepdims=True)
    normed2 = (centered * lax.rsqrt(var + EPS) * fgain_ref[...]).astype(BF)
    terms = state * head_ref[...]
    for up_ref, pk_ref in ((up0_ref, pk0_ref), (up1_ref, pk1_ref)):
        upper = jnp.maximum(dot(normed2, up_ref[0]) + pk_ref[156:157], 0.0).astype(BF).astype(F32)
        terms = terms + upper * pk_ref[155:156]
    score = jnp.sum(terms, axis=-1, keepdims=True)

    if len(out_refs) > 1:
        eye = iota((half, LANES), 0) == iota((half, LANES), 1)
        for k, out in enumerate(out_refs):
            block = score[k * half : (k + 1) * half]
            out[...] = jnp.sum(jnp.where(eye, block, 0.0), axis=0, keepdims=True)
    else:
        eye = iota((total, total), 0) == iota((total, total), 1)
        out_refs[0][...] = jnp.sum(jnp.where(eye, score, 0.0), axis=0, keepdims=True)


def finish_kernel(members, where_ref, pred0_ref, pred1_ref, *refs):
    *score_refs, out_ref = refs
    count = where_ref.shape[0]
    lane_of = where_ref[:, 0:1]
    row_of = where_ref[:, 1:2]
    length = score_refs[0].shape[1]
    lanes = iota((count, length), 1)
    found = jnp.zeros((count, length), F32)
    for k, ref in enumerate(score_refs):
        found = jnp.where(lanes + k * length == lane_of, ref[...], found)
    score = jnp.sum(found, axis=1, keepdims=True)
    hit = row_of == iota((count, out_ref.shape[1]), 1)
    replaced = jnp.sum(jnp.where(hit, score, 0.0), axis=0, keepdims=True)
    taken = jnp.sum(hit.astype(F32), axis=0, keepdims=True)
    ensemble = (pred0_ref[...] + pred1_ref[...]) * (1.0 / members)
    out_ref[...] = jnp.where(taken > 0.0, replaced, ensemble)


def cost(flops, size, trans=0):
    return pl.CostEstimate(flops=flops, bytes_accessed=size, transcendentals=trans)


def params(mib):
    return pltpu.CompilerParams(vmem_limit_bytes=mib * 2**20)


def per_device(
    features, escalated, owner_ids, member_in, member_bias, member_out, feat_weight, feat_bias,
    pred_scale, pred_shift, cls_token, attn_gain, qkv_weight, out_weight, ffn_gain, up_weight,
    up_bias, down_weight, owner_heads,
):
    n = lax.axis_size("rows")
    rows, fwidth = features.shape
    count = escalated.shape[1]
    half = max(1, count // n)
    slots = n * half
    relative = n <= 16
    blocks = n if relative else 1
    here, _, hidden = member_in.shape
    members = pred_scale.shape[0]
    width = cls_token.shape[0]
    local = qkv_weight.shape[2]

    def swap(x):
        return lax.ppermute(x, "member", [(0, 1), (1, 0)])

    row = lambda x: x.reshape(1, -1)
    cls_token, attn_gain, ffn_gain, feat_bias = map(row, (cls_token, attn_gain, ffn_gain, feat_bias))

    other_in = swap(member_in)
    other_fw = swap(feat_weight)
    other_ow = swap(out_weight)
    other_up = swap(up_weight)

    where, *sent = pl.pallas_call(
        functools.partial(route_kernel, n, half, relative),
        out_shape=[jax.ShapeDtypeStruct((count, 2), jnp.int32)]
        + [jax.ShapeDtypeStruct((slots // blocks, fwidth), BF)] * blocks,
        in_specs=[VMEM] * 3,
        out_specs=[VMEM] * (1 + blocks),
        compiler_params=params(16),
        cost_estimate=cost(2 * slots * rows * fwidth, 2 * rows * fwidth),
        name="route",
    )(escalated, owner_ids, features)

    if relative:
        got = [sent[0]] + [
            lax.ppermute(sent[k], "rows", [(i, (i + k) % n) for i in range(n)]) for k in range(1, n)
        ]
    else:
        got = [
            lax.all_to_all(
                sent[0].reshape(n, half, fwidth), "rows", split_axis=0, concat_axis=0, tiled=True
            ).reshape(slots, fwidth)
        ]

    mine, other, values = pl.pallas_call(
        constants_kernel,
        out_shape=[jax.ShapeDtypeStruct((176, width), F32)] * 2
        + [jax.ShapeDtypeStruct((width, local), BF)],
        in_specs=[VMEM] * 10,
        out_specs=[VMEM] * 3,
        compiler_params=params(16),
        cost_estimate=cost(10**8, 2 * 10**6),
        name="constants",
    )(cls_token, attn_gain, qkv_weight, pred_scale, pred_shift, member_bias, member_out, up_bias,
      down_weight, owner_heads)
    other_pk = swap(other)
    other_wv = swap(values)

    tile = min(rows, 256)
    pred = pl.pallas_call(
        ensemble_kernel,
        grid=(rows // tile,),
        out_shape=jax.ShapeDtypeStruct((1, rows), F32),
        in_specs=[
            pl.BlockSpec((tile, fwidth), lambda i: (i, 0)),
            pl.BlockSpec(member_in.shape, lambda i: (0, 0, 0)),
            pl.BlockSpec(member_bias.shape, lambda i: (0, 0)),
            pl.BlockSpec(member_out.shape, lambda i: (0, 0)),
        ],
        out_specs=pl.BlockSpec((1, tile), lambda i: (0, i)),
        compiler_params=params(24),
        cost_estimate=cost(2 * here * rows * fwidth * hidden, 4 * 10**6, here * rows * hidden),
        name="ensemble",
    )(features, member_in, member_bias, member_out)
    other_pred = swap(pred)

    scores = pl.pallas_call(
        functools.partial(stacker_kernel, n, half, blocks),
        out_shape=[jax.ShapeDtypeStruct((1, LANES if relative else slots), F32)] * blocks,
        in_specs=[VMEM] * (blocks + 19),
        out_specs=[VMEM] * blocks,
        compiler_params=params(32),
        cost_estimate=cost(2 * 2 * here * slots * fwidth * hidden, 8 * 10**6, 2 * here * slots * hidden),
        name="stacker",
    )(*got, member_in, other_in, feat_weight, other_fw, values, other_wv, out_weight, other_ow,
      up_weight, other_up, mine, other_pk, feat_bias, pred_scale, pred_shift, cls_token, attn_gain,
      ffn_gain, owner_heads)

    if relative:
        back = [scores[0]]
        far = [swap(scores[0])]
        for k in range(1, n):
            back.append(lax.ppermute(scores[k], "rows", [(i, (i - k) % n) for i in range(n)]))
            far.append(
                lax.ppermute(
                    scores[k], ("rows", "member"),
                    [(2 * i + c, 2 * ((i - k) % n) + 1 - c) for i in range(n) for c in range(2)],
                )
            )
        returned = back + far
    else:
        back = lax.all_to_all(
            scores[0].reshape(n, half), "rows", split_axis=0, concat_axis=0, tiled=True
        ).reshape(1, slots)
        returned = [back, swap(back)]

    final = pl.pallas_call(
        functools.partial(finish_kernel, members),
        out_shape=jax.ShapeDtypeStruct((1, rows), F32),
        in_specs=[VMEM] * (3 + len(returned)),
        out_specs=VMEM,
        compiler_params=params(8),
        cost_estimate=cost(10**6, 10**6),
        name="finish",
    )(where, pred, other_pred, *returned)
    return final.reshape(rows)


def solution(mesh):
    placed = (
        P(("groups", "rows"), None),
        P(("groups", "rows"), None),
        P(("groups", "rows"), None, None),
        P("member", None, None),
        P("member", None),
        P("member", None),
        P("member", None),
        P(),
        P(),
        P(),
        P(),
        P(),
        P(None, None, "member"),
        P("member", None),
        P(),
        P("rows", None, "member"),
        P("rows", "member"),
        P("rows", "member", None),
        P("rows", None),
    )
    return jax.shard_map(
        per_device, mesh=mesh, in_specs=placed, out_specs=P(("groups", "rows")), check_vma=False
    )
```

```python
import functools
import math

import jax
import jax.numpy as jnp
from jax import lax
from jax.experimental import pallas as pl
from jax.experimental.pallas import tpu as pltpu
from jax.sharding import PartitionSpec as P

HD = 64
EPS = 1e-05
LANES = 128
BF = jnp.bfloat16
F32 = jnp.float32
VMEM = pl.BlockSpec(memory_space=pltpu.VMEM)
HBM = pl.BlockSpec(memory_space=pltpu.HBM)
GELU_C = math.sqrt(2.0 / math.pi)

KMAP, VCLS, LCLS, SCALE, SHIFT, GAIN, FBIAS, CLS, FGAIN, HEAD = 0, 8, 9, 16, 24, 32, 33, 34, 35, 36
TABLE = 40


def iota(shape, dim):
    return lax.broadcasted_iota(jnp.int32, shape, dim)


def gelu2(x):
    return x + x * jnp.tanh(x * (GELU_C + (GELU_C * 0.044715) * (x * x)))


def dot(a, b):
    return lax.dot_general(a, b, (((1,), (0,)), ((), ())), preferred_element_type=F32)


def dot_t(a, b):
    return lax.dot_general(a, b, (((1,), (1,)), ((), ())), preferred_element_type=F32)


def split2(x):
    high = x.astype(BF)
    return high, (x - high.astype(F32)).astype(BF)


def split3(x):
    high, rest = x.astype(BF), x
    rest = rest - high.astype(F32)
    mid = rest.astype(BF)
    low = (rest - mid.astype(F32)).astype(BF)
    return jnp.concatenate([high.astype(F32), mid.astype(F32), low.astype(F32)], axis=0).astype(BF)


def join3(x):
    rows = x.shape[0] // 3
    return x[:rows] + x[rows : 2 * rows] + x[2 * rows :]


def centre(x):
    return x - jnp.mean(x, axis=-1, keepdims=True)


def inverse_spread(centered):
    return lax.rsqrt(jnp.mean(centered * centered, axis=-1, keepdims=True) + EPS)


def start_all(pairs, sems):
    copies = [pltpu.make_async_copy(src, dst, sems.at[i]) for i, (src, dst) in enumerate(pairs)]
    for copy in copies:
        copy.start()
    return copies


def route_kernel(
    n, half, esc_hbm, own_hbm, feat_hbm, w_hbm, bias_hbm, out_hbm,
    where_ref, place_ref, rows_ref, near_ref, far_ref,
    esc_ref, own_ref, feat_ref, w_ref, bias_ref, out_ref, sems,
):
    copies = start_all(
        [(esc_hbm, esc_ref), (own_hbm, own_ref), (feat_hbm, feat_ref), (bias_hbm, bias_ref), (out_hbm, out_ref)]
        + [(w_hbm.at[m], w_ref.at[m]) for m in range(w_hbm.shape[0])], sems)
    core = lax.axis_index("member")
    count = esc_hbm.shape[1]
    dealt = count // 2
    copies[0].wait()
    copies[1].wait()
    esc = esc_ref[...]
    own = own_ref[...]
    ii = iota((count, count), 0)
    jj = iota((count, count), 1)
    diag = ii == jj

    def to_col(row):
        return jnp.sum(jnp.where(diag, row, 0).astype(F32), axis=1, keepdims=True)

    own_col = to_col(own).astype(jnp.int32)
    before = jnp.sum((own_col < own).astype(F32), axis=0, keepdims=True).astype(jnp.int32)
    rank = jnp.sum(((own_col == own) & (ii < jj)).astype(F32), axis=0, keepdims=True).astype(jnp.int32)
    position = before + rank
    side = position & 1
    slot = rank >> 1
    place = own * half + slot
    dense = (position >> 1) + jnp.where(side == core, 0, dealt)
    where_ref[:, 0:1] = to_col(own * 2 + side).astype(jnp.int32)
    where_ref[:, 1:2] = to_col(slot).astype(jnp.int32)
    where_ref[:, 2:3] = to_col(esc).astype(jnp.int32)

    mine = dense == ii
    source = jnp.sum(jnp.where(mine, esc, 0).astype(F32), axis=1, keepdims=True).astype(jnp.int32)
    place_col = jnp.sum(jnp.where(mine, place, 0).astype(F32), axis=1, keepdims=True)
    place_ref[...] = jnp.sum(
        jnp.where(diag[:dealt, :dealt], place_col[:dealt], 0.0), axis=0, keepdims=True
    ).astype(jnp.int32)
    chosen = (source == iota((count, feat_ref.shape[0]), 1)).astype(F32).astype(BF)
    copies[2].wait()
    rows = dot(chosen, feat_ref[...]).astype(BF)
    rows_ref[...] = rows[:dealt]
    copies[3].wait()
    copies[4].wait()
    here = w_hbm.shape[0]
    lane = iota((LANES, 1), 0)
    preds = None
    for m in range(here):
        copies[5 + m].wait()
        act = gelu2(dot(rows, w_ref[m]) + bias_ref[m : m + 1]).astype(BF)
        on_lane = jnp.where(lane == core * here + m, 0.5 * out_ref[m : m + 1].astype(F32), 0.0).astype(BF)
        pred = dot_t(act, on_lane)
        preds = pred if preds is None else preds + pred
    preds = preds.astype(BF)
    near_ref[...] = preds[:dealt]
    far_ref[...] = preds[dealt:]


def constants_kernel(*refs):
    hbm, (table_ref, half_ref), vmem, sems = refs[:11], refs[11:13], refs[13:-1], refs[-1]
    copies = start_all(list(zip(hbm, vmem)), sems)
    (cls_ref, gain_ref, scale_ref, shift_ref, fbias_ref, fgain_ref, head_ref, upb_ref,
     q0_ref, q1_ref, down_ref) = vmem
    for copy in copies[:8]:
        copy.wait()
    gain = gain_ref[...]
    cls = cls_ref[...]
    centered = centre(cls)
    ncls = (centered * inverse_spread(centered) * gain).astype(BF)
    table_ref[...] = jnp.zeros_like(table_ref)
    members = scale_ref.shape[0]
    table_ref[SCALE : SCALE + members, :] = centre(scale_ref[...])
    table_ref[SHIFT : SHIFT + members, :] = centre(shift_ref[...])
    table_ref[GAIN : GAIN + 1, :] = gain
    table_ref[FBIAS : FBIAS + 1, :] = fbias_ref[...]
    table_ref[CLS : CLS + 1, :] = cls
    table_ref[FGAIN : FGAIN + 1, :] = fgain_ref[...]
    table_ref[HEAD : HEAD + 1, :] = head_ref[...]
    half_ref[...] = jnp.zeros_like(half_ref)
    half_ref[1:2, :] = upb_ref[...]
    for copy in copies[8:]:
        copy.wait()
    lhs = jnp.broadcast_to(ncls.astype(F32), (8, ncls.shape[1])).astype(BF)
    local = q0_ref.shape[2]
    heads = local // HD
    row = iota((8, local), 0)
    col = iota((8, local), 1) // HD
    kmap = None
    for i, ref in enumerate((q0_ref, q1_ref)):
        query = dot(lhs, ref[0]) * (1.0 / math.sqrt(HD))
        spread = jnp.where(row == col + i * heads, query, 0.0)
        part = join3(dot_t(split3(spread), ref[1]))
        kmap = part if kmap is None else kmap + part
        table_ref[VCLS : VCLS + 1, i * local : (i + 1) * local] = dot(lhs, ref[2])[0:1]
    table_ref[KMAP : KMAP + 8, :] = kmap
    logits = jnp.sum(kmap * ncls.astype(F32), axis=-1, keepdims=True)
    eye = iota((8, LANES), 0) == iota((8, LANES), 1)
    table_ref[LCLS : LCLS + 1, :LANES] = jnp.sum(jnp.where(eye, logits, 0.0), axis=0, keepdims=True)
    head = jnp.broadcast_to(head_ref[...], (8, head_ref.shape[1]))
    half_ref[0:1, :] = join3(dot_t(split3(head), down_ref[0]))[0:1]


def attend_kernel(
    rows_ref, near_ref, far_ref, place_ref, table_ref, fw0_ref, fw1_ref, q0_ref, q1_ref, sent_ref
):
    core = lax.axis_index("member")
    rows = rows_ref[...]
    total, fwidth = rows.shape
    local = q0_ref.shape[2]
    members = 4
    gain = table_ref[GAIN : GAIN + 1, :]
    low, high = rows[:, : fwidth // 2].astype(F32), rows[:, fwidth // 2 :].astype(F32)
    first = jnp.where(core == 0, low, high).astype(BF)
    second = jnp.where(core == 0, high, low).astype(BF)
    token = dot(first, fw0_ref[...]) + dot(second, fw1_ref[...]) + table_ref[FBIAS : FBIAS + 1, :]
    centered = centre(token)
    tokens = [(centered * inverse_spread(centered) * gain).astype(BF)]
    preds = near_ref[...].astype(F32) + far_ref[...].astype(F32)
    for m in range(members):
        centered = preds[:, m : m + 1] * table_ref[SCALE + m : SCALE + m + 1, :] + table_ref[SHIFT + m : SHIFT + m + 1, :]
        tokens.append((centered * inverse_spread(centered) * gain).astype(BF))
    normed = jnp.concatenate(tokens, axis=0)
    count = len(tokens)

    kmap = jnp.concatenate([table_ref[KMAP : KMAP + 8, :], jnp.zeros((LANES - 8, table_ref.shape[1]), F32)], axis=0)
    khigh, klow = split2(kmap)
    logits = dot_t(normed, khigh) + dot_t(normed, klow)
    expo = jnp.exp(logits)
    expo_cls = jnp.exp(table_ref[LCLS : LCLS + 1, :LANES])
    norm = expo_cls
    for t in range(count):
        norm = norm + expo[t * total : (t + 1) * total]
    inverse = 1.0 / norm
    weights = jnp.concatenate(
        [expo[t * total : (t + 1) * total] * inverse for t in range(count)] + [expo_cls * inverse], axis=0)
    expand = (iota((LANES, 2 * local), 0) == iota((LANES, 2 * local), 1) // HD).astype(F32).astype(BF)
    w_high, w_low = split2(weights)
    spread = dot(w_high, expand) + dot(w_low, expand)
    parts = []
    for i, ref in enumerate((q0_ref, q1_ref)):
        at = slice(i * local, (i + 1) * local)
        value = dot(normed, ref[2])
        mixed = spread[count * total :, at] * table_ref[VCLS : VCLS + 1, at]
        for t in range(count):
            rng = slice(t * total, (t + 1) * total)
            mixed = mixed + spread[rng, at] * value[rng]
        parts.append(mixed)
    mixed = jnp.concatenate(parts, axis=1).astype(BF)
    slots = sent_ref.shape[0]
    scatter = (place_ref[...] == iota((slots, total), 0)).astype(F32).astype(BF)
    sent_ref[...] = dot(scatter, mixed).astype(BF)


def ensemble_kernel(feat_ref, w_ref, bias_ref, out_ref, pred_ref):
    total = None
    for m in range(w_ref.shape[0]):
        hidden = gelu2(dot(feat_ref[...], w_ref[m]) + bias_ref[m : m + 1]).astype(BF)
        weights = jnp.broadcast_to(out_ref[m : m + 1].astype(F32), (8, out_ref.shape[1])).astype(BF)
        pred = dot_t(weights, hidden)[0:1]
        total = pred if total is None else total + pred
    pred_ref[...] = total


def score_kernel(got_ref, ow0_ref, ow1_ref, up0_ref, up1_ref, half0_ref, half1_ref, table_ref, out_ref):
    mixed = got_ref[...]
    local = ow0_ref.shape[0]
    total = mixed.shape[0]
    state = table_ref[CLS : CLS + 1, :] + dot(mixed[:, :local], ow0_ref[...]) + dot(mixed[:, local:], ow1_ref[...])
    centered = centre(state)
    normed = (centered * inverse_spread(centered) * table_ref[FGAIN : FGAIN + 1, :]).astype(BF)
    terms = state * table_ref[HEAD : HEAD + 1, :]
    for up_ref, half_ref in ((up0_ref, half0_ref), (up1_ref, half1_ref)):
        upper = jnp.maximum(dot(normed, up_ref[0]) + half_ref[1:2, :], 0.0).astype(BF).astype(F32)
        terms = terms + upper * half_ref[0:1, :]
    score = jnp.sum(terms, axis=-1, keepdims=True)
    eye = iota((total, total), 0) == iota((total, total), 1)
    out_ref[...] = jnp.sum(jnp.where(eye, score, 0.0), axis=0, keepdims=True)


def finish_kernel(members, half, where_ref, pred0_ref, pred1_ref, all_ref, out_ref):
    me = lax.axis_index("rows")
    count = where_ref.shape[0]
    sources, length = all_ref.shape
    pick = (where_ref[:, 0:1] == iota((count, sources), 1)).astype(F32).astype(BF)
    parts = dot(jnp.concatenate([pick] * 3, axis=1), split3(all_ref[...]))
    lane = where_ref[:, 1:2] + me * half
    score = jnp.sum(jnp.where(lane == iota((count, length), 1), parts, 0.0), axis=1, keepdims=True)
    hit = where_ref[:, 2:3] == iota((count, out_ref.shape[1]), 1)
    replaced = jnp.sum(jnp.where(hit, score, 0.0), axis=0, keepdims=True)
    taken = jnp.sum(hit.astype(F32), axis=0, keepdims=True)
    ensemble = (pred0_ref[...] + pred1_ref[...]) * (0.5 / members)
    out_ref[...] = jnp.where(taken > 0.0, replaced, ensemble)


def cost(flops, size, trans=0):
    return pl.CostEstimate(flops=flops, bytes_accessed=size, transcendentals=trans)


def params(mib):
    return pltpu.CompilerParams(vmem_limit_bytes=mib * 2**20)


def shape(dims, dtype):
    return jax.ShapeDtypeStruct(dims, dtype)


def per_device(
    features, escalated, owner_ids, member_in, member_bias, member_out, feat_weight, feat_bias,
    pred_scale, pred_shift, cls_token, attn_gain, qkv_weight, out_weight, ffn_gain, up_weight,
    up_bias, down_weight, owner_heads,
):
    n = lax.axis_size("rows")
    rows, fwidth = features.shape
    count = escalated.shape[1]
    half = max(1, count // n)
    slots = n * half
    here, _, hidden = member_in.shape
    members = pred_scale.shape[0]
    width = cls_token.shape[0]

    def swap(x):
        return lax.ppermute(x, "member", [(0, 1), (1, 0)])

    row = lambda x: x.reshape(1, -1)
    cls_token, attn_gain, ffn_gain, feat_bias = map(row, (cls_token, attn_gain, ffn_gain, feat_bias))
    owners = owner_ids.reshape(1, count)

    other_qkv = swap(qkv_weight)
    other_fw = swap(feat_weight)
    other_ow = swap(out_weight)
    other_up = swap(up_weight)

    dealt = count // 2
    ins = (escalated, owners, features, member_in, member_bias, member_out)
    where, place, mine, near, far = pl.pallas_call(
        functools.partial(route_kernel, n, half),
        out_shape=[shape((count, 4), jnp.int32), shape((1, dealt), jnp.int32), shape((dealt, fwidth), BF),
                   shape((dealt, LANES), BF), shape((dealt, LANES), BF)],
        in_specs=[HBM] * 6,
        out_specs=[VMEM] * 5,
        scratch_shapes=[pltpu.VMEM(x.shape, x.dtype) for x in ins] + [pltpu.SemaphoreType.DMA((5 + here,))],
        compiler_params=params(24),
        cost_estimate=cost(2 * count * rows * fwidth + 2 * here * count * fwidth * hidden, 3 * 10**6,
                           here * count * hidden),
        name="route",
    )(*ins)
    far = swap(far)

    ins = (cls_token, attn_gain, pred_scale, pred_shift, feat_bias, ffn_gain, owner_heads, up_bias,
           qkv_weight, other_qkv, down_weight)
    table, halves = pl.pallas_call(
        constants_kernel,
        out_shape=[shape((TABLE, width), F32), shape((8, up_bias.shape[1]), F32)],
        in_specs=[HBM] * len(ins),
        out_specs=[VMEM] * 2,
        scratch_shapes=[pltpu.VMEM(x.shape, x.dtype) for x in ins] + [pltpu.SemaphoreType.DMA((len(ins),))],
        compiler_params=params(16),
        cost_estimate=cost(10**8, 2 * 10**6),
        name="constants",
    )(*ins)
    other_halves = swap(halves)

    sent = pl.pallas_call(
        attend_kernel,
        out_shape=shape((slots, 2 * qkv_weight.shape[2]), BF),
        in_specs=[VMEM] * 9,
        out_specs=VMEM,
        compiler_params=params(24),
        cost_estimate=cost(10**9, 2 * 10**6),
        name="attend",
    )(mine, near, far, place, table, feat_weight, other_fw, qkv_weight, other_qkv)

    got = lax.all_to_all(
        sent.reshape(n, half, sent.shape[1]), "rows", split_axis=0, concat_axis=0, tiled=True
    ).reshape(slots, sent.shape[1])

    tile = min(rows, 256)
    pred = pl.pallas_call(
        ensemble_kernel,
        grid=(rows // tile,),
        out_shape=shape((1, rows), F32),
        in_specs=[
            pl.BlockSpec((tile, fwidth), lambda i: (i, 0)),
            pl.BlockSpec(member_in.shape, lambda i: (0, 0, 0)),
            pl.BlockSpec(member_bias.shape, lambda i: (0, 0)),
            pl.BlockSpec(member_out.shape, lambda i: (0, 0)),
        ],
        out_specs=pl.BlockSpec((1, tile), lambda i: (0, i)),
        compiler_params=params(24),
        cost_estimate=cost(2 * here * rows * fwidth * hidden, 4 * 10**6, here * rows * hidden),
        name="ensemble",
    )(features, member_in, member_bias, member_out)
    other_pred = swap(pred)

    scores = pl.pallas_call(
        score_kernel,
        out_shape=shape((1, slots), F32),
        in_specs=[VMEM] * 8,
        out_specs=VMEM,
        compiler_params=params(24),
        cost_estimate=cost(10**9, 2 * 10**6),
        name="score",
    )(got, out_weight, other_ow, up_weight, other_up, halves, other_halves, table)
    everyone = lax.all_gather(scores, ("rows", "member"), axis=0, tiled=True)

    final = pl.pallas_call(
        functools.partial(finish_kernel, members, half),
        out_shape=shape((1, rows), F32),
        in_specs=[VMEM] * 4,
        out_specs=VMEM,
        compiler_params=params(8),
        cost_estimate=cost(10**6, 10**6),
        name="finish",
    )(where, pred, other_pred, everyone)
    return final.reshape(rows)


def solution(mesh):
    placed = (
        P(("groups", "rows"), None),
        P(("groups", "rows"), None),
        P(("groups", "rows"), None, None),
        P("member", None, None),
        P("member", None),
        P("member", None),
        P("member", None),
        P(),
        P(),
        P(),
        P(),
        P(),
        P(None, None, "member"),
        P("member", None),
        P(),
        P("rows", None, "member"),
        P("rows", "member"),
        P("rows", "member", None),
        P("rows", None),
    )
    return jax.shard_map(
        per_device, mesh=mesh, in_specs=placed, out_specs=P(("groups", "rows")), check_vma=False
    )
```

```python
import functools
import math

import jax
import jax.numpy as jnp
from jax import lax
from jax.experimental import pallas as pl
from jax.experimental.pallas import tpu as pltpu
from jax.sharding import PartitionSpec as P

HD = 64
EPS = 1e-05
LANES = 128
BF = jnp.bfloat16
F32 = jnp.float32
VMEM = pl.BlockSpec(memory_space=pltpu.VMEM)
HBM = pl.BlockSpec(memory_space=pltpu.HBM)
GELU_C = math.sqrt(2.0 / math.pi)

KMAP, VCLS, LCLS, SCALE, SHIFT, GAIN, FBIAS, CLS, FGAIN, HEAD = 0, 8, 9, 16, 24, 32, 33, 34, 35, 36
TABLE = 40


def iota(shape, dim):
    return lax.broadcasted_iota(jnp.int32, shape, dim)


def gelu2(x):
    return x + x * jnp.tanh(x * (GELU_C + (GELU_C * 0.044715) * (x * x)))


def dot(a, b):
    return lax.dot_general(a, b, (((1,), (0,)), ((), ())), preferred_element_type=F32)


def dot_t(a, b):
    return lax.dot_general(a, b, (((1,), (1,)), ((), ())), preferred_element_type=F32)


def split2(x):
    high = x.astype(BF)
    return high, (x - high.astype(F32)).astype(BF)


def split3(x):
    high, rest = x.astype(BF), x
    rest = rest - high.astype(F32)
    mid = rest.astype(BF)
    low = (rest - mid.astype(F32)).astype(BF)
    return jnp.concatenate([high.astype(F32), mid.astype(F32), low.astype(F32)], axis=0).astype(BF)


def join3(x):
    rows = x.shape[0] // 3
    return x[:rows] + x[rows : 2 * rows] + x[2 * rows :]


def centre(x):
    return x - jnp.mean(x, axis=-1, keepdims=True)


def inverse_spread(centered):
    return lax.rsqrt(jnp.mean(centered * centered, axis=-1, keepdims=True) + EPS)


def start_all(pairs, sems):
    copies = [pltpu.make_async_copy(src, dst, sems.at[i]) for i, (src, dst) in enumerate(pairs)]
    for copy in copies:
        copy.start()
    return copies


def route_kernel(
    n, half, esc_hbm, own_hbm, feat_hbm, w_hbm, bias_hbm, out_hbm,
    where_ref, place_ref, rows_ref, near_ref, far_ref,
    esc_ref, own_ref, feat_ref, w_ref, bias_ref, out_ref, sems,
):
    copies = start_all(
        [(esc_hbm, esc_ref), (own_hbm, own_ref), (feat_hbm, feat_ref), (bias_hbm, bias_ref), (out_hbm, out_ref)]
        + [(w_hbm.at[m], w_ref.at[m]) for m in range(w_hbm.shape[0])], sems)
    core = lax.axis_index("member")
    count = esc_hbm.shape[1]
    dealt = count // 2
    copies[0].wait()
    copies[1].wait()
    esc = esc_ref[...]
    own = own_ref[...]
    ii = iota((count, count), 0)
    jj = iota((count, count), 1)
    diag = ii == jj

    def to_col(row):
        return jnp.sum(jnp.where(diag, row, 0).astype(F32), axis=1, keepdims=True)

    own_col = to_col(own).astype(jnp.int32)
    before = jnp.sum((own_col < own).astype(F32), axis=0, keepdims=True).astype(jnp.int32)
    rank = jnp.sum(((own_col == own) & (ii < jj)).astype(F32), axis=0, keepdims=True).astype(jnp.int32)
    position = before + rank
    side = position & 1
    slot = rank >> 1
    place = own * half + slot
    dense = (position >> 1) + jnp.where(side == core, 0, dealt)
    where_ref[:, 0:1] = to_col((own ^ lax.axis_index("rows")) * 2 + (side ^ core)).astype(jnp.int32)
    where_ref[:, 1:2] = to_col(slot).astype(jnp.int32)
    where_ref[:, 2:3] = to_col(esc).astype(jnp.int32)

    mine = dense == ii
    source = jnp.sum(jnp.where(mine, esc, 0).astype(F32), axis=1, keepdims=True).astype(jnp.int32)
    place_col = jnp.sum(jnp.where(mine, place, 0).astype(F32), axis=1, keepdims=True)
    place_ref[...] = jnp.sum(
        jnp.where(diag[:dealt, :dealt], place_col[:dealt], 0.0), axis=0, keepdims=True
    ).astype(jnp.int32)
    chosen = (source == iota((count, feat_ref.shape[0]), 1)).astype(F32).astype(BF)
    copies[2].wait()
    rows = dot(chosen, feat_ref[...]).astype(BF)
    rows_ref[...] = rows[:dealt]
    copies[3].wait()
    copies[4].wait()
    here = w_hbm.shape[0]
    lane = iota((LANES, 1), 0)
    preds = None
    for m in range(here):
        copies[5 + m].wait()
        act = gelu2(dot(rows, w_ref[m]) + bias_ref[m : m + 1]).astype(BF)
        on_lane = jnp.where(lane == core * here + m, 0.5 * out_ref[m : m + 1].astype(F32), 0.0).astype(BF)
        pred = dot_t(act, on_lane)
        preds = pred if preds is None else preds + pred
    preds = preds.astype(BF)
    near_ref[...] = preds[:dealt]
    far_ref[...] = preds[dealt:]


def constants_kernel(*refs):
    hbm, (table_ref, half_ref), vmem, sems = refs[:11], refs[11:13], refs[13:-1], refs[-1]
    copies = start_all(list(zip(hbm, vmem)), sems)
    (cls_ref, gain_ref, scale_ref, shift_ref, fbias_ref, fgain_ref, head_ref, upb_ref,
     q0_ref, q1_ref, down_ref) = vmem
    for copy in copies[:8]:
        copy.wait()
    gain = gain_ref[...]
    cls = cls_ref[...]
    centered = centre(cls)
    ncls = (centered * inverse_spread(centered) * gain).astype(BF)
    table_ref[...] = jnp.zeros_like(table_ref)
    members = scale_ref.shape[0]
    table_ref[SCALE : SCALE + members, :] = centre(scale_ref[...])
    table_ref[SHIFT : SHIFT + members, :] = centre(shift_ref[...])
    table_ref[GAIN : GAIN + 1, :] = gain
    table_ref[FBIAS : FBIAS + 1, :] = fbias_ref[...]
    table_ref[CLS : CLS + 1, :] = cls
    table_ref[FGAIN : FGAIN + 1, :] = fgain_ref[...]
    table_ref[HEAD : HEAD + 1, :] = head_ref[...]
    half_ref[...] = jnp.zeros_like(half_ref)
    half_ref[1:2, :] = upb_ref[...]
    for copy in copies[8:]:
        copy.wait()
    lhs = jnp.broadcast_to(ncls.astype(F32), (8, ncls.shape[1])).astype(BF)
    local = q0_ref.shape[2]
    heads = local // HD
    row = iota((8, local), 0)
    col = iota((8, local), 1) // HD
    kmap = None
    for i, ref in enumerate((q0_ref, q1_ref)):
        query = dot(lhs, ref[0]) * (1.0 / math.sqrt(HD))
        spread = jnp.where(row == col + i * heads, query, 0.0)
        part = join3(dot_t(split3(spread), ref[1]))
        kmap = part if kmap is None else kmap + part
        table_ref[VCLS : VCLS + 1, i * local : (i + 1) * local] = dot(lhs, ref[2])[0:1]
    table_ref[KMAP : KMAP + 8, :] = kmap
    logits = jnp.sum(kmap * ncls.astype(F32), axis=-1, keepdims=True)
    eye = iota((8, LANES), 0) == iota((8, LANES), 1)
    table_ref[LCLS : LCLS + 1, :LANES] = jnp.sum(jnp.where(eye, logits, 0.0), axis=0, keepdims=True)
    head = jnp.broadcast_to(head_ref[...], (8, head_ref.shape[1]))
    half_ref[0:1, :] = join3(dot_t(split3(head), down_ref[0]))[0:1]


def attend_kernel(
    members, rows_ref, near_ref, far_ref, place_ref, table_ref, fw0_ref, fw1_ref, q0_ref, q1_ref, sent_ref
):
    core = lax.axis_index("member")
    rows = rows_ref[...]
    total, fwidth = rows.shape
    local = q0_ref.shape[2]
    gain = table_ref[GAIN : GAIN + 1, :]
    low, high = rows[:, : fwidth // 2].astype(F32), rows[:, fwidth // 2 :].astype(F32)
    first = jnp.where(core == 0, low, high).astype(BF)
    second = jnp.where(core == 0, high, low).astype(BF)
    token = dot(first, fw0_ref[...]) + dot(second, fw1_ref[...]) + table_ref[FBIAS : FBIAS + 1, :]
    centered = centre(token)
    tokens = [(centered * inverse_spread(centered) * gain).astype(BF)]
    preds = near_ref[...].astype(F32) + far_ref[...].astype(F32)
    for m in range(members):
        centered = preds[:, m : m + 1] * table_ref[SCALE + m : SCALE + m + 1, :] + table_ref[SHIFT + m : SHIFT + m + 1, :]
        tokens.append((centered * inverse_spread(centered) * gain).astype(BF))
    normed = jnp.concatenate(tokens, axis=0)
    count = len(tokens)

    kmap = jnp.concatenate([table_ref[KMAP : KMAP + 8, :], jnp.zeros((LANES - 8, table_ref.shape[1]), F32)], axis=0)
    khigh, klow = split2(kmap)
    logits = dot_t(normed, khigh) + dot_t(normed, klow)
    expo = jnp.exp(logits)
    expo_cls = jnp.exp(table_ref[LCLS : LCLS + 1, :LANES])
    norm = expo_cls
    for t in range(count):
        norm = norm + expo[t * total : (t + 1) * total]
    inverse = 1.0 / norm
    weights = jnp.concatenate(
        [expo[t * total : (t + 1) * total] * inverse for t in range(count)] + [expo_cls * inverse], axis=0)
    expand = (iota((LANES, 2 * local), 0) == iota((LANES, 2 * local), 1) // HD).astype(F32).astype(BF)
    w_high, w_low = split2(weights)
    spread = dot(w_high, expand) + dot(w_low, expand)
    parts = []
    for i, ref in enumerate((q0_ref, q1_ref)):
        at = slice(i * local, (i + 1) * local)
        value = dot(normed, ref[2])
        mixed = spread[count * total :, at] * table_ref[VCLS : VCLS + 1, at]
        for t in range(count):
            rng = slice(t * total, (t + 1) * total)
            mixed = mixed + spread[rng, at] * value[rng]
        parts.append(mixed)
    mixed = jnp.concatenate(parts, axis=1).astype(BF)
    slots = sent_ref.shape[0]
    scatter = (place_ref[...] == iota((slots, total), 0)).astype(F32).astype(BF)
    sent_ref[...] = dot(scatter, mixed).astype(BF)


def ensemble_kernel(feat_ref, w_ref, bias_ref, out_ref, pred_ref):
    total = None
    for m in range(w_ref.shape[0]):
        hidden = gelu2(dot(feat_ref[...], w_ref[m]) + bias_ref[m : m + 1]).astype(BF)
        weights = jnp.broadcast_to(out_ref[m : m + 1].astype(F32), (8, out_ref.shape[1])).astype(BF)
        pred = dot_t(weights, hidden)[0:1]
        total = pred if total is None else total + pred
    pred_ref[...] = total


def score_kernel(*refs):
    hbm, out_ref, vmem, sems = refs[:8], refs[8], refs[9:-1], refs[-1]
    got_ref, ow0_ref, ow1_ref, table_ref, up0_ref, up1_ref, half0_ref, half1_ref = vmem
    copies = start_all(list(zip(hbm, vmem)), sems)
    for copy in copies[:4]:
        copy.wait()
    mixed = got_ref[...]
    local = ow0_ref.shape[0]
    total = mixed.shape[0]
    state = table_ref[CLS : CLS + 1, :] + dot(mixed[:, :local], ow0_ref[...]) + dot(mixed[:, local:], ow1_ref[...])
    centered = centre(state)
    normed = (centered * inverse_spread(centered) * table_ref[FGAIN : FGAIN + 1, :]).astype(BF)
    terms = state * table_ref[HEAD : HEAD + 1, :]
    for copy in copies[4:]:
        copy.wait()
    for up_ref, half_ref in ((up0_ref, half0_ref), (up1_ref, half1_ref)):
        upper = jnp.maximum(dot(normed, up_ref[0]) + half_ref[1:2, :], 0.0).astype(BF).astype(F32)
        terms = terms + upper * half_ref[0:1, :]
    score = jnp.sum(terms, axis=-1, keepdims=True)
    eye = iota((total, total), 0) == iota((total, total), 1)
    out_ref[...] = jnp.sum(jnp.where(eye, score, 0.0), axis=0, keepdims=True)


def finish_kernel(members, half, where_ref, pred0_ref, pred1_ref, all_ref, out_ref):
    me = lax.axis_index("rows")
    count = where_ref.shape[0]
    sources, length = all_ref.shape
    pick = (where_ref[:, 0:1] == iota((count, sources), 1)).astype(F32).astype(BF)
    parts = dot(jnp.concatenate([pick] * 3, axis=1), split3(all_ref[...]))
    lane = where_ref[:, 1:2] + me * half
    score = jnp.sum(jnp.where(lane == iota((count, length), 1), parts, 0.0), axis=1, keepdims=True)
    hit = where_ref[:, 2:3] == iota((count, out_ref.shape[1]), 1)
    replaced = jnp.sum(jnp.where(hit, score, 0.0), axis=0, keepdims=True)
    taken = jnp.sum(hit.astype(F32), axis=0, keepdims=True)
    ensemble = (pred0_ref[...] + pred1_ref[...]) * (0.5 / members)
    out_ref[...] = jnp.where(taken > 0.0, replaced, ensemble)


def cost(flops, size, trans=0):
    return pl.CostEstimate(flops=flops, bytes_accessed=size, transcendentals=trans)


def params(mib):
    return pltpu.CompilerParams(vmem_limit_bytes=mib * 2**20)


def in_hbm(arrays):
    return [pltpu.with_memory_space_constraint(x, pltpu.HBM) for x in arrays]


def shape(dims, dtype):
    return jax.ShapeDtypeStruct(dims, dtype)


def per_device(
    features, escalated, owner_ids, member_in, member_bias, member_out, feat_weight, feat_bias,
    pred_scale, pred_shift, cls_token, attn_gain, qkv_weight, out_weight, ffn_gain, up_weight,
    up_bias, down_weight, owner_heads,
):
    n = lax.axis_size("rows")
    rows, fwidth = features.shape
    count = escalated.shape[1]
    half = max(1, count // n)
    slots = n * half
    here, _, hidden = member_in.shape
    members = pred_scale.shape[0]
    width = cls_token.shape[0]

    def swap(x):
        return lax.ppermute(x, "member", [(0, 1), (1, 0)])

    row = lambda x: x.reshape(1, -1)
    cls_token, attn_gain, ffn_gain, feat_bias = map(row, (cls_token, attn_gain, ffn_gain, feat_bias))
    owners = owner_ids.reshape(1, count)

    other_qkv = swap(qkv_weight)
    other_fw = swap(feat_weight)
    other_ow = swap(out_weight)
    other_up = swap(up_weight)

    dealt = count // 2
    ins = (escalated, owners, features, member_in, member_bias, member_out)
    where, place, mine, near, far = pl.pallas_call(
        functools.partial(route_kernel, n, half),
        out_shape=[shape((count, 4), jnp.int32), shape((1, dealt), jnp.int32), shape((dealt, fwidth), BF),
                   shape((dealt, LANES), BF), shape((dealt, LANES), BF)],
        in_specs=[HBM] * 6,
        out_specs=[VMEM] * 5,
        scratch_shapes=[pltpu.VMEM(x.shape, x.dtype) for x in ins] + [pltpu.SemaphoreType.DMA((5 + here,))],
        compiler_params=params(24),
        cost_estimate=cost(2 * count * rows * fwidth + 2 * here * count * fwidth * hidden, 3 * 10**6,
                           here * count * hidden),
        name="route",
    )(*in_hbm(ins))
    far = swap(far)

    ins = (cls_token, attn_gain, pred_scale, pred_shift, feat_bias, ffn_gain, owner_heads, up_bias,
           qkv_weight, other_qkv, down_weight)
    table, halves = pl.pallas_call(
        constants_kernel,
        out_shape=[shape((TABLE, width), F32), shape((8, up_bias.shape[1]), F32)],
        in_specs=[HBM] * len(ins),
        out_specs=[VMEM] * 2,
        scratch_shapes=[pltpu.VMEM(x.shape, x.dtype) for x in ins] + [pltpu.SemaphoreType.DMA((len(ins),))],
        compiler_params=params(16),
        cost_estimate=cost(10**8, 2 * 10**6),
        name="constants",
    )(*ins)
    other_halves = swap(halves)

    sent = pl.pallas_call(
        functools.partial(attend_kernel, members),
        out_shape=shape((slots, 2 * qkv_weight.shape[2]), BF),
        in_specs=[VMEM] * 9,
        out_specs=VMEM,
        compiler_params=params(24),
        cost_estimate=cost(10**9, 2 * 10**6),
        name="attend",
    )(mine, near, far, place, table, feat_weight, other_fw, qkv_weight, other_qkv)

    got = lax.all_to_all(
        sent.reshape(n, half, sent.shape[1]), "rows", split_axis=0, concat_axis=0, tiled=True
    ).reshape(slots, sent.shape[1])

    tile = min(rows, 256)
    pred = pl.pallas_call(
        ensemble_kernel,
        grid=(rows // tile,),
        out_shape=shape((1, rows), F32),
        in_specs=[
            pl.BlockSpec((tile, fwidth), lambda i: (i, 0)),
            pl.BlockSpec(member_in.shape, lambda i: (0, 0, 0)),
            pl.BlockSpec(member_bias.shape, lambda i: (0, 0)),
            pl.BlockSpec(member_out.shape, lambda i: (0, 0)),
        ],
        out_specs=pl.BlockSpec((1, tile), lambda i: (0, i)),
        compiler_params=params(24),
        cost_estimate=cost(2 * here * rows * fwidth * hidden, 4 * 10**6, here * rows * hidden),
        name="ensemble",
    )(features, member_in, member_bias, member_out)
    other_pred = swap(pred)

    ins = (got, out_weight, other_ow, table, up_weight, other_up, halves, other_halves)
    scores = pl.pallas_call(
        score_kernel,
        out_shape=shape((1, slots), F32),
        in_specs=[HBM] * len(ins),
        out_specs=VMEM,
        scratch_shapes=[pltpu.VMEM(x.shape, x.dtype) for x in ins] + [pltpu.SemaphoreType.DMA((len(ins),))],
        compiler_params=params(24),
        cost_estimate=cost(10**9, 2 * 10**6),
        name="score",
    )(*in_hbm(ins))
    everyone = jnp.concatenate([scores, swap(scores)], axis=0)
    step = 1
    while step < n:
        there = lax.ppermute(everyone, "rows", [(i, i ^ step) for i in range(n)])
        everyone = jnp.concatenate([everyone, there], axis=0)
        step *= 2

    final = pl.pallas_call(
        functools.partial(finish_kernel, members, half),
        out_shape=shape((1, rows), F32),
        in_specs=[VMEM] * 4,
        out_specs=VMEM,
        compiler_params=params(8),
        cost_estimate=cost(10**6, 10**6),
        name="finish",
    )(where, pred, other_pred, everyone)
    return final.reshape(rows)


def solution(mesh):
    placed = (
        P(("groups", "rows"), None),
        P(("groups", "rows"), None),
        P(("groups", "rows"), None, None),
        P("member", None, None),
        P("member", None),
        P("member", None),
        P("member", None),
        P(),
        P(),
        P(),
        P(),
        P(),
        P(None, None, "member"),
        P("member", None),
        P(),
        P("rows", None, "member"),
        P("rows", "member"),
        P("rows", "member", None),
        P("rows", None),
    )
    return jax.shard_map(
        per_device, mesh=mesh, in_specs=placed, out_specs=P(("groups", "rows")), check_vma=False
    )
```

```python
import functools
import math

import jax
import jax.numpy as jnp
from jax import lax
from jax.experimental import pallas as pl
from jax.experimental.pallas import tpu as pltpu
from jax.sharding import PartitionSpec as P

HD = 64
EPS = 1e-05
LANES = 128
BF = jnp.bfloat16
F32 = jnp.float32
VMEM = pl.BlockSpec(memory_space=pltpu.VMEM)
HBM = pl.BlockSpec(memory_space=pltpu.HBM)
GELU_C = math.sqrt(2.0 / math.pi)

KMAP, VCLS, LCLS, SCALE, SHIFT, GAIN, FBIAS, CLS, FGAIN = 0, 8, 9, 16, 24, 32, 33, 34, 35
TABLE = 40
DOWN, BIAS, HEAD, EXTRA = 0, 3, 6, 16


def iota(shape, dim):
    return lax.broadcasted_iota(jnp.int32, shape, dim)


def gelu2(x):
    return x + x * jnp.tanh(x * (GELU_C + (GELU_C * 0.044715) * (x * x)))


def dot(a, b):
    return lax.dot_general(a, b, (((1,), (0,)), ((), ())), preferred_element_type=F32)


def dot_t(a, b):
    return lax.dot_general(a, b, (((1,), (1,)), ((), ())), preferred_element_type=F32)


def split2(x):
    high = x.astype(BF)
    return high, (x - high.astype(F32)).astype(BF)


def split3(x):
    high, rest = x.astype(BF), x
    rest = rest - high.astype(F32)
    mid = rest.astype(BF)
    low = (rest - mid.astype(F32)).astype(BF)
    return jnp.concatenate([high.astype(F32), mid.astype(F32), low.astype(F32)], axis=0).astype(BF)


def join3(x):
    rows = x.shape[0] // 3
    return x[:rows] + x[rows : 2 * rows] + x[2 * rows :]


def centre(x):
    return x - jnp.mean(x, axis=-1, keepdims=True)


def inverse_spread(centered):
    return lax.rsqrt(jnp.mean(centered * centered, axis=-1, keepdims=True) + EPS)


def start_all(pairs, sems):
    copies = [pltpu.make_async_copy(src, dst, sems.at[i]) for i, (src, dst) in enumerate(pairs)]
    for copy in copies:
        copy.start()
    return copies


def route_kernel(
    n, half, relative, esc_hbm, own_hbm, feat_hbm, w_hbm, bias_hbm, out_hbm,
    where_ref, place_ref, rows_ref, near_ref, far_ref,
    esc_ref, own_ref, feat_ref, w_ref, bias_ref, out_ref, sems,
):
    copies = start_all(
        [(esc_hbm, esc_ref), (own_hbm, own_ref), (feat_hbm, feat_ref), (bias_hbm, bias_ref), (out_hbm, out_ref)]
        + [(w_hbm.at[m], w_ref.at[m]) for m in range(w_hbm.shape[0])], sems)
    core = lax.axis_index("member")
    count = esc_hbm.shape[1]
    dealt = count // 2
    copies[0].wait()
    copies[1].wait()
    esc = esc_ref[...]
    own = own_ref[...]
    ii = iota((count, count), 0)
    jj = iota((count, count), 1)
    diag = ii == jj

    def to_col(row):
        return jnp.sum(jnp.where(diag, row, 0).astype(F32), axis=1, keepdims=True)

    own_col = to_col(own).astype(jnp.int32)
    before = jnp.sum((own_col < own).astype(F32), axis=0, keepdims=True).astype(jnp.int32)
    rank = jnp.sum(((own_col == own) & (ii < jj)).astype(F32), axis=0, keepdims=True).astype(jnp.int32)
    position = before + rank
    side = position & 1
    slot = rank >> 1
    me = lax.axis_index("rows")
    apart = own ^ me
    pair = (apart if relative else (own - (own & 1)) + (apart & 1))
    place = pair * half + slot
    dense = (position >> 1) + jnp.where(side == core, 0, dealt)
    where_ref[:, 0:1] = to_col((pair >> 1) + (side ^ core) * (n // 2)).astype(jnp.int32)
    where_ref[:, 1:2] = to_col((apart & 1) * half + slot).astype(jnp.int32)
    where_ref[:, 2:3] = to_col(esc).astype(jnp.int32)

    mine = dense == ii
    source = jnp.sum(jnp.where(mine, esc, 0).astype(F32), axis=1, keepdims=True).astype(jnp.int32)
    place_col = jnp.sum(jnp.where(mine, place, 0).astype(F32), axis=1, keepdims=True)
    place_ref[...] = jnp.sum(
        jnp.where(diag[:dealt, :dealt], place_col[:dealt], 0.0), axis=0, keepdims=True
    ).astype(jnp.int32)
    chosen = (source == iota((count, feat_ref.shape[0]), 1)).astype(F32).astype(BF)
    copies[2].wait()
    rows = dot(chosen, feat_ref[...]).astype(BF)
    rows_ref[...] = rows[:dealt]
    copies[3].wait()
    copies[4].wait()
    here = w_hbm.shape[0]
    lane = iota((LANES, 1), 0)
    preds = None
    for m in range(here):
        copies[5 + m].wait()
        act = gelu2(dot(rows, w_ref[m]) + bias_ref[m : m + 1]).astype(BF)
        on_lane = jnp.where(lane == core * here + m, 0.5 * out_ref[m : m + 1].astype(F32), 0.0).astype(BF)
        pred = dot_t(act, on_lane)
        preds = pred if preds is None else preds + pred
    preds = preds.astype(BF)
    near_ref[...] = preds[:dealt]
    far_ref[...] = preds[dealt:]


def prepare_kernel(up_hbm, down_hbm, bias_hbm, head_hbm, out_ref, down_ref, bias_ref, head_ref, sems):
    depth = up_hbm.shape[1]
    copies = start_all(
        [(down_hbm, down_ref), (bias_hbm, bias_ref), (head_hbm, head_ref), (up_hbm.at[0], out_ref.at[:depth])], sems)
    for copy in copies[:3]:
        copy.wait()
    head = jnp.broadcast_to(head_ref[...], (8, head_ref.shape[1]))
    down = join3(dot_t(split3(head), down_ref[0]))[0:1]
    rows = [split3(x).astype(F32) for x in (down, bias_ref[...], head_ref[...])]
    rows.append(jnp.zeros((EXTRA - 9, down.shape[1]), F32))
    out_ref[depth:, :] = jnp.concatenate(rows, axis=0).astype(BF)
    copies[3].wait()


def constants_kernel(*refs):
    hbm, table_ref, vmem, sems = refs[:8], refs[8], refs[9:-1], refs[-1]
    copies = start_all(list(zip(hbm, vmem)), sems)
    cls_ref, gain_ref, scale_ref, shift_ref, fbias_ref, fgain_ref, q0_ref, q1_ref = vmem
    for copy in copies[:6]:
        copy.wait()
    gain = gain_ref[...]
    cls = cls_ref[...]
    centered = centre(cls)
    ncls = (centered * inverse_spread(centered) * gain).astype(BF)
    table_ref[...] = jnp.zeros_like(table_ref)
    members = scale_ref.shape[0]
    table_ref[SCALE : SCALE + members, :] = centre(scale_ref[...])
    table_ref[SHIFT : SHIFT + members, :] = centre(shift_ref[...])
    table_ref[GAIN : GAIN + 1, :] = gain
    table_ref[FBIAS : FBIAS + 1, :] = fbias_ref[...]
    table_ref[CLS : CLS + 1, :] = cls
    table_ref[FGAIN : FGAIN + 1, :] = fgain_ref[...]
    for copy in copies[6:]:
        copy.wait()
    lhs = jnp.broadcast_to(ncls.astype(F32), (8, ncls.shape[1])).astype(BF)
    local = q0_ref.shape[2]
    heads = local // HD
    row = iota((8, local), 0)
    col = iota((8, local), 1) // HD
    kmap = None
    for i, ref in enumerate((q0_ref, q1_ref)):
        query = dot(lhs, ref[0]) * (1.0 / math.sqrt(HD))
        spread = jnp.where(row == col + i * heads, query, 0.0)
        part = join3(dot_t(split3(spread), ref[1]))
        kmap = part if kmap is None else kmap + part
        table_ref[VCLS : VCLS + 1, i * local : (i + 1) * local] = dot(lhs, ref[2])[0:1]
    table_ref[KMAP : KMAP + 8, :] = kmap
    logits = jnp.sum(kmap * ncls.astype(F32), axis=-1, keepdims=True)
    eye = iota((8, LANES), 0) == iota((8, LANES), 1)
    table_ref[LCLS : LCLS + 1, :LANES] = jnp.sum(jnp.where(eye, logits, 0.0), axis=0, keepdims=True)


def attend_kernel(
    members, rows_ref, near_ref, far_ref, place_ref, table_ref, fw0_ref, fw1_ref, q0_ref, q1_ref, *sent_refs
):
    core = lax.axis_index("member")
    rows = rows_ref[...]
    total, fwidth = rows.shape
    local = q0_ref.shape[2]
    gain = table_ref[GAIN : GAIN + 1, :]
    low, high = rows[:, : fwidth // 2].astype(F32), rows[:, fwidth // 2 :].astype(F32)
    first = jnp.where(core == 0, low, high).astype(BF)
    second = jnp.where(core == 0, high, low).astype(BF)
    token = dot(first, fw0_ref[...]) + dot(second, fw1_ref[...]) + table_ref[FBIAS : FBIAS + 1, :]
    centered = centre(token)
    tokens = [(centered * inverse_spread(centered) * gain).astype(BF)]
    preds = near_ref[...].astype(F32) + far_ref[...].astype(F32)
    for m in range(members):
        centered = preds[:, m : m + 1] * table_ref[SCALE + m : SCALE + m + 1, :] + table_ref[SHIFT + m : SHIFT + m + 1, :]
        tokens.append((centered * inverse_spread(centered) * gain).astype(BF))
    normed = jnp.concatenate(tokens, axis=0)
    count = len(tokens)

    kmap = jnp.concatenate([table_ref[KMAP : KMAP + 8, :], jnp.zeros((LANES - 8, table_ref.shape[1]), F32)], axis=0)
    khigh, klow = split2(kmap)
    logits = dot_t(normed, khigh) + dot_t(normed, klow)
    expo = jnp.exp(logits)
    expo_cls = jnp.exp(table_ref[LCLS : LCLS + 1, :LANES])
    norm = expo_cls
    for t in range(count):
        norm = norm + expo[t * total : (t + 1) * total]
    inverse = 1.0 / norm
    weights = jnp.concatenate(
        [expo[t * total : (t + 1) * total] * inverse for t in range(count)] + [expo_cls * inverse], axis=0)
    expand = (iota((LANES, 2 * local), 0) == iota((LANES, 2 * local), 1) // HD).astype(F32).astype(BF)
    w_high, w_low = split2(weights)
    spread = dot(w_high, expand) + dot(w_low, expand)
    parts = []
    for i, ref in enumerate((q0_ref, q1_ref)):
        at = slice(i * local, (i + 1) * local)
        value = dot(normed, ref[2])
        mixed = spread[count * total :, at] * table_ref[VCLS : VCLS + 1, at]
        for t in range(count):
            rng = slice(t * total, (t + 1) * total)
            mixed = mixed + spread[rng, at] * value[rng]
        parts.append(mixed)
    mixed = jnp.concatenate(parts, axis=1).astype(BF)
    size = sent_refs[0].shape[0]
    for k, sent_ref in enumerate(sent_refs):
        scatter = (place_ref[...] == iota((size, total), 0) + k * size).astype(F32).astype(BF)
        sent_ref[...] = dot(scatter, mixed).astype(BF)


def ensemble_kernel(feat_ref, w_ref, bias_ref, out_ref, pred_ref):
    total = None
    for m in range(w_ref.shape[0]):
        hidden = gelu2(dot(feat_ref[...], w_ref[m]) + bias_ref[m : m + 1]).astype(BF)
        weights = jnp.broadcast_to(out_ref[m : m + 1].astype(F32), (8, out_ref.shape[1])).astype(BF)
        pred = dot_t(weights, hidden)[0:1]
        total = pred if total is None else total + pred
    pred_ref[...] = total


def score_kernel(blocks, half, *refs):
    count = blocks + 7
    hbm, refs = refs[:count], refs[count + 1 :]
    out_refs, vmem, sems = refs[:blocks], refs[blocks:-1], refs[-1]
    copies = start_all(list(zip(hbm, vmem)), sems)
    got_refs = vmem[:blocks]
    table_ref, ow0_ref, ow1_ref = vmem[blocks : blocks + 3]
    segments = ((vmem[blocks + 3], vmem[blocks + 4]), (vmem[blocks + 5], vmem[blocks + 6]))
    for copy in copies[: blocks + 3]:
        copy.wait()
    if blocks == 1:
        mixed = got_refs[0][...]
    else:
        mixed = jnp.concatenate([ref[e * half : (e + 1) * half] for e in range(2) for ref in got_refs], axis=0)
    local = ow0_ref.shape[0]
    total = mixed.shape[0]
    state = table_ref[CLS : CLS + 1, :] + dot(mixed[:, :local], ow0_ref[...]) + dot(mixed[:, local:], ow1_ref[...])
    centered = centre(state)
    normed = (centered * inverse_spread(centered) * table_ref[FGAIN : FGAIN + 1, :]).astype(BF)
    for copy in copies[blocks + 3 :]:
        copy.wait()
    scores = []
    for e, halves in enumerate(segments):
        rows = slice(e * total // 2, (e + 1) * total // 2)
        terms = None
        for ref in halves:
            depth = ref.shape[0] - EXTRA
            extra = ref[depth:, :].astype(F32)
            down, bias, head = (jnp.sum(extra[i : i + 3], axis=0, keepdims=True) for i in (DOWN, BIAS, HEAD))
            if terms is None:
                terms = state[rows] * head
            upper = jnp.maximum(dot(normed[rows], ref[:depth, :]) + bias, 0.0).astype(BF).astype(F32)
            terms = terms + upper * down
        scores.append(jnp.sum(terms, axis=-1, keepdims=True))
    if blocks == 1:
        eye = iota((total // 2, total // 2), 0) == iota((total // 2, total // 2), 1)
        for e in range(2):
            out_refs[0][:, e * total // 2 : (e + 1) * total // 2] = jnp.sum(
                jnp.where(eye, scores[e], 0.0), axis=0, keepdims=True)
    else:
        row, lane = iota((half, LANES), 0), iota((half, LANES), 1)
        for k, out_ref in enumerate(out_refs):
            line = jnp.zeros((half, LANES), F32)
            for e in range(2):
                line = jnp.where(lane == row + e * half, scores[e][k * half : (k + 1) * half], line)
            out_ref[...] = jnp.sum(line, axis=0, keepdims=True)


def finish_kernel(members, where_ref, pred0_ref, pred1_ref, near_ref, far_ref, out_ref):
    count = where_ref.shape[0]
    table = jnp.concatenate([near_ref[...], far_ref[...]], axis=0)
    sources, length = table.shape
    pick = (where_ref[:, 0:1] == iota((count, sources), 1)).astype(F32).astype(BF)
    parts = dot(jnp.concatenate([pick] * 3, axis=1), split3(table))
    score = jnp.sum(jnp.where(where_ref[:, 1:2] == iota((count, length), 1), parts, 0.0), axis=1, keepdims=True)
    hit = where_ref[:, 2:3] == iota((count, out_ref.shape[1]), 1)
    replaced = jnp.sum(jnp.where(hit, score, 0.0), axis=0, keepdims=True)
    taken = jnp.sum(hit.astype(F32), axis=0, keepdims=True)
    ensemble = (pred0_ref[...] + pred1_ref[...]) * (0.5 / members)
    out_ref[...] = jnp.where(taken > 0.0, replaced, ensemble)


def cost(flops, size, trans=0):
    return pl.CostEstimate(flops=flops, bytes_accessed=size, transcendentals=trans)


def params(mib):
    return pltpu.CompilerParams(vmem_limit_bytes=mib * 2**20)


def in_hbm(arrays):
    return [pltpu.with_memory_space_constraint(x, pltpu.HBM) for x in arrays]


def shape(dims, dtype):
    return jax.ShapeDtypeStruct(dims, dtype)


def per_device(
    features, escalated, owner_ids, member_in, member_bias, member_out, feat_weight, feat_bias,
    pred_scale, pred_shift, cls_token, attn_gain, qkv_weight, out_weight, ffn_gain, up_weight,
    up_bias, down_weight, owner_heads,
):
    n = lax.axis_size("rows")
    rows, fwidth = features.shape
    count = escalated.shape[1]
    half = max(1, count // n)
    slots = n * half
    here, _, hidden = member_in.shape
    members = pred_scale.shape[0]
    width = cls_token.shape[0]

    def swap(x):
        return lax.ppermute(x, "member", [(0, 1), (1, 0)])

    row = lambda x: x.reshape(1, -1)
    cls_token, attn_gain, ffn_gain, feat_bias = map(row, (cls_token, attn_gain, ffn_gain, feat_bias))
    owners = owner_ids.reshape(1, count)

    pairs = n // 2
    relative = pairs <= 8
    blocks = pairs if relative else 1
    other_qkv = swap(qkv_weight)
    other_fw = swap(feat_weight)
    other_ow = swap(out_weight)

    depth, hidden_half = up_weight.shape[1:]
    ins = (up_weight, down_weight, up_bias, owner_heads)
    segment = pl.pallas_call(
        prepare_kernel,
        out_shape=shape((depth + EXTRA, hidden_half), BF),
        in_specs=[HBM] * 4,
        out_specs=VMEM,
        scratch_shapes=[pltpu.VMEM(x.shape, x.dtype) for x in ins[1:]] + [pltpu.SemaphoreType.DMA((4,))],
        compiler_params=params(16),
        cost_estimate=cost(10**8, 10**6),
        name="prepare",
    )(*in_hbm(ins))
    next_segment = lax.ppermute(segment, "rows", [(i, i ^ 1) for i in range(n)])
    other_segment = swap(segment)
    other_next = swap(next_segment)

    dealt = count // 2
    ins = (escalated, owners, features, member_in, member_bias, member_out)
    where, place, mine, near, far = pl.pallas_call(
        functools.partial(route_kernel, n, half, relative),
        out_shape=[shape((count, 4), jnp.int32), shape((1, dealt), jnp.int32), shape((dealt, fwidth), BF),
                   shape((dealt, LANES), BF), shape((dealt, LANES), BF)],
        in_specs=[HBM] * 6,
        out_specs=[VMEM] * 5,
        scratch_shapes=[pltpu.VMEM(x.shape, x.dtype) for x in ins] + [pltpu.SemaphoreType.DMA((5 + here,))],
        compiler_params=params(24),
        cost_estimate=cost(2 * count * rows * fwidth + 2 * here * count * fwidth * hidden, 3 * 10**6,
                           here * count * hidden),
        name="route",
    )(*in_hbm(ins))
    far = swap(far)

    ins = (cls_token, attn_gain, pred_scale, pred_shift, feat_bias, ffn_gain, qkv_weight, other_qkv)
    table = pl.pallas_call(
        constants_kernel,
        out_shape=shape((TABLE, width), F32),
        in_specs=[HBM] * len(ins),
        out_specs=VMEM,
        scratch_shapes=[pltpu.VMEM(x.shape, x.dtype) for x in ins] + [pltpu.SemaphoreType.DMA((len(ins),))],
        compiler_params=params(16),
        cost_estimate=cost(10**8, 2 * 10**6),
        name="constants",
    )(*ins)

    local = qkv_weight.shape[2]
    sent = pl.pallas_call(
        functools.partial(attend_kernel, members),
        out_shape=[shape((slots // blocks, 2 * local), BF)] * blocks,
        in_specs=[VMEM] * 9,
        out_specs=[VMEM] * blocks,
        compiler_params=params(24),
        cost_estimate=cost(10**9, 2 * 10**6),
        name="attend",
    )(mine, near, far, place, table, feat_weight, other_fw, qkv_weight, other_qkv)

    def across(x, k):
        return lax.ppermute(x, "rows", [(i, i ^ (2 * k)) for i in range(n)])

    def exchange(x):
        groups = [[2 * q + b for q in range(pairs)] for b in range(2)]
        return lax.all_to_all(x, "rows", split_axis=0, concat_axis=0, axis_index_groups=groups, tiled=True)

    if relative:
        got = [sent[0]] + [across(sent[k], k) for k in range(1, pairs)]
    else:
        got = exchange(sent[0].reshape(pairs, 2, half, 2 * local))
        got = [got.transpose(1, 0, 2, 3).reshape(slots, 2 * local)]

    tile = min(rows, 256)
    pred = pl.pallas_call(
        ensemble_kernel,
        grid=(rows // tile,),
        out_shape=shape((1, rows), F32),
        in_specs=[
            pl.BlockSpec((tile, fwidth), lambda i: (i, 0)),
            pl.BlockSpec(member_in.shape, lambda i: (0, 0, 0)),
            pl.BlockSpec(member_bias.shape, lambda i: (0, 0)),
            pl.BlockSpec(member_out.shape, lambda i: (0, 0)),
        ],
        out_specs=pl.BlockSpec((1, tile), lambda i: (0, i)),
        compiler_params=params(24),
        cost_estimate=cost(2 * here * rows * fwidth * hidden, 4 * 10**6, here * rows * hidden),
        name="ensemble",
    )(features, member_in, member_bias, member_out)
    other_pred = swap(pred)

    ins = (*got, table, out_weight, other_ow, segment, other_segment, next_segment, other_next)
    scores = pl.pallas_call(
        functools.partial(score_kernel, blocks, half),
        out_shape=[shape((1, LANES if relative else slots), F32)] * blocks,
        in_specs=[HBM] * len(ins) + [pl.BlockSpec(memory_space=pl.ANY)],
        out_specs=[VMEM] * blocks,
        scratch_shapes=[pltpu.VMEM(x.shape, x.dtype) for x in ins] + [pltpu.SemaphoreType.DMA((len(ins),))],
        compiler_params=params(24),
        cost_estimate=cost(10**9, 2 * 10**6),
        name="score",
    )(*in_hbm(ins), pred)
    if relative:
        back = jnp.concatenate([scores[0]] + [across(scores[k], k) for k in range(1, pairs)], axis=0)
    else:
        back = exchange(scores[0].reshape(2, pairs, half).transpose(1, 0, 2)).reshape(pairs, 2 * half)

    final = pl.pallas_call(
        functools.partial(finish_kernel, members),
        out_shape=shape((1, rows), F32),
        in_specs=[VMEM] * 5,
        out_specs=VMEM,
        compiler_params=params(8),
        cost_estimate=cost(10**6, 10**6),
        name="finish",
    )(where, pred, other_pred, back, swap(back))
    return final.reshape(rows)


def solution(mesh):
    placed = (
        P(("groups", "rows"), None),
        P(("groups", "rows"), None),
        P(("groups", "rows"), None, None),
        P("member", None, None),
        P("member", None),
        P("member", None),
        P("member", None),
        P(),
        P(),
        P(),
        P(),
        P(),
        P(None, None, "member"),
        P("member", None),
        P(),
        P("rows", None, "member"),
        P("rows", "member"),
        P("rows", "member", None),
        P("rows", None),
    )
    return jax.shard_map(
        per_device, mesh=mesh, in_specs=placed, out_specs=P(("groups", "rows")), check_vma=False
    )
```

```python
import functools
import math

import jax
import jax.numpy as jnp
from jax import lax
from jax.experimental import pallas as pl
from jax.experimental.pallas import tpu as pltpu
from jax.sharding import PartitionSpec as P

HD = 64
EPS = 1e-05
LANES = 128
BF = jnp.bfloat16
F32 = jnp.float32
VMEM = pl.BlockSpec(memory_space=pltpu.VMEM)
HBM = pl.BlockSpec(memory_space=pltpu.HBM)
ANY = pl.BlockSpec(memory_space=pl.ANY)
GELU_C = math.sqrt(2.0 / math.pi)

KMAP, VCLS, LCLS, SCALE, SHIFT, GAIN, FBIAS, CLS, FGAIN = 0, 8, 9, 16, 24, 32, 33, 34, 35
TABLE = 40
DOWN, BIAS, HEAD, EXTRA = 0, 3, 6, 16


def iota(shape, dim):
    return lax.broadcasted_iota(jnp.int32, shape, dim)


def gelu2(x):
    return x + x * jnp.tanh(x * (GELU_C + (GELU_C * 0.044715) * (x * x)))


def dot(a, b):
    return lax.dot_general(a, b, (((1,), (0,)), ((), ())), preferred_element_type=F32)


def dot_t(a, b):
    return lax.dot_general(a, b, (((1,), (1,)), ((), ())), preferred_element_type=F32)


def split2(x):
    high = x.astype(BF)
    return high, (x - high.astype(F32)).astype(BF)


def split3(x):
    high, rest = x.astype(BF), x
    rest = rest - high.astype(F32)
    mid = rest.astype(BF)
    low = (rest - mid.astype(F32)).astype(BF)
    return jnp.concatenate([high.astype(F32), mid.astype(F32), low.astype(F32)], axis=0).astype(BF)


def join3(x):
    rows = x.shape[0] // 3
    return x[:rows] + x[rows : 2 * rows] + x[2 * rows :]


def centre(x):
    return x - jnp.mean(x, axis=-1, keepdims=True)


def inverse_spread(centered):
    return lax.rsqrt(jnp.mean(centered * centered, axis=-1, keepdims=True) + EPS)


def start_all(pairs, sems):
    copies = [pltpu.make_async_copy(src, dst, sems.at[i]) for i, (src, dst) in enumerate(pairs)]
    for copy in copies:
        copy.start()
    return copies


def route_kernel(
    n, half, relative, esc_hbm, own_hbm, feat_hbm, w_hbm, bias_hbm, out_hbm, down_hbm, upb_hbm, head_hbm, up_hbm,
    where_ref, place_ref, rows_ref, near_ref, far_ref, segment_ref,
    esc_ref, own_ref, feat_ref, w_ref, bias_ref, out_ref, down_ref, upb_ref, head_ref, sems,
):
    depth = up_hbm.shape[1]
    copies = start_all(
        [(esc_hbm, esc_ref), (own_hbm, own_ref), (feat_hbm, feat_ref), (bias_hbm, bias_ref), (out_hbm, out_ref)]
        + [(w_hbm.at[m], w_ref.at[m]) for m in range(w_hbm.shape[0])]
        + [(head_hbm, head_ref), (upb_hbm, upb_ref), (down_hbm, down_ref), (up_hbm.at[0], segment_ref.at[:depth])],
        sems)
    core = lax.axis_index("member")
    count = esc_hbm.shape[1]
    dealt = count // 2
    copies[0].wait()
    copies[1].wait()
    esc = esc_ref[...]
    own = own_ref[...]
    ii = iota((count, count), 0)
    jj = iota((count, count), 1)
    diag = ii == jj

    def to_col(row):
        return jnp.sum(jnp.where(diag, row, 0).astype(F32), axis=1, keepdims=True)

    own_col = to_col(own).astype(jnp.int32)
    before = jnp.sum((own_col < own).astype(F32), axis=0, keepdims=True).astype(jnp.int32)
    rank = jnp.sum(((own_col == own) & (ii < jj)).astype(F32), axis=0, keepdims=True).astype(jnp.int32)
    position = before + rank
    side = position & 1
    slot = rank >> 1
    me = lax.axis_index("rows")
    apart = own ^ me
    pair = (apart if relative else (own - (own & 1)) + (apart & 1))
    place = pair * half + slot
    dense = (position >> 1) + jnp.where(side == core, 0, dealt)
    where_ref[:, 0:1] = to_col((pair >> 1) + (side ^ core) * (n // 2)).astype(jnp.int32)
    where_ref[:, 1:2] = to_col((apart & 1) * half + slot).astype(jnp.int32)
    where_ref[:, 2:3] = to_col(esc).astype(jnp.int32)
    where_ref[:, 3:4] = to_col(jnp.where((apart & 1) == 1, 2 * half + slot, -1)).astype(jnp.int32)

    mine = dense == ii
    source = jnp.sum(jnp.where(mine, esc, 0).astype(F32), axis=1, keepdims=True).astype(jnp.int32)
    place_col = jnp.sum(jnp.where(mine, place, 0).astype(F32), axis=1, keepdims=True)
    place_ref[...] = jnp.sum(
        jnp.where(diag[:dealt, :dealt], place_col[:dealt], 0.0), axis=0, keepdims=True
    ).astype(jnp.int32)
    chosen = (source == iota((count, feat_ref.shape[0]), 1)).astype(F32).astype(BF)
    copies[2].wait()
    rows = dot(chosen, feat_ref[...]).astype(BF)
    rows_ref[...] = rows[:dealt]
    copies[3].wait()
    copies[4].wait()
    here = w_hbm.shape[0]
    lane = iota((LANES, 1), 0)
    preds = None
    for m in range(here):
        copies[5 + m].wait()
        act = gelu2(dot(rows, w_ref[m]) + bias_ref[m : m + 1]).astype(BF)
        on_lane = jnp.where(lane == core * here + m, 0.5 * out_ref[m : m + 1].astype(F32), 0.0).astype(BF)
        pred = dot_t(act, on_lane)
        preds = pred if preds is None else preds + pred
    preds = preds.astype(BF)
    near_ref[...] = preds[:dealt]
    far_ref[...] = preds[dealt:]

    for copy in copies[5 + here : 8 + here]:
        copy.wait()
    head = jnp.broadcast_to(head_ref[...], (8, head_ref.shape[1]))
    down = join3(dot_t(split3(head), down_ref[0]))[0:1]
    extra = [split3(x).astype(F32) for x in (down, upb_ref[...], head_ref[...])]
    extra.append(jnp.zeros((EXTRA - 9, down.shape[1]), F32))
    segment_ref[depth:, :] = jnp.concatenate(extra, axis=0).astype(BF)
    copies[8 + here].wait()


def constants_kernel(*refs):
    hbm, table_ref, vmem, sems = refs[:8], refs[8], refs[9:-1], refs[-1]
    copies = start_all(list(zip(hbm, vmem)), sems)
    cls_ref, gain_ref, scale_ref, shift_ref, fbias_ref, fgain_ref, q0_ref, q1_ref = vmem
    for copy in copies[:6]:
        copy.wait()
    gain = gain_ref[...]
    cls = cls_ref[...]
    centered = centre(cls)
    ncls = (centered * inverse_spread(centered) * gain).astype(BF)
    table_ref[...] = jnp.zeros_like(table_ref)
    members = scale_ref.shape[0]
    table_ref[SCALE : SCALE + members, :] = centre(scale_ref[...])
    table_ref[SHIFT : SHIFT + members, :] = centre(shift_ref[...])
    table_ref[GAIN : GAIN + 1, :] = gain
    table_ref[FBIAS : FBIAS + 1, :] = fbias_ref[...]
    table_ref[CLS : CLS + 1, :] = cls
    table_ref[FGAIN : FGAIN + 1, :] = fgain_ref[...]
    for copy in copies[6:]:
        copy.wait()
    lhs = jnp.broadcast_to(ncls.astype(F32), (8, ncls.shape[1])).astype(BF)
    local = q0_ref.shape[2]
    heads = local // HD
    row = iota((8, local), 0)
    col = iota((8, local), 1) // HD
    kmap = None
    for i, ref in enumerate((q0_ref, q1_ref)):
        query = dot(lhs, ref[0]) * (1.0 / math.sqrt(HD))
        spread = jnp.where(row == col + i * heads, query, 0.0)
        part = join3(dot_t(split3(spread), ref[1]))
        kmap = part if kmap is None else kmap + part
        table_ref[VCLS : VCLS + 1, i * local : (i + 1) * local] = dot(lhs, ref[2])[0:1]
    table_ref[KMAP : KMAP + 8, :] = kmap
    logits = jnp.sum(kmap * ncls.astype(F32), axis=-1, keepdims=True)
    eye = iota((8, LANES), 0) == iota((8, LANES), 1)
    table_ref[LCLS : LCLS + 1, :LANES] = jnp.sum(jnp.where(eye, logits, 0.0), axis=0, keepdims=True)


def attend_kernel(
    members, rows_ref, near_ref, far_ref, place_ref, table_ref, fw0_ref, fw1_ref, q0_ref, q1_ref, *sent_refs
):
    core = lax.axis_index("member")
    rows = rows_ref[...]
    total, fwidth = rows.shape
    local = q0_ref.shape[2]
    gain = table_ref[GAIN : GAIN + 1, :]
    low, high = rows[:, : fwidth // 2].astype(F32), rows[:, fwidth // 2 :].astype(F32)
    first = jnp.where(core == 0, low, high).astype(BF)
    second = jnp.where(core == 0, high, low).astype(BF)
    token = dot(first, fw0_ref[...]) + dot(second, fw1_ref[...]) + table_ref[FBIAS : FBIAS + 1, :]
    centered = centre(token)
    tokens = [(centered * inverse_spread(centered) * gain).astype(BF)]
    preds = near_ref[...].astype(F32) + far_ref[...].astype(F32)
    for m in range(members):
        centered = preds[:, m : m + 1] * table_ref[SCALE + m : SCALE + m + 1, :] + table_ref[SHIFT + m : SHIFT + m + 1, :]
        tokens.append((centered * inverse_spread(centered) * gain).astype(BF))
    normed = jnp.concatenate(tokens, axis=0)
    count = len(tokens)

    kmap = jnp.concatenate([table_ref[KMAP : KMAP + 8, :], jnp.zeros((LANES - 8, table_ref.shape[1]), F32)], axis=0)
    khigh, klow = split2(kmap)
    logits = dot_t(normed, khigh) + dot_t(normed, klow)
    expo = jnp.exp(logits)
    expo_cls = jnp.exp(table_ref[LCLS : LCLS + 1, :LANES])
    norm = expo_cls
    for t in range(count):
        norm = norm + expo[t * total : (t + 1) * total]
    inverse = 1.0 / norm
    weights = jnp.concatenate(
        [expo[t * total : (t + 1) * total] * inverse for t in range(count)] + [expo_cls * inverse], axis=0)
    expand = (iota((LANES, 2 * local), 0) == iota((LANES, 2 * local), 1) // HD).astype(F32).astype(BF)
    w_high, w_low = split2(weights)
    spread = dot(w_high, expand) + dot(w_low, expand)
    parts = []
    for i, ref in enumerate((q0_ref, q1_ref)):
        at = slice(i * local, (i + 1) * local)
        value = dot(normed, ref[2])
        mixed = spread[count * total :, at] * table_ref[VCLS : VCLS + 1, at]
        for t in range(count):
            rng = slice(t * total, (t + 1) * total)
            mixed = mixed + spread[rng, at] * value[rng]
        parts.append(mixed)
    mixed = jnp.concatenate(parts, axis=1).astype(BF)
    size = sent_refs[0].shape[0]
    for k, sent_ref in enumerate(sent_refs):
        scatter = (place_ref[...] == iota((size, total), 0) + k * size).astype(F32).astype(BF)
        sent_ref[...] = dot(scatter, mixed).astype(BF)


def ensemble_kernel(feat_ref, w_ref, bias_ref, out_ref, after_ref, *refs):
    count = (len(refs) - 2) // 2
    hbm, pred_ref, vmem, sems = refs[:count], refs[count], refs[count + 1 : -1], refs[-1]
    copies = [pltpu.make_async_copy(src, dst, sems.at[i]) for i, (src, dst) in enumerate(zip(hbm, vmem))]

    @pl.when(pl.program_id(0) == 0)
    def _():
        for copy in copies:
            copy.start()

    total = None
    for m in range(w_ref.shape[0]):
        hidden = gelu2(dot(feat_ref[...], w_ref[m]) + bias_ref[m : m + 1]).astype(BF)
        weights = jnp.broadcast_to(out_ref[m : m + 1].astype(F32), (8, out_ref.shape[1])).astype(BF)
        pred = dot_t(weights, hidden)[0:1]
        total = pred if total is None else total + pred
    pred_ref[...] = total

    @pl.when(pl.program_id(0) == pl.num_programs(0) - 1)
    def _():
        for copy in copies:
            copy.wait()


def unpack(ref):
    depth = ref.shape[0] - EXTRA
    extra = ref[depth:, :].astype(F32)
    return ref[:depth, :], *(jnp.sum(extra[i : i + 3], axis=0, keepdims=True) for i in (DOWN, BIAS, HEAD))


def hidden_terms(normed, up, down, bias):
    return jnp.maximum(dot(normed, up) + bias, 0.0).astype(BF).astype(F32) * down


def arrive_kernel(blocks, half, *refs):
    got_refs = refs[:blocks]
    table_ref, ow0_ref, ow1_ref, next_hbm, state_ref, own_ref, next_ref, next_segment_ref, sems = refs[blocks:]
    (copy,) = start_all([(next_hbm, next_segment_ref)], sems)
    if blocks == 1:
        mixed = got_refs[0][...]
    else:
        mixed = jnp.concatenate([ref[e * half : (e + 1) * half] for e in range(2) for ref in got_refs], axis=0)
    rows = mixed.shape[0] // 2
    local = ow0_ref.shape[0]
    state = table_ref[CLS : CLS + 1, :] + dot(mixed[:, :local], ow0_ref[...]) + dot(mixed[:, local:], ow1_ref[...])
    state_ref[...] = state
    centered = centre(state)
    normed = (centered * inverse_spread(centered) * table_ref[FGAIN : FGAIN + 1, :]).astype(BF)
    own_ref[...] = normed[:rows]
    next_ref[...] = normed[rows:]
    copy.wait()


def near_score_kernel(state_ref, own_ref, next_ref, up0_ref, up1_ref, up2_ref, score_ref):
    rows = own_ref.shape[0]
    up, down, bias, head = unpack(up0_ref)
    terms = state_ref[:rows] * head + hidden_terms(own_ref[...], up, down, bias)
    up, down, bias, _ = unpack(up1_ref)
    terms = terms + hidden_terms(own_ref[...], up, down, bias)
    score_ref[:rows] = jnp.sum(terms, axis=-1, keepdims=True)
    up, down, bias, head = unpack(up2_ref)
    terms = state_ref[rows:] * head + hidden_terms(next_ref[...], up, down, bias)
    score_ref[rows:] = jnp.sum(terms, axis=-1, keepdims=True)


def far_score_kernel(blocks, half, near_ref, next_ref, up2_ref, *out_refs):
    rows = next_ref.shape[0]
    up, down, bias, _ = unpack(up2_ref)
    last = jnp.sum(hidden_terms(next_ref[...], up, down, bias), axis=-1, keepdims=True)
    scores = [near_ref[:rows], near_ref[rows:], last]
    if blocks == 1:
        eye = iota((rows, rows), 0) == iota((rows, rows), 1)
        for e, score in enumerate(scores):
            out_refs[0][:, e * rows : (e + 1) * rows] = jnp.sum(jnp.where(eye, score, 0.0), axis=0, keepdims=True)
    else:
        row, lane = iota((half, LANES), 0), iota((half, LANES), 1)
        for k, out_ref in enumerate(out_refs):
            line = jnp.zeros((half, LANES), F32)
            for e, score in enumerate(scores):
                line = jnp.where(lane == row + e * half, score[k * half : (k + 1) * half], line)
            out_ref[...] = jnp.sum(line, axis=0, keepdims=True)


def finish_kernel(members, where_ref, pred0_ref, pred1_ref, near_ref, far_ref, out_ref):
    count = where_ref.shape[0]
    table = jnp.concatenate([near_ref[...], far_ref[...]], axis=0)
    sources, length = table.shape
    table = split3(table)
    source = where_ref[:, 0:1]
    opposite = jnp.where(source < sources // 2, source + sources // 2, source - sources // 2)
    lanes = iota((count, length), 1)
    picked = jnp.zeros((count, length), F32)
    for line, lane in ((source, where_ref[:, 1:2]), (opposite, where_ref[:, 3:4])):
        pick = (line == iota((count, sources), 1)).astype(F32).astype(BF)
        picked = picked + jnp.where(lane == lanes, dot(jnp.concatenate([pick] * 3, axis=1), table), 0.0)
    score = jnp.sum(picked, axis=1, keepdims=True)
    hit = where_ref[:, 2:3] == iota((count, out_ref.shape[1]), 1)
    replaced = jnp.sum(jnp.where(hit, score, 0.0), axis=0, keepdims=True)
    taken = jnp.sum(hit.astype(F32), axis=0, keepdims=True)
    ensemble = (pred0_ref[...] + pred1_ref[...]) * (0.5 / members)
    out_ref[...] = jnp.where(taken > 0.0, replaced, ensemble)


def cost(flops, size, trans=0):
    return pl.CostEstimate(flops=flops, bytes_accessed=size, transcendentals=trans)


def params(mib):
    return pltpu.CompilerParams(vmem_limit_bytes=mib * 2**20)


def in_hbm(arrays):
    return [pltpu.with_memory_space_constraint(x, pltpu.HBM) for x in arrays]


def shape(dims, dtype):
    return jax.ShapeDtypeStruct(dims, dtype)


def per_device(
    features, escalated, owner_ids, member_in, member_bias, member_out, feat_weight, feat_bias,
    pred_scale, pred_shift, cls_token, attn_gain, qkv_weight, out_weight, ffn_gain, up_weight,
    up_bias, down_weight, owner_heads,
):
    n = lax.axis_size("rows")
    rows, fwidth = features.shape
    count = escalated.shape[1]
    half = max(1, count // n)
    slots = n * half
    here, _, hidden = member_in.shape
    members = pred_scale.shape[0]
    width = cls_token.shape[0]

    def swap(x):
        return lax.ppermute(x, "member", [(0, 1), (1, 0)])

    row = lambda x: x.reshape(1, -1)
    cls_token, attn_gain, ffn_gain, feat_bias = map(row, (cls_token, attn_gain, ffn_gain, feat_bias))
    owners = owner_ids.reshape(1, count)

    pairs = n // 2
    relative = pairs <= 8
    blocks = pairs if relative else 1
    other_qkv = swap(qkv_weight)
    other_fw = swap(feat_weight)
    other_ow = swap(out_weight)

    dealt = count // 2
    ins = (escalated, owners, features, member_in, member_bias, member_out, down_weight, up_bias, owner_heads, up_weight)
    where, place, mine, near, far, segment = pl.pallas_call(
        functools.partial(route_kernel, n, half, relative),
        out_shape=[shape((count, 4), jnp.int32), shape((1, dealt), jnp.int32), shape((dealt, fwidth), BF),
                   shape((dealt, LANES), BF), shape((dealt, LANES), BF),
                   shape((up_weight.shape[1] + EXTRA, up_weight.shape[2]), BF)],
        in_specs=[HBM] * len(ins),
        out_specs=[VMEM] * 6,
        scratch_shapes=[pltpu.VMEM(x.shape, x.dtype) for x in ins[:-1]] + [pltpu.SemaphoreType.DMA((9 + here,))],
        compiler_params=params(24),
        cost_estimate=cost(2 * count * rows * fwidth + 2 * here * count * fwidth * hidden, 3 * 10**6,
                           here * count * hidden),
        name="route",
    )(*in_hbm(ins))
    far = swap(far)
    next_segment = lax.ppermute(segment, "rows", [(i, i ^ 1) for i in range(n)])
    other_segment = swap(segment)

    ins = (cls_token, attn_gain, pred_scale, pred_shift, feat_bias, ffn_gain, qkv_weight, other_qkv)
    table = pl.pallas_call(
        constants_kernel,
        out_shape=shape((TABLE, width), F32),
        in_specs=[HBM] * len(ins),
        out_specs=VMEM,
        scratch_shapes=[pltpu.VMEM(x.shape, x.dtype) for x in ins] + [pltpu.SemaphoreType.DMA((len(ins),))],
        compiler_params=params(16),
        cost_estimate=cost(10**8, 2 * 10**6),
        name="constants",
    )(*ins)

    local = qkv_weight.shape[2]
    sent = pl.pallas_call(
        functools.partial(attend_kernel, members),
        out_shape=[shape((slots // blocks, 2 * local), BF)] * blocks,
        in_specs=[VMEM] * 9,
        out_specs=[VMEM] * blocks,
        compiler_params=params(24),
        cost_estimate=cost(10**9, 2 * 10**6),
        name="attend",
    )(mine, near, far, place, table, feat_weight, other_fw, qkv_weight, other_qkv)

    def across(x, k):
        return lax.ppermute(x, "rows", [(i, i ^ (2 * k)) for i in range(n)])

    def exchange(x):
        groups = [[2 * q + b for q in range(pairs)] for b in range(2)]
        return lax.all_to_all(x, "rows", split_axis=0, concat_axis=0, axis_index_groups=groups, tiled=True)

    if relative:
        got = [sent[0]] + [across(sent[k], k) for k in range(1, pairs)]
    else:
        got = exchange(sent[0].reshape(pairs, 2, half, 2 * local))
        got = [got.transpose(1, 0, 2, 3).reshape(slots, 2 * local)]

    tile = min(rows, 256)
    held = (table, out_weight, other_ow, segment, other_segment)
    pred, table, ow0, ow1, up0, up1 = pl.pallas_call(
        ensemble_kernel,
        grid=(rows // tile,),
        out_shape=[shape((1, rows), F32)] + [shape(x.shape, x.dtype) for x in held],
        in_specs=[
            pl.BlockSpec((tile, fwidth), lambda i: (i, 0)),
            pl.BlockSpec(member_in.shape, lambda i: (0, 0, 0)),
            pl.BlockSpec(member_bias.shape, lambda i: (0, 0)),
            pl.BlockSpec(member_out.shape, lambda i: (0, 0)),
            ANY,
        ] + [HBM] * len(held),
        out_specs=[pl.BlockSpec((1, tile), lambda i: (0, i))] + [VMEM] * len(held),
        scratch_shapes=[pltpu.SemaphoreType.DMA((len(held),))],
        compiler_params=params(24),
        cost_estimate=cost(2 * here * rows * fwidth * hidden, 4 * 10**6, here * rows * hidden),
        name="ensemble",
    )(features, member_in, member_bias, member_out, sent[0], *in_hbm(held))
    other_pred = swap(pred)

    state, own_rows, next_rows, up2 = pl.pallas_call(
        functools.partial(arrive_kernel, blocks, half),
        out_shape=[shape((slots, width), F32), shape((slots // 2, width), BF), shape((slots // 2, width), BF),
                   shape(next_segment.shape, BF)],
        in_specs=[VMEM] * (blocks + 3) + [ANY],
        out_specs=[VMEM] * 4,
        scratch_shapes=[pltpu.SemaphoreType.DMA((1,))],
        compiler_params=params(24),
        cost_estimate=cost(5 * 10**8, 2 * 10**6),
        name="arrive",
    )(*got, table, ow0, ow1, next_segment)
    other_rows = swap(next_rows)
    near_scores = pl.pallas_call(
        near_score_kernel,
        out_shape=shape((slots, 1), F32),
        in_specs=[VMEM] * 6,
        out_specs=VMEM,
        compiler_params=params(24),
        cost_estimate=cost(5 * 10**8, 2 * 10**6),
        name="near_score",
    )(state, own_rows, next_rows, up0, up1, up2)
    scores = pl.pallas_call(
        functools.partial(far_score_kernel, blocks, half),
        out_shape=[shape((1, LANES if relative else 3 * slots // 2), F32)] * blocks,
        in_specs=[VMEM] * 3,
        out_specs=[VMEM] * blocks,
        compiler_params=params(24),
        cost_estimate=cost(2 * 10**8, 10**6),
        name="far_score",
    )(near_scores, other_rows, up2)
    if relative:
        back = [scores[0]] + [across(scores[k], k) for k in reversed(range(1, pairs))][::-1]
        back = jnp.concatenate(back, axis=0)
    else:
        back = exchange(scores[0].reshape(3, pairs, half).transpose(1, 0, 2)).reshape(pairs, 3 * half)

    final = pl.pallas_call(
        functools.partial(finish_kernel, members),
        out_shape=shape((1, rows), F32),
        in_specs=[VMEM] * 5,
        out_specs=VMEM,
        compiler_params=params(8),
        cost_estimate=cost(10**6, 10**6),
        name="finish",
    )(where, pred, other_pred, back, swap(back))
    return final.reshape(rows)


def solution(mesh):
    placed = (
        P(("groups", "rows"), None),
        P(("groups", "rows"), None),
        P(("groups", "rows"), None, None),
        P("member", None, None),
        P("member", None),
        P("member", None),
        P("member", None),
        P(),
        P(),
        P(),
        P(),
        P(),
        P(None, None, "member"),
        P("member", None),
        P(),
        P("rows", None, "member"),
        P("rows", "member"),
        P("rows", "member", None),
        P("rows", None),
    )
    return jax.shard_map(
        per_device, mesh=mesh, in_specs=placed, out_specs=P(("groups", "rows")), check_vma=False
    )
```

```python
import functools
import math

import jax
import jax.numpy as jnp
from jax import lax
from jax.experimental import pallas as pl
from jax.experimental.pallas import tpu as pltpu
from jax.sharding import PartitionSpec as P

HD = 64
EPS = 1e-05
LANES = 128
BF = jnp.bfloat16
F32 = jnp.float32
VMEM = pl.BlockSpec(memory_space=pltpu.VMEM)
HBM = pl.BlockSpec(memory_space=pltpu.HBM)
ANY = pl.BlockSpec(memory_space=pl.ANY)
GELU_C = math.sqrt(2.0 / math.pi)

KMAP, VCLS, LCLS, SCALE, SHIFT, GAIN, FBIAS, CLS, FGAIN = 0, 8, 9, 16, 24, 32, 33, 34, 35
TABLE = 40
DOWN, BIAS, HEAD, EXTRA = 0, 3, 6, 16


def iota(shape, dim):
    return lax.broadcasted_iota(jnp.int32, shape, dim)


def gelu2(x):
    return x + x * jnp.tanh(x * (GELU_C + (GELU_C * 0.044715) * (x * x)))


def dot(a, b):
    return lax.dot_general(a, b, (((1,), (0,)), ((), ())), preferred_element_type=F32)


def dot_t(a, b):
    return lax.dot_general(a, b, (((1,), (1,)), ((), ())), preferred_element_type=F32)


def split2(x):
    high = x.astype(BF)
    return high, (x - high.astype(F32)).astype(BF)


def split3(x):
    high, rest = x.astype(BF), x
    rest = rest - high.astype(F32)
    mid = rest.astype(BF)
    low = (rest - mid.astype(F32)).astype(BF)
    return jnp.concatenate([high.astype(F32), mid.astype(F32), low.astype(F32)], axis=0).astype(BF)


def join3(x):
    rows = x.shape[0] // 3
    return x[:rows] + x[rows : 2 * rows] + x[2 * rows :]


def centre(x):
    return x - jnp.mean(x, axis=-1, keepdims=True)


def inverse_spread(centered):
    return lax.rsqrt(jnp.mean(centered * centered, axis=-1, keepdims=True) + EPS)


def start_all(pairs, sems):
    copies = [pltpu.make_async_copy(src, dst, sems.at[i]) for i, (src, dst) in enumerate(pairs)]
    for copy in copies:
        copy.start()
    return copies


def route_kernel(
    n, half, relative, esc_hbm, own_hbm, feat_hbm, w_hbm, bias_hbm, out_hbm, down_hbm, upb_hbm, head_hbm, up_hbm,
    where_ref, place_ref, rows_ref, near_ref, far_ref, segment_ref,
    esc_ref, own_ref, feat_ref, w_ref, bias_ref, out_ref, down_ref, upb_ref, head_ref, sems,
):
    depth = up_hbm.shape[1]
    copies = start_all(
        [(esc_hbm, esc_ref), (own_hbm, own_ref), (feat_hbm, feat_ref), (bias_hbm, bias_ref), (out_hbm, out_ref)]
        + [(w_hbm.at[m], w_ref.at[m]) for m in range(w_hbm.shape[0])]
        + [(head_hbm, head_ref), (upb_hbm, upb_ref), (down_hbm, down_ref), (up_hbm.at[0], segment_ref.at[:depth])],
        sems)
    core = lax.axis_index("member")
    count = esc_hbm.shape[1]
    dealt = count // 2
    copies[0].wait()
    copies[1].wait()
    esc = esc_ref[...]
    own = own_ref[...]
    ii = iota((count, count), 0)
    jj = iota((count, count), 1)
    diag = ii == jj

    def to_col(row):
        return jnp.sum(jnp.where(diag, row, 0).astype(F32), axis=1, keepdims=True)

    own_col = to_col(own).astype(jnp.int32)
    before = jnp.sum((own_col < own).astype(F32), axis=0, keepdims=True).astype(jnp.int32)
    rank = jnp.sum(((own_col == own) & (ii < jj)).astype(F32), axis=0, keepdims=True).astype(jnp.int32)
    position = before + rank
    side = position & 1
    slot = rank >> 1
    me = lax.axis_index("rows")
    apart = own ^ me
    pair = (apart if relative else (own - (own & 1)) + (apart & 1))
    place = pair * half + slot
    dense = (position >> 1) + jnp.where(side == core, 0, dealt)
    mine = dense == ii
    source = jnp.sum(jnp.where(mine, esc, 0).astype(F32), axis=1, keepdims=True).astype(jnp.int32)
    chosen = (source == iota((count, feat_ref.shape[0]), 1)).astype(F32).astype(BF)
    here = w_hbm.shape[0]
    for copy in copies[2 : 5 + here]:
        copy.wait()
    rows = dot(chosen, feat_ref[...]).astype(BF)
    rows_ref[...] = rows[:dealt]
    lane = iota((LANES, 1), 0)
    preds = None
    for m in range(here):
        act = gelu2(dot(rows, w_ref[m]) + bias_ref[m : m + 1]).astype(BF)
        on_lane = jnp.where(lane == core * here + m, 0.5 * out_ref[m : m + 1].astype(F32), 0.0).astype(BF)
        pred = dot_t(act, on_lane)
        preds = pred if preds is None else preds + pred
    preds = preds.astype(BF)
    near_ref[...] = preds[:dealt]
    far_ref[...] = preds[dealt:]

    line = pair >> 1
    line = line * (n // 2 + 1) + (side ^ core) * (n // 2) ** 2 if relative else line + (side ^ core) * (n // 2)
    where_ref[:, 0:1] = to_col(line).astype(jnp.int32)
    where_ref[:, 1:2] = to_col((apart & 1) * half + slot).astype(jnp.int32)
    where_ref[:, 2:3] = to_col(esc).astype(jnp.int32)
    where_ref[:, 3:4] = to_col(jnp.where((apart & 1) == 1, 2 * half + slot, -1)).astype(jnp.int32)

    place_col = jnp.sum(jnp.where(mine, place, 0).astype(F32), axis=1, keepdims=True)
    place_ref[...] = jnp.sum(
        jnp.where(diag[:dealt, :dealt], place_col[:dealt], 0.0), axis=0, keepdims=True
    ).astype(jnp.int32)
    for copy in copies[5 + here : 8 + here]:
        copy.wait()
    head = jnp.broadcast_to(head_ref[...], (8, head_ref.shape[1]))
    down = join3(dot_t(split3(head), down_ref[0]))[0:1]
    extra = [split3(x).astype(F32) for x in (down, upb_ref[...], head_ref[...])]
    extra.append(jnp.zeros((EXTRA - 9, down.shape[1]), F32))
    segment_ref[depth:, :] = jnp.concatenate(extra, axis=0).astype(BF)
    copies[8 + here].wait()


def constants_kernel(*refs):
    hbm, table_ref, vmem, sems = refs[:8], refs[10], refs[11:-1], refs[-1]
    copies = start_all(list(zip(hbm, vmem)), sems)
    cls_ref, gain_ref, scale_ref, shift_ref, fbias_ref, fgain_ref, q0_ref, q1_ref = vmem
    for copy in copies[:6]:
        copy.wait()
    gain = gain_ref[...]
    cls = cls_ref[...]
    centered = centre(cls)
    ncls = (centered * inverse_spread(centered) * gain).astype(BF)
    table_ref[...] = jnp.zeros_like(table_ref)
    members = scale_ref.shape[0]
    table_ref[SCALE : SCALE + members, :] = centre(scale_ref[...])
    table_ref[SHIFT : SHIFT + members, :] = centre(shift_ref[...])
    table_ref[GAIN : GAIN + 1, :] = gain
    table_ref[FBIAS : FBIAS + 1, :] = fbias_ref[...]
    table_ref[CLS : CLS + 1, :] = cls
    table_ref[FGAIN : FGAIN + 1, :] = fgain_ref[...]
    for copy in copies[6:]:
        copy.wait()
    lhs = jnp.broadcast_to(ncls.astype(F32), (8, ncls.shape[1])).astype(BF)
    local = q0_ref.shape[2]
    heads = local // HD
    row = iota((8, local), 0)
    col = iota((8, local), 1) // HD
    kmap = None
    for i, ref in enumerate((q0_ref, q1_ref)):
        query = dot(lhs, ref[0]) * (1.0 / math.sqrt(HD))
        spread = jnp.where(row == col + i * heads, query, 0.0)
        part = join3(dot_t(split3(spread), ref[1]))
        kmap = part if kmap is None else kmap + part
        table_ref[VCLS : VCLS + 1, i * local : (i + 1) * local] = dot(lhs, ref[2])[0:1]
    table_ref[KMAP : KMAP + 8, :] = kmap
    logits = jnp.sum(kmap * ncls.astype(F32), axis=-1, keepdims=True)
    eye = iota((8, LANES), 0) == iota((8, LANES), 1)
    table_ref[LCLS : LCLS + 1, :LANES] = jnp.sum(jnp.where(eye, logits, 0.0), axis=0, keepdims=True)


def attend_kernel(
    members, rows_ref, near_ref, far_ref, place_ref, table_ref, fw0_ref, fw1_ref, q0_ref, q1_ref, *sent_refs
):
    core = lax.axis_index("member")
    rows = rows_ref[...]
    total, fwidth = rows.shape
    local = q0_ref.shape[2]
    gain = table_ref[GAIN : GAIN + 1, :]
    low, high = rows[:, : fwidth // 2].astype(F32), rows[:, fwidth // 2 :].astype(F32)
    first = jnp.where(core == 0, low, high).astype(BF)
    second = jnp.where(core == 0, high, low).astype(BF)
    token = dot(first, fw0_ref[...]) + dot(second, fw1_ref[...]) + table_ref[FBIAS : FBIAS + 1, :]
    centered = centre(token)
    tokens = [(centered * inverse_spread(centered) * gain).astype(BF)]
    preds = near_ref[...].astype(F32) + far_ref[...].astype(F32)
    for m in range(members):
        centered = preds[:, m : m + 1] * table_ref[SCALE + m : SCALE + m + 1, :] + table_ref[SHIFT + m : SHIFT + m + 1, :]
        tokens.append((centered * inverse_spread(centered) * gain).astype(BF))
    normed = jnp.concatenate(tokens, axis=0)
    count = len(tokens)

    kmap = jnp.concatenate([table_ref[KMAP : KMAP + 8, :], jnp.zeros((LANES - 8, table_ref.shape[1]), F32)], axis=0)
    logits = dot_t(normed, jnp.concatenate(split2(kmap), axis=0))
    logits = logits[:, :LANES] + logits[:, LANES:]
    expo = jnp.exp(logits)
    expo_cls = jnp.exp(table_ref[LCLS : LCLS + 1, :LANES])
    norm = expo_cls
    for t in range(count):
        norm = norm + expo[t * total : (t + 1) * total]
    inverse = 1.0 / norm
    weights = jnp.concatenate(
        [expo[t * total : (t + 1) * total] * inverse for t in range(count)] + [expo_cls * inverse], axis=0)
    expand = (iota((2 * LANES, 2 * local), 0) & (LANES - 1)) == iota((2 * LANES, 2 * local), 1) // HD
    spread = dot(jnp.concatenate(split2(weights), axis=1), expand.astype(F32).astype(BF))
    parts = []
    for i, ref in enumerate((q0_ref, q1_ref)):
        at = slice(i * local, (i + 1) * local)
        value = dot(normed, ref[2])
        mixed = spread[count * total :, at] * table_ref[VCLS : VCLS + 1, at]
        for t in range(count):
            rng = slice(t * total, (t + 1) * total)
            mixed = mixed + spread[rng, at] * value[rng]
        parts.append(mixed)
    mixed = jnp.concatenate(parts, axis=1).astype(BF)
    size = sent_refs[0].shape[0]
    scatter = (place_ref[...] == iota((size * len(sent_refs), total), 0)).astype(F32).astype(BF)
    sent = dot(scatter, mixed).astype(BF)
    for k, sent_ref in enumerate(sent_refs):
        sent_ref[...] = sent[k * size : (k + 1) * size]


def ensemble_kernel(feat_ref, w_ref, bias_ref, out_ref, after_ref, *refs):
    count = (len(refs) - 2) // 2
    hbm, pred_ref, vmem, sems = refs[:count], refs[count], refs[count + 1 : -1], refs[-1]
    copies = [pltpu.make_async_copy(src, dst, sems.at[i]) for i, (src, dst) in enumerate(zip(hbm, vmem))]

    @pl.when(pl.program_id(0) == 0)
    def _():
        for copy in copies:
            copy.start()

    total = None
    for m in range(w_ref.shape[0]):
        hidden = gelu2(dot(feat_ref[...], w_ref[m]) + bias_ref[m : m + 1]).astype(BF)
        weights = jnp.broadcast_to(out_ref[m : m + 1].astype(F32), (8, out_ref.shape[1])).astype(BF)
        pred = dot_t(weights, hidden)[0:1]
        total = pred if total is None else total + pred
    pred_ref[...] = total

    @pl.when(pl.program_id(0) == pl.num_programs(0) - 1)
    def _():
        for copy in copies:
            copy.wait()


def unpack(ref):
    depth = ref.shape[0] - EXTRA
    extra = ref[depth:, :].astype(F32)
    return ref[:depth, :], *(jnp.sum(extra[i : i + 3], axis=0, keepdims=True) for i in (DOWN, BIAS, HEAD))


def hidden_terms(normed, up, down, bias):
    return jnp.maximum(dot(normed, up) + bias, 0.0).astype(BF).astype(F32) * down


def arrive_kernel(blocks, half, *refs):
    got_refs = refs[:blocks][::-1]
    table_ref, ow0_ref, ow1_ref, next_hbm, state_ref, own_ref, next_ref, next_segment_ref, sems = refs[blocks:]
    (copy,) = start_all([(next_hbm, next_segment_ref)], sems)
    if blocks == 1:
        mixed = got_refs[0][...]
    else:
        mixed = jnp.concatenate([ref[e * half : (e + 1) * half] for e in range(2) for ref in got_refs], axis=0)
    rows = mixed.shape[0] // 2
    local = ow0_ref.shape[0]
    state = table_ref[CLS : CLS + 1, :] + dot(mixed[:, :local], ow0_ref[...]) + dot(mixed[:, local:], ow1_ref[...])
    state_ref[...] = state
    centered = centre(state)
    normed = (centered * inverse_spread(centered) * table_ref[FGAIN : FGAIN + 1, :]).astype(BF)
    own_ref[...] = normed[:rows]
    next_ref[...] = normed[rows:]
    copy.wait()


def near_score_kernel(state_ref, own_ref, next_ref, up0_ref, up1_ref, up2_ref, score_ref):
    rows = own_ref.shape[0]
    up, down, bias, head = unpack(up0_ref)
    terms = state_ref[:rows] * head + hidden_terms(own_ref[...], up, down, bias)
    up, down, bias, _ = unpack(up1_ref)
    terms = terms + hidden_terms(own_ref[...], up, down, bias)
    score_ref[:rows] = jnp.sum(terms, axis=-1, keepdims=True)
    up, down, bias, head = unpack(up2_ref)
    terms = state_ref[rows:] * head + hidden_terms(next_ref[...], up, down, bias)
    score_ref[rows:] = jnp.sum(terms, axis=-1, keepdims=True)


def far_score_kernel(blocks, half, near_ref, next_ref, up2_ref, out_ref):
    rows = next_ref.shape[0]
    up, down, bias, _ = unpack(up2_ref)
    last = jnp.sum(hidden_terms(next_ref[...], up, down, bias), axis=-1, keepdims=True)
    scores = [near_ref[:rows], near_ref[rows:], last]
    if blocks == 1:
        eye = iota((rows, rows), 0) == iota((rows, rows), 1)
        for e, score in enumerate(scores):
            out_ref[:, e * rows : (e + 1) * rows] = jnp.sum(jnp.where(eye, score, 0.0), axis=0, keepdims=True)
    else:
        row, lane = iota((half, LANES), 0), iota((half, LANES), 1)
        for k in range(blocks):
            line = jnp.zeros((half, LANES), F32)
            for e, score in enumerate(scores):
                line = jnp.where(lane == row + e * half, score[k * half : (k + 1) * half], line)
            out_ref[k : k + 1, :] = jnp.sum(line, axis=0, keepdims=True)


def finish_kernel(members, where_ref, pred0_ref, pred1_ref, near_ref, far_ref, out_ref):
    count = where_ref.shape[0]
    table = jnp.concatenate([near_ref[...], far_ref[...]], axis=0)
    sources, length = table.shape
    table = split3(table)
    source = where_ref[:, 0:1]
    opposite = jnp.where(source < sources // 2, source + sources // 2, source - sources // 2)
    lanes = iota((count, length), 1)
    picked = jnp.zeros((count, length), F32)
    for line, lane in ((source, where_ref[:, 1:2]), (opposite, where_ref[:, 3:4])):
        pick = (line == iota((count, sources), 1)).astype(F32).astype(BF)
        picked = picked + jnp.where(lane == lanes, dot(jnp.concatenate([pick] * 3, axis=1), table), 0.0)
    score = jnp.sum(picked, axis=1, keepdims=True)
    hit = where_ref[:, 2:3] == iota((count, out_ref.shape[1]), 1)
    replaced = jnp.sum(jnp.where(hit, score, 0.0), axis=0, keepdims=True)
    taken = jnp.sum(hit.astype(F32), axis=0, keepdims=True)
    ensemble = (pred0_ref[...] + pred1_ref[...]) * (0.5 / members)
    out_ref[...] = jnp.where(taken > 0.0, replaced, ensemble)


def cost(flops, size, trans=0):
    return pl.CostEstimate(flops=flops, bytes_accessed=size, transcendentals=trans)


def params(mib):
    return pltpu.CompilerParams(vmem_limit_bytes=mib * 2**20)


def in_hbm(arrays):
    return [pltpu.with_memory_space_constraint(x, pltpu.HBM) for x in arrays]


def shape(dims, dtype):
    return jax.ShapeDtypeStruct(dims, dtype)


def per_device(
    features, escalated, owner_ids, member_in, member_bias, member_out, feat_weight, feat_bias,
    pred_scale, pred_shift, cls_token, attn_gain, qkv_weight, out_weight, ffn_gain, up_weight,
    up_bias, down_weight, owner_heads,
):
    n = lax.axis_size("rows")
    rows, fwidth = features.shape
    count = escalated.shape[1]
    half = max(1, count // n)
    slots = n * half
    here, _, hidden = member_in.shape
    members = pred_scale.shape[0]
    width = cls_token.shape[0]

    def swap(x):
        return lax.ppermute(x, "member", [(0, 1), (1, 0)])

    row = lambda x: x.reshape(1, -1)
    cls_token, attn_gain, ffn_gain, feat_bias = map(row, (cls_token, attn_gain, ffn_gain, feat_bias))
    owners = owner_ids.reshape(1, count)

    pairs = n // 2
    relative = pairs <= 8
    blocks = pairs if relative else 1
    other_qkv = swap(qkv_weight)
    other_fw = swap(feat_weight)
    other_ow = swap(out_weight)

    dealt = count // 2
    ins = (escalated, owners, features, member_in, member_bias, member_out, down_weight, up_bias, owner_heads, up_weight)
    where, place, mine, near, far, segment = pl.pallas_call(
        functools.partial(route_kernel, n, half, relative),
        out_shape=[shape((count, 4), jnp.int32), shape((1, dealt), jnp.int32), shape((dealt, fwidth), BF),
                   shape((dealt, LANES), BF), shape((dealt, LANES), BF),
                   shape((up_weight.shape[1] + EXTRA, up_weight.shape[2]), BF)],
        in_specs=[HBM] * len(ins),
        out_specs=[VMEM] * 6,
        scratch_shapes=[pltpu.VMEM(x.shape, x.dtype) for x in ins[:-1]] + [pltpu.SemaphoreType.DMA((9 + here,))],
        compiler_params=params(24),
        cost_estimate=cost(2 * count * rows * fwidth + 2 * here * count * fwidth * hidden, 3 * 10**6,
                           here * count * hidden),
        name="route",
    )(*in_hbm(ins))
    far = swap(far)
    next_segment = lax.ppermute(segment, "rows", [(i, i ^ 1) for i in range(n)])
    other_segment = swap(segment)

    ins = (cls_token, attn_gain, pred_scale, pred_shift, feat_bias, ffn_gain, qkv_weight, other_qkv)
    table = pl.pallas_call(
        constants_kernel,
        out_shape=shape((TABLE, width), F32),
        in_specs=[HBM] * len(ins) + [ANY] * 2,
        out_specs=VMEM,
        scratch_shapes=[pltpu.VMEM(x.shape, x.dtype) for x in ins] + [pltpu.SemaphoreType.DMA((len(ins),))],
        compiler_params=params(16),
        cost_estimate=cost(10**8, 2 * 10**6),
        name="constants",
    )(*ins, other_fw, other_ow)

    local = qkv_weight.shape[2]
    sent = pl.pallas_call(
        functools.partial(attend_kernel, members),
        out_shape=[shape((slots // blocks, 2 * local), BF)] * blocks,
        in_specs=[VMEM] * 9,
        out_specs=[VMEM] * blocks,
        compiler_params=params(24),
        cost_estimate=cost(10**9, 2 * 10**6),
        name="attend",
    )(mine, near, far, place, table, feat_weight, other_fw, qkv_weight, other_qkv)

    def across(x, k):
        return lax.ppermute(x, "rows", [(i, i ^ (2 * k)) for i in range(n)])

    def exchange(x):
        groups = [[2 * q + b for q in range(pairs)] for b in range(2)]
        return lax.all_to_all(x, "rows", split_axis=0, concat_axis=0, axis_index_groups=groups, tiled=True)

    if relative:
        got = [sent[0]] + [across(sent[k], k) for k in range(1, pairs)]
    else:
        got = exchange(sent[0].reshape(pairs, 2, half, 2 * local))
        got = [got.transpose(1, 0, 2, 3).reshape(slots, 2 * local)]

    tile = min(rows, 256)
    held = (table, out_weight, other_ow, segment, other_segment)
    pred, table, ow0, ow1, up0, up1 = pl.pallas_call(
        ensemble_kernel,
        grid=(rows // tile,),
        out_shape=[shape((1, rows), F32)] + [shape(x.shape, x.dtype) for x in held],
        in_specs=[
            pl.BlockSpec((tile, fwidth), lambda i: (i, 0)),
            pl.BlockSpec(member_in.shape, lambda i: (0, 0, 0)),
            pl.BlockSpec(member_bias.shape, lambda i: (0, 0)),
            pl.BlockSpec(member_out.shape, lambda i: (0, 0)),
            ANY,
        ] + [ANY] * len(held),
        out_specs=[pl.BlockSpec((1, tile), lambda i: (0, i))] + [VMEM] * len(held),
        scratch_shapes=[pltpu.SemaphoreType.DMA((len(held),))],
        compiler_params=params(24),
        cost_estimate=cost(2 * here * rows * fwidth * hidden, 4 * 10**6, here * rows * hidden),
        name="ensemble",
    )(features, member_in, member_bias, member_out, sent[0], *held)
    other_pred = swap(pred)

    state, own_rows, next_rows, up2 = pl.pallas_call(
        functools.partial(arrive_kernel, blocks, half),
        out_shape=[shape((slots, width), F32), shape((slots // 2, width), BF), shape((slots // 2, width), BF),
                   shape(next_segment.shape, BF)],
        in_specs=[VMEM] * (blocks + 3) + [ANY],
        out_specs=[VMEM] * 4,
        scratch_shapes=[pltpu.SemaphoreType.DMA((1,))],
        compiler_params=params(24),
        cost_estimate=cost(5 * 10**8, 2 * 10**6),
        name="arrive",
    )(*got[::-1], table, ow0, ow1, next_segment)
    other_rows = swap(next_rows)
    near_scores = pl.pallas_call(
        near_score_kernel,
        out_shape=shape((slots, 1), F32),
        in_specs=[VMEM] * 6,
        out_specs=VMEM,
        compiler_params=params(24),
        cost_estimate=cost(5 * 10**8, 2 * 10**6),
        name="near_score",
    )(state, own_rows, next_rows, up0, up1, up2)
    scores = pl.pallas_call(
        functools.partial(far_score_kernel, blocks, half),
        out_shape=shape((blocks, LANES if relative else 3 * slots // 2), F32),
        in_specs=[VMEM] * 3,
        out_specs=VMEM,
        compiler_params=params(24),
        cost_estimate=cost(2 * 10**8, 10**6),
        name="far_score",
    )(near_scores, other_rows, up2)
    back = scores
    if relative:
        step = 1
        while step < pairs:
            back = jnp.concatenate([back, across(back, step)], axis=0)
            step *= 2
    else:
        back = exchange(back.reshape(3, pairs, half).transpose(1, 0, 2)).reshape(pairs, 3 * half)

    final = pl.pallas_call(
        functools.partial(finish_kernel, members),
        out_shape=shape((1, rows), F32),
        in_specs=[VMEM] * 5,
        out_specs=VMEM,
        compiler_params=params(8),
        cost_estimate=cost(10**6, 10**6),
        name="finish",
    )(where, pred, other_pred, back, swap(back))
    return final.reshape(rows)


def solution(mesh):
    placed = (
        P(("groups", "rows"), None),
        P(("groups", "rows"), None),
        P(("groups", "rows"), None, None),
        P("member", None, None),
        P("member", None),
        P("member", None),
        P("member", None),
        P(),
        P(),
        P(),
        P(),
        P(),
        P(None, None, "member"),
        P("member", None),
        P(),
        P("rows", None, "member"),
        P("rows", "member"),
        P("rows", "member", None),
        P("rows", None),
    )
    return jax.shard_map(
        per_device, mesh=mesh, in_specs=placed, out_specs=P(("groups", "rows")), check_vma=False
    )
```

```python
import functools
import math

import jax
import jax.numpy as jnp
from jax import lax
from jax.experimental import pallas as pl
from jax.experimental.pallas import tpu as pltpu
from jax.sharding import PartitionSpec as P

HD = 64
EPS = 1e-05
LANES = 128
BF = jnp.bfloat16
F32 = jnp.float32
VMEM = pl.BlockSpec(memory_space=pltpu.VMEM)
HBM = pl.BlockSpec(memory_space=pltpu.HBM)
ANY = pl.BlockSpec(memory_space=pl.ANY)
GELU_C = math.sqrt(2.0 / math.pi)

KMAP, VCLS, LCLS, SCALE, SHIFT, GAIN, FBIAS, CLS, FGAIN = 0, 8, 9, 16, 24, 32, 33, 34, 35
TABLE = 40
DOWN, BIAS, HEAD, EXTRA = 0, 3, 6, 16


def iota(shape, dim):
    return lax.broadcasted_iota(jnp.int32, shape, dim)


def gelu2(x):
    return x + x * jnp.tanh(x * (GELU_C + (GELU_C * 0.044715) * (x * x)))


def dot(a, b):
    return lax.dot_general(a, b, (((1,), (0,)), ((), ())), preferred_element_type=F32)


def dot_t(a, b):
    return lax.dot_general(a, b, (((1,), (1,)), ((), ())), preferred_element_type=F32)


def split2(x):
    high = x.astype(BF)
    return high, (x - high.astype(F32)).astype(BF)


def split3(x):
    high, rest = x.astype(BF), x
    rest = rest - high.astype(F32)
    mid = rest.astype(BF)
    low = (rest - mid.astype(F32)).astype(BF)
    return jnp.concatenate([high.astype(F32), mid.astype(F32), low.astype(F32)], axis=0).astype(BF)


def join3(x):
    rows = x.shape[0] // 3
    return x[:rows] + x[rows : 2 * rows] + x[2 * rows :]


def centre(x):
    return x - jnp.mean(x, axis=-1, keepdims=True)


def inverse_spread(centered):
    return lax.rsqrt(jnp.mean(centered * centered, axis=-1, keepdims=True) + EPS)


def start_all(pairs, sems):
    copies = [pltpu.make_async_copy(src, dst, sems.at[i]) for i, (src, dst) in enumerate(pairs)]
    for copy in copies:
        copy.start()
    return copies


def route_kernel(
    n, half, relative, esc_hbm, own_hbm, feat_hbm, w_hbm, bias_hbm, out_hbm, down_hbm, upb_hbm, head_hbm, up_hbm,
    qkv_hbm, fw_hbm, ow_hbm, where_ref, place_ref, rows_ref, near_ref, far_ref, segment_ref, qkv_ref, fw_ref, ow_ref,
    esc_ref, own_ref, feat_ref, w_ref, bias_ref, out_ref, down_ref, upb_ref, head_ref, sems,
):
    depth = up_hbm.shape[1]
    here = w_hbm.shape[0]
    copies = start_all(
        [(esc_hbm, esc_ref), (own_hbm, own_ref), (feat_hbm, feat_ref), (bias_hbm, bias_ref), (out_hbm, out_ref)]
        + [(w_hbm.at[m], w_ref.at[m]) for m in range(here)], sems)
    core = lax.axis_index("member")
    count = esc_hbm.shape[1]
    dealt = count // 2
    copies[0].wait()
    copies[1].wait()
    esc = esc_ref[...]
    own = own_ref[...]
    ii = iota((count, count), 0)
    jj = iota((count, count), 1)
    diag = ii == jj

    def to_col(row):
        return jnp.sum(jnp.where(diag, row, 0).astype(F32), axis=1, keepdims=True)

    own_col = to_col(own).astype(jnp.int32)
    before = jnp.sum((own_col < own).astype(F32), axis=0, keepdims=True).astype(jnp.int32)
    rank = jnp.sum(((own_col == own) & (ii < jj)).astype(F32), axis=0, keepdims=True).astype(jnp.int32)
    position = before + rank
    side = position & 1
    slot = rank >> 1
    me = lax.axis_index("rows")
    apart = own ^ me
    pair = (apart if relative else (own - (own & 1)) + (apart & 1))
    place = pair * half + slot
    dense = (position >> 1) + jnp.where(side == core, 0, dealt)
    mine = dense == ii
    source = jnp.sum(jnp.where(mine, esc, 0).astype(F32), axis=1, keepdims=True).astype(jnp.int32)
    chosen = (source == iota((count, feat_ref.shape[0]), 1)).astype(F32).astype(BF)
    copies[2].wait()
    copies += start_all(
        [(head_hbm, head_ref), (upb_hbm, upb_ref), (down_hbm, down_ref), (fw_hbm, fw_ref), (ow_hbm, ow_ref),
         (up_hbm.at[0], segment_ref.at[:depth]), (qkv_hbm, qkv_ref)], sems.at[pl.ds(5 + here, 7)])
    rows = dot(chosen, feat_ref[...]).astype(BF)
    rows_ref[...] = rows[:dealt]
    lane = iota((LANES, 1), 0)
    preds = None
    copies[3].wait()
    copies[4].wait()
    for m in range(here):
        copies[5 + m].wait()
        act = gelu2(dot(rows, w_ref[m]) + bias_ref[m : m + 1]).astype(BF)
        on_lane = jnp.where(lane == core * here + m, 0.5 * out_ref[m : m + 1].astype(F32), 0.0).astype(BF)
        pred = dot_t(act, on_lane)
        preds = pred if preds is None else preds + pred
    preds = preds.astype(BF)
    near_ref[...] = preds[:dealt]
    far_ref[...] = preds[dealt:]

    line = pair >> 1
    line = line * (n // 2 + 1) + (side ^ core) * (n // 2) ** 2 if relative else line + (side ^ core) * (n // 2)
    where_ref[:, 0:1] = to_col(line).astype(jnp.int32)
    where_ref[:, 1:2] = to_col((apart & 1) * half + slot).astype(jnp.int32)
    where_ref[:, 2:3] = to_col(esc).astype(jnp.int32)

    place_col = jnp.sum(jnp.where(mine, place, 0).astype(F32), axis=1, keepdims=True)
    place_ref[...] = jnp.sum(
        jnp.where(diag[:dealt, :dealt], place_col[:dealt], 0.0), axis=0, keepdims=True
    ).astype(jnp.int32)
    for copy in copies[5 + here : 8 + here]:
        copy.wait()
    head = jnp.broadcast_to(head_ref[...], (8, head_ref.shape[1]))
    down = join3(dot_t(split3(head), down_ref[0]))[0:1]
    extra = [split3(x).astype(F32) for x in (down, upb_ref[...], head_ref[...])]
    extra.append(jnp.zeros((EXTRA - 9, down.shape[1]), F32))
    segment_ref[depth:, :] = jnp.concatenate(extra, axis=0).astype(BF)
    for copy in copies[8 + here :]:
        copy.wait()


def constants_kernel(
    cls_ref, gain_ref, scale_ref, shift_ref, fbias_ref, fgain_ref, q0_ref, q1_ref, _, __, table_ref
):
    gain = gain_ref[...]
    cls = cls_ref[...]
    centered = centre(cls)
    ncls = (centered * inverse_spread(centered) * gain).astype(BF)
    table_ref[...] = jnp.zeros_like(table_ref)
    members = scale_ref.shape[0]
    table_ref[SCALE : SCALE + members, :] = centre(scale_ref[...])
    table_ref[SHIFT : SHIFT + members, :] = centre(shift_ref[...])
    table_ref[GAIN : GAIN + 1, :] = gain
    table_ref[FBIAS : FBIAS + 1, :] = fbias_ref[...]
    table_ref[CLS : CLS + 1, :] = cls
    table_ref[FGAIN : FGAIN + 1, :] = fgain_ref[...]
    lhs = jnp.broadcast_to(ncls.astype(F32), (8, ncls.shape[1])).astype(BF)
    local = q0_ref.shape[2]
    heads = local // HD
    row = iota((8, local), 0)
    col = iota((8, local), 1) // HD
    kmap = None
    for i, ref in enumerate((q0_ref, q1_ref)):
        query = dot(lhs, ref[0]) * (1.0 / math.sqrt(HD))
        spread = jnp.where(row == col + i * heads, query, 0.0)
        part = join3(dot_t(split3(spread), ref[1]))
        kmap = part if kmap is None else kmap + part
        table_ref[VCLS : VCLS + 1, i * local : (i + 1) * local] = dot(lhs, ref[2])[0:1]
    table_ref[KMAP : KMAP + 8, :] = kmap
    logits = jnp.sum(kmap * ncls.astype(F32), axis=-1, keepdims=True)
    eye = iota((8, LANES), 0) == iota((8, LANES), 1)
    table_ref[LCLS : LCLS + 1, :LANES] = jnp.sum(jnp.where(eye, logits, 0.0), axis=0, keepdims=True)


def attend_kernel(
    members, rows_ref, near_ref, far_ref, place_ref, table_ref, fw0_ref, fw1_ref, q0_ref, q1_ref, *sent_refs
):
    core = lax.axis_index("member")
    rows = rows_ref[...]
    total, fwidth = rows.shape
    local = q0_ref.shape[2]
    gain = table_ref[GAIN : GAIN + 1, :]
    low, high = rows[:, : fwidth // 2].astype(F32), rows[:, fwidth // 2 :].astype(F32)
    first = jnp.where(core == 0, low, high).astype(BF)
    second = jnp.where(core == 0, high, low).astype(BF)
    token = dot(first, fw0_ref[...]) + dot(second, fw1_ref[...]) + table_ref[FBIAS : FBIAS + 1, :]
    centered = centre(token)
    tokens = [(centered * inverse_spread(centered) * gain).astype(BF)]
    preds = near_ref[...].astype(F32) + far_ref[...].astype(F32)
    for m in range(members):
        centered = preds[:, m : m + 1] * table_ref[SCALE + m : SCALE + m + 1, :] + table_ref[SHIFT + m : SHIFT + m + 1, :]
        tokens.append((centered * inverse_spread(centered) * gain).astype(BF))
    normed = jnp.concatenate(tokens, axis=0)
    count = len(tokens)

    kmap = jnp.concatenate([table_ref[KMAP : KMAP + 8, :], jnp.zeros((LANES - 8, table_ref.shape[1]), F32)], axis=0)
    logits = dot_t(normed, jnp.concatenate(split2(kmap), axis=0))
    logits = logits[:, :LANES] + logits[:, LANES:]
    expo = jnp.exp(logits)
    expo_cls = jnp.exp(table_ref[LCLS : LCLS + 1, :LANES])
    norm = expo_cls
    for t in range(count):
        norm = norm + expo[t * total : (t + 1) * total]
    inverse = 1.0 / norm
    weights = jnp.concatenate(
        [expo[t * total : (t + 1) * total] * inverse for t in range(count)] + [expo_cls * inverse], axis=0)
    expand = (iota((2 * LANES, 2 * local), 0) & (LANES - 1)) == iota((2 * LANES, 2 * local), 1) // HD
    spread = dot(jnp.concatenate(split2(weights), axis=1), expand.astype(F32).astype(BF))
    parts = []
    for i, ref in enumerate((q0_ref, q1_ref)):
        at = slice(i * local, (i + 1) * local)
        value = dot(normed, ref[2])
        mixed = spread[count * total :, at] * table_ref[VCLS : VCLS + 1, at]
        for t in range(count):
            rng = slice(t * total, (t + 1) * total)
            mixed = mixed + spread[rng, at] * value[rng]
        parts.append(mixed)
    mixed = jnp.concatenate(parts, axis=1).astype(BF)
    size = sent_refs[0].shape[0]
    scatter = (place_ref[...] == iota((size * len(sent_refs), total), 0)).astype(F32).astype(BF)
    sent = dot(scatter, mixed).astype(BF)
    for k, sent_ref in enumerate(sent_refs):
        sent_ref[...] = sent[k * size : (k + 1) * size]


def ensemble_kernel(feat_ref, w_ref, bias_ref, out_ref, after_ref, *refs):
    count = (len(refs) - 2) // 2
    hbm, pred_ref, vmem, sems = refs[:count], refs[count], refs[count + 1 : -1], refs[-1]
    copies = [pltpu.make_async_copy(src, dst, sems.at[i]) for i, (src, dst) in enumerate(zip(hbm, vmem))]

    @pl.when(pl.program_id(0) == 0)
    def _():
        for copy in copies:
            copy.start()

    total = None
    for m in range(w_ref.shape[0]):
        hidden = gelu2(dot(feat_ref[...], w_ref[m]) + bias_ref[m : m + 1]).astype(BF)
        weights = jnp.broadcast_to(out_ref[m : m + 1].astype(F32), (8, out_ref.shape[1])).astype(BF)
        pred = dot_t(weights, hidden)[0:1]
        total = pred if total is None else total + pred
    first = pl.program_id(0) * (total.shape[1] // LANES)
    for i in range(total.shape[1] // LANES):
        pred_ref[pl.ds(first + i, 1), :] = total[:, i * LANES : (i + 1) * LANES]

    @pl.when(pl.program_id(0) == pl.num_programs(0) - 1)
    def _():
        for copy in copies:
            copy.wait()


def unpack(ref):
    depth = ref.shape[0] - EXTRA
    extra = ref[depth:, :].astype(F32)
    return ref[:depth, :], *(jnp.sum(extra[i : i + 3], axis=0, keepdims=True) for i in (DOWN, BIAS, HEAD))


def hidden_terms(normed, up, down, bias):
    return jnp.maximum(dot(normed, up) + bias, 0.0).astype(BF).astype(F32) * down


def states(mixed, table_ref, ow0_ref, ow1_ref):
    local = ow0_ref.shape[0]
    state = table_ref[CLS : CLS + 1, :] + dot(mixed[:, :local], ow0_ref[...]) + dot(mixed[:, local:], ow1_ref[...])
    centered = centre(state)
    return state, (centered * inverse_spread(centered) * table_ref[FGAIN : FGAIN + 1, :]).astype(BF)


def arrived(got_refs, half, e):
    if len(got_refs) == 1:
        rows = got_refs[0].shape[0] // 2
        return got_refs[0][e * rows : (e + 1) * rows]
    return jnp.concatenate([ref[e * half : (e + 1) * half] for ref in got_refs], axis=0)


def arrive_kernel(blocks, half, *refs):
    table_ref, ow0_ref, ow1_ref, next_hbm, state_ref, normed_ref, next_segment_ref, sems = refs[blocks:]
    (copy,) = start_all([(next_hbm, next_segment_ref)], sems)
    state_ref[...], normed_ref[...] = states(arrived(refs[:blocks][::-1], half, 1), table_ref, ow0_ref, ow1_ref)
    copy.wait()


def near_score_kernel(blocks, half, *refs):
    (table_ref, ow0_ref, ow1_ref, up0_ref, up1_ref, up2_ref, state_ref, next_ref, where_ref,
     score_ref, taken_ref) = refs[blocks:]
    state, normed = states(arrived(refs[:blocks][::-1], half, 0), table_ref, ow0_ref, ow1_ref)
    rows = state.shape[0]
    up, down, bias, head = unpack(up0_ref)
    terms = state * head + hidden_terms(normed, up, down, bias)
    up, down, bias, _ = unpack(up1_ref)
    terms = terms + hidden_terms(normed, up, down, bias)
    score_ref[:rows] = jnp.sum(terms, axis=-1, keepdims=True)
    up, down, bias, head = unpack(up2_ref)
    terms = state_ref[...] * head + hidden_terms(next_ref[...], up, down, bias)
    score_ref[rows:] = jnp.sum(terms, axis=-1, keepdims=True)
    hit = where_ref[:, 2:3] == iota((where_ref.shape[0], taken_ref.shape[1]), 1)
    taken_ref[...] = jnp.sum(hit.astype(F32), axis=0, keepdims=True)


def far_score_kernel(blocks, half, near_ref, next_ref, up2_ref, out_ref):
    rows = next_ref.shape[0]
    up, down, bias, _ = unpack(up2_ref)
    last = jnp.sum(hidden_terms(next_ref[...], up, down, bias), axis=-1, keepdims=True)
    scores = [near_ref[:rows], near_ref[rows:], last]
    if blocks == 1:
        eye = iota((rows, rows), 0) == iota((rows, rows), 1)
        for e, score in enumerate(scores):
            out_ref[:, e * rows : (e + 1) * rows] = jnp.sum(jnp.where(eye, score, 0.0), axis=0, keepdims=True)
    else:
        row, lane = iota((half, LANES), 0), iota((half, LANES), 1)
        for k in range(blocks):
            line = jnp.zeros((half, LANES), F32)
            for e, score in enumerate(scores):
                line = jnp.where(lane == row + e * half, score[k * half : (k + 1) * half], line)
            out_ref[k : k + 1, :] = jnp.sum(line, axis=0, keepdims=True)


def finish_kernel(members, half, lines, where_ref, taken_ref, near_ref, far_ref, out_ref):
    near, far = near_ref[...], far_ref[...]
    ensemble = (near[lines:] + far[lines:]) * (0.5 / members)
    ensemble = jnp.concatenate([ensemble[i : i + 1] for i in range(ensemble.shape[0])], axis=1)
    lanes = iota((lines, LANES), 1)
    last = (lanes >= half) & (lanes < 2 * half)

    def whole(mine, others):
        return mine[:lines] + jnp.where(last, pltpu.roll(others[:lines], LANES - half, 1), 0.0)

    table = split3(jnp.concatenate([whole(near, far), whole(far, near)], axis=0))
    count = where_ref.shape[0]
    pick = (where_ref[:, 0:1] == iota((count, 2 * lines), 1)).astype(F32).astype(BF)
    picked = dot(jnp.concatenate([pick] * 3, axis=1), table)
    score = jnp.sum(jnp.where(where_ref[:, 1:2] == iota((count, LANES), 1), picked, 0.0), axis=1, keepdims=True)
    hit = where_ref[:, 2:3] == iota((count, out_ref.shape[1]), 1)
    replaced = jnp.sum(jnp.where(hit, score, 0.0), axis=0, keepdims=True)
    out_ref[...] = jnp.where(taken_ref[...] > 0.0, replaced, ensemble)


def cost(flops, size, trans=0):
    return pl.CostEstimate(flops=flops, bytes_accessed=size, transcendentals=trans)


def params(mib):
    return pltpu.CompilerParams(vmem_limit_bytes=mib * 2**20)


def in_hbm(arrays):
    return [pltpu.with_memory_space_constraint(x, pltpu.HBM) for x in arrays]


def shape(dims, dtype):
    return jax.ShapeDtypeStruct(dims, dtype)


def per_device(
    features, escalated, owner_ids, member_in, member_bias, member_out, feat_weight, feat_bias,
    pred_scale, pred_shift, cls_token, attn_gain, qkv_weight, out_weight, ffn_gain, up_weight,
    up_bias, down_weight, owner_heads,
):
    n = lax.axis_size("rows")
    rows, fwidth = features.shape
    count = escalated.shape[1]
    half = max(1, count // n)
    slots = n * half
    here, _, hidden = member_in.shape
    members = pred_scale.shape[0]
    width = cls_token.shape[0]

    def swap(x):
        return lax.ppermute(x, "member", [(0, 1), (1, 0)])

    row = lambda x: x.reshape(1, -1)
    cls_token, attn_gain, ffn_gain, feat_bias = map(row, (cls_token, attn_gain, ffn_gain, feat_bias))
    owners = owner_ids.reshape(1, count)

    pairs = n // 2
    relative = pairs <= 8
    blocks = pairs if relative else 1
    other_qkv = swap(qkv_weight)

    dealt = count // 2
    ins = (escalated, owners, features, member_in, member_bias, member_out, down_weight, up_bias, owner_heads, up_weight,
           qkv_weight, feat_weight, out_weight)
    where, place, mine, near, far, segment, own_qkv, own_fw, own_ow = pl.pallas_call(
        functools.partial(route_kernel, n, half, relative),
        out_shape=[shape((count, 4), jnp.int32), shape((1, dealt), jnp.int32), shape((dealt, fwidth), BF),
                   shape((dealt, LANES), BF), shape((dealt, LANES), BF),
                   shape((up_weight.shape[1] + EXTRA, up_weight.shape[2]), BF), shape(qkv_weight.shape, BF),
                   shape(feat_weight.shape, BF), shape(out_weight.shape, BF)],
        in_specs=[HBM] * len(ins),
        out_specs=[VMEM] * 9,
        scratch_shapes=[pltpu.VMEM(x.shape, x.dtype) for x in ins[:9]] + [pltpu.SemaphoreType.DMA((12 + here,))],
        compiler_params=params(24),
        cost_estimate=cost(2 * count * rows * fwidth + 2 * here * count * fwidth * hidden, 3 * 10**6,
                           here * count * hidden),
        name="route",
    )(*in_hbm(ins))
    far = swap(far)
    other_fw = swap(own_fw)
    other_ow = swap(own_ow)
    next_segment = lax.ppermute(segment, "rows", [(i, i ^ 1) for i in range(n)])
    other_segment = swap(segment)

    ins = (cls_token, attn_gain, pred_scale, pred_shift, feat_bias, ffn_gain, own_qkv, other_qkv)
    table = pl.pallas_call(
        constants_kernel,
        out_shape=shape((TABLE, width), F32),
        in_specs=[VMEM] * len(ins) + [ANY] * 2,
        out_specs=VMEM,
        compiler_params=params(16),
        cost_estimate=cost(10**8, 2 * 10**6),
        name="constants",
    )(*ins, other_fw, other_ow)

    local = qkv_weight.shape[2]
    sent = pl.pallas_call(
        functools.partial(attend_kernel, members),
        out_shape=[shape((slots // blocks, 2 * local), BF)] * blocks,
        in_specs=[VMEM] * 9,
        out_specs=[VMEM] * blocks,
        compiler_params=params(24),
        cost_estimate=cost(10**9, 2 * 10**6),
        name="attend",
    )(mine, near, far, place, table, own_fw, other_fw, own_qkv, other_qkv)

    def across(x, k):
        return lax.ppermute(x, "rows", [(i, i ^ (2 * k)) for i in range(n)])

    def exchange(x):
        groups = [[2 * q + b for q in range(pairs)] for b in range(2)]
        return lax.all_to_all(x, "rows", split_axis=0, concat_axis=0, axis_index_groups=groups, tiled=True)

    if relative:
        got = [sent[0]] + [across(sent[k], k) for k in range(1, pairs)]
    else:
        got = exchange(sent[0].reshape(pairs, 2, half, 2 * local))
        got = [got.transpose(1, 0, 2, 3).reshape(slots, 2 * local)]

    tile = min(rows, 256)
    held = (table, own_ow, other_ow, segment, other_segment)
    pred, table, ow0, ow1, up0, up1 = pl.pallas_call(
        ensemble_kernel,
        grid=(rows // tile,),
        out_shape=[shape((rows // LANES, LANES), F32)] + [shape(x.shape, x.dtype) for x in held],
        in_specs=[
            pl.BlockSpec((tile, fwidth), lambda i: (i, 0)),
            pl.BlockSpec(member_in.shape, lambda i: (0, 0, 0)),
            pl.BlockSpec(member_bias.shape, lambda i: (0, 0)),
            pl.BlockSpec(member_out.shape, lambda i: (0, 0)),
            ANY,
        ] + [ANY] * len(held),
        out_specs=[pl.BlockSpec((rows // LANES, LANES), lambda i: (0, 0))] + [VMEM] * len(held),
        scratch_shapes=[pltpu.SemaphoreType.DMA((len(held),))],
        compiler_params=params(24),
        cost_estimate=cost(2 * here * rows * fwidth * hidden, 4 * 10**6, here * rows * hidden),
        name="ensemble",
    )(features, member_in, member_bias, member_out, sent[0], *held)

    state, next_rows, up2 = pl.pallas_call(
        functools.partial(arrive_kernel, blocks, half),
        out_shape=[shape((slots // 2, width), F32), shape((slots // 2, width), BF), shape(next_segment.shape, BF)],
        in_specs=[VMEM] * (blocks + 3) + [ANY],
        out_specs=[VMEM] * 3,
        scratch_shapes=[pltpu.SemaphoreType.DMA((1,))],
        compiler_params=params(24),
        cost_estimate=cost(2 * 10**8, 2 * 10**6),
        name="arrive",
    )(*got[::-1], table, ow0, ow1, next_segment)
    other_rows = swap(next_rows)
    near_scores, taken = pl.pallas_call(
        functools.partial(near_score_kernel, blocks, half),
        out_shape=[shape((slots, 1), F32), shape((1, rows), F32)],
        in_specs=[VMEM] * (blocks + 9),
        out_specs=[VMEM] * 2,
        compiler_params=params(24),
        cost_estimate=cost(5 * 10**8, 2 * 10**6),
        name="near_score",
    )(*got[::-1], table, ow0, ow1, up0, up1, up2, state, next_rows, where)
    scores = pl.pallas_call(
        functools.partial(far_score_kernel, blocks, half),
        out_shape=shape((blocks, LANES if relative else 3 * slots // 2), F32),
        in_specs=[VMEM] * 3,
        out_specs=VMEM,
        compiler_params=params(24),
        cost_estimate=cost(2 * 10**8, 10**6),
        name="far_score",
    )(near_scores, other_rows, up2)
    back = scores
    if relative:
        step = 1
        while step < pairs:
            back = jnp.concatenate([back, across(back, step)], axis=0)
            step *= 2
    else:
        back = exchange(back.reshape(3, pairs, half).transpose(1, 0, 2)).reshape(pairs, 3 * half)
        back = jnp.pad(back, ((0, 0), (0, LANES - 3 * half)))
    lines = back.shape[0]
    near_lines = jnp.concatenate([back, pred], axis=0)

    final = pl.pallas_call(
        functools.partial(finish_kernel, members, half, lines),
        out_shape=shape((1, rows), F32),
        in_specs=[VMEM] * 4,
        out_specs=VMEM,
        compiler_params=params(8),
        cost_estimate=cost(10**6, 10**6),
        name="finish",
    )(where, taken, near_lines, swap(near_lines))
    return final.reshape(rows)


def solution(mesh):
    placed = (
        P(("groups", "rows"), None),
        P(("groups", "rows"), None),
        P(("groups", "rows"), None, None),
        P("member", None, None),
        P("member", None),
        P("member", None),
        P("member", None),
        P(),
        P(),
        P(),
        P(),
        P(),
        P(None, None, "member"),
        P("member", None),
        P(),
        P("rows", None, "member"),
        P("rows", "member"),
        P("rows", "member", None),
        P("rows", None),
    )
    return jax.shard_map(
        per_device, mesh=mesh, in_specs=placed, out_specs=P(("groups", "rows")), check_vma=False
    )
```

```python
import functools
import math

import jax
import jax.numpy as jnp
from jax import lax
from jax.experimental import pallas as pl
from jax.experimental.pallas import tpu as pltpu
from jax.sharding import PartitionSpec as P

HD = 64
EPS = 1e-05
LANES = 128
BF = jnp.bfloat16
F32 = jnp.float32
VMEM = pl.BlockSpec(memory_space=pltpu.VMEM)
HBM = pl.BlockSpec(memory_space=pltpu.HBM)
ANY = pl.BlockSpec(memory_space=pl.ANY)
GELU_C = math.sqrt(2.0 / math.pi)

KMAP, VCLS, LCLS, SCALE, SHIFT, GAIN, FBIAS, CLS, FGAIN = 0, 8, 9, 16, 24, 32, 33, 34, 35
TABLE = 40
DOWN, BIAS, HEAD, EXTRA = 0, 3, 6, 16


def iota(shape, dim):
    return lax.broadcasted_iota(jnp.int32, shape, dim)


def gelu2(x):
    return x + x * jnp.tanh(x * (GELU_C + (GELU_C * 0.044715) * (x * x)))


def dot(a, b):
    return lax.dot_general(a, b, (((1,), (0,)), ((), ())), preferred_element_type=F32)


def dot_t(a, b):
    return lax.dot_general(a, b, (((1,), (1,)), ((), ())), preferred_element_type=F32)


def split2(x):
    high = x.astype(BF)
    return high, (x - high.astype(F32)).astype(BF)


def split3(x):
    high, rest = x.astype(BF), x
    rest = rest - high.astype(F32)
    mid = rest.astype(BF)
    low = (rest - mid.astype(F32)).astype(BF)
    return jnp.concatenate([high.astype(F32), mid.astype(F32), low.astype(F32)], axis=0).astype(BF)


def join3(x):
    rows = x.shape[0] // 3
    return x[:rows] + x[rows : 2 * rows] + x[2 * rows :]


def centre(x):
    return x - jnp.mean(x, axis=-1, keepdims=True)


def inverse_spread(centered):
    return lax.rsqrt(jnp.mean(centered * centered, axis=-1, keepdims=True) + EPS)


def start_all(pairs, sems):
    copies = [pltpu.make_async_copy(src, dst, sems.at[i]) for i, (src, dst) in enumerate(pairs)]
    for copy in copies:
        copy.start()
    return copies


def route_kernel(
    n, half, relative, esc_hbm, own_hbm, feat_hbm, w_hbm, bias_hbm, out_hbm, down_hbm, upb_hbm, head_hbm, up_hbm,
    qkv_hbm, fw_hbm, ow_hbm, index_ref, rows_ref, near_ref, far_ref, segment_ref, qkv_ref, both_ref,
    esc_ref, own_ref, feat_ref, w_ref, bias_ref, out_ref, down_ref, upb_ref, head_ref, sems,
):
    depth = up_hbm.shape[1]
    here = w_hbm.shape[0]
    copies = start_all(
        [(esc_hbm, esc_ref), (own_hbm, own_ref), (feat_hbm, feat_ref), (bias_hbm, bias_ref), (out_hbm, out_ref)]
        + [(w_hbm.at[m], w_ref.at[m]) for m in range(here)], sems)
    core = lax.axis_index("member")
    count = esc_hbm.shape[1]
    dealt = count // 2
    copies[0].wait()
    copies[1].wait()
    esc = esc_ref[...]
    own = own_ref[...]
    ii = iota((count, count), 0)
    jj = iota((count, count), 1)
    diag = ii == jj

    def to_col(row):
        return jnp.sum(jnp.where(diag, row, 0).astype(F32), axis=1, keepdims=True)

    own_col = to_col(own).astype(jnp.int32)
    before = jnp.sum((own_col < own).astype(F32), axis=0, keepdims=True).astype(jnp.int32)
    rank = jnp.sum(((own_col == own) & (ii < jj)).astype(F32), axis=0, keepdims=True).astype(jnp.int32)
    position = before + rank
    side = position & 1
    slot = rank >> 1
    me = lax.axis_index("rows")
    apart = own ^ me
    pair = (apart if relative else (own - (own & 1)) + (apart & 1))
    place = pair * half + slot
    dense = (position >> 1) + jnp.where(side == core, 0, dealt)
    mine = dense == ii
    source = jnp.sum(jnp.where(mine, esc, 0).astype(F32), axis=1, keepdims=True).astype(jnp.int32)
    chosen = (source == iota((count, feat_ref.shape[0]), 1)).astype(F32).astype(BF)
    copies[2].wait()
    copies += start_all(
        [(head_hbm, head_ref), (upb_hbm, upb_ref), (down_hbm, down_ref), (fw_hbm, both_ref.at[: fw_hbm.shape[0]]),
         (ow_hbm, both_ref.at[fw_hbm.shape[0] :]),
         (up_hbm.at[0], segment_ref.at[:depth]), (qkv_hbm, qkv_ref)], sems.at[pl.ds(5 + here, 7)])
    rows = dot(chosen, feat_ref[...]).astype(BF)
    rows_ref[...] = rows[:dealt]
    lane = iota((LANES, 1), 0)
    preds = None
    copies[3].wait()
    copies[4].wait()
    for m in range(here):
        copies[5 + m].wait()
        act = gelu2(dot(rows, w_ref[m]) + bias_ref[m : m + 1]).astype(BF)
        on_lane = jnp.where(lane == core * here + m, 0.5 * out_ref[m : m + 1].astype(F32), 0.0).astype(BF)
        pred = dot_t(act, on_lane)
        preds = pred if preds is None else preds + pred
    preds = preds.astype(BF)
    near_ref[...] = preds[:dealt]
    far_ref[...] = preds[dealt:]

    line = pair >> 1
    line = line * (n // 2 + 1) + (side ^ core) * (n // 2) ** 2 if relative else line + (side ^ core) * (n // 2)
    for i, row in enumerate((line, (apart & 1) * half + slot, esc, place, dense)):
        index_ref[i : i + 1, :] = row

    for copy in copies[5 + here : 8 + here]:
        copy.wait()
    head = jnp.broadcast_to(head_ref[...], (8, head_ref.shape[1]))
    down = join3(dot_t(split3(head), down_ref[0]))[0:1]
    extra = [split3(x).astype(F32) for x in (down, upb_ref[...], head_ref[...])]
    extra.append(jnp.zeros((EXTRA - 9, down.shape[1]), F32))
    segment_ref[depth:, :] = jnp.concatenate(extra, axis=0).astype(BF)
    for copy in copies[8 + here :]:
        copy.wait()


def constants_kernel(
    cls_ref, gain_ref, scale_ref, shift_ref, fbias_ref, fgain_ref, q0_ref, q1_ref, index_ref,
    table_ref, where_ref, place_ref,
):
    count = index_ref.shape[1]
    diag = iota((count, count), 0) == iota((count, count), 1)
    cols = [
        jnp.sum(jnp.where(diag, index_ref[i : i + 1, :], 0).astype(F32), axis=1, keepdims=True) for i in range(5)]
    for i in range(3):
        where_ref[:, i : i + 1] = cols[i].astype(jnp.int32)
    dealt = place_ref.shape[1]
    placed = cols[4].astype(jnp.int32) == iota((count, dealt), 1)
    place_ref[...] = jnp.sum(jnp.where(placed, cols[3], 0.0), axis=0, keepdims=True).astype(jnp.int32)
    gain = gain_ref[...]
    cls = cls_ref[...]
    centered = centre(cls)
    ncls = (centered * inverse_spread(centered) * gain).astype(BF)
    table_ref[...] = jnp.zeros_like(table_ref)
    members = scale_ref.shape[0]
    table_ref[SCALE : SCALE + members, :] = centre(scale_ref[...])
    table_ref[SHIFT : SHIFT + members, :] = centre(shift_ref[...])
    table_ref[GAIN : GAIN + 1, :] = gain
    table_ref[FBIAS : FBIAS + 1, :] = fbias_ref[...]
    table_ref[CLS : CLS + 1, :] = cls
    table_ref[FGAIN : FGAIN + 1, :] = fgain_ref[...]
    lhs = jnp.broadcast_to(ncls.astype(F32), (8, ncls.shape[1])).astype(BF)
    local = q0_ref.shape[2]
    heads = local // HD
    row = iota((8, local), 0)
    col = iota((8, local), 1) // HD
    kmap = None
    for i, ref in enumerate((q0_ref, q1_ref)):
        query = dot(lhs, ref[0]) * (1.0 / math.sqrt(HD))
        spread = jnp.where(row == col + i * heads, query, 0.0)
        part = join3(dot_t(split3(spread), ref[1]))
        kmap = part if kmap is None else kmap + part
        table_ref[VCLS : VCLS + 1, i * local : (i + 1) * local] = dot(lhs, ref[2])[0:1]
    table_ref[KMAP : KMAP + 8, :] = kmap
    logits = jnp.sum(kmap * ncls.astype(F32), axis=-1, keepdims=True)
    eye = iota((8, LANES), 0) == iota((8, LANES), 1)
    table_ref[LCLS : LCLS + 1, :LANES] = jnp.sum(jnp.where(eye, logits, 0.0), axis=0, keepdims=True)


def attend_kernel(
    members, rows_ref, near_ref, far_ref, place_ref, table_ref, fw0_ref, fw1_ref, q0_ref, q1_ref, *sent_refs
):
    core = lax.axis_index("member")
    rows = rows_ref[...]
    total, fwidth = rows.shape
    local = q0_ref.shape[2]
    gain = table_ref[GAIN : GAIN + 1, :]
    low, high = rows[:, : fwidth // 2].astype(F32), rows[:, fwidth // 2 :].astype(F32)
    first = jnp.where(core == 0, low, high).astype(BF)
    second = jnp.where(core == 0, high, low).astype(BF)
    token = dot(first, fw0_ref[: fwidth // 2]) + dot(second, fw1_ref[: fwidth // 2]) + table_ref[FBIAS : FBIAS + 1, :]
    centered = centre(token)
    tokens = [(centered * inverse_spread(centered) * gain).astype(BF)]
    preds = near_ref[...].astype(F32) + far_ref[...].astype(F32)
    for m in range(members):
        centered = preds[:, m : m + 1] * table_ref[SCALE + m : SCALE + m + 1, :] + table_ref[SHIFT + m : SHIFT + m + 1, :]
        tokens.append((centered * inverse_spread(centered) * gain).astype(BF))
    normed = jnp.concatenate(tokens, axis=0)
    count = len(tokens)

    kmap = jnp.concatenate([table_ref[KMAP : KMAP + 8, :], jnp.zeros((LANES - 8, table_ref.shape[1]), F32)], axis=0)
    logits = dot_t(normed, jnp.concatenate(split2(kmap), axis=0))
    logits = logits[:, :LANES] + logits[:, LANES:]
    expo = jnp.exp(logits)
    expo_cls = jnp.exp(table_ref[LCLS : LCLS + 1, :LANES])
    norm = expo_cls
    for t in range(count):
        norm = norm + expo[t * total : (t + 1) * total]
    inverse = 1.0 / norm
    weights = jnp.concatenate(
        [expo[t * total : (t + 1) * total] * inverse for t in range(count)] + [expo_cls * inverse], axis=0)
    expand = (iota((2 * LANES, 2 * local), 0) & (LANES - 1)) == iota((2 * LANES, 2 * local), 1) // HD
    spread = dot(jnp.concatenate(split2(weights), axis=1), expand.astype(F32).astype(BF))
    parts = []
    for i, ref in enumerate((q0_ref, q1_ref)):
        at = slice(i * local, (i + 1) * local)
        value = dot(normed, ref[2])
        mixed = spread[count * total :, at] * table_ref[VCLS : VCLS + 1, at]
        for t in range(count):
            rng = slice(t * total, (t + 1) * total)
            mixed = mixed + spread[rng, at] * value[rng]
        parts.append(mixed)
    mixed = jnp.concatenate(parts, axis=1).astype(BF)
    size = sent_refs[0].shape[0]
    scatter = (place_ref[...] == iota((size * len(sent_refs), total), 0)).astype(F32).astype(BF)
    sent = dot(scatter, mixed).astype(BF)
    for k, sent_ref in enumerate(sent_refs):
        sent_ref[...] = sent[k * size : (k + 1) * size]


def ensemble_kernel(first, count, tile, feat_ref, w_ref, bias_ref, out_ref, after_ref, *refs):
    held = (len(refs) - 1) // 2
    copies = start_all(list(zip(refs[:held], refs[held + 1 :])), refs[-1]) if held else []
    pred_ref = refs[held]
    for t in range(count):
        rows = feat_ref[(first + t) * tile : (first + t + 1) * tile]
        total = None
        for m in range(w_ref.shape[0]):
            hidden = gelu2(dot(rows, w_ref[m]) + bias_ref[m : m + 1]).astype(BF)
            weights = jnp.broadcast_to(out_ref[m : m + 1].astype(F32), (8, out_ref.shape[1])).astype(BF)
            pred = dot_t(weights, hidden)[0:1]
            total = pred if total is None else total + pred
        per = tile // LANES
        for i in range(per):
            pred_ref[t * per + i : t * per + i + 1, :] = total[:, i * LANES : (i + 1) * LANES]
    for copy in copies:
        copy.wait()


def unpack(ref):
    depth = ref.shape[0] - EXTRA
    extra = ref[depth:, :].astype(F32)
    return ref[:depth, :], *(jnp.sum(extra[i : i + 3], axis=0, keepdims=True) for i in (DOWN, BIAS, HEAD))


def hidden_terms(normed, up, down, bias):
    return jnp.maximum(dot(normed, up) + bias, 0.0).astype(BF).astype(F32) * down


def states(mixed, table_ref, both0_ref, both1_ref):
    local = mixed.shape[1] // 2
    ow0, ow1 = (ref[ref.shape[0] - local :] for ref in (both0_ref, both1_ref))
    state = table_ref[CLS : CLS + 1, :] + dot(mixed[:, :local], ow0) + dot(mixed[:, local:], ow1)
    centered = centre(state)
    return state, (centered * inverse_spread(centered) * table_ref[FGAIN : FGAIN + 1, :]).astype(BF)


def arrived(got_refs, half, e):
    if len(got_refs) == 1:
        rows = got_refs[0].shape[0] // 2
        return got_refs[0][e * rows : (e + 1) * rows]
    return jnp.concatenate([ref[e * half : (e + 1) * half] for ref in got_refs], axis=0)


def arrive_kernel(blocks, half, *refs):
    table_ref, both0_ref, both1_ref, next_hbm, state_ref, normed_ref, next_segment_ref, sems = refs[blocks:]
    (copy,) = start_all([(next_hbm, next_segment_ref)], sems)
    state_ref[...], normed_ref[...] = states(arrived(refs[:blocks][::-1], half, 1), table_ref, both0_ref, both1_ref)
    copy.wait()


def near_score_kernel(blocks, half, *refs):
    (table_ref, both0_ref, both1_ref, up0_ref, up1_ref, up2_ref, state_ref, next_ref, where_ref,
     score_ref, taken_ref) = refs[blocks:]
    state, normed = states(arrived(refs[:blocks][::-1], half, 0), table_ref, both0_ref, both1_ref)
    rows = state.shape[0]
    up, down, bias, head = unpack(up0_ref)
    terms = state * head + hidden_terms(normed, up, down, bias)
    up, down, bias, _ = unpack(up1_ref)
    terms = terms + hidden_terms(normed, up, down, bias)
    score_ref[:rows] = jnp.sum(terms, axis=-1, keepdims=True)
    up, down, bias, head = unpack(up2_ref)
    terms = state_ref[...] * head + hidden_terms(next_ref[...], up, down, bias)
    score_ref[rows:] = jnp.sum(terms, axis=-1, keepdims=True)
    hit = where_ref[:, 2:3] == iota((where_ref.shape[0], taken_ref.shape[1]), 1)
    taken_ref[...] = jnp.sum(hit.astype(F32), axis=0, keepdims=True)


def far_score_kernel(blocks, half, near_ref, next_ref, up2_ref, out_ref):
    rows = next_ref.shape[0]
    up, down, bias, _ = unpack(up2_ref)
    last = jnp.sum(hidden_terms(next_ref[...], up, down, bias), axis=-1, keepdims=True)
    scores = [near_ref[:rows], near_ref[rows:], last]
    if blocks == 1:
        eye = iota((rows, rows), 0) == iota((rows, rows), 1)
        for e, score in enumerate(scores):
            out_ref[:, e * rows : (e + 1) * rows] = jnp.sum(jnp.where(eye, score, 0.0), axis=0, keepdims=True)
    else:
        row, lane = iota((half, LANES), 0), iota((half, LANES), 1)
        for k in range(blocks):
            line = jnp.zeros((half, LANES), F32)
            for e, score in enumerate(scores):
                line = jnp.where(lane == row + e * half, score[k * half : (k + 1) * half], line)
            out_ref[k : k + 1, :] = jnp.sum(line, axis=0, keepdims=True)


def finish_kernel(members, half, lines, where_ref, taken_ref, near_ref, far_ref, out_ref):
    near, far = near_ref[...], far_ref[...]
    ensemble = (near[lines:] + far[lines:]) * (0.5 / members)
    ensemble = jnp.concatenate([ensemble[i : i + 1] for i in range(ensemble.shape[0])], axis=1)
    lanes = iota((lines, LANES), 1)
    last = (lanes >= half) & (lanes < 2 * half)

    def whole(mine, others):
        return mine[:lines] + jnp.where(last, pltpu.roll(others[:lines], LANES - half, 1), 0.0)

    table = split3(jnp.concatenate([whole(near, far), whole(far, near)], axis=0))
    count = where_ref.shape[0]
    pick = (where_ref[:, 0:1] == iota((count, 2 * lines), 1)).astype(F32).astype(BF)
    picked = dot(jnp.concatenate([pick] * 3, axis=1), table)
    score = jnp.sum(jnp.where(where_ref[:, 1:2] == iota((count, LANES), 1), picked, 0.0), axis=1, keepdims=True)
    hit = where_ref[:, 2:3] == iota((count, out_ref.shape[1]), 1)
    replaced = jnp.sum(jnp.where(hit, score, 0.0), axis=0, keepdims=True)
    out_ref[...] = jnp.where(taken_ref[...] > 0.0, replaced, ensemble)


def cost(flops, size, trans=0):
    return pl.CostEstimate(flops=flops, bytes_accessed=size, transcendentals=trans)


def params(mib):
    return pltpu.CompilerParams(vmem_limit_bytes=mib * 2**20)


def in_hbm(arrays):
    return [pltpu.with_memory_space_constraint(x, pltpu.HBM) for x in arrays]


def shape(dims, dtype):
    return jax.ShapeDtypeStruct(dims, dtype)


def per_device(
    features, escalated, owner_ids, member_in, member_bias, member_out, feat_weight, feat_bias,
    pred_scale, pred_shift, cls_token, attn_gain, qkv_weight, out_weight, ffn_gain, up_weight,
    up_bias, down_weight, owner_heads,
):
    n = lax.axis_size("rows")
    rows, fwidth = features.shape
    count = escalated.shape[1]
    half = max(1, count // n)
    slots = n * half
    here, _, hidden = member_in.shape
    members = pred_scale.shape[0]
    width = cls_token.shape[0]

    def swap(x):
        return lax.ppermute(x, "member", [(0, 1), (1, 0)])

    row = lambda x: x.reshape(1, -1)
    cls_token, attn_gain, ffn_gain, feat_bias = map(row, (cls_token, attn_gain, ffn_gain, feat_bias))
    owners = owner_ids.reshape(1, count)

    pairs = n // 2
    relative = pairs <= 8
    blocks = pairs if relative else 1
    other_qkv = swap(qkv_weight)

    dealt = count // 2
    ins = (escalated, owners, features, member_in, member_bias, member_out, down_weight, up_bias, owner_heads, up_weight,
           qkv_weight, feat_weight, out_weight)
    index, mine, near, far, segment, own_qkv, own_both = pl.pallas_call(
        functools.partial(route_kernel, n, half, relative),
        out_shape=[shape((8, count), jnp.int32), shape((dealt, fwidth), BF), shape((dealt, LANES), BF),
                   shape((dealt, LANES), BF), shape((up_weight.shape[1] + EXTRA, up_weight.shape[2]), BF),
                   shape(qkv_weight.shape, BF), shape((feat_weight.shape[0] + out_weight.shape[0], width), BF)],
        in_specs=[HBM] * len(ins),
        out_specs=[VMEM] * 7,
        scratch_shapes=[pltpu.VMEM(x.shape, x.dtype) for x in ins[:9]] + [pltpu.SemaphoreType.DMA((12 + here,))],
        compiler_params=params(24),
        cost_estimate=cost(2 * count * rows * fwidth + 2 * here * count * fwidth * hidden, 3 * 10**6,
                           here * count * hidden),
        name="route",
    )(*in_hbm(ins))
    far = swap(far)
    other_both = swap(own_both)
    next_segment = lax.ppermute(segment, "rows", [(i, i ^ 1) for i in range(n)])
    other_segment = swap(segment)

    ins = (cls_token, attn_gain, pred_scale, pred_shift, feat_bias, ffn_gain, own_qkv, other_qkv, index)
    table, where, place = pl.pallas_call(
        constants_kernel,
        out_shape=[shape((TABLE, width), F32), shape((count, 3), jnp.int32), shape((1, dealt), jnp.int32)],
        in_specs=[VMEM] * len(ins),
        out_specs=[VMEM] * 3,
        compiler_params=params(16),
        cost_estimate=cost(10**8, 2 * 10**6),
        name="constants",
    )(*ins)

    local = qkv_weight.shape[2]
    sent = pl.pallas_call(
        functools.partial(attend_kernel, members),
        out_shape=[shape((slots // blocks, 2 * local), BF)] * blocks,
        in_specs=[VMEM] * 9,
        out_specs=[VMEM] * blocks,
        compiler_params=params(24),
        cost_estimate=cost(10**9, 2 * 10**6),
        name="attend",
    )(mine, near, far, place, table, own_both, other_both, own_qkv, other_qkv)

    def across(x, k):
        return lax.ppermute(x, "rows", [(i, i ^ (2 * k)) for i in range(n)])

    def exchange(x):
        groups = [[2 * q + b for q in range(pairs)] for b in range(2)]
        return lax.all_to_all(x, "rows", split_axis=0, concat_axis=0, axis_index_groups=groups, tiled=True)

    if relative:
        got = [sent[0]] + [across(sent[k], k) for k in range(1, pairs)]
    else:
        got = exchange(sent[0].reshape(pairs, 2, half, 2 * local))
        got = [got.transpose(1, 0, 2, 3).reshape(slots, 2 * local)]

    tile = min(rows, 256)
    tiles = rows // tile

    def ensemble(first, number, after, held=()):
        return pl.pallas_call(
            functools.partial(ensemble_kernel, first, number, tile),
            out_shape=[shape((number * tile // LANES, LANES), F32)] + [shape(x.shape, x.dtype) for x in held],
            in_specs=[VMEM] * 4 + [ANY] * (1 + len(held)),
            out_specs=[VMEM] * (1 + len(held)),
            scratch_shapes=[pltpu.SemaphoreType.DMA((len(held),))] if held else [],
            compiler_params=params(24),
            cost_estimate=cost(2 * here * number * tile * fwidth * hidden, 10**6, here * number * tile * hidden),
            name="ensemble",
        )(features, member_in, member_bias, member_out, after, *held)

    early = (tiles + 1) // 2
    preds, table, both0, both1, up0, up1 = ensemble(
        0, early, sent[0], (table, own_both, other_both, segment, other_segment))
    preds = [preds]

    state, next_rows, up2 = pl.pallas_call(
        functools.partial(arrive_kernel, blocks, half),
        out_shape=[shape((slots // 2, width), F32), shape((slots // 2, width), BF), shape(next_segment.shape, BF)],
        in_specs=[VMEM] * (blocks + 3) + [ANY],
        out_specs=[VMEM] * 3,
        scratch_shapes=[pltpu.SemaphoreType.DMA((1,))],
        compiler_params=params(24),
        cost_estimate=cost(2 * 10**8, 2 * 10**6),
        name="arrive",
    )(*got[::-1], table, both0, both1, next_segment)
    other_rows = swap(next_rows)
    near_scores, taken = pl.pallas_call(
        functools.partial(near_score_kernel, blocks, half),
        out_shape=[shape((slots, 1), F32), shape((1, rows), F32)],
        in_specs=[VMEM] * (blocks + 9),
        out_specs=[VMEM] * 2,
        compiler_params=params(24),
        cost_estimate=cost(5 * 10**8, 2 * 10**6),
        name="near_score",
    )(*got[::-1], table, both0, both1, up0, up1, up2, state, next_rows, where)
    scores = pl.pallas_call(
        functools.partial(far_score_kernel, blocks, half),
        out_shape=shape((blocks, LANES if relative else 3 * slots // 2), F32),
        in_specs=[VMEM] * 3,
        out_specs=VMEM,
        compiler_params=params(24),
        cost_estimate=cost(2 * 10**8, 10**6),
        name="far_score",
    )(near_scores, other_rows, up2)
    for first in range(early, tiles):
        preds += ensemble(first, 1, scores)
    back = scores
    if relative:
        step = 1
        while step < pairs:
            back = jnp.concatenate([back, across(back, step)], axis=0)
            step *= 2
    else:
        back = exchange(back.reshape(3, pairs, half).transpose(1, 0, 2)).reshape(pairs, 3 * half)
        back = jnp.pad(back, ((0, 0), (0, LANES - 3 * half)))
    lines = back.shape[0]
    near_lines = jnp.concatenate([back, *preds], axis=0)

    final = pl.pallas_call(
        functools.partial(finish_kernel, members, half, lines),
        out_shape=shape((1, rows), F32),
        in_specs=[VMEM] * 4,
        out_specs=VMEM,
        compiler_params=params(8),
        cost_estimate=cost(10**6, 10**6),
        name="finish",
    )(where, taken, near_lines, swap(near_lines))
    return final.reshape(rows)


def solution(mesh):
    placed = (
        P(("groups", "rows"), None),
        P(("groups", "rows"), None),
        P(("groups", "rows"), None, None),
        P("member", None, None),
        P("member", None),
        P("member", None),
        P("member", None),
        P(),
        P(),
        P(),
        P(),
        P(),
        P(None, None, "member"),
        P("member", None),
        P(),
        P("rows", None, "member"),
        P("rows", "member"),
        P("rows", "member", None),
        P("rows", None),
    )
    return jax.shard_map(
        per_device, mesh=mesh, in_specs=placed, out_specs=P(("groups", "rows")), check_vma=False
    )
```

```python
import functools
import math

import jax
import jax.numpy as jnp
from jax import lax
from jax.experimental import pallas as pl
from jax.experimental.pallas import tpu as pltpu
from jax.sharding import PartitionSpec as P

HD = 64
EPS = 1e-05
LANES = 128
BF = jnp.bfloat16
F32 = jnp.float32
VMEM = pl.BlockSpec(memory_space=pltpu.VMEM)
HBM = pl.BlockSpec(memory_space=pltpu.HBM)
ANY = pl.BlockSpec(memory_space=pl.ANY)
GELU_C = math.sqrt(2.0 / math.pi)

KMAP, VCLS, LCLS, SCALE, SHIFT, GAIN, FBIAS, CLS, FGAIN = 0, 8, 9, 16, 24, 32, 33, 34, 35
TABLE = 40
DOWN, BIAS, HEAD, EXTRA = 0, 3, 6, 16


def iota(shape, dim):
    return lax.broadcasted_iota(jnp.int32, shape, dim)


def gelu2(x):
    return x + x * jnp.tanh(x * (GELU_C + (GELU_C * 0.044715) * (x * x)))


def dot(a, b):
    return lax.dot_general(a, b, (((1,), (0,)), ((), ())), preferred_element_type=F32)


def dot_t(a, b):
    return lax.dot_general(a, b, (((1,), (1,)), ((), ())), preferred_element_type=F32)


def split2(x):
    high = x.astype(BF)
    return high, (x - high.astype(F32)).astype(BF)


def split3(x):
    high, rest = x.astype(BF), x
    rest = rest - high.astype(F32)
    mid = rest.astype(BF)
    low = (rest - mid.astype(F32)).astype(BF)
    return jnp.concatenate([high.astype(F32), mid.astype(F32), low.astype(F32)], axis=0).astype(BF)


def join3(x):
    rows = x.shape[0] // 3
    return x[:rows] + x[rows : 2 * rows] + x[2 * rows :]


def centre(x):
    return x - jnp.mean(x, axis=-1, keepdims=True)


def inverse_spread(centered):
    return lax.rsqrt(jnp.mean(centered * centered, axis=-1, keepdims=True) + EPS)


def start_all(pairs, sems):
    copies = [pltpu.make_async_copy(src, dst, sems.at[i]) for i, (src, dst) in enumerate(pairs)]
    for copy in copies:
        copy.start()
    return copies


def route_kernel(
    n, half, relative, esc_hbm, own_hbm, feat_hbm, w_hbm, bias_hbm, out_hbm, down_hbm, upb_hbm, head_hbm, up_hbm,
    qkv_hbm, fw_hbm, ow_hbm, index_ref, rows_ref, near_ref, far_ref, segment_ref, qkv_ref, both_ref,
    esc_ref, own_ref, feat_ref, w_ref, bias_ref, out_ref, down_ref, upb_ref, head_ref, sems,
):
    depth = up_hbm.shape[1]
    here = w_hbm.shape[0]
    copies = start_all(
        [(esc_hbm, esc_ref), (own_hbm, own_ref), (feat_hbm, feat_ref), (bias_hbm, bias_ref), (out_hbm, out_ref)]
        + [(w_hbm.at[m], w_ref.at[m]) for m in range(here)], sems)
    core = lax.axis_index("member")
    count = esc_hbm.shape[1]
    dealt = count // 2
    copies[0].wait()
    copies[1].wait()
    esc = esc_ref[...]
    own = own_ref[...]
    ii = iota((count, count), 0)
    jj = iota((count, count), 1)
    diag = ii == jj

    def to_col(row):
        return jnp.sum(jnp.where(diag, row, 0).astype(F32), axis=1, keepdims=True)

    own_col = to_col(own).astype(jnp.int32)
    before = jnp.sum((own_col < own).astype(F32), axis=0, keepdims=True).astype(jnp.int32)
    rank = jnp.sum(((own_col == own) & (ii < jj)).astype(F32), axis=0, keepdims=True).astype(jnp.int32)
    position = before + rank
    side = position & 1
    slot = rank >> 1
    me = lax.axis_index("rows")
    apart = own ^ me
    pair = (apart if relative else (own - (own & 1)) + (apart & 1))
    place = pair * half + slot
    dense = (position >> 1) + jnp.where(side == core, 0, dealt)
    mine = dense == ii
    source = jnp.sum(jnp.where(mine, esc, 0).astype(F32), axis=1, keepdims=True).astype(jnp.int32)
    chosen = (source == iota((count, feat_ref.shape[0]), 1)).astype(F32).astype(BF)
    copies[2].wait()
    copies += start_all(
        [(head_hbm, head_ref), (upb_hbm, upb_ref), (down_hbm, down_ref), (fw_hbm, both_ref.at[: fw_hbm.shape[0]]),
         (ow_hbm, both_ref.at[fw_hbm.shape[0] :]),
         (up_hbm.at[0], segment_ref.at[:depth]), (qkv_hbm, qkv_ref)], sems.at[pl.ds(5 + here, 7)])
    rows = dot(chosen, feat_ref[...]).astype(BF)
    rows_ref[...] = rows[:dealt]
    lane = iota((LANES, 1), 0)
    preds = None
    copies[3].wait()
    copies[4].wait()
    for m in range(here):
        copies[5 + m].wait()
        act = gelu2(dot(rows, w_ref[m]) + bias_ref[m : m + 1]).astype(BF)
        on_lane = jnp.where(lane == core * here + m, 0.5 * out_ref[m : m + 1].astype(F32), 0.0).astype(BF)
        pred = dot_t(act, on_lane)
        preds = pred if preds is None else preds + pred
    preds = preds.astype(BF)
    near_ref[...] = preds[:dealt]
    far_ref[...] = preds[dealt:]

    line = pair >> 1
    line = line * (n // 2 + 1) + (side ^ core) * (n // 2) ** 2 if relative else line + (side ^ core) * (n // 2)
    for i, row in enumerate((line, (apart & 1) * half + slot, esc, place, dense)):
        index_ref[i : i + 1, :] = row

    for copy in copies[5 + here : 8 + here]:
        copy.wait()
    head = jnp.broadcast_to(head_ref[...], (8, head_ref.shape[1]))
    down = join3(dot_t(split3(head), down_ref[0]))[0:1]
    extra = [split3(x).astype(F32) for x in (down, upb_ref[...], head_ref[...])]
    extra.append(jnp.zeros((EXTRA - 9, down.shape[1]), F32))
    segment_ref[depth:, :] = jnp.concatenate(extra, axis=0).astype(BF)
    for copy in copies[8 + here :]:
        copy.wait()


def constants_kernel(
    cls_ref, gain_ref, scale_ref, shift_ref, fbias_ref, fgain_ref, q0_ref, q1_ref, index_ref,
    table_ref, where_ref, place_ref,
):
    count = index_ref.shape[1]
    diag = iota((count, count), 0) == iota((count, count), 1)
    cols = [
        jnp.sum(jnp.where(diag, index_ref[i : i + 1, :], 0).astype(F32), axis=1, keepdims=True) for i in range(5)]
    for i in range(3):
        where_ref[:, i : i + 1] = cols[i].astype(jnp.int32)
    dealt = place_ref.shape[1]
    placed = cols[4].astype(jnp.int32) == iota((count, dealt), 1)
    place_ref[...] = jnp.sum(jnp.where(placed, cols[3], 0.0), axis=0, keepdims=True).astype(jnp.int32)
    gain = gain_ref[...]
    cls = cls_ref[...]
    centered = centre(cls)
    ncls = (centered * inverse_spread(centered) * gain).astype(BF)
    table_ref[...] = jnp.zeros_like(table_ref)
    members = scale_ref.shape[0]
    table_ref[SCALE : SCALE + members, :] = centre(scale_ref[...])
    table_ref[SHIFT : SHIFT + members, :] = centre(shift_ref[...])
    table_ref[GAIN : GAIN + 1, :] = gain
    table_ref[FBIAS : FBIAS + 1, :] = fbias_ref[...]
    table_ref[CLS : CLS + 1, :] = cls
    table_ref[FGAIN : FGAIN + 1, :] = fgain_ref[...]
    lhs = jnp.broadcast_to(ncls.astype(F32), (8, ncls.shape[1])).astype(BF)
    local = q0_ref.shape[2]
    heads = local // HD
    row = iota((8, local), 0)
    col = iota((8, local), 1) // HD
    kmap = None
    for i, ref in enumerate((q0_ref, q1_ref)):
        query = dot(lhs, ref[0]) * (1.0 / math.sqrt(HD))
        spread = jnp.where(row == col + i * heads, query, 0.0)
        part = join3(dot_t(split3(spread), ref[1]))
        kmap = part if kmap is None else kmap + part
        table_ref[VCLS : VCLS + 1, i * local : (i + 1) * local] = dot(lhs, ref[2])[0:1]
    table_ref[KMAP : KMAP + 8, :] = kmap
    logits = jnp.sum(kmap * ncls.astype(F32), axis=-1, keepdims=True)
    eye = iota((8, LANES), 0) == iota((8, LANES), 1)
    table_ref[LCLS : LCLS + 1, :LANES] = jnp.sum(jnp.where(eye, logits, 0.0), axis=0, keepdims=True)


def attend_kernel(
    members, rows_ref, near_ref, far_ref, place_ref, table_ref, fw0_ref, fw1_ref, q0_ref, q1_ref, *sent_refs
):
    core = lax.axis_index("member")
    rows = rows_ref[...]
    total, fwidth = rows.shape
    local = q0_ref.shape[2]
    gain = table_ref[GAIN : GAIN + 1, :]
    low, high = rows[:, : fwidth // 2].astype(F32), rows[:, fwidth // 2 :].astype(F32)
    first = jnp.where(core == 0, low, high).astype(BF)
    second = jnp.where(core == 0, high, low).astype(BF)
    token = dot(first, fw0_ref[: fwidth // 2]) + dot(second, fw1_ref[: fwidth // 2]) + table_ref[FBIAS : FBIAS + 1, :]
    centered = centre(token)
    tokens = [(centered * inverse_spread(centered) * gain).astype(BF)]
    preds = near_ref[...].astype(F32) + far_ref[...].astype(F32)
    for m in range(members):
        centered = preds[:, m : m + 1] * table_ref[SCALE + m : SCALE + m + 1, :] + table_ref[SHIFT + m : SHIFT + m + 1, :]
        tokens.append((centered * inverse_spread(centered) * gain).astype(BF))
    normed = jnp.concatenate(tokens, axis=0)
    count = len(tokens)

    kmap = jnp.concatenate([table_ref[KMAP : KMAP + 8, :], jnp.zeros((LANES - 8, table_ref.shape[1]), F32)], axis=0)
    logits = dot_t(normed, jnp.concatenate(split2(kmap), axis=0))
    logits = logits[:, :LANES] + logits[:, LANES:]
    expo = jnp.exp(logits)
    expo_cls = jnp.exp(table_ref[LCLS : LCLS + 1, :LANES])
    norm = expo_cls
    for t in range(count):
        norm = norm + expo[t * total : (t + 1) * total]
    inverse = 1.0 / norm
    weights = jnp.concatenate(
        [expo[t * total : (t + 1) * total] * inverse for t in range(count)] + [expo_cls * inverse], axis=0)
    expand = (iota((2 * LANES, 2 * local), 0) & (LANES - 1)) == iota((2 * LANES, 2 * local), 1) // HD
    spread = dot(jnp.concatenate(split2(weights), axis=1), expand.astype(F32).astype(BF))
    parts = []
    for i, ref in enumerate((q0_ref, q1_ref)):
        at = slice(i * local, (i + 1) * local)
        value = dot(normed, ref[2])
        mixed = spread[count * total :, at] * table_ref[VCLS : VCLS + 1, at]
        for t in range(count):
            rng = slice(t * total, (t + 1) * total)
            mixed = mixed + spread[rng, at] * value[rng]
        parts.append(mixed)
    mixed = jnp.concatenate(parts, axis=1).astype(BF)
    size = sent_refs[0].shape[0]
    scatter = (place_ref[...] == iota((size * len(sent_refs), total), 0)).astype(F32).astype(BF)
    sent = dot(scatter, mixed).astype(BF)
    for k, sent_ref in enumerate(sent_refs):
        sent_ref[...] = sent[k * size : (k + 1) * size]


def ensemble_kernel(first, count, tile, feat_ref, w_ref, bias_ref, out_ref, after_ref, *refs):
    held = (len(refs) - 1) // 2
    copies = start_all(list(zip(refs[:held], refs[held + 1 :])), refs[-1]) if held else []
    pred_ref = refs[held]
    for t in range(count):
        rows = feat_ref[(first + t) * tile : (first + t + 1) * tile]
        total = None
        for m in range(w_ref.shape[0]):
            hidden = gelu2(dot(rows, w_ref[m]) + bias_ref[m : m + 1]).astype(BF)
            weights = jnp.broadcast_to(out_ref[m : m + 1].astype(F32), (8, out_ref.shape[1])).astype(BF)
            pred = dot_t(weights, hidden)[0:1]
            total = pred if total is None else total + pred
        per = tile // LANES
        for i in range(per):
            pred_ref[t * per + i : t * per + i + 1, :] = total[:, i * LANES : (i + 1) * LANES]
    for copy in copies:
        copy.wait()


def unpack(ref):
    depth = ref.shape[0] - EXTRA
    extra = ref[depth:, :].astype(F32)
    return ref[:depth, :], *(jnp.sum(extra[i : i + 3], axis=0, keepdims=True) for i in (DOWN, BIAS, HEAD))


def hidden_terms(normed, up, down, bias):
    return jnp.maximum(dot(normed, up) + bias, 0.0).astype(BF).astype(F32) * down


def states(mixed, table_ref, both0_ref, both1_ref):
    local = mixed.shape[1] // 2
    ow0, ow1 = (ref[ref.shape[0] - local :] for ref in (both0_ref, both1_ref))
    state = table_ref[CLS : CLS + 1, :] + dot(mixed[:, :local], ow0) + dot(mixed[:, local:], ow1)
    centered = centre(state)
    return state, (centered * inverse_spread(centered) * table_ref[FGAIN : FGAIN + 1, :]).astype(BF)


def arrived(got_refs, half, e):
    if len(got_refs) == 1:
        rows = got_refs[0].shape[0] // 2
        return got_refs[0][e * rows : (e + 1) * rows]
    return jnp.concatenate([ref[e * half : (e + 1) * half] for ref in got_refs], axis=0)


def arrive_kernel(blocks, half, *refs):
    table_ref, both0_ref, both1_ref, state_ref, normed_ref = refs[blocks:]
    state_ref[...], normed_ref[...] = states(arrived(refs[:blocks][::-1], half, 1), table_ref, both0_ref, both1_ref)


def near_score_kernel(blocks, half, *refs):
    table_ref, both0_ref, both1_ref, up0_ref, up1_ref, next_hbm, score_ref, next_ref, sems = refs[blocks:]
    (copy,) = start_all([(next_hbm, next_ref)], sems)
    state, normed = states(arrived(refs[:blocks][::-1], half, 0), table_ref, both0_ref, both1_ref)
    up, down, bias, head = unpack(up0_ref)
    terms = state * head + hidden_terms(normed, up, down, bias)
    up, down, bias, _ = unpack(up1_ref)
    terms = terms + hidden_terms(normed, up, down, bias)
    score_ref[...] = jnp.sum(terms, axis=-1, keepdims=True)
    copy.wait()


def far_score_kernel(blocks, half, near_ref, state_ref, mine_ref, other_ref, up2_ref, out_ref):
    rows = near_ref.shape[0]
    up, down, bias, head = unpack(up2_ref)
    terms = hidden_terms(jnp.concatenate([mine_ref[...], other_ref[...]], axis=0), up, down, bias)
    scores = [
        near_ref[...],
        jnp.sum(terms[:rows] + state_ref[...] * head, axis=-1, keepdims=True),
        jnp.sum(terms[rows:], axis=-1, keepdims=True),
    ]
    if blocks == 1:
        eye = iota((rows, rows), 0) == iota((rows, rows), 1)
        for e, score in enumerate(scores):
            out_ref[:, e * rows : (e + 1) * rows] = jnp.sum(jnp.where(eye, score, 0.0), axis=0, keepdims=True)
    else:
        row, lane = iota((half, LANES), 0), iota((half, LANES), 1)
        for k in range(blocks):
            line = jnp.zeros((half, LANES), F32)
            for e, score in enumerate(scores):
                line = jnp.where(lane == row + e * half, score[k * half : (k + 1) * half], line)
            out_ref[k : k + 1, :] = jnp.sum(line, axis=0, keepdims=True)


def expand_kernel(lines, where_ref, after_ref, line_ref, lane_ref):
    rows = lane_ref.shape[1]
    hit = where_ref[:, 2:3] == iota((where_ref.shape[0], rows), 1)

    def by_row(i):
        return jnp.sum(jnp.where(hit, where_ref[:, i : i + 1] + 1, 0).astype(F32), axis=0, keepdims=True).astype(jnp.int32)

    line = (by_row(0) - 1 == iota((lines, rows), 0)).astype(F32)
    line_ref[...] = jnp.concatenate([line] * 3, axis=0).astype(BF)
    lane_ref[...] = by_row(1) - 1


def finish_kernel(members, half, lines, line_ref, lane_ref, near_ref, far_ref, out_ref):
    near, far = near_ref[...], far_ref[...]
    ensemble = (near[lines:] + far[lines:]) * (0.5 / members)
    ensemble = jnp.concatenate([ensemble[i : i + 1] for i in range(ensemble.shape[0])], axis=1)
    lanes = iota((lines, LANES), 1)
    last = (lanes >= half) & (lanes < 2 * half)

    def whole(mine, others):
        return mine[:lines] + jnp.where(last, pltpu.roll(others[:lines], LANES - half, 1), 0.0)

    table = split3(jnp.concatenate([whole(near, far), whole(far, near)], axis=0))
    by_lane = lax.dot_general(table, line_ref[...], (((0,), (0,)), ((), ())), preferred_element_type=F32)
    lane = lane_ref[...]
    replaced = jnp.sum(jnp.where(lane == iota(by_lane.shape, 0), by_lane, 0.0), axis=0, keepdims=True)
    out_ref[...] = jnp.where(lane >= 0, replaced, ensemble)


def cost(flops, size, trans=0):
    return pl.CostEstimate(flops=flops, bytes_accessed=size, transcendentals=trans)


def params(mib):
    return pltpu.CompilerParams(vmem_limit_bytes=mib * 2**20)


def in_hbm(arrays):
    return [pltpu.with_memory_space_constraint(x, pltpu.HBM) for x in arrays]


def shape(dims, dtype):
    return jax.ShapeDtypeStruct(dims, dtype)


def per_device(
    features, escalated, owner_ids, member_in, member_bias, member_out, feat_weight, feat_bias,
    pred_scale, pred_shift, cls_token, attn_gain, qkv_weight, out_weight, ffn_gain, up_weight,
    up_bias, down_weight, owner_heads,
):
    n = lax.axis_size("rows")
    rows, fwidth = features.shape
    count = escalated.shape[1]
    half = max(1, count // n)
    slots = n * half
    here, _, hidden = member_in.shape
    members = pred_scale.shape[0]
    width = cls_token.shape[0]

    def swap(x):
        return lax.ppermute(x, "member", [(0, 1), (1, 0)])

    row = lambda x: x.reshape(1, -1)
    cls_token, attn_gain, ffn_gain, feat_bias = map(row, (cls_token, attn_gain, ffn_gain, feat_bias))
    owners = owner_ids.reshape(1, count)

    pairs = n // 2
    relative = pairs <= 8
    blocks = pairs if relative else 1
    other_qkv = swap(qkv_weight)

    dealt = count // 2
    ins = (escalated, owners, features, member_in, member_bias, member_out, down_weight, up_bias, owner_heads, up_weight,
           qkv_weight, feat_weight, out_weight)
    index, mine, near, far, segment, own_qkv, own_both = pl.pallas_call(
        functools.partial(route_kernel, n, half, relative),
        out_shape=[shape((8, count), jnp.int32), shape((dealt, fwidth), BF), shape((dealt, LANES), BF),
                   shape((dealt, LANES), BF), shape((up_weight.shape[1] + EXTRA, up_weight.shape[2]), BF),
                   shape(qkv_weight.shape, BF), shape((feat_weight.shape[0] + out_weight.shape[0], width), BF)],
        in_specs=[HBM] * len(ins),
        out_specs=[VMEM] * 7,
        scratch_shapes=[pltpu.VMEM(x.shape, x.dtype) for x in ins[:9]] + [pltpu.SemaphoreType.DMA((12 + here,))],
        compiler_params=params(24),
        cost_estimate=cost(2 * count * rows * fwidth + 2 * here * count * fwidth * hidden, 3 * 10**6,
                           here * count * hidden),
        name="route",
    )(*in_hbm(ins))
    far = swap(far)
    other_both = swap(own_both)
    next_segment = lax.ppermute(segment, "rows", [(i, i ^ 1) for i in range(n)])
    other_segment = swap(segment)

    ins = (cls_token, attn_gain, pred_scale, pred_shift, feat_bias, ffn_gain, own_qkv, other_qkv, index)
    table, where, place = pl.pallas_call(
        constants_kernel,
        out_shape=[shape((TABLE, width), F32), shape((count, 3), jnp.int32), shape((1, dealt), jnp.int32)],
        in_specs=[VMEM] * len(ins),
        out_specs=[VMEM] * 3,
        compiler_params=params(16),
        cost_estimate=cost(10**8, 2 * 10**6),
        name="constants",
    )(*ins)

    local = qkv_weight.shape[2]
    sent = pl.pallas_call(
        functools.partial(attend_kernel, members),
        out_shape=[shape((slots // blocks, 2 * local), BF)] * blocks,
        in_specs=[VMEM] * 9,
        out_specs=[VMEM] * blocks,
        compiler_params=params(24),
        cost_estimate=cost(10**9, 2 * 10**6),
        name="attend",
    )(mine, near, far, place, table, own_both, other_both, own_qkv, other_qkv)

    def across(x, k):
        return lax.ppermute(x, "rows", [(i, i ^ (2 * k)) for i in range(n)])

    def exchange(x):
        groups = [[2 * q + b for q in range(pairs)] for b in range(2)]
        return lax.all_to_all(x, "rows", split_axis=0, concat_axis=0, axis_index_groups=groups, tiled=True)

    if relative:
        got = [sent[0]] + [across(sent[k], k) for k in range(1, pairs)]
    else:
        got = exchange(sent[0].reshape(pairs, 2, half, 2 * local))
        got = [got.transpose(1, 0, 2, 3).reshape(slots, 2 * local)]

    tile = min(rows, 256)
    tiles = rows // tile

    def ensemble(first, number, after, held=()):
        return pl.pallas_call(
            functools.partial(ensemble_kernel, first, number, tile),
            out_shape=[shape((number * tile // LANES, LANES), F32)] + [shape(x.shape, x.dtype) for x in held],
            in_specs=[VMEM] * 4 + [ANY] * (1 + len(held)),
            out_specs=[VMEM] * (1 + len(held)),
            scratch_shapes=[pltpu.SemaphoreType.DMA((len(held),))] if held else [],
            compiler_params=params(24),
            cost_estimate=cost(2 * here * number * tile * fwidth * hidden, 10**6, here * number * tile * hidden),
            name="ensemble",
        )(features, member_in, member_bias, member_out, after, *held)

    early = (tiles + 1) // 2
    preds, table, both0, both1, up0, up1 = ensemble(
        0, early, sent[0], (table, own_both, other_both, segment, other_segment))
    preds = [preds]

    state, next_rows = pl.pallas_call(
        functools.partial(arrive_kernel, blocks, half),
        out_shape=[shape((slots // 2, width), F32), shape((slots // 2, width), BF)],
        in_specs=[VMEM] * (blocks + 3),
        out_specs=[VMEM] * 2,
        compiler_params=params(24),
        cost_estimate=cost(2 * 10**8, 2 * 10**6),
        name="arrive",
    )(*got[::-1], table, both0, both1)
    other_rows = swap(next_rows)
    near_scores, up2 = pl.pallas_call(
        functools.partial(near_score_kernel, blocks, half),
        out_shape=[shape((slots // 2, 1), F32), shape(next_segment.shape, BF)],
        in_specs=[VMEM] * (blocks + 5) + [ANY],
        out_specs=[VMEM] * 2,
        scratch_shapes=[pltpu.SemaphoreType.DMA((1,))],
        compiler_params=params(24),
        cost_estimate=cost(5 * 10**8, 2 * 10**6),
        name="near_score",
    )(*got[::-1], table, both0, both1, up0, up1, next_segment)
    scores = pl.pallas_call(
        functools.partial(far_score_kernel, blocks, half),
        out_shape=shape((blocks, LANES if relative else 3 * slots // 2), F32),
        in_specs=[VMEM] * 5,
        out_specs=VMEM,
        compiler_params=params(24),
        cost_estimate=cost(2 * 10**8, 10**6),
        name="far_score",
    )(near_scores, state, next_rows, other_rows, up2)
    for first in range(early, tiles):
        preds += ensemble(first, 1, scores)
    back = scores
    if relative:
        step = 1
        while step < pairs:
            back = jnp.concatenate([back, across(back, step)], axis=0)
            step *= 2
    else:
        back = exchange(back.reshape(3, pairs, half).transpose(1, 0, 2)).reshape(pairs, 3 * half)
        back = jnp.pad(back, ((0, 0), (0, LANES - 3 * half)))
    lines = back.shape[0]
    near_lines = jnp.concatenate([back, *preds], axis=0)
    line_of, lane_of = pl.pallas_call(
        functools.partial(expand_kernel, 2 * lines),
        out_shape=[shape((6 * lines, rows), BF), shape((1, rows), jnp.int32)],
        in_specs=[VMEM, ANY],
        out_specs=[VMEM] * 2,
        compiler_params=params(16),
        cost_estimate=cost(10**8, 10**6),
        name="expand",
    )(where, preds[-1])

    final = pl.pallas_call(
        functools.partial(finish_kernel, members, half, lines),
        out_shape=shape((1, rows), F32),
        in_specs=[VMEM] * 4,
        out_specs=VMEM,
        compiler_params=params(8),
        cost_estimate=cost(10**6, 10**6),
        name="finish",
    )(line_of, lane_of, near_lines, swap(near_lines))
    return final.reshape(rows)


def solution(mesh):
    placed = (
        P(("groups", "rows"), None),
        P(("groups", "rows"), None),
        P(("groups", "rows"), None, None),
        P("member", None, None),
        P("member", None),
        P("member", None),
        P("member", None),
        P(),
        P(),
        P(),
        P(),
        P(),
        P(None, None, "member"),
        P("member", None),
        P(),
        P("rows", None, "member"),
        P("rows", "member"),
        P("rows", "member", None),
        P("rows", None),
    )
    return jax.shard_map(
        per_device, mesh=mesh, in_specs=placed, out_specs=P(("groups", "rows")), check_vma=False
    )
```

```python
import functools
import math

import jax
import jax.numpy as jnp
from jax import lax
from jax.experimental import pallas as pl
from jax.experimental.pallas import tpu as pltpu
from jax.sharding import PartitionSpec as P

HD = 64
EPS = 1e-05
LANES = 128
BF = jnp.bfloat16
F32 = jnp.float32
VMEM = pl.BlockSpec(memory_space=pltpu.VMEM)
HBM = pl.BlockSpec(memory_space=pltpu.HBM)
ANY = pl.BlockSpec(memory_space=pl.ANY)
GELU_C = math.sqrt(2.0 / math.pi)

KMAP, VCLS, LCLS, SCALE, SHIFT, GAIN, FBIAS, CLS, FGAIN = 0, 8, 9, 16, 24, 32, 33, 34, 35
TABLE = 40
DOWN, BIAS, HEAD, EXTRA = 0, 3, 6, 16


def iota(shape, dim):
    return lax.broadcasted_iota(jnp.int32, shape, dim)


def gelu2(x):
    return x + x * jnp.tanh(x * (GELU_C + (GELU_C * 0.044715) * (x * x)))


def dot(a, b):
    return lax.dot_general(a, b, (((1,), (0,)), ((), ())), preferred_element_type=F32)


def dot_t(a, b):
    return lax.dot_general(a, b, (((1,), (1,)), ((), ())), preferred_element_type=F32)


def split2(x):
    high = x.astype(BF)
    return high, (x - high.astype(F32)).astype(BF)


def split3(x):
    high, rest = x.astype(BF), x
    rest = rest - high.astype(F32)
    mid = rest.astype(BF)
    low = (rest - mid.astype(F32)).astype(BF)
    return jnp.concatenate([high.astype(F32), mid.astype(F32), low.astype(F32)], axis=0).astype(BF)


def join3(x):
    rows = x.shape[0] // 3
    return x[:rows] + x[rows : 2 * rows] + x[2 * rows :]


def centre(x):
    return x - jnp.mean(x, axis=-1, keepdims=True)


def inverse_spread(centered):
    return lax.rsqrt(jnp.mean(centered * centered, axis=-1, keepdims=True) + EPS)


def start_all(pairs, sems):
    copies = [pltpu.make_async_copy(src, dst, sems.at[i]) for i, (src, dst) in enumerate(pairs)]
    for copy in copies:
        copy.start()
    return copies


def route_kernel(
    n, half, relative, esc_hbm, own_hbm, feat_hbm, w_hbm, bias_hbm, out_hbm, down_hbm, upb_hbm, head_hbm, up_hbm,
    qkv_hbm, fw_hbm, ow_hbm, index_ref, rows_ref, near_ref, far_ref, segment_ref, qkv_ref, both_ref,
    esc_ref, own_ref, feat_ref, w_ref, bias_ref, out_ref, down_ref, upb_ref, head_ref, sems,
):
    depth = up_hbm.shape[1]
    here = w_hbm.shape[0]
    copies = start_all(
        [(esc_hbm, esc_ref), (own_hbm, own_ref), (feat_hbm, feat_ref), (bias_hbm, bias_ref), (out_hbm, out_ref)]
        + [(w_hbm.at[m], w_ref.at[m]) for m in range(here)], sems)
    core = lax.axis_index("member")
    count = esc_hbm.shape[1]
    dealt = count // 2
    copies[0].wait()
    copies[1].wait()
    esc = esc_ref[...]
    own = own_ref[...]
    ii = iota((count, count), 0)
    jj = iota((count, count), 1)
    diag = ii == jj

    def to_col(row):
        return jnp.sum(jnp.where(diag, row, 0).astype(F32), axis=1, keepdims=True)

    own_col = to_col(own).astype(jnp.int32)
    before = jnp.sum((own_col < own).astype(F32), axis=0, keepdims=True).astype(jnp.int32)
    rank = jnp.sum(((own_col == own) & (ii < jj)).astype(F32), axis=0, keepdims=True).astype(jnp.int32)
    position = before + rank
    side = position & 1
    slot = rank >> 1
    me = lax.axis_index("rows")
    apart = own ^ me
    pair = (apart if relative else (own - (own & 1)) + (apart & 1))
    place = pair * half + slot
    dense = (position >> 1) + jnp.where(side == core, 0, dealt)
    mine = dense == ii
    source = jnp.sum(jnp.where(mine, esc, 0).astype(F32), axis=1, keepdims=True).astype(jnp.int32)
    chosen = (source == iota((count, feat_ref.shape[0]), 1)).astype(F32).astype(BF)
    copies[2].wait()
    copies += start_all(
        [(head_hbm, head_ref), (upb_hbm, upb_ref), (down_hbm, down_ref), (fw_hbm, both_ref.at[: fw_hbm.shape[0]]),
         (ow_hbm, both_ref.at[fw_hbm.shape[0] :]),
         (up_hbm.at[0], segment_ref.at[:depth]), (qkv_hbm, qkv_ref)], sems.at[pl.ds(5 + here, 7)])
    rows = dot(chosen, feat_ref[...]).astype(BF)
    rows_ref[...] = rows[:dealt]
    lane = iota((LANES, 1), 0)
    preds = None
    copies[3].wait()
    copies[4].wait()
    for m in range(here):
        copies[5 + m].wait()
        act = gelu2(dot(rows, w_ref[m]) + bias_ref[m : m + 1]).astype(BF)
        on_lane = jnp.where(lane == core * here + m, 0.5 * out_ref[m : m + 1].astype(F32), 0.0).astype(BF)
        pred = dot_t(act, on_lane)
        preds = pred if preds is None else preds + pred
    preds = preds.astype(BF)
    near_ref[...] = preds[:dealt]
    far_ref[...] = preds[dealt:]

    line = pair >> 1
    line = line * (n // 2 + 1) + (side ^ core) * (n // 2) ** 2 if relative else line + (side ^ core) * (n // 2)
    for i, row in enumerate((line, (apart & 1) * half + slot, esc, place, dense)):
        index_ref[i : i + 1, :] = row

    for copy in copies[5 + here : 8 + here]:
        copy.wait()
    head = jnp.broadcast_to(head_ref[...], (8, head_ref.shape[1]))
    down = join3(dot_t(split3(head), down_ref[0]))[0:1]
    extra = [split3(x).astype(F32) for x in (down, upb_ref[...], head_ref[...])]
    extra.append(jnp.zeros((EXTRA - 9, down.shape[1]), F32))
    segment_ref[depth:, :] = jnp.concatenate(extra, axis=0).astype(BF)
    for copy in copies[8 + here :]:
        copy.wait()


def constants_kernel(
    cls_ref, gain_ref, scale_ref, shift_ref, fbias_ref, fgain_ref, q0_ref, q1_ref, index_ref,
    table_ref, where_ref, place_ref,
):
    count = index_ref.shape[1]
    diag = iota((count, count), 0) == iota((count, count), 1)
    cols = [
        jnp.sum(jnp.where(diag, index_ref[i : i + 1, :], 0).astype(F32), axis=1, keepdims=True) for i in range(5)]
    for i in range(3):
        where_ref[:, i : i + 1] = cols[i].astype(jnp.int32)
    dealt = place_ref.shape[1]
    placed = cols[4].astype(jnp.int32) == iota((count, dealt), 1)
    place_ref[...] = jnp.sum(jnp.where(placed, cols[3], 0.0), axis=0, keepdims=True).astype(jnp.int32)
    gain = gain_ref[...]
    cls = cls_ref[...]
    centered = centre(cls)
    ncls = (centered * inverse_spread(centered) * gain).astype(BF)
    table_ref[...] = jnp.zeros_like(table_ref)
    members = scale_ref.shape[0]
    table_ref[SCALE : SCALE + members, :] = centre(scale_ref[...])
    table_ref[SHIFT : SHIFT + members, :] = centre(shift_ref[...])
    table_ref[GAIN : GAIN + 1, :] = gain
    table_ref[FBIAS : FBIAS + 1, :] = fbias_ref[...]
    table_ref[CLS : CLS + 1, :] = cls
    table_ref[FGAIN : FGAIN + 1, :] = fgain_ref[...]
    lhs = jnp.broadcast_to(ncls.astype(F32), (8, ncls.shape[1])).astype(BF)
    local = q0_ref.shape[2]
    heads = local // HD
    row = iota((8, local), 0)
    col = iota((8, local), 1) // HD
    kmap = None
    for i, ref in enumerate((q0_ref, q1_ref)):
        query = dot(lhs, ref[0]) * (1.0 / math.sqrt(HD))
        spread = jnp.where(row == col + i * heads, query, 0.0)
        part = join3(dot_t(split3(spread), ref[1]))
        kmap = part if kmap is None else kmap + part
        table_ref[VCLS : VCLS + 1, i * local : (i + 1) * local] = dot(lhs, ref[2])[0:1]
    table_ref[KMAP : KMAP + 8, :] = kmap
    logits = jnp.sum(kmap * ncls.astype(F32), axis=-1, keepdims=True)
    eye = iota((8, LANES), 0) == iota((8, LANES), 1)
    table_ref[LCLS : LCLS + 1, :LANES] = jnp.sum(jnp.where(eye, logits, 0.0), axis=0, keepdims=True)


def attend_kernel(
    members, rows_ref, near_ref, far_ref, place_ref, table_ref, fw0_ref, fw1_ref, q0_ref, q1_ref, *sent_refs
):
    core = lax.axis_index("member")
    rows = rows_ref[...]
    total, fwidth = rows.shape
    local = q0_ref.shape[2]
    gain = table_ref[GAIN : GAIN + 1, :]
    low, high = rows[:, : fwidth // 2].astype(F32), rows[:, fwidth // 2 :].astype(F32)
    first = jnp.where(core == 0, low, high).astype(BF)
    second = jnp.where(core == 0, high, low).astype(BF)
    token = dot(first, fw0_ref[: fwidth // 2]) + dot(second, fw1_ref[: fwidth // 2]) + table_ref[FBIAS : FBIAS + 1, :]
    centered = centre(token)
    tokens = [(centered * inverse_spread(centered) * gain).astype(BF)]
    preds = near_ref[...].astype(F32) + far_ref[...].astype(F32)
    for m in range(members):
        centered = preds[:, m : m + 1] * table_ref[SCALE + m : SCALE + m + 1, :] + table_ref[SHIFT + m : SHIFT + m + 1, :]
        tokens.append((centered * inverse_spread(centered) * gain).astype(BF))
    normed = jnp.concatenate(tokens, axis=0)
    count = len(tokens)

    kmap = jnp.concatenate([table_ref[KMAP : KMAP + 8, :], jnp.zeros((LANES - 8, table_ref.shape[1]), F32)], axis=0)
    logits = dot_t(normed, jnp.concatenate(split2(kmap), axis=0))
    logits = logits[:, :LANES] + logits[:, LANES:]
    expo = jnp.exp(logits)
    expo_cls = jnp.exp(table_ref[LCLS : LCLS + 1, :LANES])
    norm = expo_cls
    for t in range(count):
        norm = norm + expo[t * total : (t + 1) * total]
    inverse = 1.0 / norm
    weights = jnp.concatenate(
        [expo[t * total : (t + 1) * total] * inverse for t in range(count)] + [expo_cls * inverse], axis=0)
    expand = (iota((2 * LANES, 2 * local), 0) & (LANES - 1)) == iota((2 * LANES, 2 * local), 1) // HD
    spread = dot(jnp.concatenate(split2(weights), axis=1), expand.astype(F32).astype(BF))
    parts = []
    for i, ref in enumerate((q0_ref, q1_ref)):
        at = slice(i * local, (i + 1) * local)
        value = dot(normed, ref[2])
        mixed = spread[count * total :, at] * table_ref[VCLS : VCLS + 1, at]
        for t in range(count):
            rng = slice(t * total, (t + 1) * total)
            mixed = mixed + spread[rng, at] * value[rng]
        parts.append(mixed)
    mixed = jnp.concatenate(parts, axis=1).astype(BF)
    size = sent_refs[0].shape[0]
    scatter = (place_ref[...] == iota((size * len(sent_refs), total), 0)).astype(F32).astype(BF)
    sent = dot(scatter, mixed).astype(BF)
    for k, sent_ref in enumerate(sent_refs):
        sent_ref[...] = sent[k * size : (k + 1) * size]


def ensemble_kernel(first, count, tile, feat_ref, w_ref, bias_ref, out_ref, after_ref, *refs):
    held = (len(refs) - 1) // 2
    copies = start_all(list(zip(refs[:held], refs[held + 1 :])), refs[-1]) if held else []
    pred_ref = refs[held]
    for t in range(count):
        rows = feat_ref[(first + t) * tile : (first + t + 1) * tile]
        total = None
        for m in range(w_ref.shape[0]):
            hidden = gelu2(dot(rows, w_ref[m]) + bias_ref[m : m + 1]).astype(BF)
            weights = jnp.broadcast_to(out_ref[m : m + 1].astype(F32), (8, out_ref.shape[1])).astype(BF)
            pred = dot_t(weights, hidden)[0:1]
            total = pred if total is None else total + pred
        per = tile // LANES
        for i in range(per):
            pred_ref[t * per + i : t * per + i + 1, :] = total[:, i * LANES : (i + 1) * LANES]
    for copy in copies:
        copy.wait()


def unpack(ref):
    depth = ref.shape[0] - EXTRA
    extra = ref[depth:, :].astype(F32)
    return ref[:depth, :], *(jnp.sum(extra[i : i + 3], axis=0, keepdims=True) for i in (DOWN, BIAS, HEAD))


def hidden_terms(normed, up, down, bias):
    return jnp.maximum(dot(normed, up) + bias, 0.0).astype(BF).astype(F32) * down


def states(mixed, table_ref, both0_ref, both1_ref):
    local = mixed.shape[1] // 2
    ow0, ow1 = (ref[ref.shape[0] - local :] for ref in (both0_ref, both1_ref))
    state = table_ref[CLS : CLS + 1, :] + dot(mixed[:, :local], ow0) + dot(mixed[:, local:], ow1)
    centered = centre(state)
    return state, (centered * inverse_spread(centered) * table_ref[FGAIN : FGAIN + 1, :]).astype(BF)


def arrived(got_refs, half, e):
    if len(got_refs) == 1:
        rows = got_refs[0].shape[0] // 2
        return got_refs[0][e * rows : (e + 1) * rows]
    return jnp.concatenate([ref[e * half : (e + 1) * half] for ref in got_refs], axis=0)


def arrive_kernel(blocks, half, *refs):
    table_ref, both0_ref, both1_ref, state_ref, normed_ref = refs[blocks:]
    state_ref[...], normed_ref[...] = states(arrived(refs[:blocks][::-1], half, 1), table_ref, both0_ref, both1_ref)


def near_score_kernel(blocks, half, *refs):
    table_ref, both0_ref, both1_ref, up0_ref, up1_ref, score_ref = refs[blocks:]
    state, normed = states(arrived(refs[:blocks][::-1], half, 0), table_ref, both0_ref, both1_ref)
    up, down, bias, head = unpack(up0_ref)
    terms = state * head + hidden_terms(normed, up, down, bias)
    up, down, bias, _ = unpack(up1_ref)
    terms = terms + hidden_terms(normed, up, down, bias)
    score_ref[...] = jnp.sum(terms, axis=-1, keepdims=True)


def far_score_kernel(blocks, half, near_ref, state_ref, mine_ref, other_ref, up2_ref, out_ref):
    rows = near_ref.shape[0]
    up, down, bias, head = unpack(up2_ref)
    terms = hidden_terms(jnp.concatenate([mine_ref[...], other_ref[...]], axis=0), up, down, bias)
    scores = [
        near_ref[...],
        jnp.sum(terms[:rows] + state_ref[...] * head, axis=-1, keepdims=True),
        jnp.sum(terms[rows:], axis=-1, keepdims=True),
    ]
    if blocks == 1:
        eye = iota((rows, rows), 0) == iota((rows, rows), 1)
        for e, score in enumerate(scores):
            out_ref[:, e * rows : (e + 1) * rows] = jnp.sum(jnp.where(eye, score, 0.0), axis=0, keepdims=True)
    else:
        row, lane = iota((half, LANES), 0), iota((half, LANES), 1)
        for k in range(blocks):
            line = jnp.zeros((half, LANES), F32)
            for e, score in enumerate(scores):
                line = jnp.where(lane == row + e * half, score[k * half : (k + 1) * half], line)
            out_ref[k : k + 1, :] = jnp.sum(line, axis=0, keepdims=True)


def expand_kernel(lines, where_ref, after_ref, line_ref, lane_ref):
    rows = lane_ref.shape[1]
    hit = where_ref[:, 2:3] == iota((where_ref.shape[0], rows), 1)

    def by_row(i):
        return jnp.sum(jnp.where(hit, where_ref[:, i : i + 1] + 1, 0).astype(F32), axis=0, keepdims=True).astype(jnp.int32)

    line = (by_row(0) - 1 == iota((lines, rows), 0)).astype(F32)
    line_ref[...] = jnp.concatenate([line] * 3, axis=0).astype(BF)
    lane_ref[...] = by_row(1) - 1


def finish_kernel(members, half, lines, line_ref, lane_ref, near_ref, far_ref, out_ref):
    near, far = near_ref[...], far_ref[...]
    ensemble = (near[lines:] + far[lines:]) * (0.5 / members)
    ensemble = jnp.concatenate([ensemble[i : i + 1] for i in range(ensemble.shape[0])], axis=1)
    lanes = iota((lines, LANES), 1)
    last = (lanes >= half) & (lanes < 2 * half)

    def whole(mine, others):
        return mine[:lines] + jnp.where(last, pltpu.roll(others[:lines], LANES - half, 1), 0.0)

    table = split3(jnp.concatenate([whole(near, far), whole(far, near)], axis=0))
    by_lane = lax.dot_general(table, line_ref[...], (((0,), (0,)), ((), ())), preferred_element_type=F32)
    lane = lane_ref[...]
    replaced = jnp.sum(jnp.where(lane == iota(by_lane.shape, 0), by_lane, 0.0), axis=0, keepdims=True)
    out_ref[...] = jnp.where(lane >= 0, replaced, ensemble)


def cost(flops, size, trans=0):
    return pl.CostEstimate(flops=flops, bytes_accessed=size, transcendentals=trans)


def params(mib):
    return pltpu.CompilerParams(vmem_limit_bytes=mib * 2**20)


def in_hbm(arrays):
    return [pltpu.with_memory_space_constraint(x, pltpu.HBM) for x in arrays]


def shape(dims, dtype):
    return jax.ShapeDtypeStruct(dims, dtype)


def per_device(
    features, escalated, owner_ids, member_in, member_bias, member_out, feat_weight, feat_bias,
    pred_scale, pred_shift, cls_token, attn_gain, qkv_weight, out_weight, ffn_gain, up_weight,
    up_bias, down_weight, owner_heads,
):
    n = lax.axis_size("rows")
    rows, fwidth = features.shape
    count = escalated.shape[1]
    half = max(1, count // n)
    slots = n * half
    here, _, hidden = member_in.shape
    members = pred_scale.shape[0]
    width = cls_token.shape[0]

    def swap(x):
        return lax.ppermute(x, "member", [(0, 1), (1, 0)])

    row = lambda x: x.reshape(1, -1)
    cls_token, attn_gain, ffn_gain, feat_bias = map(row, (cls_token, attn_gain, ffn_gain, feat_bias))
    owners = owner_ids.reshape(1, count)

    pairs = n // 2
    relative = pairs <= 8
    blocks = pairs if relative else 1
    other_qkv = swap(qkv_weight)

    dealt = count // 2
    ins = (escalated, owners, features, member_in, member_bias, member_out, down_weight, up_bias, owner_heads, up_weight,
           qkv_weight, feat_weight, out_weight)
    index, mine, near, far, segment, own_qkv, own_both = pl.pallas_call(
        functools.partial(route_kernel, n, half, relative),
        out_shape=[shape((8, count), jnp.int32), shape((dealt, fwidth), BF), shape((dealt, LANES), BF),
                   shape((dealt, LANES), BF), shape((up_weight.shape[1] + EXTRA, up_weight.shape[2]), BF),
                   shape(qkv_weight.shape, BF), shape((feat_weight.shape[0] + out_weight.shape[0], width), BF)],
        in_specs=[HBM] * len(ins),
        out_specs=[VMEM] * 7,
        scratch_shapes=[pltpu.VMEM(x.shape, x.dtype) for x in ins[:9]] + [pltpu.SemaphoreType.DMA((12 + here,))],
        compiler_params=params(24),
        cost_estimate=cost(2 * count * rows * fwidth + 2 * here * count * fwidth * hidden, 3 * 10**6,
                           here * count * hidden),
        name="route",
    )(*in_hbm(ins))
    far = swap(far)
    other_both = swap(own_both)
    next_segment = lax.ppermute(segment, "rows", [(i, i ^ 1) for i in range(n)])
    other_segment = swap(segment)

    ins = (cls_token, attn_gain, pred_scale, pred_shift, feat_bias, ffn_gain, own_qkv, other_qkv, index)
    table, where, place = pl.pallas_call(
        constants_kernel,
        out_shape=[shape((TABLE, width), F32), shape((count, 3), jnp.int32), shape((1, dealt), jnp.int32)],
        in_specs=[VMEM] * len(ins),
        out_specs=[VMEM] * 3,
        compiler_params=params(16),
        cost_estimate=cost(10**8, 2 * 10**6),
        name="constants",
    )(*ins)

    local = qkv_weight.shape[2]
    sent = pl.pallas_call(
        functools.partial(attend_kernel, members),
        out_shape=[shape((slots // blocks, 2 * local), BF)] * blocks,
        in_specs=[VMEM] * 9,
        out_specs=[VMEM] * blocks,
        compiler_params=params(24),
        cost_estimate=cost(10**9, 2 * 10**6),
        name="attend",
    )(mine, near, far, place, table, own_both, other_both, own_qkv, other_qkv)

    def across(x, k):
        return lax.ppermute(x, "rows", [(i, i ^ (2 * k)) for i in range(n)])

    def exchange(x):
        groups = [[2 * q + b for q in range(pairs)] for b in range(2)]
        return lax.all_to_all(x, "rows", split_axis=0, concat_axis=0, axis_index_groups=groups, tiled=True)

    if relative:
        got = [sent[0]] + [across(sent[k], k) for k in range(1, pairs)]
    else:
        got = exchange(sent[0].reshape(pairs, 2, half, 2 * local))
        got = [got.transpose(1, 0, 2, 3).reshape(slots, 2 * local)]

    tile = min(rows, 256)
    tiles = rows // tile

    def ensemble(first, number, after, held=()):
        return pl.pallas_call(
            functools.partial(ensemble_kernel, first, number, tile),
            out_shape=[shape((number * tile // LANES, LANES), F32)] + [shape(x.shape, x.dtype) for x in held],
            in_specs=[VMEM] * 4 + [ANY] * (1 + len(held)),
            out_specs=[VMEM] * (1 + len(held)),
            scratch_shapes=[pltpu.SemaphoreType.DMA((len(held),))] if held else [],
            compiler_params=params(24),
            cost_estimate=cost(2 * here * number * tile * fwidth * hidden, 10**6, here * number * tile * hidden),
            name="ensemble",
        )(features, member_in, member_bias, member_out, after, *held)

    early = (tiles + 1) // 2
    preds, table, both0, both1, up0, up1 = ensemble(
        0, early, sent[0], (table, own_both, other_both, segment, other_segment))
    preds = [preds]

    state, next_rows = pl.pallas_call(
        functools.partial(arrive_kernel, blocks, half),
        out_shape=[shape((slots // 2, width), F32), shape((slots // 2, width), BF)],
        in_specs=[VMEM] * (blocks + 3),
        out_specs=[VMEM] * 2,
        compiler_params=params(24),
        cost_estimate=cost(2 * 10**8, 2 * 10**6),
        name="arrive",
    )(*got[::-1], table, both0, both1)
    other_rows = swap(next_rows)
    near_scores = pl.pallas_call(
        functools.partial(near_score_kernel, blocks, half),
        out_shape=shape((slots // 2, 1), F32),
        in_specs=[VMEM] * (blocks + 5),
        out_specs=VMEM,
        compiler_params=params(24),
        cost_estimate=cost(5 * 10**8, 2 * 10**6),
        name="near_score",
    )(*got[::-1], table, both0, both1, up0, up1)
    scores = pl.pallas_call(
        functools.partial(far_score_kernel, blocks, half),
        out_shape=shape((blocks, LANES if relative else 3 * slots // 2), F32),
        in_specs=[VMEM] * 5,
        out_specs=VMEM,
        compiler_params=params(24),
        cost_estimate=cost(2 * 10**8, 10**6),
        name="far_score",
    )(near_scores, state, next_rows, other_rows, next_segment)
    for first in range(early, tiles):
        preds += ensemble(first, 1, scores)
    back = scores
    if relative:
        step = 1
        while step < pairs:
            back = jnp.concatenate([back, across(back, step)], axis=0)
            step *= 2
    else:
        back = exchange(back.reshape(3, pairs, half).transpose(1, 0, 2)).reshape(pairs, 3 * half)
        back = jnp.pad(back, ((0, 0), (0, LANES - 3 * half)))
    lines = back.shape[0]
    near_lines = jnp.concatenate([back, *preds], axis=0)
    line_of, lane_of = pl.pallas_call(
        functools.partial(expand_kernel, 2 * lines),
        out_shape=[shape((6 * lines, rows), BF), shape((1, rows), jnp.int32)],
        in_specs=[VMEM, ANY],
        out_specs=[VMEM] * 2,
        compiler_params=params(16),
        cost_estimate=cost(10**8, 10**6),
        name="expand",
    )(where, preds[-1])

    final = pl.pallas_call(
        functools.partial(finish_kernel, members, half, lines),
        out_shape=shape((1, rows), F32),
        in_specs=[VMEM] * 4,
        out_specs=VMEM,
        compiler_params=params(8),
        cost_estimate=cost(10**6, 10**6),
        name="finish",
    )(line_of, lane_of, near_lines, swap(near_lines))
    return final.reshape(rows)


def solution(mesh):
    placed = (
        P(("groups", "rows"), None),
        P(("groups", "rows"), None),
        P(("groups", "rows"), None, None),
        P("member", None, None),
        P("member", None),
        P("member", None),
        P("member", None),
        P(),
        P(),
        P(),
        P(),
        P(),
        P(None, None, "member"),
        P("member", None),
        P(),
        P("rows", None, "member"),
        P("rows", "member"),
        P("rows", "member", None),
        P("rows", None),
    )
    return jax.shard_map(
        per_device, mesh=mesh, in_specs=placed, out_specs=P(("groups", "rows")), check_vma=False
    )
```

```python
import functools
import math

import jax
import jax.numpy as jnp
from jax import lax
from jax.experimental import pallas as pl
from jax.experimental.pallas import tpu as pltpu
from jax.sharding import PartitionSpec as P

HD = 64
EPS = 1e-05
LANES = 128
BF = jnp.bfloat16
F32 = jnp.float32
VMEM = pl.BlockSpec(memory_space=pltpu.VMEM)
HBM = pl.BlockSpec(memory_space=pltpu.HBM)
ANY = pl.BlockSpec(memory_space=pl.ANY)
GELU_C = math.sqrt(2.0 / math.pi)

KMAP, VCLS, LCLS, SCALE, SHIFT, GAIN, FBIAS, CLS, FGAIN = 0, 8, 9, 16, 24, 32, 33, 34, 35
TABLE = 40
DOWN, BIAS, HEAD, EXTRA = 0, 3, 6, 16


def iota(shape, dim):
    return lax.broadcasted_iota(jnp.int32, shape, dim)


def gelu2(x):
    return x + x * jnp.tanh(x * (GELU_C + (GELU_C * 0.044715) * (x * x)))


def dot(a, b):
    return lax.dot_general(a, b, (((1,), (0,)), ((), ())), preferred_element_type=F32)


def dot_t(a, b):
    return lax.dot_general(a, b, (((1,), (1,)), ((), ())), preferred_element_type=F32)


def split2(x):
    high = x.astype(BF)
    return high, (x - high.astype(F32)).astype(BF)


def split3(x):
    high, rest = x.astype(BF), x
    rest = rest - high.astype(F32)
    mid = rest.astype(BF)
    low = (rest - mid.astype(F32)).astype(BF)
    return jnp.concatenate([high.astype(F32), mid.astype(F32), low.astype(F32)], axis=0).astype(BF)


def join3(x):
    rows = x.shape[0] // 3
    return x[:rows] + x[rows : 2 * rows] + x[2 * rows :]


def centre(x):
    return x - jnp.mean(x, axis=-1, keepdims=True)


def inverse_spread(centered):
    return lax.rsqrt(jnp.mean(centered * centered, axis=-1, keepdims=True) + EPS)


def start_all(pairs, sems, second=()):
    copies = [pltpu.make_async_copy(src, dst, sems.at[i]) for i, (src, dst) in enumerate(pairs)]
    for i, copy in enumerate(copies):
        copy.start(priority=int(i in second))
    return copies


def route_kernel(
    n, half, relative, esc_hbm, own_hbm, feat_hbm, w_hbm, bias_hbm, out_hbm, down_hbm, upb_hbm, head_hbm, up_hbm,
    index_ref, rows_ref, near_ref, far_ref, segment_ref,
    esc_ref, own_ref, feat_ref, w_ref, bias_ref, out_ref, down_ref, upb_ref, head_ref, sems,
):
    depth = up_hbm.shape[1]
    here = w_hbm.shape[0]
    copies = start_all(
        [(esc_hbm, esc_ref), (own_hbm, own_ref), (feat_hbm, feat_ref), (bias_hbm, bias_ref), (out_hbm, out_ref)]
        + [(w_hbm.at[m], w_ref.at[m]) for m in range(here)]
        + [(head_hbm, head_ref), (upb_hbm, upb_ref), (down_hbm, down_ref), (up_hbm.at[0], segment_ref.at[:depth])],
        sems, second=range(5, 5 + here))
    core = lax.axis_index("member")
    count = esc_hbm.shape[1]
    dealt = count // 2
    copies[0].wait()
    copies[1].wait()
    esc = esc_ref[...]
    own = own_ref[...]
    ii = iota((count, count), 0)
    jj = iota((count, count), 1)
    diag = ii == jj

    def to_col(row):
        return jnp.sum(jnp.where(diag, row, 0).astype(F32), axis=1, keepdims=True)

    own_col = to_col(own).astype(jnp.int32)
    before = jnp.sum((own_col < own).astype(F32), axis=0, keepdims=True).astype(jnp.int32)
    rank = jnp.sum(((own_col == own) & (ii < jj)).astype(F32), axis=0, keepdims=True).astype(jnp.int32)
    position = before + rank
    side = position & 1
    slot = rank >> 1
    me = lax.axis_index("rows")
    apart = own ^ me
    pair = (apart if relative else (own - (own & 1)) + (apart & 1))
    place = pair * half + slot
    dense = (position >> 1) + jnp.where(side == core, 0, dealt)
    mine = dense == ii
    source = jnp.sum(jnp.where(mine, esc, 0).astype(F32), axis=1, keepdims=True).astype(jnp.int32)
    chosen = (source == iota((count, feat_ref.shape[0]), 1)).astype(F32).astype(BF)
    copies[2].wait()
    rows = dot(chosen, feat_ref[...]).astype(BF)
    rows_ref[...] = rows[:dealt]
    lane = iota((LANES, 1), 0)
    preds = None
    copies[3].wait()
    copies[4].wait()
    for m in range(here):
        copies[5 + m].wait()
        act = gelu2(dot(rows, w_ref[m]) + bias_ref[m : m + 1]).astype(BF)
        on_lane = jnp.where(lane == core * here + m, 0.5 * out_ref[m : m + 1].astype(F32), 0.0).astype(BF)
        pred = dot_t(act, on_lane)
        preds = pred if preds is None else preds + pred
    preds = preds.astype(BF)
    near_ref[...] = preds[:dealt]
    far_ref[...] = preds[dealt:]

    line = pair >> 1
    line = line * (n // 2 + 1) + (side ^ core) * (n // 2) ** 2 if relative else line + (side ^ core) * (n // 2)
    for i, row in enumerate((line, (apart & 1) * half + slot, esc, place, dense)):
        index_ref[i : i + 1, :] = row

    for copy in copies[5 + here : 8 + here]:
        copy.wait()
    head = jnp.broadcast_to(head_ref[...], (8, head_ref.shape[1]))
    down = join3(dot_t(split3(head), down_ref[0]))[0:1]
    extra = [split3(x).astype(F32) for x in (down, upb_ref[...], head_ref[...])]
    extra.append(jnp.zeros((EXTRA - 9, down.shape[1]), F32))
    segment_ref[depth:, :] = jnp.concatenate(extra, axis=0).astype(BF)
    copies[8 + here].wait()


def constants_kernel(
    cls_ref, gain_ref, scale_ref, shift_ref, fbias_ref, fgain_ref, q0_ref, q1_ref, index_ref,
    table_ref, where_ref, place_ref,
):
    count = index_ref.shape[1]
    diag = iota((count, count), 0) == iota((count, count), 1)
    cols = [
        jnp.sum(jnp.where(diag, index_ref[i : i + 1, :], 0).astype(F32), axis=1, keepdims=True) for i in range(5)]
    for i in range(3):
        where_ref[:, i : i + 1] = cols[i].astype(jnp.int32)
    dealt = place_ref.shape[1]
    placed = cols[4].astype(jnp.int32) == iota((count, dealt), 1)
    place_ref[...] = jnp.sum(jnp.where(placed, cols[3], 0.0), axis=0, keepdims=True).astype(jnp.int32)
    gain = gain_ref[...]
    cls = cls_ref[...]
    centered = centre(cls)
    ncls = (centered * inverse_spread(centered) * gain).astype(BF)
    table_ref[...] = jnp.zeros_like(table_ref)
    members = scale_ref.shape[0]
    table_ref[SCALE : SCALE + members, :] = centre(scale_ref[...])
    table_ref[SHIFT : SHIFT + members, :] = centre(shift_ref[...])
    table_ref[GAIN : GAIN + 1, :] = gain
    table_ref[FBIAS : FBIAS + 1, :] = fbias_ref[...]
    table_ref[CLS : CLS + 1, :] = cls
    table_ref[FGAIN : FGAIN + 1, :] = fgain_ref[...]
    lhs = jnp.broadcast_to(ncls.astype(F32), (8, ncls.shape[1])).astype(BF)
    local = q0_ref.shape[2]
    heads = local // HD
    row = iota((8, local), 0)
    col = iota((8, local), 1) // HD
    kmap = None
    for i, ref in enumerate((q0_ref, q1_ref)):
        query = dot(lhs, ref[0]) * (1.0 / math.sqrt(HD))
        spread = jnp.where(row == col + i * heads, query, 0.0)
        part = join3(dot_t(split3(spread), ref[1]))
        kmap = part if kmap is None else kmap + part
        table_ref[VCLS : VCLS + 1, i * local : (i + 1) * local] = dot(lhs, ref[2])[0:1]
    table_ref[KMAP : KMAP + 8, :] = kmap
    logits = jnp.sum(kmap * ncls.astype(F32), axis=-1, keepdims=True)
    eye = iota((8, LANES), 0) == iota((8, LANES), 1)
    table_ref[LCLS : LCLS + 1, :LANES] = jnp.sum(jnp.where(eye, logits, 0.0), axis=0, keepdims=True)


def attend_kernel(
    members, rows_ref, near_ref, far_ref, place_ref, table_ref, fw0_ref, fw1_ref, q0_ref, q1_ref, *sent_refs
):
    core = lax.axis_index("member")
    rows = rows_ref[...]
    total, fwidth = rows.shape
    local = q0_ref.shape[2]
    gain = table_ref[GAIN : GAIN + 1, :]
    low, high = rows[:, : fwidth // 2].astype(F32), rows[:, fwidth // 2 :].astype(F32)
    first = jnp.where(core == 0, low, high).astype(BF)
    second = jnp.where(core == 0, high, low).astype(BF)
    token = dot(first, fw0_ref[...]) + dot(second, fw1_ref[...]) + table_ref[FBIAS : FBIAS + 1, :]
    centered = centre(token)
    tokens = [(centered * inverse_spread(centered) * gain).astype(BF)]
    preds = near_ref[...].astype(F32) + far_ref[...].astype(F32)
    for m in range(members):
        centered = preds[:, m : m + 1] * table_ref[SCALE + m : SCALE + m + 1, :] + table_ref[SHIFT + m : SHIFT + m + 1, :]
        tokens.append((centered * inverse_spread(centered) * gain).astype(BF))
    normed = jnp.concatenate(tokens, axis=0)
    count = len(tokens)

    kmap = jnp.concatenate([table_ref[KMAP : KMAP + 8, :], jnp.zeros((LANES - 8, table_ref.shape[1]), F32)], axis=0)
    logits = dot_t(normed, jnp.concatenate(split2(kmap), axis=0))
    logits = logits[:, :LANES] + logits[:, LANES:]
    expo = jnp.exp(logits)
    expo_cls = jnp.exp(table_ref[LCLS : LCLS + 1, :LANES])
    norm = expo_cls
    for t in range(count):
        norm = norm + expo[t * total : (t + 1) * total]
    inverse = 1.0 / norm
    weights = jnp.concatenate(
        [expo[t * total : (t + 1) * total] * inverse for t in range(count)] + [expo_cls * inverse], axis=0)
    expand = (iota((2 * LANES, 2 * local), 0) & (LANES - 1)) == iota((2 * LANES, 2 * local), 1) // HD
    spread = dot(jnp.concatenate(split2(weights), axis=1), expand.astype(F32).astype(BF))
    parts = []
    for i, ref in enumerate((q0_ref, q1_ref)):
        at = slice(i * local, (i + 1) * local)
        value = dot(normed, ref[2])
        mixed = spread[count * total :, at] * table_ref[VCLS : VCLS + 1, at]
        for t in range(count):
            rng = slice(t * total, (t + 1) * total)
            mixed = mixed + spread[rng, at] * value[rng]
        parts.append(mixed)
    mixed = jnp.concatenate(parts, axis=1).astype(BF)
    size = sent_refs[0].shape[0]
    scatter = (place_ref[...] == iota((size * len(sent_refs), total), 0)).astype(F32).astype(BF)
    sent = dot(scatter, mixed).astype(BF)
    for k, sent_ref in enumerate(sent_refs):
        sent_ref[...] = sent[k * size : (k + 1) * size]


def ensemble_kernel(first, count, tile, feat_ref, w_ref, bias_ref, out_ref, after_ref, *refs):
    held = (len(refs) - 1) // 2
    copies = start_all(list(zip(refs[:held], refs[held + 1 :])), refs[-1]) if held else []
    pred_ref = refs[held]
    for t in range(count):
        rows = feat_ref[(first + t) * tile : (first + t + 1) * tile]
        total = None
        for m in range(w_ref.shape[0]):
            hidden = gelu2(dot(rows, w_ref[m]) + bias_ref[m : m + 1]).astype(BF)
            weights = jnp.broadcast_to(out_ref[m : m + 1].astype(F32), (8, out_ref.shape[1])).astype(BF)
            pred = dot_t(weights, hidden)[0:1]
            total = pred if total is None else total + pred
        per = tile // LANES
        for i in range(per):
            pred_ref[t * per + i : t * per + i + 1, :] = total[:, i * LANES : (i + 1) * LANES]
    for copy in copies:
        copy.wait()


def unpack(ref):
    depth = ref.shape[0] - EXTRA
    extra = ref[depth:, :].astype(F32)
    return ref[:depth, :], *(jnp.sum(extra[i : i + 3], axis=0, keepdims=True) for i in (DOWN, BIAS, HEAD))


def hidden_terms(normed, up, down, bias):
    return jnp.maximum(dot(normed, up) + bias, 0.0).astype(BF).astype(F32) * down


def states(mixed, table_ref, ow0_ref, ow1_ref):
    local = mixed.shape[1] // 2
    state = table_ref[CLS : CLS + 1, :] + dot(mixed[:, :local], ow0_ref[...]) + dot(mixed[:, local:], ow1_ref[...])
    centered = centre(state)
    return state, (centered * inverse_spread(centered) * table_ref[FGAIN : FGAIN + 1, :]).astype(BF)


def in_order(refs):
    first = len(refs) // 2
    return refs[len(refs) - first :][::-1] + refs[: len(refs) - first]


def arrived(got_refs, half, e):
    if len(got_refs) == 1:
        rows = got_refs[0].shape[0] // 2
        return got_refs[0][e * rows : (e + 1) * rows]
    return jnp.concatenate([ref[e * half : (e + 1) * half] for ref in got_refs], axis=0)


def arrive_kernel(blocks, half, *refs):
    table_ref, ow0_ref, ow1_ref, state_ref, normed_ref = refs[blocks:]
    state_ref[...], normed_ref[...] = states(arrived(in_order(refs[:blocks]), half, 1), table_ref, ow0_ref, ow1_ref)


def near_score_kernel(blocks, half, *refs):
    table_ref, ow0_ref, ow1_ref, up0_ref, up1_ref, score_ref = refs[blocks:]
    state, normed = states(arrived(in_order(refs[:blocks]), half, 0), table_ref, ow0_ref, ow1_ref)
    up, down, bias, head = unpack(up0_ref)
    terms = state * head + hidden_terms(normed, up, down, bias)
    up, down, bias, _ = unpack(up1_ref)
    terms = terms + hidden_terms(normed, up, down, bias)
    score_ref[...] = jnp.sum(terms, axis=-1, keepdims=True)


def far_score_kernel(blocks, half, near_ref, state_ref, mine_ref, other_ref, up2_ref, out_ref):
    rows = near_ref.shape[0]
    up, down, bias, head = unpack(up2_ref)
    terms = hidden_terms(jnp.concatenate([mine_ref[...], other_ref[...]], axis=0), up, down, bias)
    scores = [
        near_ref[...],
        jnp.sum(terms[:rows] + state_ref[...] * head, axis=-1, keepdims=True),
        jnp.sum(terms[rows:], axis=-1, keepdims=True),
    ]
    if blocks == 1:
        eye = iota((rows, rows), 0) == iota((rows, rows), 1)
        for e, score in enumerate(scores):
            out_ref[:, e * rows : (e + 1) * rows] = jnp.sum(jnp.where(eye, score, 0.0), axis=0, keepdims=True)
    else:
        row, lane = iota((half, LANES), 0), iota((half, LANES), 1)
        for k in range(blocks):
            line = jnp.zeros((half, LANES), F32)
            for e, score in enumerate(scores):
                line = jnp.where(lane == row + e * half, score[k * half : (k + 1) * half], line)
            out_ref[k : k + 1, :] = jnp.sum(line, axis=0, keepdims=True)


def expand_kernel(lines, where_ref, after_ref, line_ref, lane_ref):
    rows = lane_ref.shape[1]
    hit = where_ref[:, 2:3] == iota((where_ref.shape[0], rows), 1)

    def by_row(i):
        return jnp.sum(jnp.where(hit, where_ref[:, i : i + 1] + 1, 0).astype(F32), axis=0, keepdims=True).astype(jnp.int32)

    line = (by_row(0) - 1 == iota((lines, rows), 0)).astype(F32)
    line_ref[...] = jnp.concatenate([line] * 3, axis=0).astype(BF)
    lane_ref[...] = by_row(1) - 1


def finish_kernel(members, half, lines, line_ref, lane_ref, near_ref, far_ref, out_ref):
    near, far = near_ref[...], far_ref[...]
    ensemble = (near[lines:] + far[lines:]) * (0.5 / members)
    ensemble = jnp.concatenate([ensemble[i : i + 1] for i in range(ensemble.shape[0])], axis=1)
    lanes = iota((lines, LANES), 1)
    last = (lanes >= half) & (lanes < 2 * half)

    def whole(mine, others):
        return mine[:lines] + jnp.where(last, pltpu.roll(others[:lines], LANES - half, 1), 0.0)

    table = split3(jnp.concatenate([whole(near, far), whole(far, near)], axis=0))
    by_lane = lax.dot_general(table, line_ref[...], (((0,), (0,)), ((), ())), preferred_element_type=F32)
    lane = lane_ref[...]
    replaced = jnp.sum(jnp.where(lane == iota(by_lane.shape, 0), by_lane, 0.0), axis=0, keepdims=True)
    out_ref[...] = jnp.where(lane >= 0, replaced, ensemble)


def cost(flops, size, trans=0):
    return pl.CostEstimate(flops=flops, bytes_accessed=size, transcendentals=trans)


def params(mib):
    return pltpu.CompilerParams(vmem_limit_bytes=mib * 2**20)


def in_hbm(arrays):
    return [pltpu.with_memory_space_constraint(x, pltpu.HBM) for x in arrays]


def shape(dims, dtype):
    return jax.ShapeDtypeStruct(dims, dtype)


def per_device(
    features, escalated, owner_ids, member_in, member_bias, member_out, feat_weight, feat_bias,
    pred_scale, pred_shift, cls_token, attn_gain, qkv_weight, out_weight, ffn_gain, up_weight,
    up_bias, down_weight, owner_heads,
):
    n = lax.axis_size("rows")
    rows, fwidth = features.shape
    count = escalated.shape[1]
    half = max(1, count // n)
    slots = n * half
    here, _, hidden = member_in.shape
    members = pred_scale.shape[0]
    width = cls_token.shape[0]

    def swap(x):
        return lax.ppermute(x, "member", [(0, 1), (1, 0)])

    row = lambda x: x.reshape(1, -1)
    cls_token, attn_gain, ffn_gain, feat_bias = map(row, (cls_token, attn_gain, ffn_gain, feat_bias))
    owners = owner_ids.reshape(1, count)

    pairs = n // 2
    relative = pairs <= 8
    blocks = pairs if relative else 1
    other_qkv = swap(qkv_weight)

    dealt = count // 2
    ins = (escalated, owners, features, member_in, member_bias, member_out, down_weight, up_bias, owner_heads, up_weight)
    index, mine, near, far, segment = pl.pallas_call(
        functools.partial(route_kernel, n, half, relative),
        out_shape=[shape((8, count), jnp.int32), shape((dealt, fwidth), BF), shape((dealt, LANES), BF),
                   shape((dealt, LANES), BF), shape((up_weight.shape[1] + EXTRA, up_weight.shape[2]), BF)],
        in_specs=[HBM] * len(ins),
        out_specs=[VMEM] * 5,
        scratch_shapes=[pltpu.VMEM(x.shape, x.dtype) for x in ins[:9]] + [pltpu.SemaphoreType.DMA((9 + here,))],
        compiler_params=params(24),
        cost_estimate=cost(2 * count * rows * fwidth + 2 * here * count * fwidth * hidden, 3 * 10**6,
                           here * count * hidden),
        name="route",
    )(*in_hbm(ins))
    far = swap(far)
    other_fw = swap(feat_weight)
    other_ow = swap(out_weight)
    next_segment = lax.ppermute(segment, "rows", [(i, i ^ 1) for i in range(n)])
    other_segment = swap(segment)

    ins = (cls_token, attn_gain, pred_scale, pred_shift, feat_bias, ffn_gain, qkv_weight, other_qkv, index)
    table, where, place = pl.pallas_call(
        constants_kernel,
        out_shape=[shape((TABLE, width), F32), shape((count, 3), jnp.int32), shape((1, dealt), jnp.int32)],
        in_specs=[VMEM] * len(ins),
        out_specs=[VMEM] * 3,
        compiler_params=params(16),
        cost_estimate=cost(10**8, 2 * 10**6),
        name="constants",
    )(*ins)

    local = qkv_weight.shape[2]
    sent = pl.pallas_call(
        functools.partial(attend_kernel, members),
        out_shape=[shape((slots // blocks, 2 * local), BF)] * blocks,
        in_specs=[VMEM] * 9,
        out_specs=[VMEM] * blocks,
        compiler_params=params(24),
        cost_estimate=cost(10**9, 2 * 10**6),
        name="attend",
    )(mine, near, far, place, table, feat_weight, other_fw, qkv_weight, other_qkv)

    def across(x, k):
        return lax.ppermute(x, "rows", [(i, i ^ (2 * k)) for i in range(n)])

    def exchange(x):
        groups = [[2 * q + b for q in range(pairs)] for b in range(2)]
        return lax.all_to_all(x, "rows", split_axis=0, concat_axis=0, axis_index_groups=groups, tiled=True)

    if relative:
        got = [sent[0]] + [across(sent[k], k) for k in range(1, pairs)]
    else:
        got = exchange(sent[0].reshape(pairs, 2, half, 2 * local))
        got = [got.transpose(1, 0, 2, 3).reshape(slots, 2 * local)]

    tile = min(rows, 256)
    tiles = rows // tile

    def ensemble(first, number, after, held=()):
        return pl.pallas_call(
            functools.partial(ensemble_kernel, first, number, tile),
            out_shape=[shape((number * tile // LANES, LANES), F32)] + [shape(x.shape, x.dtype) for x in held],
            in_specs=[VMEM] * 4 + [ANY] * (1 + len(held)),
            out_specs=[VMEM] * (1 + len(held)),
            scratch_shapes=[pltpu.SemaphoreType.DMA((len(held),))] if held else [],
            compiler_params=params(24),
            cost_estimate=cost(2 * here * number * tile * fwidth * hidden, 10**6, here * number * tile * hidden),
            name="ensemble",
        )(features, member_in, member_bias, member_out, after, *held)

    early = (tiles + 1) // 2
    preds, table, ow0, ow1, up0, up1 = ensemble(
        0, early, sent[0], (table, out_weight, other_ow, segment, other_segment))
    preds = [preds]

    first = blocks // 2
    blocks_in = got[first:] + got[:first][::-1]
    state, next_rows = pl.pallas_call(
        functools.partial(arrive_kernel, blocks, half),
        out_shape=[shape((slots // 2, width), F32), shape((slots // 2, width), BF)],
        in_specs=[VMEM] * (blocks + 3),
        out_specs=[VMEM] * 2,
        compiler_params=params(24),
        cost_estimate=cost(2 * 10**8, 2 * 10**6),
        name="arrive",
    )(*blocks_in, table, ow0, ow1)
    other_rows = swap(next_rows)
    near_scores = pl.pallas_call(
        functools.partial(near_score_kernel, blocks, half),
        out_shape=shape((slots // 2, 1), F32),
        in_specs=[VMEM] * (blocks + 5),
        out_specs=VMEM,
        compiler_params=params(24),
        cost_estimate=cost(5 * 10**8, 2 * 10**6),
        name="near_score",
    )(*blocks_in, table, ow0, ow1, up0, up1)
    scores = pl.pallas_call(
        functools.partial(far_score_kernel, blocks, half),
        out_shape=shape((blocks, LANES if relative else 3 * slots // 2), F32),
        in_specs=[VMEM] * 5,
        out_specs=VMEM,
        compiler_params=params(24),
        cost_estimate=cost(2 * 10**8, 10**6),
        name="far_score",
    )(near_scores, state, next_rows, other_rows, next_segment)
    for first in range(early, tiles):
        preds += ensemble(first, 1, scores)
    back = scores
    if relative:
        step = 1
        while step < pairs:
            back = jnp.concatenate([back, across(back, step)], axis=0)
            step *= 2
    else:
        back = exchange(back.reshape(3, pairs, half).transpose(1, 0, 2)).reshape(pairs, 3 * half)
        back = jnp.pad(back, ((0, 0), (0, LANES - 3 * half)))
    lines = back.shape[0]
    near_lines = jnp.concatenate([back, *preds], axis=0)
    line_of, lane_of = pl.pallas_call(
        functools.partial(expand_kernel, 2 * lines),
        out_shape=[shape((6 * lines, rows), BF), shape((1, rows), jnp.int32)],
        in_specs=[VMEM, ANY],
        out_specs=[VMEM] * 2,
        compiler_params=params(16),
        cost_estimate=cost(10**8, 10**6),
        name="expand",
    )(where, preds[-1])

    final = pl.pallas_call(
        functools.partial(finish_kernel, members, half, lines),
        out_shape=shape((1, rows), F32),
        in_specs=[VMEM] * 4,
        out_specs=VMEM,
        compiler_params=params(8),
        cost_estimate=cost(10**6, 10**6),
        name="finish",
    )(line_of, lane_of, near_lines, swap(near_lines))
    return final.reshape(rows)


def solution(mesh):
    placed = (
        P(("groups", "rows"), None),
        P(("groups", "rows"), None),
        P(("groups", "rows"), None, None),
        P("member", None, None),
        P("member", None),
        P("member", None),
        P("member", None),
        P(),
        P(),
        P(),
        P(),
        P(),
        P(None, None, "member"),
        P("member", None),
        P(),
        P("rows", None, "member"),
        P("rows", "member"),
        P("rows", "member", None),
        P("rows", None),
    )
    return jax.shard_map(
        per_device, mesh=mesh, in_specs=placed, out_specs=P(("groups", "rows")), check_vma=False
    )
```

```python
import functools
import math

import jax
import jax.numpy as jnp
from jax import lax
from jax.experimental import pallas as pl
from jax.experimental.pallas import tpu as pltpu
from jax.sharding import PartitionSpec as P

HD = 64
EPS = 1e-05
LANES = 128
BF = jnp.bfloat16
F32 = jnp.float32
VMEM = pl.BlockSpec(memory_space=pltpu.VMEM)
HBM = pl.BlockSpec(memory_space=pltpu.HBM)
ANY = pl.BlockSpec(memory_space=pl.ANY)
GELU_C = math.sqrt(2.0 / math.pi)

KMAP, VCLS, LCLS, SCALE, SHIFT, GAIN, FBIAS, CLS, FGAIN = 0, 8, 9, 16, 24, 32, 33, 34, 35
TABLE = 40
DOWN, BIAS, HEAD, EXTRA = 0, 3, 6, 16


def iota(shape, dim):
    return lax.broadcasted_iota(jnp.int32, shape, dim)


def gelu2(x):
    return x + x * jnp.tanh(x * (GELU_C + (GELU_C * 0.044715) * (x * x)))


def dot(a, b):
    return lax.dot_general(a, b, (((1,), (0,)), ((), ())), preferred_element_type=F32)


def dot_t(a, b):
    return lax.dot_general(a, b, (((1,), (1,)), ((), ())), preferred_element_type=F32)


def split2(x):
    high = x.astype(BF)
    return high, (x - high.astype(F32)).astype(BF)


def split3(x):
    high, rest = x.astype(BF), x
    rest = rest - high.astype(F32)
    mid = rest.astype(BF)
    low = (rest - mid.astype(F32)).astype(BF)
    return jnp.concatenate([high.astype(F32), mid.astype(F32), low.astype(F32)], axis=0).astype(BF)


def join3(x):
    rows = x.shape[0] // 3
    return x[:rows] + x[rows : 2 * rows] + x[2 * rows :]


def centre(x):
    return x - jnp.mean(x, axis=-1, keepdims=True)


def inverse_spread(centered):
    return lax.rsqrt(jnp.mean(centered * centered, axis=-1, keepdims=True) + EPS)


def start_all(pairs, sems):
    copies = [pltpu.make_async_copy(src, dst, sems.at[i]) for i, (src, dst) in enumerate(pairs)]
    for copy in copies:
        copy.start()
    return copies


def route_kernel(
    n, half, relative, esc_hbm, own_hbm, feat_hbm, w_hbm, bias_hbm, out_hbm, down_hbm, upb_hbm, head_hbm, up_hbm,
    qkv_hbm, fw_hbm, ow_hbm, index_ref, rows_ref, near_ref, far_ref, segment_ref, qkv_ref, both_ref,
    esc_ref, own_ref, feat_ref, w_ref, bias_ref, out_ref, down_ref, upb_ref, head_ref, sems,
):
    depth = up_hbm.shape[1]
    here = w_hbm.shape[0]
    copies = start_all(
        [(esc_hbm, esc_ref), (own_hbm, own_ref), (feat_hbm, feat_ref), (bias_hbm, bias_ref), (out_hbm, out_ref)]
        + [(w_hbm.at[m], w_ref.at[m]) for m in range(here)], sems)
    core = lax.axis_index("member")
    count = esc_hbm.shape[1]
    dealt = count // 2
    copies[0].wait()
    copies[1].wait()
    esc = esc_ref[...]
    own = own_ref[...]
    ii = iota((count, count), 0)
    jj = iota((count, count), 1)
    diag = ii == jj

    def to_col(row):
        return jnp.sum(jnp.where(diag, row, 0).astype(F32), axis=1, keepdims=True)

    own_col = to_col(own).astype(jnp.int32)
    before = jnp.sum((own_col < own).astype(F32), axis=0, keepdims=True).astype(jnp.int32)
    rank = jnp.sum(((own_col == own) & (ii < jj)).astype(F32), axis=0, keepdims=True).astype(jnp.int32)
    position = before + rank
    side = position & 1
    slot = rank >> 1
    me = lax.axis_index("rows")
    apart = own ^ me
    pair = (apart if relative else (own - (own & 1)) + (apart & 1))
    place = pair * half + slot
    dense = (position >> 1) + jnp.where(side == core, 0, dealt)
    mine = dense == ii
    source = jnp.sum(jnp.where(mine, esc, 0).astype(F32), axis=1, keepdims=True).astype(jnp.int32)
    chosen = (source == iota((count, feat_ref.shape[0]), 1)).astype(F32).astype(BF)
    copies[2].wait()
    rows = dot(chosen, feat_ref[...]).astype(BF)
    rows_ref[...] = rows[:dealt]
    lane = iota((LANES, 1), 0)
    preds = None
    copies[3].wait()
    copies[4].wait()
    for m in range(here):
        copies[5 + m].wait()
        if m == 0:
            copies += start_all(
                [(head_hbm, head_ref), (upb_hbm, upb_ref), (down_hbm, down_ref), (qkv_hbm, qkv_ref),
                 (up_hbm.at[0], segment_ref.at[:depth]), (fw_hbm, both_ref.at[: fw_hbm.shape[0]]),
                 (ow_hbm, both_ref.at[fw_hbm.shape[0] :])], sems.at[pl.ds(5 + here, 7)])
        act = gelu2(dot(rows, w_ref[m]) + bias_ref[m : m + 1]).astype(BF)
        on_lane = jnp.where(lane == core * here + m, 0.5 * out_ref[m : m + 1].astype(F32), 0.0).astype(BF)
        pred = dot_t(act, on_lane)
        preds = pred if preds is None else preds + pred
    preds = preds.astype(BF)
    near_ref[...] = preds[:dealt]
    far_ref[...] = preds[dealt:]

    line = pair >> 1
    line = line * (n // 2 + 1) + (side ^ core) * (n // 2) ** 2 if relative else line + (side ^ core) * (n // 2)
    for i, row in enumerate((line, (apart & 1) * half + slot, esc, place, dense)):
        index_ref[i : i + 1, :] = row

    for copy in copies[5 + here : 8 + here]:
        copy.wait()
    head = jnp.broadcast_to(head_ref[...], (8, head_ref.shape[1]))
    down = join3(dot_t(split3(head), down_ref[0]))[0:1]
    extra = [split3(x).astype(F32) for x in (down, upb_ref[...], head_ref[...])]
    extra.append(jnp.zeros((EXTRA - 9, down.shape[1]), F32))
    segment_ref[depth:, :] = jnp.concatenate(extra, axis=0).astype(BF)
    for copy in copies[8 + here :]:
        copy.wait()


def constants_kernel(
    cls_ref, gain_ref, scale_ref, shift_ref, fbias_ref, fgain_ref, q0_ref, q1_ref, index_ref,
    table_ref, where_ref, place_ref,
):
    count = index_ref.shape[1]
    diag = iota((count, count), 0) == iota((count, count), 1)
    cols = [
        jnp.sum(jnp.where(diag, index_ref[i : i + 1, :], 0).astype(F32), axis=1, keepdims=True) for i in range(5)]
    for i in range(3):
        where_ref[:, i : i + 1] = cols[i].astype(jnp.int32)
    dealt = place_ref.shape[1]
    placed = cols[4].astype(jnp.int32) == iota((count, dealt), 1)
    place_ref[...] = jnp.sum(jnp.where(placed, cols[3], 0.0), axis=0, keepdims=True).astype(jnp.int32)
    gain = gain_ref[...]
    cls = cls_ref[...]
    centered = centre(cls)
    ncls = (centered * inverse_spread(centered) * gain).astype(BF)
    table_ref[...] = jnp.zeros_like(table_ref)
    members = scale_ref.shape[0]
    table_ref[SCALE : SCALE + members, :] = centre(scale_ref[...])
    table_ref[SHIFT : SHIFT + members, :] = centre(shift_ref[...])
    table_ref[GAIN : GAIN + 1, :] = gain
    table_ref[FBIAS : FBIAS + 1, :] = fbias_ref[...]
    table_ref[CLS : CLS + 1, :] = cls
    table_ref[FGAIN : FGAIN + 1, :] = fgain_ref[...]
    lhs = jnp.broadcast_to(ncls.astype(F32), (8, ncls.shape[1])).astype(BF)
    local = q0_ref.shape[2]
    heads = local // HD
    row = iota((8, local), 0)
    col = iota((8, local), 1) // HD
    kmap = None
    for i, ref in enumerate((q0_ref, q1_ref)):
        query = dot(lhs, ref[0]) * (1.0 / math.sqrt(HD))
        spread = jnp.where(row == col + i * heads, query, 0.0)
        part = join3(dot_t(split3(spread), ref[1]))
        kmap = part if kmap is None else kmap + part
        table_ref[VCLS : VCLS + 1, i * local : (i + 1) * local] = dot(lhs, ref[2])[0:1]
    table_ref[KMAP : KMAP + 8, :] = kmap
    logits = jnp.sum(kmap * ncls.astype(F32), axis=-1, keepdims=True)
    eye = iota((8, LANES), 0) == iota((8, LANES), 1)
    table_ref[LCLS : LCLS + 1, :LANES] = jnp.sum(jnp.where(eye, logits, 0.0), axis=0, keepdims=True)


def attend_kernel(
    members, rows_ref, near_ref, far_ref, place_ref, table_ref, fw0_ref, fw1_ref, q0_ref, q1_ref, *sent_refs
):
    core = lax.axis_index("member")
    rows = rows_ref[...]
    total, fwidth = rows.shape
    local = q0_ref.shape[2]
    gain = table_ref[GAIN : GAIN + 1, :]
    low, high = rows[:, : fwidth // 2].astype(F32), rows[:, fwidth // 2 :].astype(F32)
    first = jnp.where(core == 0, low, high).astype(BF)
    second = jnp.where(core == 0, high, low).astype(BF)
    token = dot(first, fw0_ref[: fwidth // 2]) + dot(second, fw1_ref[: fwidth // 2]) + table_ref[FBIAS : FBIAS + 1, :]
    centered = centre(token)
    tokens = [(centered * inverse_spread(centered) * gain).astype(BF)]
    preds = near_ref[...].astype(F32) + far_ref[...].astype(F32)
    for m in range(members):
        centered = preds[:, m : m + 1] * table_ref[SCALE + m : SCALE + m + 1, :] + table_ref[SHIFT + m : SHIFT + m + 1, :]
        tokens.append((centered * inverse_spread(centered) * gain).astype(BF))
    normed = jnp.concatenate(tokens, axis=0)
    count = len(tokens)

    kmap = jnp.concatenate([table_ref[KMAP : KMAP + 8, :], jnp.zeros((LANES - 8, table_ref.shape[1]), F32)], axis=0)
    logits = dot_t(normed, jnp.concatenate(split2(kmap), axis=0))
    logits = logits[:, :LANES] + logits[:, LANES:]
    expo = jnp.exp(logits)
    expo_cls = jnp.exp(table_ref[LCLS : LCLS + 1, :LANES])
    norm = expo_cls
    for t in range(count):
        norm = norm + expo[t * total : (t + 1) * total]
    inverse = 1.0 / norm
    weights = jnp.concatenate(
        [expo[t * total : (t + 1) * total] * inverse for t in range(count)] + [expo_cls * inverse], axis=0)
    expand = (iota((2 * LANES, 2 * local), 0) & (LANES - 1)) == iota((2 * LANES, 2 * local), 1) // HD
    spread = dot(jnp.concatenate(split2(weights), axis=1), expand.astype(F32).astype(BF))
    parts = []
    for i, ref in enumerate((q0_ref, q1_ref)):
        at = slice(i * local, (i + 1) * local)
        value = dot(normed, ref[2])
        mixed = spread[count * total :, at] * table_ref[VCLS : VCLS + 1, at]
        for t in range(count):
            rng = slice(t * total, (t + 1) * total)
            mixed = mixed + spread[rng, at] * value[rng]
        parts.append(mixed)
    mixed = jnp.concatenate(parts, axis=1).astype(BF)
    size = sent_refs[0].shape[0]
    scatter = (place_ref[...] == iota((size * len(sent_refs), total), 0)).astype(F32).astype(BF)
    sent = dot(scatter, mixed).astype(BF)
    for k, sent_ref in enumerate(sent_refs):
        sent_ref[...] = sent[k * size : (k + 1) * size]


def ensemble_kernel(first, count, tile, feat_ref, w_ref, bias_ref, out_ref, after_ref, *refs):
    held = (len(refs) - 1) // 2
    copies = start_all(list(zip(refs[:held], refs[held + 1 :])), refs[-1]) if held else []
    pred_ref = refs[held]
    for t in range(count):
        rows = feat_ref[(first + t) * tile : (first + t + 1) * tile]
        total = None
        for m in range(w_ref.shape[0]):
            hidden = gelu2(dot(rows, w_ref[m]) + bias_ref[m : m + 1]).astype(BF)
            weights = jnp.broadcast_to(out_ref[m : m + 1].astype(F32), (8, out_ref.shape[1])).astype(BF)
            pred = dot_t(weights, hidden)[0:1]
            total = pred if total is None else total + pred
        per = tile // LANES
        for i in range(per):
            pred_ref[t * per + i : t * per + i + 1, :] = total[:, i * LANES : (i + 1) * LANES]
    for copy in copies:
        copy.wait()


def unpack(ref):
    depth = ref.shape[0] - EXTRA
    extra = ref[depth:, :].astype(F32)
    return ref[:depth, :], *(jnp.sum(extra[i : i + 3], axis=0, keepdims=True) for i in (DOWN, BIAS, HEAD))


def hidden_terms(normed, up, down, bias):
    return jnp.maximum(dot(normed, up) + bias, 0.0).astype(BF).astype(F32) * down


def states(mixed, table_ref, both0_ref, both1_ref):
    local = mixed.shape[1] // 2
    ow0, ow1 = (ref[ref.shape[0] - local :] for ref in (both0_ref, both1_ref))
    state = table_ref[CLS : CLS + 1, :] + dot(mixed[:, :local], ow0) + dot(mixed[:, local:], ow1)
    centered = centre(state)
    return state, (centered * inverse_spread(centered) * table_ref[FGAIN : FGAIN + 1, :]).astype(BF)


def arrived(got_refs, half, e):
    if len(got_refs) == 1:
        rows = got_refs[0].shape[0] // 2
        return got_refs[0][e * rows : (e + 1) * rows]
    return jnp.concatenate([ref[e * half : (e + 1) * half] for ref in got_refs], axis=0)


def arrive_kernel(blocks, half, *refs):
    table_ref, both0_ref, both1_ref, state_ref, normed_ref = refs[blocks:]
    state_ref[...], normed_ref[...] = states(arrived(refs[:blocks][::-1], half, 1), table_ref, both0_ref, both1_ref)


def near_score_kernel(blocks, half, *refs):
    table_ref, both0_ref, both1_ref, up0_ref, up1_ref, score_ref = refs[blocks:]
    state, normed = states(arrived(refs[:blocks][::-1], half, 0), table_ref, both0_ref, both1_ref)
    up, down, bias, head = unpack(up0_ref)
    terms = state * head + hidden_terms(normed, up, down, bias)
    up, down, bias, _ = unpack(up1_ref)
    terms = terms + hidden_terms(normed, up, down, bias)
    score_ref[...] = jnp.sum(terms, axis=-1, keepdims=True)


def far_score_kernel(blocks, half, near_ref, state_ref, mine_ref, other_ref, up2_ref, out_ref):
    rows = near_ref.shape[0]
    up, down, bias, head = unpack(up2_ref)
    terms = hidden_terms(jnp.concatenate([mine_ref[...], other_ref[...]], axis=0), up, down, bias)
    scores = [
        near_ref[...],
        jnp.sum(terms[:rows] + state_ref[...] * head, axis=-1, keepdims=True),
        jnp.sum(terms[rows:], axis=-1, keepdims=True),
    ]
    if blocks == 1:
        eye = iota((rows, rows), 0) == iota((rows, rows), 1)
        for e, score in enumerate(scores):
            out_ref[:, e * rows : (e + 1) * rows] = jnp.sum(jnp.where(eye, score, 0.0), axis=0, keepdims=True)
    else:
        row, lane = iota((half, LANES), 0), iota((half, LANES), 1)
        for k in range(blocks):
            line = jnp.zeros((half, LANES), F32)
            for e, score in enumerate(scores):
                line = jnp.where(lane == row + e * half, score[k * half : (k + 1) * half], line)
            out_ref[k : k + 1, :] = jnp.sum(line, axis=0, keepdims=True)


def expand_kernel(lines, where_ref, after_ref, line_ref, lane_ref):
    rows = lane_ref.shape[1]
    hit = where_ref[:, 2:3] == iota((where_ref.shape[0], rows), 1)

    def by_row(i):
        return jnp.sum(jnp.where(hit, where_ref[:, i : i + 1] + 1, 0).astype(F32), axis=0, keepdims=True).astype(jnp.int32)

    line = (by_row(0) - 1 == iota((lines, rows), 0)).astype(F32)
    line_ref[...] = jnp.concatenate([line] * 3, axis=0).astype(BF)
    lane_ref[...] = by_row(1) - 1


def finish_kernel(members, half, lines, line_ref, lane_ref, near_ref, far_ref, out_ref):
    near, far = near_ref[...], far_ref[...]
    ensemble = (near[lines:] + far[lines:]) * (0.5 / members)
    ensemble = jnp.concatenate([ensemble[i : i + 1] for i in range(ensemble.shape[0])], axis=1)
    lanes = iota((lines, LANES), 1)
    last = (lanes >= half) & (lanes < 2 * half)

    def whole(mine, others):
        return mine[:lines] + jnp.where(last, pltpu.roll(others[:lines], LANES - half, 1), 0.0)

    table = split3(jnp.concatenate([whole(near, far), whole(far, near)], axis=0))
    by_lane = lax.dot_general(table, line_ref[...], (((0,), (0,)), ((), ())), preferred_element_type=F32)
    lane = lane_ref[...]
    replaced = jnp.sum(jnp.where(lane == iota(by_lane.shape, 0), by_lane, 0.0), axis=0, keepdims=True)
    out_ref[...] = jnp.where(lane >= 0, replaced, ensemble)


def cost(flops, size, trans=0):
    return pl.CostEstimate(flops=flops, bytes_accessed=size, transcendentals=trans)


def params(mib):
    return pltpu.CompilerParams(vmem_limit_bytes=mib * 2**20)


def in_hbm(arrays):
    return [pltpu.with_memory_space_constraint(x, pltpu.HBM) for x in arrays]


def shape(dims, dtype):
    return jax.ShapeDtypeStruct(dims, dtype)


def per_device(
    features, escalated, owner_ids, member_in, member_bias, member_out, feat_weight, feat_bias,
    pred_scale, pred_shift, cls_token, attn_gain, qkv_weight, out_weight, ffn_gain, up_weight,
    up_bias, down_weight, owner_heads,
):
    n = lax.axis_size("rows")
    rows, fwidth = features.shape
    count = escalated.shape[1]
    half = max(1, count // n)
    slots = n * half
    here, _, hidden = member_in.shape
    members = pred_scale.shape[0]
    width = cls_token.shape[0]

    def swap(x):
        return lax.ppermute(x, "member", [(0, 1), (1, 0)])

    row = lambda x: x.reshape(1, -1)
    cls_token, attn_gain, ffn_gain, feat_bias = map(row, (cls_token, attn_gain, ffn_gain, feat_bias))
    owners = owner_ids.reshape(1, count)

    pairs = n // 2
    relative = pairs <= 8
    blocks = pairs if relative else 1

    dealt = count // 2
    ins = (escalated, owners, features, member_in, member_bias, member_out, down_weight, up_bias, owner_heads, up_weight,
           qkv_weight, feat_weight, out_weight)
    index, mine, near, far, segment, own_qkv, own_both = pl.pallas_call(
        functools.partial(route_kernel, n, half, relative),
        out_shape=[shape((8, count), jnp.int32), shape((dealt, fwidth), BF), shape((dealt, LANES), BF),
                   shape((dealt, LANES), BF), shape((up_weight.shape[1] + EXTRA, up_weight.shape[2]), BF),
                   shape(qkv_weight.shape, BF), shape((feat_weight.shape[0] + out_weight.shape[0], width), BF)],
        in_specs=[HBM] * len(ins),
        out_specs=[VMEM] * 7,
        scratch_shapes=[pltpu.VMEM(x.shape, x.dtype) for x in ins[:9]] + [pltpu.SemaphoreType.DMA((12 + here,))],
        compiler_params=params(24),
        cost_estimate=cost(2 * count * rows * fwidth + 2 * here * count * fwidth * hidden, 3 * 10**6,
                           here * count * hidden),
        name="route",
    )(*in_hbm(ins))
    far = swap(far)
    other_qkv = swap(own_qkv)
    other_both = swap(own_both)
    next_segment = lax.ppermute(segment, "rows", [(i, i ^ 1) for i in range(n)])
    other_segment = swap(segment)

    ins = (cls_token, attn_gain, pred_scale, pred_shift, feat_bias, ffn_gain, own_qkv, other_qkv, index)
    table, where, place = pl.pallas_call(
        constants_kernel,
        out_shape=[shape((TABLE, width), F32), shape((count, 3), jnp.int32), shape((1, dealt), jnp.int32)],
        in_specs=[VMEM] * len(ins),
        out_specs=[VMEM] * 3,
        compiler_params=params(16),
        cost_estimate=cost(10**8, 2 * 10**6),
        name="constants",
    )(*ins)

    local = qkv_weight.shape[2]
    sent = pl.pallas_call(
        functools.partial(attend_kernel, members),
        out_shape=[shape((slots // blocks, 2 * local), BF)] * blocks,
        in_specs=[VMEM] * 9,
        out_specs=[VMEM] * blocks,
        compiler_params=params(24),
        cost_estimate=cost(10**9, 2 * 10**6),
        name="attend",
    )(mine, near, far, place, table, own_both, other_both, own_qkv, other_qkv)

    def across(x, k):
        return lax.ppermute(x, "rows", [(i, i ^ (2 * k)) for i in range(n)])

    def exchange(x):
        groups = [[2 * q + b for q in range(pairs)] for b in range(2)]
        return lax.all_to_all(x, "rows", split_axis=0, concat_axis=0, axis_index_groups=groups, tiled=True)

    if relative:
        got = [sent[0]] + [across(sent[k], k) for k in range(1, pairs)]
    else:
        got = exchange(sent[0].reshape(pairs, 2, half, 2 * local))
        got = [got.transpose(1, 0, 2, 3).reshape(slots, 2 * local)]

    tile = min(rows, 256)
    tiles = rows // tile

    def ensemble(first, number, after, held=()):
        return pl.pallas_call(
            functools.partial(ensemble_kernel, first, number, tile),
            out_shape=[shape((number * tile // LANES, LANES), F32)] + [shape(x.shape, x.dtype) for x in held],
            in_specs=[VMEM] * 4 + [ANY] * (1 + len(held)),
            out_specs=[VMEM] * (1 + len(held)),
            scratch_shapes=[pltpu.SemaphoreType.DMA((len(held),))] if held else [],
            compiler_params=params(24),
            cost_estimate=cost(2 * here * number * tile * fwidth * hidden, 10**6, here * number * tile * hidden),
            name="ensemble",
        )(features, member_in, member_bias, member_out, after, *held)

    early = (tiles + 1) // 2
    preds, table, both0, both1, up0, up1 = ensemble(
        0, early, sent[0], (table, own_both, other_both, segment, other_segment))
    preds = [preds]

    state, next_rows = pl.pallas_call(
        functools.partial(arrive_kernel, blocks, half),
        out_shape=[shape((slots // 2, width), F32), shape((slots // 2, width), BF)],
        in_specs=[VMEM] * (blocks + 3),
        out_specs=[VMEM] * 2,
        compiler_params=params(24),
        cost_estimate=cost(2 * 10**8, 2 * 10**6),
        name="arrive",
    )(*got[::-1], table, both0, both1)
    other_rows = swap(next_rows)
    near_scores = pl.pallas_call(
        functools.partial(near_score_kernel, blocks, half),
        out_shape=shape((slots // 2, 1), F32),
        in_specs=[VMEM] * (blocks + 5),
        out_specs=VMEM,
        compiler_params=params(24),
        cost_estimate=cost(5 * 10**8, 2 * 10**6),
        name="near_score",
    )(*got[::-1], table, both0, both1, up0, up1)
    scores = pl.pallas_call(
        functools.partial(far_score_kernel, blocks, half),
        out_shape=shape((blocks, LANES if relative else 3 * slots // 2), F32),
        in_specs=[VMEM] * 5,
        out_specs=VMEM,
        compiler_params=params(24),
        cost_estimate=cost(2 * 10**8, 10**6),
        name="far_score",
    )(near_scores, state, next_rows, other_rows, next_segment)
    for first in range(early, tiles):
        preds += ensemble(first, 1, scores)
    back = scores
    if relative:
        step = 1
        while step < pairs:
            back = jnp.concatenate([back, across(back, step)], axis=0)
            step *= 2
    else:
        back = exchange(back.reshape(3, pairs, half).transpose(1, 0, 2)).reshape(pairs, 3 * half)
        back = jnp.pad(back, ((0, 0), (0, LANES - 3 * half)))
    lines = back.shape[0]
    near_lines = jnp.concatenate([back, *preds], axis=0)
    line_of, lane_of = pl.pallas_call(
        functools.partial(expand_kernel, 2 * lines),
        out_shape=[shape((6 * lines, rows), BF), shape((1, rows), jnp.int32)],
        in_specs=[VMEM, ANY],
        out_specs=[VMEM] * 2,
        compiler_params=params(16),
        cost_estimate=cost(10**8, 10**6),
        name="expand",
    )(where, preds[-1])

    final = pl.pallas_call(
        functools.partial(finish_kernel, members, half, lines),
        out_shape=shape((1, rows), F32),
        in_specs=[VMEM] * 4,
        out_specs=VMEM,
        compiler_params=params(8),
        cost_estimate=cost(10**6, 10**6),
        name="finish",
    )(line_of, lane_of, near_lines, swap(near_lines))
    return final.reshape(rows)


def solution(mesh):
    placed = (
        P(("groups", "rows"), None),
        P(("groups", "rows"), None),
        P(("groups", "rows"), None, None),
        P("member", None, None),
        P("member", None),
        P("member", None),
        P("member", None),
        P(),
        P(),
        P(),
        P(),
        P(),
        P(None, None, "member"),
        P("member", None),
        P(),
        P("rows", None, "member"),
        P("rows", "member"),
        P("rows", "member", None),
        P("rows", None),
    )
    return jax.shard_map(
        per_device, mesh=mesh, in_specs=placed, out_specs=P(("groups", "rows")), check_vma=False
    )
```

```python
import functools
import math

import jax
import jax.numpy as jnp
from jax import lax
from jax.experimental import pallas as pl
from jax.experimental.pallas import tpu as pltpu
from jax.sharding import PartitionSpec as P

HD = 64
EPS = 1e-05
LANES = 128
BF = jnp.bfloat16
F32 = jnp.float32
VMEM = pl.BlockSpec(memory_space=pltpu.VMEM)
HBM = pl.BlockSpec(memory_space=pltpu.HBM)
ANY = pl.BlockSpec(memory_space=pl.ANY)
GELU_C = math.sqrt(2.0 / math.pi)

KMAP, VCLS, LCLS, SCALE, SHIFT, GAIN, FBIAS, CLS, FGAIN = 0, 8, 9, 16, 24, 32, 33, 34, 35
TABLE = 40
DOWN, BIAS, HEAD, EXTRA = 0, 3, 6, 16


def iota(shape, dim):
    return lax.broadcasted_iota(jnp.int32, shape, dim)


def gelu2(x):
    return x + x * jnp.tanh(x * (GELU_C + (GELU_C * 0.044715) * (x * x)))


def dot(a, b):
    return lax.dot_general(a, b, (((1,), (0,)), ((), ())), preferred_element_type=F32)


def dot_t(a, b):
    return lax.dot_general(a, b, (((1,), (1,)), ((), ())), preferred_element_type=F32)


def split2(x):
    high = x.astype(BF)
    return high, (x - high.astype(F32)).astype(BF)


def split3(x):
    high, rest = x.astype(BF), x
    rest = rest - high.astype(F32)
    mid = rest.astype(BF)
    low = (rest - mid.astype(F32)).astype(BF)
    return jnp.concatenate([high.astype(F32), mid.astype(F32), low.astype(F32)], axis=0).astype(BF)


def join3(x):
    rows = x.shape[0] // 3
    return x[:rows] + x[rows : 2 * rows] + x[2 * rows :]


def centre(x):
    return x - jnp.mean(x, axis=-1, keepdims=True)


def inverse_spread(centered):
    return lax.rsqrt(jnp.mean(centered * centered, axis=-1, keepdims=True) + EPS)


def start_all(pairs, sems):
    copies = [pltpu.make_async_copy(src, dst, sems.at[i]) for i, (src, dst) in enumerate(pairs)]
    for copy in copies:
        copy.start()
    return copies


def route_kernel(
    n, half, relative, esc_hbm, own_hbm, feat_hbm, qkv_hbm, fw_hbm, ow_hbm,
    index_ref, rows_ref, qkv_ref, both_ref, esc_ref, own_ref, feat_ref, sems,
):
    copies = start_all(
        [(esc_hbm, esc_ref), (own_hbm, own_ref), (feat_hbm, feat_ref), (qkv_hbm, qkv_ref),
         (fw_hbm, both_ref.at[: fw_hbm.shape[0]]), (ow_hbm, both_ref.at[fw_hbm.shape[0] :])], sems)
    core = lax.axis_index("member")
    count = esc_hbm.shape[1]
    dealt = count // 2
    copies[0].wait()
    copies[1].wait()
    esc = esc_ref[...]
    own = own_ref[...]
    ii = iota((count, count), 0)
    jj = iota((count, count), 1)
    own_col = jnp.sum(jnp.where(ii == jj, own, 0).astype(F32), axis=1, keepdims=True).astype(jnp.int32)
    before = jnp.sum((own_col < own).astype(F32), axis=0, keepdims=True).astype(jnp.int32)
    rank = jnp.sum(((own_col == own) & (ii < jj)).astype(F32), axis=0, keepdims=True).astype(jnp.int32)
    position = before + rank
    side = position & 1
    slot = rank >> 1
    apart = own ^ lax.axis_index("rows")
    pair = apart if relative else (own - (own & 1)) + (apart & 1)
    place = pair * half + slot
    dense = (position >> 1) + jnp.where(side == core, 0, dealt)
    source = jnp.sum(jnp.where(dense == ii, esc, 0).astype(F32), axis=1, keepdims=True).astype(jnp.int32)
    chosen = (source == iota((count, feat_ref.shape[0]), 1)).astype(F32).astype(BF)
    line = pair >> 1
    line = line * (n // 2 + 1) + (side ^ core) * (n // 2) ** 2 if relative else line + (side ^ core) * (n // 2)
    for i, row in enumerate((line, (apart & 1) * half + slot, esc, place, dense)):
        index_ref[i : i + 1, :] = row
    copies[2].wait()
    rows_ref[...] = dot(chosen, feat_ref[...]).astype(BF)
    for copy in copies[3:]:
        copy.wait()


def predict_kernel(
    rows_ref, w_ref, bias_ref, out_ref, upb_ref, head_ref, down_hbm, up_hbm, near_ref, far_ref, segment_ref,
    down_ref, sems,
):
    depth = up_hbm.shape[1]
    copies = start_all([(down_hbm.at[0], down_ref), (up_hbm.at[0], segment_ref.at[:depth])], sems)
    here = w_ref.shape[0]
    core = lax.axis_index("member")
    dealt = near_ref.shape[0]
    lane = iota((LANES, 1), 0)
    preds = None
    for m in range(here):
        act = gelu2(dot(rows_ref[...], w_ref[m]) + bias_ref[m : m + 1]).astype(BF)
        on_lane = jnp.where(lane == core * here + m, 0.5 * out_ref[m : m + 1].astype(F32), 0.0).astype(BF)
        pred = dot_t(act, on_lane)
        preds = pred if preds is None else preds + pred
    preds = preds.astype(BF)
    near_ref[...] = preds[:dealt]
    far_ref[...] = preds[dealt:]
    head = jnp.broadcast_to(head_ref[...], (8, head_ref.shape[1]))
    copies[0].wait()
    down = join3(dot_t(split3(head), down_ref[...]))[0:1]
    extra = [split3(x).astype(F32) for x in (down, upb_ref[...], head_ref[...])]
    extra.append(jnp.zeros((EXTRA - 9, down.shape[1]), F32))
    segment_ref[depth:, :] = jnp.concatenate(extra, axis=0).astype(BF)
    copies[1].wait()


def constants_kernel(
    cls_ref, gain_ref, scale_ref, shift_ref, fbias_ref, fgain_ref, q0_ref, q1_ref, index_ref,
    table_ref, where_ref, place_ref,
):
    count = index_ref.shape[1]
    diag = iota((count, count), 0) == iota((count, count), 1)
    cols = [
        jnp.sum(jnp.where(diag, index_ref[i : i + 1, :], 0).astype(F32), axis=1, keepdims=True) for i in range(5)]
    for i in range(3):
        where_ref[:, i : i + 1] = cols[i].astype(jnp.int32)
    dealt = place_ref.shape[1]
    placed = cols[4].astype(jnp.int32) == iota((count, dealt), 1)
    place_ref[...] = jnp.sum(jnp.where(placed, cols[3], 0.0), axis=0, keepdims=True).astype(jnp.int32)
    gain = gain_ref[...]
    cls = cls_ref[...]
    centered = centre(cls)
    ncls = (centered * inverse_spread(centered) * gain).astype(BF)
    table_ref[...] = jnp.zeros_like(table_ref)
    members = scale_ref.shape[0]
    table_ref[SCALE : SCALE + members, :] = centre(scale_ref[...])
    table_ref[SHIFT : SHIFT + members, :] = centre(shift_ref[...])
    table_ref[GAIN : GAIN + 1, :] = gain
    table_ref[FBIAS : FBIAS + 1, :] = fbias_ref[...]
    table_ref[CLS : CLS + 1, :] = cls
    table_ref[FGAIN : FGAIN + 1, :] = fgain_ref[...]
    lhs = jnp.broadcast_to(ncls.astype(F32), (8, ncls.shape[1])).astype(BF)
    local = q0_ref.shape[2]
    heads = local // HD
    row = iota((8, local), 0)
    col = iota((8, local), 1) // HD
    kmap = None
    for i, ref in enumerate((q0_ref, q1_ref)):
        query = dot(lhs, ref[0]) * (1.0 / math.sqrt(HD))
        spread = jnp.where(row == col + i * heads, query, 0.0)
        part = join3(dot_t(split3(spread), ref[1]))
        kmap = part if kmap is None else kmap + part
        table_ref[VCLS : VCLS + 1, i * local : (i + 1) * local] = dot(lhs, ref[2])[0:1]
    table_ref[KMAP : KMAP + 8, :] = kmap
    logits = jnp.sum(kmap * ncls.astype(F32), axis=-1, keepdims=True)
    eye = iota((8, LANES), 0) == iota((8, LANES), 1)
    table_ref[LCLS : LCLS + 1, :LANES] = jnp.sum(jnp.where(eye, logits, 0.0), axis=0, keepdims=True)


def attend_kernel(
    members, rows_ref, near_ref, far_ref, place_ref, table_ref, fw0_ref, fw1_ref, q0_ref, q1_ref, *sent_refs
):
    core = lax.axis_index("member")
    total = near_ref.shape[0]
    fwidth = rows_ref.shape[1]
    rows = rows_ref[:total]
    local = q0_ref.shape[2]
    gain = table_ref[GAIN : GAIN + 1, :]
    low, high = rows[:, : fwidth // 2].astype(F32), rows[:, fwidth // 2 :].astype(F32)
    first = jnp.where(core == 0, low, high).astype(BF)
    second = jnp.where(core == 0, high, low).astype(BF)
    token = dot(first, fw0_ref[: fwidth // 2]) + dot(second, fw1_ref[: fwidth // 2]) + table_ref[FBIAS : FBIAS + 1, :]
    centered = centre(token)
    tokens = [(centered * inverse_spread(centered) * gain).astype(BF)]
    preds = near_ref[...].astype(F32) + far_ref[...].astype(F32)
    for m in range(members):
        centered = preds[:, m : m + 1] * table_ref[SCALE + m : SCALE + m + 1, :] + table_ref[SHIFT + m : SHIFT + m + 1, :]
        tokens.append((centered * inverse_spread(centered) * gain).astype(BF))
    normed = jnp.concatenate(tokens, axis=0)
    count = len(tokens)

    kmap = jnp.concatenate([table_ref[KMAP : KMAP + 8, :], jnp.zeros((LANES - 8, table_ref.shape[1]), F32)], axis=0)
    logits = dot_t(normed, jnp.concatenate(split2(kmap), axis=0))
    logits = logits[:, :LANES] + logits[:, LANES:]
    expo = jnp.exp(logits)
    expo_cls = jnp.exp(table_ref[LCLS : LCLS + 1, :LANES])
    norm = expo_cls
    for t in range(count):
        norm = norm + expo[t * total : (t + 1) * total]
    inverse = 1.0 / norm
    weights = jnp.concatenate(
        [expo[t * total : (t + 1) * total] * inverse for t in range(count)] + [expo_cls * inverse], axis=0)
    expand = (iota((2 * LANES, 2 * local), 0) & (LANES - 1)) == iota((2 * LANES, 2 * local), 1) // HD
    spread = dot(jnp.concatenate(split2(weights), axis=1), expand.astype(F32).astype(BF))
    parts = []
    for i, ref in enumerate((q0_ref, q1_ref)):
        at = slice(i * local, (i + 1) * local)
        value = dot(normed, ref[2])
        mixed = spread[count * total :, at] * table_ref[VCLS : VCLS + 1, at]
        for t in range(count):
            rng = slice(t * total, (t + 1) * total)
            mixed = mixed + spread[rng, at] * value[rng]
        parts.append(mixed)
    mixed = jnp.concatenate(parts, axis=1).astype(BF)
    size = sent_refs[0].shape[0]
    scatter = (place_ref[...] == iota((size * len(sent_refs), total), 0)).astype(F32).astype(BF)
    sent = dot(scatter, mixed).astype(BF)
    for k, sent_ref in enumerate(sent_refs):
        sent_ref[...] = sent[k * size : (k + 1) * size]


def ensemble_kernel(first, count, tile, feat_ref, w_ref, bias_ref, out_ref, after_ref, *refs):
    held = (len(refs) - 1) // 2
    copies = start_all(list(zip(refs[:held], refs[held + 1 :])), refs[-1]) if held else []
    pred_ref = refs[held]
    for t in range(count):
        rows = feat_ref[(first + t) * tile : (first + t + 1) * tile]
        total = None
        for m in range(w_ref.shape[0]):
            hidden = gelu2(dot(rows, w_ref[m]) + bias_ref[m : m + 1]).astype(BF)
            weights = jnp.broadcast_to(out_ref[m : m + 1].astype(F32), (8, out_ref.shape[1])).astype(BF)
            pred = dot_t(weights, hidden)[0:1]
            total = pred if total is None else total + pred
        per = tile // LANES
        for i in range(per):
            pred_ref[t * per + i : t * per + i + 1, :] = total[:, i * LANES : (i + 1) * LANES]
    for copy in copies:
        copy.wait()


def unpack(ref):
    depth = ref.shape[0] - EXTRA
    extra = ref[depth:, :].astype(F32)
    return ref[:depth, :], *(jnp.sum(extra[i : i + 3], axis=0, keepdims=True) for i in (DOWN, BIAS, HEAD))


def hidden_terms(normed, up, down, bias):
    return jnp.maximum(dot(normed, up) + bias, 0.0).astype(BF).astype(F32) * down


def states(mixed, table_ref, both0_ref, both1_ref):
    local = mixed.shape[1] // 2
    ow0, ow1 = (ref[ref.shape[0] - local :] for ref in (both0_ref, both1_ref))
    state = table_ref[CLS : CLS + 1, :] + dot(mixed[:, :local], ow0) + dot(mixed[:, local:], ow1)
    centered = centre(state)
    return state, (centered * inverse_spread(centered) * table_ref[FGAIN : FGAIN + 1, :]).astype(BF)


def arrived(got_refs, half, e):
    if len(got_refs) == 1:
        rows = got_refs[0].shape[0] // 2
        return got_refs[0][e * rows : (e + 1) * rows]
    return jnp.concatenate([ref[e * half : (e + 1) * half] for ref in got_refs], axis=0)


def arrive_kernel(blocks, half, *refs):
    table_ref, both0_ref, both1_ref, state_ref, normed_ref = refs[blocks:]
    state_ref[...], normed_ref[...] = states(arrived(refs[:blocks][::-1], half, 1), table_ref, both0_ref, both1_ref)


def near_score_kernel(blocks, half, *refs):
    table_ref, both0_ref, both1_ref, up0_ref, up1_ref, score_ref = refs[blocks:]
    state, normed = states(arrived(refs[:blocks][::-1], half, 0), table_ref, both0_ref, both1_ref)
    up, down, bias, head = unpack(up0_ref)
    terms = state * head + hidden_terms(normed, up, down, bias)
    up, down, bias, _ = unpack(up1_ref)
    terms = terms + hidden_terms(normed, up, down, bias)
    score_ref[...] = jnp.sum(terms, axis=-1, keepdims=True)


def far_score_kernel(blocks, half, near_ref, state_ref, mine_ref, other_ref, up2_ref, out_ref):
    rows = near_ref.shape[0]
    up, down, bias, head = unpack(up2_ref)
    terms = hidden_terms(jnp.concatenate([mine_ref[...], other_ref[...]], axis=0), up, down, bias)
    scores = [
        near_ref[...],
        jnp.sum(terms[:rows] + state_ref[...] * head, axis=-1, keepdims=True),
        jnp.sum(terms[rows:], axis=-1, keepdims=True),
    ]
    if blocks == 1:
        eye = iota((rows, rows), 0) == iota((rows, rows), 1)
        for e, score in enumerate(scores):
            out_ref[:, e * rows : (e + 1) * rows] = jnp.sum(jnp.where(eye, score, 0.0), axis=0, keepdims=True)
    else:
        row, lane = iota((half, LANES), 0), iota((half, LANES), 1)
        for k in range(blocks):
            line = jnp.zeros((half, LANES), F32)
            for e, score in enumerate(scores):
                line = jnp.where(lane == row + e * half, score[k * half : (k + 1) * half], line)
            out_ref[k : k + 1, :] = jnp.sum(line, axis=0, keepdims=True)


def expand_kernel(lines, where_ref, after_ref, line_ref, lane_ref):
    rows = lane_ref.shape[1]
    hit = where_ref[:, 2:3] == iota((where_ref.shape[0], rows), 1)

    def by_row(i):
        return jnp.sum(jnp.where(hit, where_ref[:, i : i + 1] + 1, 0).astype(F32), axis=0, keepdims=True).astype(jnp.int32)

    line = (by_row(0) - 1 == iota((lines, rows), 0)).astype(F32)
    line_ref[...] = jnp.concatenate([line] * 3, axis=0).astype(BF)
    lane_ref[...] = by_row(1) - 1


def finish_kernel(members, half, lines, line_ref, lane_ref, near_ref, far_ref, out_ref):
    near, far = near_ref[...], far_ref[...]
    ensemble = (near[lines:] + far[lines:]) * (0.5 / members)
    ensemble = jnp.concatenate([ensemble[i : i + 1] for i in range(ensemble.shape[0])], axis=1)
    lanes = iota((lines, LANES), 1)
    last = (lanes >= half) & (lanes < 2 * half)

    def whole(mine, others):
        return mine[:lines] + jnp.where(last, pltpu.roll(others[:lines], LANES - half, 1), 0.0)

    table = split3(jnp.concatenate([whole(near, far), whole(far, near)], axis=0))
    by_lane = lax.dot_general(table, line_ref[...], (((0,), (0,)), ((), ())), preferred_element_type=F32)
    lane = lane_ref[...]
    replaced = jnp.sum(jnp.where(lane == iota(by_lane.shape, 0), by_lane, 0.0), axis=0, keepdims=True)
    out_ref[...] = jnp.where(lane >= 0, replaced, ensemble)


def cost(flops, size, trans=0):
    return pl.CostEstimate(flops=flops, bytes_accessed=size, transcendentals=trans)


def params(mib):
    return pltpu.CompilerParams(vmem_limit_bytes=mib * 2**20)


def in_hbm(arrays):
    return [pltpu.with_memory_space_constraint(x, pltpu.HBM) for x in arrays]


def shape(dims, dtype):
    return jax.ShapeDtypeStruct(dims, dtype)


def per_device(
    features, escalated, owner_ids, member_in, member_bias, member_out, feat_weight, feat_bias,
    pred_scale, pred_shift, cls_token, attn_gain, qkv_weight, out_weight, ffn_gain, up_weight,
    up_bias, down_weight, owner_heads,
):
    n = lax.axis_size("rows")
    rows, fwidth = features.shape
    count = escalated.shape[1]
    half = max(1, count // n)
    slots = n * half
    here, _, hidden = member_in.shape
    members = pred_scale.shape[0]
    width = cls_token.shape[0]

    def swap(x):
        return lax.ppermute(x, "member", [(0, 1), (1, 0)])

    row = lambda x: x.reshape(1, -1)
    cls_token, attn_gain, ffn_gain, feat_bias = map(row, (cls_token, attn_gain, ffn_gain, feat_bias))
    owners = owner_ids.reshape(1, count)

    pairs = n // 2
    relative = pairs <= 8
    blocks = pairs if relative else 1
    other_qkv = swap(qkv_weight)

    dealt = count // 2
    ins = (escalated, owners, features, qkv_weight, feat_weight, out_weight)
    index, mine, own_qkv, own_both = pl.pallas_call(
        functools.partial(route_kernel, n, half, relative),
        out_shape=[shape((8, count), jnp.int32), shape((count, fwidth), BF), shape(qkv_weight.shape, BF),
                   shape((feat_weight.shape[0] + out_weight.shape[0], width), BF)],
        in_specs=[HBM] * len(ins),
        out_specs=[VMEM] * 4,
        scratch_shapes=[pltpu.VMEM(x.shape, x.dtype) for x in ins[:3]] + [pltpu.SemaphoreType.DMA((6,))],
        compiler_params=params(24),
        cost_estimate=cost(2 * count * rows * fwidth, 3 * 10**6),
        name="route",
    )(*in_hbm(ins))
    near, far, segment = pl.pallas_call(
        predict_kernel,
        out_shape=[shape((dealt, LANES), BF), shape((dealt, LANES), BF),
                   shape((up_weight.shape[1] + EXTRA, up_weight.shape[2]), BF)],
        in_specs=[VMEM] * 6 + [HBM] * 2,
        out_specs=[VMEM] * 3,
        scratch_shapes=[pltpu.VMEM(down_weight.shape[1:], BF), pltpu.SemaphoreType.DMA((2,))],
        compiler_params=params(24),
        cost_estimate=cost(2 * here * count * fwidth * hidden, 3 * 10**6, here * count * hidden),
        name="predict",
    )(mine, member_in, member_bias, member_out, up_bias, owner_heads, *in_hbm([down_weight, up_weight]))
    far = swap(far)
    other_both = swap(own_both)
    next_segment = lax.ppermute(segment, "rows", [(i, i ^ 1) for i in range(n)])
    other_segment = swap(segment)

    ins = (cls_token, attn_gain, pred_scale, pred_shift, feat_bias, ffn_gain, own_qkv, other_qkv, index)
    table, where, place = pl.pallas_call(
        constants_kernel,
        out_shape=[shape((TABLE, width), F32), shape((count, 3), jnp.int32), shape((1, dealt), jnp.int32)],
        in_specs=[VMEM] * len(ins),
        out_specs=[VMEM] * 3,
        compiler_params=params(16),
        cost_estimate=cost(10**8, 2 * 10**6),
        name="constants",
    )(*ins)

    local = qkv_weight.shape[2]
    sent = pl.pallas_call(
        functools.partial(attend_kernel, members),
        out_shape=[shape((slots // blocks, 2 * local), BF)] * blocks,
        in_specs=[VMEM] * 9,
        out_specs=[VMEM] * blocks,
        compiler_params=params(24),
        cost_estimate=cost(10**9, 2 * 10**6),
        name="attend",
    )(mine, near, far, place, table, own_both, other_both, own_qkv, other_qkv)

    def across(x, k):
        return lax.ppermute(x, "rows", [(i, i ^ (2 * k)) for i in range(n)])

    def exchange(x):
        groups = [[2 * q + b for q in range(pairs)] for b in range(2)]
        return lax.all_to_all(x, "rows", split_axis=0, concat_axis=0, axis_index_groups=groups, tiled=True)

    if relative:
        got = [sent[0]] + [across(sent[k], k) for k in range(1, pairs)]
    else:
        got = exchange(sent[0].reshape(pairs, 2, half, 2 * local))
        got = [got.transpose(1, 0, 2, 3).reshape(slots, 2 * local)]

    tile = min(rows, 256)
    tiles = rows // tile

    def ensemble(first, number, after, held=()):
        return pl.pallas_call(
            functools.partial(ensemble_kernel, first, number, tile),
            out_shape=[shape((number * tile // LANES, LANES), F32)] + [shape(x.shape, x.dtype) for x in held],
            in_specs=[VMEM] * 4 + [ANY] * (1 + len(held)),
            out_specs=[VMEM] * (1 + len(held)),
            scratch_shapes=[pltpu.SemaphoreType.DMA((len(held),))] if held else [],
            compiler_params=params(24),
            cost_estimate=cost(2 * here * number * tile * fwidth * hidden, 10**6, here * number * tile * hidden),
            name="ensemble",
        )(features, member_in, member_bias, member_out, after, *held)

    early = (tiles + 1) // 2
    preds, table, both0, both1, up0, up1 = ensemble(
        0, early, sent[0], (table, own_both, other_both, segment, other_segment))
    preds = [preds]

    state, next_rows = pl.pallas_call(
        functools.partial(arrive_kernel, blocks, half),
        out_shape=[shape((slots // 2, width), F32), shape((slots // 2, width), BF)],
        in_specs=[VMEM] * (blocks + 3),
        out_specs=[VMEM] * 2,
        compiler_params=params(24),
        cost_estimate=cost(2 * 10**8, 2 * 10**6),
        name="arrive",
    )(*got[::-1], table, both0, both1)
    other_rows = swap(next_rows)
    near_scores = pl.pallas_call(
        functools.partial(near_score_kernel, blocks, half),
        out_shape=shape((slots // 2, 1), F32),
        in_specs=[VMEM] * (blocks + 5),
        out_specs=VMEM,
        compiler_params=params(24),
        cost_estimate=cost(5 * 10**8, 2 * 10**6),
        name="near_score",
    )(*got[::-1], table, both0, both1, up0, up1)
    scores = pl.pallas_call(
        functools.partial(far_score_kernel, blocks, half),
        out_shape=shape((blocks, LANES if relative else 3 * slots // 2), F32),
        in_specs=[VMEM] * 5,
        out_specs=VMEM,
        compiler_params=params(24),
        cost_estimate=cost(2 * 10**8, 10**6),
        name="far_score",
    )(near_scores, state, next_rows, other_rows, next_segment)
    for first in range(early, tiles):
        preds += ensemble(first, 1, scores)
    back = scores
    if relative:
        step = 1
        while step < pairs:
            back = jnp.concatenate([back, across(back, step)], axis=0)
            step *= 2
    else:
        back = exchange(back.reshape(3, pairs, half).transpose(1, 0, 2)).reshape(pairs, 3 * half)
        back = jnp.pad(back, ((0, 0), (0, LANES - 3 * half)))
    lines = back.shape[0]
    near_lines = jnp.concatenate([back, *preds], axis=0)
    line_of, lane_of = pl.pallas_call(
        functools.partial(expand_kernel, 2 * lines),
        out_shape=[shape((6 * lines, rows), BF), shape((1, rows), jnp.int32)],
        in_specs=[VMEM, ANY],
        out_specs=[VMEM] * 2,
        compiler_params=params(16),
        cost_estimate=cost(10**8, 10**6),
        name="expand",
    )(where, preds[-1])

    final = pl.pallas_call(
        functools.partial(finish_kernel, members, half, lines),
        out_shape=shape((1, rows), F32),
        in_specs=[VMEM] * 4,
        out_specs=VMEM,
        compiler_params=params(8),
        cost_estimate=cost(10**6, 10**6),
        name="finish",
    )(line_of, lane_of, near_lines, swap(near_lines))
    return final.reshape(rows)


def solution(mesh):
    placed = (
        P(("groups", "rows"), None),
        P(("groups", "rows"), None),
        P(("groups", "rows"), None, None),
        P("member", None, None),
        P("member", None),
        P("member", None),
        P("member", None),
        P(),
        P(),
        P(),
        P(),
        P(),
        P(None, None, "member"),
        P("member", None),
        P(),
        P("rows", None, "member"),
        P("rows", "member"),
        P("rows", "member", None),
        P("rows", None),
    )
    return jax.shard_map(
        per_device, mesh=mesh, in_specs=placed, out_specs=P(("groups", "rows")), check_vma=False
    )
```

```python
import functools
import math

import jax
import jax.numpy as jnp
from jax import lax
from jax.experimental import pallas as pl
from jax.experimental.pallas import tpu as pltpu
from jax.sharding import PartitionSpec as P

HD = 64
EPS = 1e-05
LANES = 128
BF = jnp.bfloat16
F32 = jnp.float32
VMEM = pl.BlockSpec(memory_space=pltpu.VMEM)
HBM = pl.BlockSpec(memory_space=pltpu.HBM)
ANY = pl.BlockSpec(memory_space=pl.ANY)
GELU_C = math.sqrt(2.0 / math.pi)

KMAP, VCLS, LCLS, SCALE, SHIFT, GAIN, FBIAS, CLS, FGAIN = 0, 8, 9, 16, 24, 32, 33, 34, 35
TABLE = 40
DOWN, BIAS, HEAD, EXTRA = 0, 3, 6, 16


def iota(shape, dim):
    return lax.broadcasted_iota(jnp.int32, shape, dim)


def gelu2(x):
    return x + x * jnp.tanh(x * (GELU_C + (GELU_C * 0.044715) * (x * x)))


def dot(a, b):
    return lax.dot_general(a, b, (((1,), (0,)), ((), ())), preferred_element_type=F32)


def dot_t(a, b):
    return lax.dot_general(a, b, (((1,), (1,)), ((), ())), preferred_element_type=F32)


def split2(x):
    high = x.astype(BF)
    return high, (x - high.astype(F32)).astype(BF)


def split3(x):
    high, rest = x.astype(BF), x
    rest = rest - high.astype(F32)
    mid = rest.astype(BF)
    low = (rest - mid.astype(F32)).astype(BF)
    return jnp.concatenate([high.astype(F32), mid.astype(F32), low.astype(F32)], axis=0).astype(BF)


def join3(x):
    rows = x.shape[0] // 3
    return x[:rows] + x[rows : 2 * rows] + x[2 * rows :]


def centre(x):
    return x - jnp.mean(x, axis=-1, keepdims=True)


def inverse_spread(centered):
    return lax.rsqrt(jnp.mean(centered * centered, axis=-1, keepdims=True) + EPS)


def start_all(pairs, sems):
    copies = [pltpu.make_async_copy(src, dst, sems.at[i]) for i, (src, dst) in enumerate(pairs)]
    for copy in copies:
        copy.start()
    return copies


def route_kernel(
    n, half, relative, esc_hbm, own_hbm, feat_hbm, qkv_hbm, fw_hbm, ow_hbm,
    index_ref, rows_ref, qkv_ref, both_ref, esc_ref, own_ref, feat_ref, sems,
):
    copies = start_all(
        [(esc_hbm, esc_ref), (own_hbm, own_ref), (feat_hbm, feat_ref), (qkv_hbm, qkv_ref),
         (fw_hbm, both_ref.at[: fw_hbm.shape[0]]), (ow_hbm, both_ref.at[fw_hbm.shape[0] :])], sems)
    core = lax.axis_index("member")
    count = esc_hbm.shape[1]
    dealt = count // 2
    copies[0].wait()
    copies[1].wait()
    esc = esc_ref[...]
    own = own_ref[...]
    ii = iota((count, count), 0)
    jj = iota((count, count), 1)
    own_col = jnp.sum(jnp.where(ii == jj, own, 0).astype(F32), axis=1, keepdims=True).astype(jnp.int32)
    before = jnp.sum((own_col < own).astype(F32), axis=0, keepdims=True).astype(jnp.int32)
    rank = jnp.sum(((own_col == own) & (ii < jj)).astype(F32), axis=0, keepdims=True).astype(jnp.int32)
    position = before + rank
    side = position & 1
    slot = rank >> 1
    apart = own ^ lax.axis_index("rows")
    pair = apart if relative else (own - (own & 1)) + (apart & 1)
    place = pair * half + slot
    dense = (position >> 1) + jnp.where(side == core, 0, dealt)
    source = jnp.sum(jnp.where(dense == ii, esc, 0).astype(F32), axis=1, keepdims=True).astype(jnp.int32)
    chosen = (source == iota((count, feat_ref.shape[0]), 1)).astype(F32).astype(BF)
    line = pair >> 1
    line = line * (n // 2 + 1) + (side ^ core) * (n // 2) ** 2 if relative else line + (side ^ core) * (n // 2)
    for i, row in enumerate((line, (apart & 1) * half + slot, esc, place, dense)):
        index_ref[i : i + 1, :] = row
    copies[2].wait()
    rows_ref[...] = dot(chosen, feat_ref[...]).astype(BF)
    for copy in copies[3:]:
        copy.wait()


def predict_kernel(
    rows_ref, w_ref, bias_ref, out_ref, upb_ref, head_ref, down_hbm, up_hbm, near_ref, far_ref, segment_ref,
    down_ref, sems,
):
    depth = up_hbm.shape[1]
    copies = start_all([(down_hbm.at[0], down_ref), (up_hbm.at[0], segment_ref.at[:depth])], sems)
    here = w_ref.shape[0]
    core = lax.axis_index("member")
    dealt = near_ref.shape[0]
    lane = iota((8, 1), 0)
    preds = None
    for m in range(here):
        act = gelu2(dot(rows_ref[...], w_ref[m]) + bias_ref[m : m + 1]).astype(BF)
        on_lane = jnp.where(lane == core * here + m, 0.5 * out_ref[m : m + 1].astype(F32), 0.0).astype(BF)
        pred = dot_t(act, on_lane)
        preds = pred if preds is None else preds + pred
    preds = preds.astype(BF)
    near_ref[...] = preds[:dealt]
    far_ref[...] = preds[dealt:]
    head = split3(head_ref[...]).astype(F32)
    head = jnp.concatenate([head, jnp.zeros((LANES - 3, head.shape[1]), F32)], axis=0).astype(BF)
    copies[0].wait()
    down = jnp.sum(dot_t(down_ref[...], head).T[:8], axis=0, keepdims=True)
    extra = [split3(x).astype(F32) for x in (down, upb_ref[...], head_ref[...])]
    extra.append(jnp.zeros((EXTRA - 9, down.shape[1]), F32))
    segment_ref[depth:, :] = jnp.concatenate(extra, axis=0).astype(BF)
    copies[1].wait()


def constants_kernel(
    cls_ref, gain_ref, scale_ref, shift_ref, fbias_ref, fgain_ref, q0_ref, q1_ref, index_ref,
    table_ref, where_ref, place_ref,
):
    count = index_ref.shape[1]
    diag = iota((count, count), 0) == iota((count, count), 1)
    cols = [
        jnp.sum(jnp.where(diag, index_ref[i : i + 1, :], 0).astype(F32), axis=1, keepdims=True) for i in range(5)]
    for i in range(3):
        where_ref[:, i : i + 1] = cols[i].astype(jnp.int32)
    dealt = place_ref.shape[1]
    placed = cols[4].astype(jnp.int32) == iota((count, dealt), 1)
    place_ref[...] = jnp.sum(jnp.where(placed, cols[3], 0.0), axis=0, keepdims=True).astype(jnp.int32)
    gain = gain_ref[...]
    cls = cls_ref[...]
    centered = centre(cls)
    ncls = (centered * inverse_spread(centered) * gain).astype(BF)
    table_ref[...] = jnp.zeros_like(table_ref)
    members = scale_ref.shape[0]
    table_ref[SCALE : SCALE + members, :] = centre(scale_ref[...])
    table_ref[SHIFT : SHIFT + members, :] = centre(shift_ref[...])
    table_ref[GAIN : GAIN + 1, :] = gain
    table_ref[FBIAS : FBIAS + 1, :] = fbias_ref[...]
    table_ref[CLS : CLS + 1, :] = cls
    table_ref[FGAIN : FGAIN + 1, :] = fgain_ref[...]
    lhs = jnp.broadcast_to(ncls.astype(F32), (8, ncls.shape[1])).astype(BF)
    local = q0_ref.shape[2]
    heads = local // HD
    row = iota((8, local), 0)
    col = iota((8, local), 1) // HD
    kmap = None
    for i, ref in enumerate((q0_ref, q1_ref)):
        query = dot(lhs, ref[0]) * (1.0 / math.sqrt(HD))
        spread = jnp.where(row == col + i * heads, query, 0.0)
        part = join3(dot_t(split3(spread), ref[1]))
        kmap = part if kmap is None else kmap + part
        table_ref[VCLS : VCLS + 1, i * local : (i + 1) * local] = dot(lhs, ref[2])[0:1]
    table_ref[KMAP : KMAP + 8, :] = kmap
    logits = jnp.sum(kmap * ncls.astype(F32), axis=-1, keepdims=True)
    eye = iota((8, LANES), 0) == iota((8, LANES), 1)
    table_ref[LCLS : LCLS + 1, :LANES] = jnp.sum(jnp.where(eye, logits, 0.0), axis=0, keepdims=True)


def attend_kernel(
    members, rows_ref, near_ref, far_ref, place_ref, table_ref, fw0_ref, fw1_ref, q0_ref, q1_ref, *sent_refs
):
    core = lax.axis_index("member")
    total = near_ref.shape[0]
    fwidth = rows_ref.shape[1]
    rows = rows_ref[:total]
    local = q0_ref.shape[2]
    gain = table_ref[GAIN : GAIN + 1, :]
    low, high = rows[:, : fwidth // 2].astype(F32), rows[:, fwidth // 2 :].astype(F32)
    first = jnp.where(core == 0, low, high).astype(BF)
    second = jnp.where(core == 0, high, low).astype(BF)
    token = dot(first, fw0_ref[: fwidth // 2]) + dot(second, fw1_ref[: fwidth // 2]) + table_ref[FBIAS : FBIAS + 1, :]
    centered = centre(token)
    tokens = [(centered * inverse_spread(centered) * gain).astype(BF)]
    preds = near_ref[...].astype(F32) + far_ref[...].astype(F32)
    for m in range(members):
        centered = preds[:, m : m + 1] * table_ref[SCALE + m : SCALE + m + 1, :] + table_ref[SHIFT + m : SHIFT + m + 1, :]
        tokens.append((centered * inverse_spread(centered) * gain).astype(BF))
    normed = jnp.concatenate(tokens, axis=0)
    count = len(tokens)

    kmap = jnp.concatenate([table_ref[KMAP : KMAP + 8, :], jnp.zeros((LANES - 8, table_ref.shape[1]), F32)], axis=0)
    logits = dot_t(normed, jnp.concatenate(split2(kmap), axis=0))
    logits = logits[:, :LANES] + logits[:, LANES:]
    expo = jnp.exp(logits)
    expo_cls = jnp.exp(table_ref[LCLS : LCLS + 1, :LANES])
    norm = expo_cls
    for t in range(count):
        norm = norm + expo[t * total : (t + 1) * total]
    inverse = 1.0 / norm
    weights = jnp.concatenate(
        [expo[t * total : (t + 1) * total] * inverse for t in range(count)] + [expo_cls * inverse], axis=0)
    expand = (iota((2 * LANES, 2 * local), 0) & (LANES - 1)) == iota((2 * LANES, 2 * local), 1) // HD
    spread = dot(jnp.concatenate(split2(weights), axis=1), expand.astype(F32).astype(BF))
    parts = []
    for i, ref in enumerate((q0_ref, q1_ref)):
        at = slice(i * local, (i + 1) * local)
        value = dot(normed, ref[2])
        mixed = spread[count * total :, at] * table_ref[VCLS : VCLS + 1, at]
        for t in range(count):
            rng = slice(t * total, (t + 1) * total)
            mixed = mixed + spread[rng, at] * value[rng]
        parts.append(mixed)
    mixed = jnp.concatenate(parts, axis=1).astype(BF)
    size = sent_refs[0].shape[0]
    scatter = (place_ref[...] == iota((size * len(sent_refs), total), 0)).astype(F32).astype(BF)
    sent = dot(scatter, mixed).astype(BF)
    for k, sent_ref in enumerate(sent_refs):
        sent_ref[...] = sent[k * size : (k + 1) * size]


def ensemble_kernel(first, count, tile, feat_ref, w_ref, bias_ref, out_ref, after_ref, *refs):
    held = (len(refs) - 1) // 2
    copies = start_all(list(zip(refs[:held], refs[held + 1 :])), refs[-1]) if held else []
    pred_ref = refs[held]
    for t in range(count):
        rows = feat_ref[(first + t) * tile : (first + t + 1) * tile]
        total = None
        for m in range(w_ref.shape[0]):
            hidden = gelu2(dot(rows, w_ref[m]) + bias_ref[m : m + 1]).astype(BF)
            weights = jnp.broadcast_to(out_ref[m : m + 1].astype(F32), (8, out_ref.shape[1])).astype(BF)
            pred = dot_t(weights, hidden)[0:1]
            total = pred if total is None else total + pred
        per = tile // LANES
        for i in range(per):
            pred_ref[t * per + i : t * per + i + 1, :] = total[:, i * LANES : (i + 1) * LANES]
    for copy in copies:
        copy.wait()


def unpack(ref):
    depth = ref.shape[0] - EXTRA
    extra = ref[depth:, :].astype(F32)
    return ref[:depth, :], *(jnp.sum(extra[i : i + 3], axis=0, keepdims=True) for i in (DOWN, BIAS, HEAD))


def hidden_terms(normed, up, down, bias):
    return jnp.maximum(dot(normed, up) + bias, 0.0).astype(BF).astype(F32) * down


def states(mixed, table_ref, both0_ref, both1_ref):
    local = mixed.shape[1] // 2
    ow0, ow1 = (ref[ref.shape[0] - local :] for ref in (both0_ref, both1_ref))
    state = table_ref[CLS : CLS + 1, :] + dot(mixed[:, :local], ow0) + dot(mixed[:, local:], ow1)
    centered = centre(state)
    return state, (centered * inverse_spread(centered) * table_ref[FGAIN : FGAIN + 1, :]).astype(BF)


def arrived(got_refs, half, e):
    if len(got_refs) == 1:
        rows = got_refs[0].shape[0] // 2
        return got_refs[0][e * rows : (e + 1) * rows]
    return jnp.concatenate([ref[e * half : (e + 1) * half] for ref in got_refs], axis=0)


def arrive_kernel(blocks, half, *refs):
    table_ref, both0_ref, both1_ref, state_ref, normed_ref = refs[blocks:]
    state_ref[...], normed_ref[...] = states(arrived(refs[:blocks][::-1], half, 1), table_ref, both0_ref, both1_ref)


def near_score_kernel(blocks, half, *refs):
    table_ref, both0_ref, both1_ref, up0_ref, up1_ref, score_ref = refs[blocks:]
    state, normed = states(arrived(refs[:blocks][::-1], half, 0), table_ref, both0_ref, both1_ref)
    up, down, bias, head = unpack(up0_ref)
    terms = state * head + hidden_terms(normed, up, down, bias)
    up, down, bias, _ = unpack(up1_ref)
    terms = terms + hidden_terms(normed, up, down, bias)
    score_ref[...] = jnp.sum(terms, axis=-1, keepdims=True)


def far_score_kernel(blocks, half, near_ref, state_ref, mine_ref, other_ref, up2_ref, out_ref):
    rows = near_ref.shape[0]
    up, down, bias, head = unpack(up2_ref)
    terms = hidden_terms(jnp.concatenate([mine_ref[...], other_ref[...]], axis=0), up, down, bias)
    scores = [
        near_ref[...],
        jnp.sum(terms[:rows] + state_ref[...] * head, axis=-1, keepdims=True),
        jnp.sum(terms[rows:], axis=-1, keepdims=True),
    ]
    if blocks == 1:
        eye = iota((rows, rows), 0) == iota((rows, rows), 1)
        for e, score in enumerate(scores):
            out_ref[:, e * rows : (e + 1) * rows] = jnp.sum(jnp.where(eye, score, 0.0), axis=0, keepdims=True)
    else:
        row, lane = iota((half, LANES), 0), iota((half, LANES), 1)
        for k in range(blocks):
            line = jnp.zeros((half, LANES), F32)
            for e, score in enumerate(scores):
                line = jnp.where(lane == row + e * half, score[k * half : (k + 1) * half], line)
            out_ref[k : k + 1, :] = jnp.sum(line, axis=0, keepdims=True)


def expand_kernel(lines, where_ref, after_ref, line_ref, lane_ref):
    rows = lane_ref.shape[1]
    hit = where_ref[:, 2:3] == iota((where_ref.shape[0], rows), 1)

    def by_row(i):
        return jnp.sum(jnp.where(hit, where_ref[:, i : i + 1] + 1, 0).astype(F32), axis=0, keepdims=True).astype(jnp.int32)

    line = (by_row(0) - 1 == iota((lines, rows), 0)).astype(F32)
    line_ref[...] = jnp.concatenate([line] * 3, axis=0).astype(BF)
    lane_ref[...] = by_row(1) - 1


def finish_kernel(members, half, lines, line_ref, lane_ref, near_ref, far_ref, out_ref):
    near, far = near_ref[...], far_ref[...]
    ensemble = (near[lines:] + far[lines:]) * (0.5 / members)
    ensemble = jnp.concatenate([ensemble[i : i + 1] for i in range(ensemble.shape[0])], axis=1)
    lanes = iota((lines, LANES), 1)
    last = (lanes >= half) & (lanes < 2 * half)

    def whole(mine, others):
        return mine[:lines] + jnp.where(last, pltpu.roll(others[:lines], LANES - half, 1), 0.0)

    table = split3(jnp.concatenate([whole(near, far), whole(far, near)], axis=0))
    by_lane = lax.dot_general(table, line_ref[...], (((0,), (0,)), ((), ())), preferred_element_type=F32)
    lane = lane_ref[...]
    replaced = jnp.sum(jnp.where(lane == iota(by_lane.shape, 0), by_lane, 0.0), axis=0, keepdims=True)
    out_ref[...] = jnp.where(lane >= 0, replaced, ensemble)


def cost(flops, size, trans=0):
    return pl.CostEstimate(flops=flops, bytes_accessed=size, transcendentals=trans)


def params(mib):
    return pltpu.CompilerParams(vmem_limit_bytes=mib * 2**20)


def in_hbm(arrays):
    return [pltpu.with_memory_space_constraint(x, pltpu.HBM) for x in arrays]


def shape(dims, dtype):
    return jax.ShapeDtypeStruct(dims, dtype)


def per_device(
    features, escalated, owner_ids, member_in, member_bias, member_out, feat_weight, feat_bias,
    pred_scale, pred_shift, cls_token, attn_gain, qkv_weight, out_weight, ffn_gain, up_weight,
    up_bias, down_weight, owner_heads,
):
    n = lax.axis_size("rows")
    rows, fwidth = features.shape
    count = escalated.shape[1]
    half = max(1, count // n)
    slots = n * half
    here, _, hidden = member_in.shape
    members = pred_scale.shape[0]
    width = cls_token.shape[0]

    def swap(x):
        return lax.ppermute(x, "member", [(0, 1), (1, 0)])

    row = lambda x: x.reshape(1, -1)
    cls_token, attn_gain, ffn_gain, feat_bias = map(row, (cls_token, attn_gain, ffn_gain, feat_bias))
    owners = owner_ids.reshape(1, count)

    pairs = n // 2
    relative = pairs <= 8
    blocks = pairs if relative else 1
    other_qkv = swap(qkv_weight)

    dealt = count // 2
    ins = (escalated, owners, features, qkv_weight, feat_weight, out_weight)
    index, mine, own_qkv, own_both = pl.pallas_call(
        functools.partial(route_kernel, n, half, relative),
        out_shape=[shape((8, count), jnp.int32), shape((count, fwidth), BF), shape(qkv_weight.shape, BF),
                   shape((feat_weight.shape[0] + out_weight.shape[0], width), BF)],
        in_specs=[HBM] * len(ins),
        out_specs=[VMEM] * 4,
        scratch_shapes=[pltpu.VMEM(x.shape, x.dtype) for x in ins[:3]] + [pltpu.SemaphoreType.DMA((6,))],
        compiler_params=params(24),
        cost_estimate=cost(2 * count * rows * fwidth, 3 * 10**6),
        name="route",
    )(*in_hbm(ins))
    near, far, segment = pl.pallas_call(
        predict_kernel,
        out_shape=[shape((dealt, 8), BF), shape((dealt, 8), BF),
                   shape((up_weight.shape[1] + EXTRA, up_weight.shape[2]), BF)],
        in_specs=[VMEM] * 6 + [HBM] * 2,
        out_specs=[VMEM] * 3,
        scratch_shapes=[pltpu.VMEM(down_weight.shape[1:], BF), pltpu.SemaphoreType.DMA((2,))],
        compiler_params=params(24),
        cost_estimate=cost(2 * here * count * fwidth * hidden, 3 * 10**6, here * count * hidden),
        name="predict",
    )(mine, member_in, member_bias, member_out, up_bias, owner_heads, *in_hbm([down_weight, up_weight]))
    far = swap(far)
    other_both = swap(own_both)
    next_segment = lax.ppermute(segment, "rows", [(i, i ^ 1) for i in range(n)])
    other_segment = swap(segment)

    ins = (cls_token, attn_gain, pred_scale, pred_shift, feat_bias, ffn_gain, own_qkv, other_qkv, index)
    table, where, place = pl.pallas_call(
        constants_kernel,
        out_shape=[shape((TABLE, width), F32), shape((count, 3), jnp.int32), shape((1, dealt), jnp.int32)],
        in_specs=[VMEM] * len(ins),
        out_specs=[VMEM] * 3,
        compiler_params=params(16),
        cost_estimate=cost(10**8, 2 * 10**6),
        name="constants",
    )(*ins)

    local = qkv_weight.shape[2]
    sent = pl.pallas_call(
        functools.partial(attend_kernel, members),
        out_shape=[shape((slots // blocks, 2 * local), BF)] * blocks,
        in_specs=[VMEM] * 9,
        out_specs=[VMEM] * blocks,
        compiler_params=params(24),
        cost_estimate=cost(10**9, 2 * 10**6),
        name="attend",
    )(mine, near, far, place, table, own_both, other_both, own_qkv, other_qkv)

    def across(x, k):
        return lax.ppermute(x, "rows", [(i, i ^ (2 * k)) for i in range(n)])

    def exchange(x):
        groups = [[2 * q + b for q in range(pairs)] for b in range(2)]
        return lax.all_to_all(x, "rows", split_axis=0, concat_axis=0, axis_index_groups=groups, tiled=True)

    if relative:
        got = [sent[0]] + [across(sent[k], k) for k in range(1, pairs)]
    else:
        got = exchange(sent[0].reshape(pairs, 2, half, 2 * local))
        got = [got.transpose(1, 0, 2, 3).reshape(slots, 2 * local)]

    tile = min(rows, 256)
    tiles = rows // tile

    def ensemble(first, number, after, held=()):
        return pl.pallas_call(
            functools.partial(ensemble_kernel, first, number, tile),
            out_shape=[shape((number * tile // LANES, LANES), F32)] + [shape(x.shape, x.dtype) for x in held],
            in_specs=[VMEM] * 4 + [ANY] * (1 + len(held)),
            out_specs=[VMEM] * (1 + len(held)),
            scratch_shapes=[pltpu.SemaphoreType.DMA((len(held),))] if held else [],
            compiler_params=params(24),
            cost_estimate=cost(2 * here * number * tile * fwidth * hidden, 10**6, here * number * tile * hidden),
            name="ensemble",
        )(features, member_in, member_bias, member_out, after, *held)

    early = (tiles + 1) // 2
    preds, table, both0, both1, up0, up1 = ensemble(
        0, early, sent[0], (table, own_both, other_both, segment, other_segment))
    preds = [preds]

    state, next_rows = pl.pallas_call(
        functools.partial(arrive_kernel, blocks, half),
        out_shape=[shape((slots // 2, width), F32), shape((slots // 2, width), BF)],
        in_specs=[VMEM] * (blocks + 3),
        out_specs=[VMEM] * 2,
        compiler_params=params(24),
        cost_estimate=cost(2 * 10**8, 2 * 10**6),
        name="arrive",
    )(*got[::-1], table, both0, both1)
    other_rows = swap(next_rows)
    near_scores = pl.pallas_call(
        functools.partial(near_score_kernel, blocks, half),
        out_shape=shape((slots // 2, 1), F32),
        in_specs=[VMEM] * (blocks + 5),
        out_specs=VMEM,
        compiler_params=params(24),
        cost_estimate=cost(5 * 10**8, 2 * 10**6),
        name="near_score",
    )(*got[::-1], table, both0, both1, up0, up1)
    scores = pl.pallas_call(
        functools.partial(far_score_kernel, blocks, half),
        out_shape=shape((blocks, LANES if relative else 3 * slots // 2), F32),
        in_specs=[VMEM] * 5,
        out_specs=VMEM,
        compiler_params=params(24),
        cost_estimate=cost(2 * 10**8, 10**6),
        name="far_score",
    )(near_scores, state, next_rows, other_rows, next_segment)
    for first in range(early, tiles):
        preds += ensemble(first, 1, scores)
    back = scores
    if relative:
        step = 1
        while step < pairs:
            back = jnp.concatenate([back, across(back, step)], axis=0)
            step *= 2
    else:
        back = exchange(back.reshape(3, pairs, half).transpose(1, 0, 2)).reshape(pairs, 3 * half)
        back = jnp.pad(back, ((0, 0), (0, LANES - 3 * half)))
    lines = back.shape[0]
    near_lines = jnp.concatenate([back, *preds], axis=0)
    line_of, lane_of = pl.pallas_call(
        functools.partial(expand_kernel, 2 * lines),
        out_shape=[shape((6 * lines, rows), BF), shape((1, rows), jnp.int32)],
        in_specs=[VMEM, ANY],
        out_specs=[VMEM] * 2,
        compiler_params=params(16),
        cost_estimate=cost(10**8, 10**6),
        name="expand",
    )(where, preds[-1])

    final = pl.pallas_call(
        functools.partial(finish_kernel, members, half, lines),
        out_shape=shape((1, rows), F32),
        in_specs=[VMEM] * 4,
        out_specs=VMEM,
        compiler_params=params(8),
        cost_estimate=cost(10**6, 10**6),
        name="finish",
    )(line_of, lane_of, near_lines, swap(near_lines))
    return final.reshape(rows)


def solution(mesh):
    placed = (
        P(("groups", "rows"), None),
        P(("groups", "rows"), None),
        P(("groups", "rows"), None, None),
        P("member", None, None),
        P("member", None),
        P("member", None),
        P("member", None),
        P(),
        P(),
        P(),
        P(),
        P(),
        P(None, None, "member"),
        P("member", None),
        P(),
        P("rows", None, "member"),
        P("rows", "member"),
        P("rows", "member", None),
        P("rows", None),
    )
    return jax.shard_map(
        per_device, mesh=mesh, in_specs=placed, out_specs=P(("groups", "rows")), check_vma=False
    )
```

```python
import functools
import math

import jax
import jax.numpy as jnp
from jax import lax
from jax.experimental import pallas as pl
from jax.experimental.pallas import tpu as pltpu
from jax.sharding import PartitionSpec as P

HD = 64
EPS = 1e-05
LANES = 128
BF = jnp.bfloat16
F32 = jnp.float32
VMEM = pl.BlockSpec(memory_space=pltpu.VMEM)
HBM = pl.BlockSpec(memory_space=pltpu.HBM)
ANY = pl.BlockSpec(memory_space=pl.ANY)
GELU_C = math.sqrt(2.0 / math.pi)

KMAP, VCLS, LCLS, SCALE, SHIFT, GAIN, FBIAS, CLS, FGAIN = 0, 8, 9, 16, 24, 32, 33, 34, 35
TABLE = 40
DOWN, BIAS, HEAD, EXTRA = 0, 3, 6, 16


def iota(shape, dim):
    return lax.broadcasted_iota(jnp.int32, shape, dim)


def gelu2(x):
    return x + x * jnp.tanh(x * (GELU_C + (GELU_C * 0.044715) * (x * x)))


def dot(a, b):
    return lax.dot_general(a, b, (((1,), (0,)), ((), ())), preferred_element_type=F32)


def dot_t(a, b):
    return lax.dot_general(a, b, (((1,), (1,)), ((), ())), preferred_element_type=F32)


def split2(x):
    high = x.astype(BF)
    return high, (x - high.astype(F32)).astype(BF)


def split3(x):
    high, rest = x.astype(BF), x
    rest = rest - high.astype(F32)
    mid = rest.astype(BF)
    low = (rest - mid.astype(F32)).astype(BF)
    return jnp.concatenate([high.astype(F32), mid.astype(F32), low.astype(F32)], axis=0).astype(BF)


def join3(x):
    rows = x.shape[0] // 3
    return x[:rows] + x[rows : 2 * rows] + x[2 * rows :]


def centre(x):
    return x - jnp.mean(x, axis=-1, keepdims=True)


def inverse_spread(centered):
    return lax.rsqrt(jnp.mean(centered * centered, axis=-1, keepdims=True) + EPS)


def start_all(pairs, sems):
    copies = [pltpu.make_async_copy(src, dst, sems.at[i]) for i, (src, dst) in enumerate(pairs)]
    for copy in copies:
        copy.start()
    return copies


def route_kernel(
    n, half, relative, esc_hbm, own_hbm, feat_hbm, down_hbm, up_hbm, qkv_hbm,
    index_ref, rows_ref, down_ref, segment_ref, qkv_ref, esc_ref, own_ref, feat_ref, sems,
):
    copies = start_all(
        [(esc_hbm, esc_ref), (own_hbm, own_ref), (feat_hbm, feat_ref), (down_hbm.at[0], down_ref),
         (up_hbm.at[0], segment_ref.at[: up_hbm.shape[1]]), (qkv_hbm, qkv_ref)], sems)
    segment_ref[up_hbm.shape[1] :, :] = jnp.zeros((EXTRA, up_hbm.shape[2]), BF)
    core = lax.axis_index("member")
    count = esc_hbm.shape[1]
    dealt = count // 2
    copies[0].wait()
    copies[1].wait()
    esc = esc_ref[...]
    own = own_ref[...]
    ii = iota((count, count), 0)
    jj = iota((count, count), 1)
    own_col = jnp.sum(jnp.where(ii == jj, own, 0).astype(F32), axis=1, keepdims=True).astype(jnp.int32)
    before = jnp.sum((own_col < own).astype(F32), axis=0, keepdims=True).astype(jnp.int32)
    rank = jnp.sum(((own_col == own) & (ii < jj)).astype(F32), axis=0, keepdims=True).astype(jnp.int32)
    position = before + rank
    side = position & 1
    slot = rank >> 1
    apart = own ^ lax.axis_index("rows")
    pair = apart if relative else (own - (own & 1)) + (apart & 1)
    place = pair * half + slot
    dense = (position >> 1) + jnp.where(side == core, 0, dealt)
    source = jnp.sum(jnp.where(dense == ii, esc, 0).astype(F32), axis=1, keepdims=True).astype(jnp.int32)
    chosen = (source == iota((count, feat_ref.shape[0]), 1)).astype(F32).astype(BF)
    line = pair >> 1
    line = line * (n // 2 + 1) + (side ^ core) * (n // 2) ** 2 if relative else line + (side ^ core) * (n // 2)
    for i, row in enumerate((line, (apart & 1) * half + slot, esc, place, dense)):
        index_ref[i : i + 1, :] = row
    copies[2].wait()
    rows_ref[...] = dot(chosen, feat_ref[...]).astype(BF)
    for copy in copies[3:]:
        copy.wait()


def predict_kernel(
    rows_ref, w_ref, bias_ref, out_ref, upb_ref, head_ref, down_ref, raw_ref, fw_hbm, ow_hbm,
    near_ref, far_ref, segment_ref, both_ref, sems,
):
    depth = raw_ref.shape[0] - EXTRA
    copies = start_all(
        [(fw_hbm, both_ref.at[: fw_hbm.shape[0]]), (ow_hbm, both_ref.at[fw_hbm.shape[0] :])], sems)
    here = w_ref.shape[0]
    core = lax.axis_index("member")
    dealt = near_ref.shape[0]
    lane = iota((8, 1), 0)
    preds = None
    for m in range(here):
        act = gelu2(dot(rows_ref[...], w_ref[m]) + bias_ref[m : m + 1]).astype(BF)
        on_lane = jnp.where(lane == core * here + m, 0.5 * out_ref[m : m + 1].astype(F32), 0.0).astype(BF)
        pred = dot_t(act, on_lane)
        preds = pred if preds is None else preds + pred
    preds = preds.astype(BF)
    near_ref[...] = preds[:dealt]
    far_ref[...] = preds[dealt:]
    head = split3(head_ref[...]).astype(F32)
    head = jnp.concatenate([head, jnp.zeros((LANES - 3, head.shape[1]), F32)], axis=0).astype(BF)
    down = jnp.sum(dot_t(down_ref[...], head).T[:8], axis=0, keepdims=True)
    extra = [split3(x).astype(F32) for x in (down, upb_ref[...], head_ref[...])]
    extra.append(jnp.zeros((EXTRA - 9, down.shape[1]), F32))
    segment_ref[depth:, :] = jnp.concatenate(extra, axis=0).astype(BF)
    for copy in copies:
        copy.wait()


def constants_kernel(
    cls_ref, gain_ref, scale_ref, shift_ref, fbias_ref, fgain_ref, q0_ref, q1_ref, index_ref,
    table_ref, where_ref, place_ref,
):
    count = index_ref.shape[1]
    diag = iota((count, count), 0) == iota((count, count), 1)
    cols = [
        jnp.sum(jnp.where(diag, index_ref[i : i + 1, :], 0).astype(F32), axis=1, keepdims=True) for i in range(5)]
    for i in range(3):
        where_ref[:, i : i + 1] = cols[i].astype(jnp.int32)
    dealt = place_ref.shape[1]
    placed = cols[4].astype(jnp.int32) == iota((count, dealt), 1)
    place_ref[...] = jnp.sum(jnp.where(placed, cols[3], 0.0), axis=0, keepdims=True).astype(jnp.int32)
    gain = gain_ref[...]
    cls = cls_ref[...]
    centered = centre(cls)
    ncls = (centered * inverse_spread(centered) * gain).astype(BF)
    table_ref[...] = jnp.zeros_like(table_ref)
    members = scale_ref.shape[0]
    table_ref[SCALE : SCALE + members, :] = centre(scale_ref[...])
    table_ref[SHIFT : SHIFT + members, :] = centre(shift_ref[...])
    table_ref[GAIN : GAIN + 1, :] = gain
    table_ref[FBIAS : FBIAS + 1, :] = fbias_ref[...]
    table_ref[CLS : CLS + 1, :] = cls
    table_ref[FGAIN : FGAIN + 1, :] = fgain_ref[...]
    lhs = jnp.broadcast_to(ncls.astype(F32), (8, ncls.shape[1])).astype(BF)
    local = q0_ref.shape[2]
    heads = local // HD
    row = iota((8, local), 0)
    col = iota((8, local), 1) // HD
    kmap = None
    for i, ref in enumerate((q0_ref, q1_ref)):
        query = dot(lhs, ref[0]) * (1.0 / math.sqrt(HD))
        spread = jnp.where(row == col + i * heads, query, 0.0)
        part = join3(dot_t(split3(spread), ref[1]))
        kmap = part if kmap is None else kmap + part
        table_ref[VCLS : VCLS + 1, i * local : (i + 1) * local] = dot(lhs, ref[2])[0:1]
    table_ref[KMAP : KMAP + 8, :] = kmap
    logits = jnp.sum(kmap * ncls.astype(F32), axis=-1, keepdims=True)
    eye = iota((8, LANES), 0) == iota((8, LANES), 1)
    table_ref[LCLS : LCLS + 1, :LANES] = jnp.sum(jnp.where(eye, logits, 0.0), axis=0, keepdims=True)


def attend_kernel(
    members, rows_ref, near_ref, far_ref, place_ref, table_ref, fw0_ref, fw1_ref, q0_ref, q1_ref, *sent_refs
):
    core = lax.axis_index("member")
    total = near_ref.shape[0]
    fwidth = rows_ref.shape[1]
    rows = rows_ref[:total]
    local = q0_ref.shape[2]
    gain = table_ref[GAIN : GAIN + 1, :]
    low, high = rows[:, : fwidth // 2].astype(F32), rows[:, fwidth // 2 :].astype(F32)
    first = jnp.where(core == 0, low, high).astype(BF)
    second = jnp.where(core == 0, high, low).astype(BF)
    token = dot(first, fw0_ref[: fwidth // 2]) + dot(second, fw1_ref[: fwidth // 2]) + table_ref[FBIAS : FBIAS + 1, :]
    centered = centre(token)
    tokens = [(centered * inverse_spread(centered) * gain).astype(BF)]
    preds = near_ref[...].astype(F32) + far_ref[...].astype(F32)
    for m in range(members):
        centered = preds[:, m : m + 1] * table_ref[SCALE + m : SCALE + m + 1, :] + table_ref[SHIFT + m : SHIFT + m + 1, :]
        tokens.append((centered * inverse_spread(centered) * gain).astype(BF))
    normed = jnp.concatenate(tokens, axis=0)
    count = len(tokens)

    kmap = jnp.concatenate([table_ref[KMAP : KMAP + 8, :], jnp.zeros((LANES - 8, table_ref.shape[1]), F32)], axis=0)
    logits = dot_t(normed, jnp.concatenate(split2(kmap), axis=0))
    logits = logits[:, :LANES] + logits[:, LANES:]
    expo = jnp.exp(logits)
    expo_cls = jnp.exp(table_ref[LCLS : LCLS + 1, :LANES])
    norm = expo_cls
    for t in range(count):
        norm = norm + expo[t * total : (t + 1) * total]
    inverse = 1.0 / norm
    weights = jnp.concatenate(
        [expo[t * total : (t + 1) * total] * inverse for t in range(count)] + [expo_cls * inverse], axis=0)
    expand = (iota((2 * LANES, 2 * local), 0) & (LANES - 1)) == iota((2 * LANES, 2 * local), 1) // HD
    spread = dot(jnp.concatenate(split2(weights), axis=1), expand.astype(F32).astype(BF))
    parts = []
    for i, ref in enumerate((q0_ref, q1_ref)):
        at = slice(i * local, (i + 1) * local)
        value = dot(normed, ref[2])
        mixed = spread[count * total :, at] * table_ref[VCLS : VCLS + 1, at]
        for t in range(count):
            rng = slice(t * total, (t + 1) * total)
            mixed = mixed + spread[rng, at] * value[rng]
        parts.append(mixed)
    mixed = jnp.concatenate(parts, axis=1).astype(BF)
    size = sent_refs[0].shape[0]
    scatter = (place_ref[...] == iota((size * len(sent_refs), total), 0)).astype(F32).astype(BF)
    sent = dot(scatter, mixed).astype(BF)
    for k, sent_ref in enumerate(sent_refs):
        sent_ref[...] = sent[k * size : (k + 1) * size]


def ensemble_kernel(first, count, tile, feat_ref, w_ref, bias_ref, out_ref, after_ref, *refs):
    held = (len(refs) - 1) // 2
    copies = start_all(list(zip(refs[:held], refs[held + 1 :])), refs[-1]) if held else []
    pred_ref = refs[held]
    for t in range(count):
        rows = feat_ref[(first + t) * tile : (first + t + 1) * tile]
        total = None
        for m in range(w_ref.shape[0]):
            hidden = gelu2(dot(rows, w_ref[m]) + bias_ref[m : m + 1]).astype(BF)
            weights = jnp.broadcast_to(out_ref[m : m + 1].astype(F32), (8, out_ref.shape[1])).astype(BF)
            pred = dot_t(weights, hidden)[0:1]
            total = pred if total is None else total + pred
        per = tile // LANES
        for i in range(per):
            pred_ref[t * per + i : t * per + i + 1, :] = total[:, i * LANES : (i + 1) * LANES]
    for copy in copies:
        copy.wait()


def unpack(ref):
    depth = ref.shape[0] - EXTRA
    extra = ref[depth:, :].astype(F32)
    return ref[:depth, :], *(jnp.sum(extra[i : i + 3], axis=0, keepdims=True) for i in (DOWN, BIAS, HEAD))


def hidden_terms(normed, up, down, bias):
    return jnp.maximum(dot(normed, up) + bias, 0.0).astype(BF).astype(F32) * down


def states(mixed, table_ref, both0_ref, both1_ref):
    local = mixed.shape[1] // 2
    ow0, ow1 = (ref[ref.shape[0] - local :] for ref in (both0_ref, both1_ref))
    state = table_ref[CLS : CLS + 1, :] + dot(mixed[:, :local], ow0) + dot(mixed[:, local:], ow1)
    centered = centre(state)
    return state, (centered * inverse_spread(centered) * table_ref[FGAIN : FGAIN + 1, :]).astype(BF)


def arrived(got_refs, half, e):
    if len(got_refs) == 1:
        rows = got_refs[0].shape[0] // 2
        return got_refs[0][e * rows : (e + 1) * rows]
    return jnp.concatenate([ref[e * half : (e + 1) * half] for ref in got_refs], axis=0)


def arrive_kernel(blocks, half, *refs):
    table_ref, both0_ref, both1_ref, state_ref, normed_ref = refs[blocks:]
    state_ref[...], normed_ref[...] = states(arrived(refs[:blocks][::-1], half, 1), table_ref, both0_ref, both1_ref)


def near_score_kernel(blocks, half, *refs):
    table_ref, both0_ref, both1_ref, up0_ref, up1_ref, score_ref = refs[blocks:]
    state, normed = states(arrived(refs[:blocks][::-1], half, 0), table_ref, both0_ref, both1_ref)
    up, down, bias, head = unpack(up0_ref)
    terms = state * head + hidden_terms(normed, up, down, bias)
    up, down, bias, _ = unpack(up1_ref)
    terms = terms + hidden_terms(normed, up, down, bias)
    score_ref[...] = jnp.sum(terms, axis=-1, keepdims=True)


def far_score_kernel(blocks, half, near_ref, state_ref, mine_ref, other_ref, up2_ref, out_ref):
    rows = near_ref.shape[0]
    up, down, bias, head = unpack(up2_ref)
    terms = hidden_terms(jnp.concatenate([mine_ref[...], other_ref[...]], axis=0), up, down, bias)
    scores = [
        near_ref[...],
        jnp.sum(terms[:rows] + state_ref[...] * head, axis=-1, keepdims=True),
        jnp.sum(terms[rows:], axis=-1, keepdims=True),
    ]
    if blocks == 1:
        eye = iota((rows, rows), 0) == iota((rows, rows), 1)
        for e, score in enumerate(scores):
            out_ref[:, e * rows : (e + 1) * rows] = jnp.sum(jnp.where(eye, score, 0.0), axis=0, keepdims=True)
    else:
        row, lane = iota((half, LANES), 0), iota((half, LANES), 1)
        for k in range(blocks):
            line = jnp.zeros((half, LANES), F32)
            for e, score in enumerate(scores):
                line = jnp.where(lane == row + e * half, score[k * half : (k + 1) * half], line)
            out_ref[k : k + 1, :] = jnp.sum(line, axis=0, keepdims=True)


def expand_kernel(lines, where_ref, after_ref, line_ref, lane_ref):
    rows = lane_ref.shape[1]
    hit = where_ref[:, 2:3] == iota((where_ref.shape[0], rows), 1)

    def by_row(i):
        return jnp.sum(jnp.where(hit, where_ref[:, i : i + 1] + 1, 0).astype(F32), axis=0, keepdims=True).astype(jnp.int32)

    line = (by_row(0) - 1 == iota((lines, rows), 0)).astype(F32)
    line_ref[...] = jnp.concatenate([line] * 3, axis=0).astype(BF)
    lane_ref[...] = by_row(1) - 1


def finish_kernel(members, half, lines, line_ref, lane_ref, near_ref, far_ref, out_ref):
    near, far = near_ref[...], far_ref[...]
    ensemble = (near[lines:] + far[lines:]) * (0.5 / members)
    ensemble = jnp.concatenate([ensemble[i : i + 1] for i in range(ensemble.shape[0])], axis=1)
    lanes = iota((lines, LANES), 1)
    last = (lanes >= half) & (lanes < 2 * half)

    def whole(mine, others):
        return mine[:lines] + jnp.where(last, pltpu.roll(others[:lines], LANES - half, 1), 0.0)

    table = split3(jnp.concatenate([whole(near, far), whole(far, near)], axis=0))
    by_lane = lax.dot_general(table, line_ref[...], (((0,), (0,)), ((), ())), preferred_element_type=F32)
    lane = lane_ref[...]
    replaced = jnp.sum(jnp.where(lane == iota(by_lane.shape, 0), by_lane, 0.0), axis=0, keepdims=True)
    out_ref[...] = jnp.where(lane >= 0, replaced, ensemble)


def cost(flops, size, trans=0):
    return pl.CostEstimate(flops=flops, bytes_accessed=size, transcendentals=trans)


def params(mib):
    return pltpu.CompilerParams(vmem_limit_bytes=mib * 2**20)


def in_hbm(arrays):
    return [pltpu.with_memory_space_constraint(x, pltpu.HBM) for x in arrays]


def shape(dims, dtype):
    return jax.ShapeDtypeStruct(dims, dtype)


def per_device(
    features, escalated, owner_ids, member_in, member_bias, member_out, feat_weight, feat_bias,
    pred_scale, pred_shift, cls_token, attn_gain, qkv_weight, out_weight, ffn_gain, up_weight,
    up_bias, down_weight, owner_heads,
):
    n = lax.axis_size("rows")
    rows, fwidth = features.shape
    count = escalated.shape[1]
    half = max(1, count // n)
    slots = n * half
    here, _, hidden = member_in.shape
    members = pred_scale.shape[0]
    width = cls_token.shape[0]

    def swap(x):
        return lax.ppermute(x, "member", [(0, 1), (1, 0)])

    row = lambda x: x.reshape(1, -1)
    cls_token, attn_gain, ffn_gain, feat_bias = map(row, (cls_token, attn_gain, ffn_gain, feat_bias))
    owners = owner_ids.reshape(1, count)

    pairs = n // 2
    relative = pairs <= 8
    blocks = pairs if relative else 1
    other_qkv = swap(qkv_weight)

    dealt = count // 2
    ins = (escalated, owners, features, down_weight, up_weight, qkv_weight)
    index, mine, down, segment, own_qkv = pl.pallas_call(
        functools.partial(route_kernel, n, half, relative),
        out_shape=[shape((8, count), jnp.int32), shape((count, fwidth), BF), shape(down_weight.shape[1:], BF),
                   shape((up_weight.shape[1] + EXTRA, up_weight.shape[2]), BF), shape(qkv_weight.shape, BF)],
        in_specs=[HBM] * len(ins),
        out_specs=[VMEM] * 5,
        scratch_shapes=[pltpu.VMEM(x.shape, x.dtype) for x in ins[:3]] + [pltpu.SemaphoreType.DMA((6,))],
        compiler_params=params(24),
        cost_estimate=cost(2 * count * rows * fwidth, 3 * 10**6),
        name="route",
    )(*in_hbm(ins))
    near, far, segment, own_both = pl.pallas_call(
        predict_kernel,
        out_shape=[shape((dealt, 8), BF), shape((dealt, 8), BF), shape(segment.shape, BF),
                   shape((feat_weight.shape[0] + out_weight.shape[0], width), BF)],
        in_specs=[VMEM] * 8 + [HBM] * 2,
        out_specs=[VMEM] * 4,
        scratch_shapes=[pltpu.SemaphoreType.DMA((2,))],
        input_output_aliases={7: 2},
        compiler_params=params(24),
        cost_estimate=cost(2 * here * count * fwidth * hidden, 3 * 10**6, here * count * hidden),
        name="predict",
    )(mine, member_in, member_bias, member_out, up_bias, owner_heads, down, segment,
      *in_hbm([feat_weight, out_weight]))
    far = swap(far)
    other_both = swap(own_both)
    next_segment = lax.ppermute(segment, "rows", [(i, i ^ 1) for i in range(n)])
    other_segment = swap(segment)

    ins = (cls_token, attn_gain, pred_scale, pred_shift, feat_bias, ffn_gain, own_qkv, other_qkv, index)
    table, where, place = pl.pallas_call(
        constants_kernel,
        out_shape=[shape((TABLE, width), F32), shape((count, 3), jnp.int32), shape((1, dealt), jnp.int32)],
        in_specs=[VMEM] * len(ins),
        out_specs=[VMEM] * 3,
        compiler_params=params(16),
        cost_estimate=cost(10**8, 2 * 10**6),
        name="constants",
    )(*ins)

    local = qkv_weight.shape[2]
    sent = pl.pallas_call(
        functools.partial(attend_kernel, members),
        out_shape=[shape((slots // blocks, 2 * local), BF)] * blocks,
        in_specs=[VMEM] * 9,
        out_specs=[VMEM] * blocks,
        compiler_params=params(24),
        cost_estimate=cost(10**9, 2 * 10**6),
        name="attend",
    )(mine, near, far, place, table, own_both, other_both, own_qkv, other_qkv)

    def across(x, k):
        return lax.ppermute(x, "rows", [(i, i ^ (2 * k)) for i in range(n)])

    def exchange(x):
        groups = [[2 * q + b for q in range(pairs)] for b in range(2)]
        return lax.all_to_all(x, "rows", split_axis=0, concat_axis=0, axis_index_groups=groups, tiled=True)

    if relative:
        got = [sent[0]] + [across(sent[k], k) for k in range(1, pairs)]
    else:
        got = exchange(sent[0].reshape(pairs, 2, half, 2 * local))
        got = [got.transpose(1, 0, 2, 3).reshape(slots, 2 * local)]

    tile = min(rows, 256)
    tiles = rows // tile

    def ensemble(first, number, after, held=()):
        return pl.pallas_call(
            functools.partial(ensemble_kernel, first, number, tile),
            out_shape=[shape((number * tile // LANES, LANES), F32)] + [shape(x.shape, x.dtype) for x in held],
            in_specs=[VMEM] * 4 + [ANY] * (1 + len(held)),
            out_specs=[VMEM] * (1 + len(held)),
            scratch_shapes=[pltpu.SemaphoreType.DMA((len(held),))] if held else [],
            compiler_params=params(24),
            cost_estimate=cost(2 * here * number * tile * fwidth * hidden, 10**6, here * number * tile * hidden),
            name="ensemble",
        )(features, member_in, member_bias, member_out, after, *held)

    early = (tiles + 1) // 2
    preds, table, both0, both1, up0, up1 = ensemble(
        0, early, sent[0], (table, own_both, other_both, segment, other_segment))
    preds = [preds]

    state, next_rows = pl.pallas_call(
        functools.partial(arrive_kernel, blocks, half),
        out_shape=[shape((slots // 2, width), F32), shape((slots // 2, width), BF)],
        in_specs=[VMEM] * (blocks + 3),
        out_specs=[VMEM] * 2,
        compiler_params=params(24),
        cost_estimate=cost(2 * 10**8, 2 * 10**6),
        name="arrive",
    )(*got[::-1], table, both0, both1)
    other_rows = swap(next_rows)
    near_scores = pl.pallas_call(
        functools.partial(near_score_kernel, blocks, half),
        out_shape=shape((slots // 2, 1), F32),
        in_specs=[VMEM] * (blocks + 5),
        out_specs=VMEM,
        compiler_params=params(24),
        cost_estimate=cost(5 * 10**8, 2 * 10**6),
        name="near_score",
    )(*got[::-1], table, both0, both1, up0, up1)
    scores = pl.pallas_call(
        functools.partial(far_score_kernel, blocks, half),
        out_shape=shape((blocks, LANES if relative else 3 * slots // 2), F32),
        in_specs=[VMEM] * 5,
        out_specs=VMEM,
        compiler_params=params(24),
        cost_estimate=cost(2 * 10**8, 10**6),
        name="far_score",
    )(near_scores, state, next_rows, other_rows, next_segment)
    for first in range(early, tiles):
        preds += ensemble(first, 1, scores)
    back = scores
    if relative:
        step = 1
        while step < pairs:
            back = jnp.concatenate([back, across(back, step)], axis=0)
            step *= 2
    else:
        back = exchange(back.reshape(3, pairs, half).transpose(1, 0, 2)).reshape(pairs, 3 * half)
        back = jnp.pad(back, ((0, 0), (0, LANES - 3 * half)))
    lines = back.shape[0]
    near_lines = jnp.concatenate([back, *preds], axis=0)
    line_of, lane_of = pl.pallas_call(
        functools.partial(expand_kernel, 2 * lines),
        out_shape=[shape((6 * lines, rows), BF), shape((1, rows), jnp.int32)],
        in_specs=[VMEM, ANY],
        out_specs=[VMEM] * 2,
        compiler_params=params(16),
        cost_estimate=cost(10**8, 10**6),
        name="expand",
    )(where, preds[-1])

    final = pl.pallas_call(
        functools.partial(finish_kernel, members, half, lines),
        out_shape=shape((1, rows), F32),
        in_specs=[VMEM] * 4,
        out_specs=VMEM,
        compiler_params=params(8),
        cost_estimate=cost(10**6, 10**6),
        name="finish",
    )(line_of, lane_of, near_lines, swap(near_lines))
    return final.reshape(rows)


def solution(mesh):
    placed = (
        P(("groups", "rows"), None),
        P(("groups", "rows"), None),
        P(("groups", "rows"), None, None),
        P("member", None, None),
        P("member", None),
        P("member", None),
        P("member", None),
        P(),
        P(),
        P(),
        P(),
        P(),
        P(None, None, "member"),
        P("member", None),
        P(),
        P("rows", None, "member"),
        P("rows", "member"),
        P("rows", "member", None),
        P("rows", None),
    )
    return jax.shard_map(
        per_device, mesh=mesh, in_specs=placed, out_specs=P(("groups", "rows")), check_vma=False
    )
```

```python
import functools
import math

import jax
import jax.numpy as jnp
from jax import lax
from jax.experimental import pallas as pl
from jax.experimental.pallas import tpu as pltpu
from jax.sharding import PartitionSpec as P

HD = 64
EPS = 1e-05
LANES = 128
BF = jnp.bfloat16
F32 = jnp.float32
VMEM = pl.BlockSpec(memory_space=pltpu.VMEM)
HBM = pl.BlockSpec(memory_space=pltpu.HBM)
ANY = pl.BlockSpec(memory_space=pl.ANY)
GELU_C = math.sqrt(2.0 / math.pi)

KMAP, VCLS, LCLS, SCALE, SHIFT, GAIN, FBIAS, CLS, FGAIN = 0, 8, 9, 16, 24, 32, 33, 34, 35
TABLE = 40
DOWN, BIAS, HEAD, EXTRA = 0, 3, 6, 16


def iota(shape, dim):
    return lax.broadcasted_iota(jnp.int32, shape, dim)


def gelu2(x):
    return x + x * jnp.tanh(x * (GELU_C + (GELU_C * 0.044715) * (x * x)))


def dot(a, b):
    return lax.dot_general(a, b, (((1,), (0,)), ((), ())), preferred_element_type=F32)


def dot_t(a, b):
    return lax.dot_general(a, b, (((1,), (1,)), ((), ())), preferred_element_type=F32)


def split2(x):
    high = x.astype(BF)
    return high, (x - high.astype(F32)).astype(BF)


def split3(x):
    high, rest = x.astype(BF), x
    rest = rest - high.astype(F32)
    mid = rest.astype(BF)
    low = (rest - mid.astype(F32)).astype(BF)
    return jnp.concatenate([high.astype(F32), mid.astype(F32), low.astype(F32)], axis=0).astype(BF)


def join3(x):
    rows = x.shape[0] // 3
    return x[:rows] + x[rows : 2 * rows] + x[2 * rows :]


def centre(x):
    return x - jnp.mean(x, axis=-1, keepdims=True)


def inverse_spread(centered):
    return lax.rsqrt(jnp.mean(centered * centered, axis=-1, keepdims=True) + EPS)


def start_all(pairs, sems):
    copies = [pltpu.make_async_copy(src, dst, sems.at[i]) for i, (src, dst) in enumerate(pairs)]
    for copy in copies:
        copy.start()
    return copies


def route_kernel(
    n, half, relative, esc_hbm, own_hbm, feat_hbm, down_hbm, up_hbm, fw_hbm, ow_hbm, qkv_hbm,
    index_ref, rows_ref, down_ref, segment_ref, both_ref, qkv_ref, esc_ref, own_ref, feat_ref, sems,
):
    copies = start_all(
        [(esc_hbm, esc_ref), (own_hbm, own_ref), (feat_hbm, feat_ref), (down_hbm.at[0], down_ref),
         (fw_hbm, both_ref.at[: fw_hbm.shape[0]]), (ow_hbm, both_ref.at[fw_hbm.shape[0] :]),
         (up_hbm.at[0], segment_ref.at[: up_hbm.shape[1]]), (qkv_hbm, qkv_ref)], sems)
    segment_ref[up_hbm.shape[1] :, :] = jnp.zeros((EXTRA, up_hbm.shape[2]), BF)
    core = lax.axis_index("member")
    count = esc_hbm.shape[1]
    dealt = count // 2
    copies[0].wait()
    copies[1].wait()
    esc = esc_ref[...]
    own = own_ref[...]
    ii = iota((count, count), 0)
    jj = iota((count, count), 1)
    own_col = jnp.sum(jnp.where(ii == jj, own, 0).astype(F32), axis=1, keepdims=True).astype(jnp.int32)
    before = jnp.sum((own_col < own).astype(F32), axis=0, keepdims=True).astype(jnp.int32)
    rank = jnp.sum(((own_col == own) & (ii < jj)).astype(F32), axis=0, keepdims=True).astype(jnp.int32)
    position = before + rank
    side = position & 1
    slot = rank >> 1
    apart = own ^ lax.axis_index("rows")
    pair = apart if relative else (own - (own & 1)) + (apart & 1)
    place = pair * half + slot
    dense = (position >> 1) + jnp.where(side == core, 0, dealt)
    source = jnp.sum(jnp.where(dense == ii, esc, 0).astype(F32), axis=1, keepdims=True).astype(jnp.int32)
    chosen = (source == iota((count, feat_ref.shape[0]), 1)).astype(F32).astype(BF)
    line = pair >> 1
    line = line * (n // 2 + 1) + (side ^ core) * (n // 2) ** 2 if relative else line + (side ^ core) * (n // 2)
    for i, row in enumerate((line, (apart & 1) * half + slot, esc, place, dense)):
        index_ref[i : i + 1, :] = row
    copies[2].wait()
    rows_ref[...] = dot(chosen, feat_ref[...]).astype(BF)
    for copy in copies[3:]:
        copy.wait()


def predict_kernel(
    rows_ref, w_ref, bias_ref, out_ref, upb_ref, head_ref, down_ref, raw_ref,
    near_ref, far_ref, segment_ref,
):
    depth = raw_ref.shape[0] - EXTRA
    here = w_ref.shape[0]
    core = lax.axis_index("member")
    dealt = near_ref.shape[0]
    lane = iota((8, 1), 0)
    preds = None
    for m in range(here):
        act = gelu2(dot(rows_ref[...], w_ref[m]) + bias_ref[m : m + 1]).astype(BF)
        on_lane = jnp.where(lane == core * here + m, 0.5 * out_ref[m : m + 1].astype(F32), 0.0).astype(BF)
        pred = dot_t(act, on_lane)
        preds = pred if preds is None else preds + pred
    preds = preds.astype(BF)
    near_ref[...] = preds[:dealt]
    far_ref[...] = preds[dealt:]
    head = split3(head_ref[...]).astype(F32)
    head = jnp.concatenate([head, jnp.zeros((LANES - 3, head.shape[1]), F32)], axis=0).astype(BF)
    down = jnp.sum(dot_t(down_ref[...], head).T[:8], axis=0, keepdims=True)
    extra = [split3(x).astype(F32) for x in (down, upb_ref[...], head_ref[...])]
    extra.append(jnp.zeros((EXTRA - 9, down.shape[1]), F32))
    segment_ref[depth:, :] = jnp.concatenate(extra, axis=0).astype(BF)


def constants_kernel(
    cls_ref, gain_ref, scale_ref, shift_ref, fbias_ref, fgain_ref, q0_ref, q1_ref, index_ref,
    table_ref, where_ref, place_ref,
):
    count = index_ref.shape[1]
    diag = iota((count, count), 0) == iota((count, count), 1)
    cols = [
        jnp.sum(jnp.where(diag, index_ref[i : i + 1, :], 0).astype(F32), axis=1, keepdims=True) for i in range(5)]
    for i in range(3):
        where_ref[:, i : i + 1] = cols[i].astype(jnp.int32)
    dealt = place_ref.shape[1]
    placed = cols[4].astype(jnp.int32) == iota((count, dealt), 1)
    place_ref[...] = jnp.sum(jnp.where(placed, cols[3], 0.0), axis=0, keepdims=True).astype(jnp.int32)
    gain = gain_ref[...]
    cls = cls_ref[...]
    centered = centre(cls)
    ncls = (centered * inverse_spread(centered) * gain).astype(BF)
    table_ref[...] = jnp.zeros_like(table_ref)
    members = scale_ref.shape[0]
    table_ref[SCALE : SCALE + members, :] = centre(scale_ref[...])
    table_ref[SHIFT : SHIFT + members, :] = centre(shift_ref[...])
    table_ref[GAIN : GAIN + 1, :] = gain
    table_ref[FBIAS : FBIAS + 1, :] = fbias_ref[...]
    table_ref[CLS : CLS + 1, :] = cls
    table_ref[FGAIN : FGAIN + 1, :] = fgain_ref[...]
    lhs = jnp.broadcast_to(ncls.astype(F32), (8, ncls.shape[1])).astype(BF)
    local = q0_ref.shape[2]
    heads = local // HD
    row = iota((8, local), 0)
    col = iota((8, local), 1) // HD
    kmap = None
    for i, ref in enumerate((q0_ref, q1_ref)):
        query = dot(lhs, ref[0]) * (1.0 / math.sqrt(HD))
        spread = jnp.where(row == col + i * heads, query, 0.0)
        part = join3(dot_t(split3(spread), ref[1]))
        kmap = part if kmap is None else kmap + part
        table_ref[VCLS : VCLS + 1, i * local : (i + 1) * local] = dot(lhs, ref[2])[0:1]
    table_ref[KMAP : KMAP + 8, :] = kmap
    logits = jnp.sum(kmap * ncls.astype(F32), axis=-1, keepdims=True)
    eye = iota((8, LANES), 0) == iota((8, LANES), 1)
    table_ref[LCLS : LCLS + 1, :LANES] = jnp.sum(jnp.where(eye, logits, 0.0), axis=0, keepdims=True)


def attend_kernel(
    members, rows_ref, near_ref, far_ref, place_ref, table_ref, fw0_ref, fw1_ref, q0_ref, q1_ref, *sent_refs
):
    core = lax.axis_index("member")
    total = near_ref.shape[0]
    fwidth = rows_ref.shape[1]
    rows = rows_ref[:total]
    local = q0_ref.shape[2]
    gain = table_ref[GAIN : GAIN + 1, :]
    low, high = rows[:, : fwidth // 2].astype(F32), rows[:, fwidth // 2 :].astype(F32)
    first = jnp.where(core == 0, low, high).astype(BF)
    second = jnp.where(core == 0, high, low).astype(BF)
    token = dot(first, fw0_ref[: fwidth // 2]) + dot(second, fw1_ref[: fwidth // 2]) + table_ref[FBIAS : FBIAS + 1, :]
    centered = centre(token)
    tokens = [(centered * inverse_spread(centered) * gain).astype(BF)]
    preds = near_ref[...].astype(F32) + far_ref[...].astype(F32)
    for m in range(members):
        centered = preds[:, m : m + 1] * table_ref[SCALE + m : SCALE + m + 1, :] + table_ref[SHIFT + m : SHIFT + m + 1, :]
        tokens.append((centered * inverse_spread(centered) * gain).astype(BF))
    normed = jnp.concatenate(tokens, axis=0)
    count = len(tokens)

    kmap = jnp.concatenate([table_ref[KMAP : KMAP + 8, :], jnp.zeros((LANES - 8, table_ref.shape[1]), F32)], axis=0)
    logits = dot_t(normed, jnp.concatenate(split2(kmap), axis=0))
    logits = logits[:, :LANES] + logits[:, LANES:]
    expo = jnp.exp(logits)
    expo_cls = jnp.exp(table_ref[LCLS : LCLS + 1, :LANES])
    norm = expo_cls
    for t in range(count):
        norm = norm + expo[t * total : (t + 1) * total]
    inverse = 1.0 / norm
    weights = jnp.concatenate(
        [expo[t * total : (t + 1) * total] * inverse for t in range(count)] + [expo_cls * inverse], axis=0)
    expand = (iota((2 * LANES, 2 * local), 0) & (LANES - 1)) == iota((2 * LANES, 2 * local), 1) // HD
    spread = dot(jnp.concatenate(split2(weights), axis=1), expand.astype(F32).astype(BF))
    parts = []
    for i, ref in enumerate((q0_ref, q1_ref)):
        at = slice(i * local, (i + 1) * local)
        value = dot(normed, ref[2])
        mixed = spread[count * total :, at] * table_ref[VCLS : VCLS + 1, at]
        for t in range(count):
            rng = slice(t * total, (t + 1) * total)
            mixed = mixed + spread[rng, at] * value[rng]
        parts.append(mixed)
    mixed = jnp.concatenate(parts, axis=1).astype(BF)
    size = sent_refs[0].shape[0]
    scatter = (place_ref[...] == iota((size * len(sent_refs), total), 0)).astype(F32).astype(BF)
    sent = dot(scatter, mixed).astype(BF)
    for k, sent_ref in enumerate(sent_refs):
        sent_ref[...] = sent[k * size : (k + 1) * size]


def ensemble_kernel(first, count, tile, feat_ref, w_ref, bias_ref, out_ref, after_ref, *refs):
    held = (len(refs) - 1) // 2
    copies = start_all(list(zip(refs[:held], refs[held + 1 :])), refs[-1]) if held else []
    pred_ref = refs[held]
    for t in range(count):
        rows = feat_ref[(first + t) * tile : (first + t + 1) * tile]
        total = None
        for m in range(w_ref.shape[0]):
            hidden = gelu2(dot(rows, w_ref[m]) + bias_ref[m : m + 1]).astype(BF)
            weights = jnp.broadcast_to(out_ref[m : m + 1].astype(F32), (8, out_ref.shape[1])).astype(BF)
            pred = dot_t(weights, hidden)[0:1]
            total = pred if total is None else total + pred
        per = tile // LANES
        for i in range(per):
            pred_ref[t * per + i : t * per + i + 1, :] = total[:, i * LANES : (i + 1) * LANES]
    for copy in copies:
        copy.wait()


def unpack(ref):
    depth = ref.shape[0] - EXTRA
    extra = ref[depth:, :].astype(F32)
    return ref[:depth, :], *(jnp.sum(extra[i : i + 3], axis=0, keepdims=True) for i in (DOWN, BIAS, HEAD))


def hidden_terms(normed, up, down, bias):
    return jnp.maximum(dot(normed, up) + bias, 0.0).astype(BF).astype(F32) * down


def states(mixed, table_ref, both0_ref, both1_ref):
    local = mixed.shape[1] // 2
    ow0, ow1 = (ref[ref.shape[0] - local :] for ref in (both0_ref, both1_ref))
    state = table_ref[CLS : CLS + 1, :] + dot(mixed[:, :local], ow0) + dot(mixed[:, local:], ow1)
    centered = centre(state)
    return state, (centered * inverse_spread(centered) * table_ref[FGAIN : FGAIN + 1, :]).astype(BF)


def arrived(got_refs, half, e):
    if len(got_refs) == 1:
        rows = got_refs[0].shape[0] // 2
        return got_refs[0][e * rows : (e + 1) * rows]
    return jnp.concatenate([ref[e * half : (e + 1) * half] for ref in got_refs], axis=0)


def arrive_kernel(blocks, half, *refs):
    table_ref, both0_ref, both1_ref, state_ref, normed_ref = refs[blocks:]
    state_ref[...], normed_ref[...] = states(arrived(refs[:blocks][::-1], half, 1), table_ref, both0_ref, both1_ref)


def near_score_kernel(blocks, half, *refs):
    table_ref, both0_ref, both1_ref, up0_ref, up1_ref, score_ref = refs[blocks:]
    state, normed = states(arrived(refs[:blocks][::-1], half, 0), table_ref, both0_ref, both1_ref)
    up, down, bias, head = unpack(up0_ref)
    terms = state * head + hidden_terms(normed, up, down, bias)
    up, down, bias, _ = unpack(up1_ref)
    terms = terms + hidden_terms(normed, up, down, bias)
    score_ref[...] = jnp.sum(terms, axis=-1, keepdims=True)


def far_score_kernel(blocks, half, near_ref, state_ref, mine_ref, other_ref, up2_ref, out_ref):
    rows = near_ref.shape[0]
    up, down, bias, head = unpack(up2_ref)
    terms = hidden_terms(jnp.concatenate([mine_ref[...], other_ref[...]], axis=0), up, down, bias)
    scores = [
        near_ref[...],
        jnp.sum(terms[:rows] + state_ref[...] * head, axis=-1, keepdims=True),
        jnp.sum(terms[rows:], axis=-1, keepdims=True),
    ]
    if blocks == 1:
        eye = iota((rows, rows), 0) == iota((rows, rows), 1)
        for e, score in enumerate(scores):
            out_ref[:, e * rows : (e + 1) * rows] = jnp.sum(jnp.where(eye, score, 0.0), axis=0, keepdims=True)
    else:
        row, lane = iota((half, LANES), 0), iota((half, LANES), 1)
        for k in range(blocks):
            line = jnp.zeros((half, LANES), F32)
            for e, score in enumerate(scores):
                line = jnp.where(lane == row + e * half, score[k * half : (k + 1) * half], line)
            out_ref[k : k + 1, :] = jnp.sum(line, axis=0, keepdims=True)


def expand_kernel(lines, where_ref, after_ref, line_ref, lane_ref):
    rows = lane_ref.shape[1]
    hit = where_ref[:, 2:3] == iota((where_ref.shape[0], rows), 1)

    def by_row(i):
        return jnp.sum(jnp.where(hit, where_ref[:, i : i + 1] + 1, 0).astype(F32), axis=0, keepdims=True).astype(jnp.int32)

    line = (by_row(0) - 1 == iota((lines, rows), 0)).astype(F32)
    line_ref[...] = jnp.concatenate([line] * 3, axis=0).astype(BF)
    lane_ref[...] = by_row(1) - 1


def finish_kernel(members, half, lines, line_ref, lane_ref, near_ref, far_ref, out_ref):
    near, far = near_ref[...], far_ref[...]
    ensemble = (near[lines:] + far[lines:]) * (0.5 / members)
    ensemble = jnp.concatenate([ensemble[i : i + 1] for i in range(ensemble.shape[0])], axis=1)
    lanes = iota((lines, LANES), 1)
    last = (lanes >= half) & (lanes < 2 * half)

    def whole(mine, others):
        return mine[:lines] + jnp.where(last, pltpu.roll(others[:lines], LANES - half, 1), 0.0)

    table = split3(jnp.concatenate([whole(near, far), whole(far, near)], axis=0))
    by_lane = lax.dot_general(table, line_ref[...], (((0,), (0,)), ((), ())), preferred_element_type=F32)
    lane = lane_ref[...]
    replaced = jnp.sum(jnp.where(lane == iota(by_lane.shape, 0), by_lane, 0.0), axis=0, keepdims=True)
    out_ref[...] = jnp.where(lane >= 0, replaced, ensemble)


def cost(flops, size, trans=0):
    return pl.CostEstimate(flops=flops, bytes_accessed=size, transcendentals=trans)


def params(mib):
    return pltpu.CompilerParams(vmem_limit_bytes=mib * 2**20)


def in_hbm(arrays):
    return [pltpu.with_memory_space_constraint(x, pltpu.HBM) for x in arrays]


def shape(dims, dtype):
    return jax.ShapeDtypeStruct(dims, dtype)


def per_device(
    features, escalated, owner_ids, member_in, member_bias, member_out, feat_weight, feat_bias,
    pred_scale, pred_shift, cls_token, attn_gain, qkv_weight, out_weight, ffn_gain, up_weight,
    up_bias, down_weight, owner_heads,
):
    n = lax.axis_size("rows")
    rows, fwidth = features.shape
    count = escalated.shape[1]
    half = max(1, count // n)
    slots = n * half
    here, _, hidden = member_in.shape
    members = pred_scale.shape[0]
    width = cls_token.shape[0]

    def swap(x):
        return lax.ppermute(x, "member", [(0, 1), (1, 0)])

    row = lambda x: x.reshape(1, -1)
    cls_token, attn_gain, ffn_gain, feat_bias = map(row, (cls_token, attn_gain, ffn_gain, feat_bias))
    owners = owner_ids.reshape(1, count)

    pairs = n // 2
    relative = pairs <= 8
    blocks = pairs if relative else 1
    other_qkv = swap(qkv_weight)

    dealt = count // 2
    ins = (escalated, owners, features, down_weight, up_weight, feat_weight, out_weight, qkv_weight)
    index, mine, down, segment, own_both, own_qkv = pl.pallas_call(
        functools.partial(route_kernel, n, half, relative),
        out_shape=[shape((8, count), jnp.int32), shape((count, fwidth), BF), shape(down_weight.shape[1:], BF),
                   shape((up_weight.shape[1] + EXTRA, up_weight.shape[2]), BF),
                   shape((feat_weight.shape[0] + out_weight.shape[0], width), BF), shape(qkv_weight.shape, BF)],
        in_specs=[HBM] * len(ins),
        out_specs=[VMEM] * 6,
        scratch_shapes=[pltpu.VMEM(x.shape, x.dtype) for x in ins[:3]] + [pltpu.SemaphoreType.DMA((8,))],
        compiler_params=params(24),
        cost_estimate=cost(2 * count * rows * fwidth, 3 * 10**6),
        name="route",
    )(*in_hbm(ins))
    near, far, segment = pl.pallas_call(
        predict_kernel,
        out_shape=[shape((dealt, 8), BF), shape((dealt, 8), BF), shape(segment.shape, BF)],
        in_specs=[VMEM] * 8,
        out_specs=[VMEM] * 3,
        input_output_aliases={7: 2},
        compiler_params=params(24),
        cost_estimate=cost(2 * here * count * fwidth * hidden, 3 * 10**6, here * count * hidden),
        name="predict",
    )(mine, member_in, member_bias, member_out, up_bias, owner_heads, down, segment)
    far = swap(far)
    other_both = swap(own_both)
    next_segment = lax.ppermute(segment, "rows", [(i, i ^ 1) for i in range(n)])
    other_segment = swap(segment)

    ins = (cls_token, attn_gain, pred_scale, pred_shift, feat_bias, ffn_gain, own_qkv, other_qkv, index)
    table, where, place = pl.pallas_call(
        constants_kernel,
        out_shape=[shape((TABLE, width), F32), shape((count, 3), jnp.int32), shape((1, dealt), jnp.int32)],
        in_specs=[VMEM] * len(ins),
        out_specs=[VMEM] * 3,
        compiler_params=params(16),
        cost_estimate=cost(10**8, 2 * 10**6),
        name="constants",
    )(*ins)

    local = qkv_weight.shape[2]
    sent = pl.pallas_call(
        functools.partial(attend_kernel, members),
        out_shape=[shape((slots // blocks, 2 * local), BF)] * blocks,
        in_specs=[VMEM] * 9,
        out_specs=[VMEM] * blocks,
        compiler_params=params(24),
        cost_estimate=cost(10**9, 2 * 10**6),
        name="attend",
    )(mine, near, far, place, table, own_both, other_both, own_qkv, other_qkv)

    def across(x, k):
        return lax.ppermute(x, "rows", [(i, i ^ (2 * k)) for i in range(n)])

    def exchange(x):
        groups = [[2 * q + b for q in range(pairs)] for b in range(2)]
        return lax.all_to_all(x, "rows", split_axis=0, concat_axis=0, axis_index_groups=groups, tiled=True)

    if relative:
        got = [sent[0]] + [across(sent[k], k) for k in range(1, pairs)]
    else:
        got = exchange(sent[0].reshape(pairs, 2, half, 2 * local))
        got = [got.transpose(1, 0, 2, 3).reshape(slots, 2 * local)]

    tile = min(rows, 256)
    tiles = rows // tile

    def ensemble(first, number, after, held=()):
        return pl.pallas_call(
            functools.partial(ensemble_kernel, first, number, tile),
            out_shape=[shape((number * tile // LANES, LANES), F32)] + [shape(x.shape, x.dtype) for x in held],
            in_specs=[VMEM] * 4 + [ANY] * (1 + len(held)),
            out_specs=[VMEM] * (1 + len(held)),
            scratch_shapes=[pltpu.SemaphoreType.DMA((len(held),))] if held else [],
            compiler_params=params(24),
            cost_estimate=cost(2 * here * number * tile * fwidth * hidden, 10**6, here * number * tile * hidden),
            name="ensemble",
        )(features, member_in, member_bias, member_out, after, *held)

    early = (tiles + 1) // 2
    preds, table, both0, both1, up0, up1 = ensemble(
        0, early, sent[0], (table, own_both, other_both, segment, other_segment))
    preds = [preds]

    state, next_rows = pl.pallas_call(
        functools.partial(arrive_kernel, blocks, half),
        out_shape=[shape((slots // 2, width), F32), shape((slots // 2, width), BF)],
        in_specs=[VMEM] * (blocks + 3),
        out_specs=[VMEM] * 2,
        compiler_params=params(24),
        cost_estimate=cost(2 * 10**8, 2 * 10**6),
        name="arrive",
    )(*got[::-1], table, both0, both1)
    other_rows = swap(next_rows)
    near_scores = pl.pallas_call(
        functools.partial(near_score_kernel, blocks, half),
        out_shape=shape((slots // 2, 1), F32),
        in_specs=[VMEM] * (blocks + 5),
        out_specs=VMEM,
        compiler_params=params(24),
        cost_estimate=cost(5 * 10**8, 2 * 10**6),
        name="near_score",
    )(*got[::-1], table, both0, both1, up0, up1)
    scores = pl.pallas_call(
        functools.partial(far_score_kernel, blocks, half),
        out_shape=shape((blocks, LANES if relative else 3 * slots // 2), F32),
        in_specs=[VMEM] * 5,
        out_specs=VMEM,
        compiler_params=params(24),
        cost_estimate=cost(2 * 10**8, 10**6),
        name="far_score",
    )(near_scores, state, next_rows, other_rows, next_segment)
    for first in range(early, tiles):
        preds += ensemble(first, 1, scores)
    back = scores
    if relative:
        step = 1
        while step < pairs:
            back = jnp.concatenate([back, across(back, step)], axis=0)
            step *= 2
    else:
        back = exchange(back.reshape(3, pairs, half).transpose(1, 0, 2)).reshape(pairs, 3 * half)
        back = jnp.pad(back, ((0, 0), (0, LANES - 3 * half)))
    lines = back.shape[0]
    near_lines = jnp.concatenate([back, *preds], axis=0)
    line_of, lane_of = pl.pallas_call(
        functools.partial(expand_kernel, 2 * lines),
        out_shape=[shape((6 * lines, rows), BF), shape((1, rows), jnp.int32)],
        in_specs=[VMEM, ANY],
        out_specs=[VMEM] * 2,
        compiler_params=params(16),
        cost_estimate=cost(10**8, 10**6),
        name="expand",
    )(where, preds[-1])

    final = pl.pallas_call(
        functools.partial(finish_kernel, members, half, lines),
        out_shape=shape((1, rows), F32),
        in_specs=[VMEM] * 4,
        out_specs=VMEM,
        compiler_params=params(8),
        cost_estimate=cost(10**6, 10**6),
        name="finish",
    )(line_of, lane_of, near_lines, swap(near_lines))
    return final.reshape(rows)


def solution(mesh):
    placed = (
        P(("groups", "rows"), None),
        P(("groups", "rows"), None),
        P(("groups", "rows"), None, None),
        P("member", None, None),
        P("member", None),
        P("member", None),
        P("member", None),
        P(),
        P(),
        P(),
        P(),
        P(),
        P(None, None, "member"),
        P("member", None),
        P(),
        P("rows", None, "member"),
        P("rows", "member"),
        P("rows", "member", None),
        P("rows", None),
    )
    return jax.shard_map(
        per_device, mesh=mesh, in_specs=placed, out_specs=P(("groups", "rows")), check_vma=False
    )
```

```python
import functools
import math

import jax
import jax.numpy as jnp
from jax import lax
from jax.experimental import pallas as pl
from jax.experimental.pallas import tpu as pltpu
from jax.sharding import PartitionSpec as P

HD = 64
EPS = 1e-05
LANES = 128
BF = jnp.bfloat16
F32 = jnp.float32
VMEM = pl.BlockSpec(memory_space=pltpu.VMEM)
HBM = pl.BlockSpec(memory_space=pltpu.HBM)
ANY = pl.BlockSpec(memory_space=pl.ANY)
GELU_C = math.sqrt(2.0 / math.pi)

KMAP, VCLS, LCLS, SCALE, SHIFT, GAIN, FBIAS, CLS, FGAIN = 0, 8, 9, 16, 24, 32, 33, 34, 35
TABLE = 40
DOWN, BIAS, HEAD, EXTRA = 0, 3, 6, 16


def iota(shape, dim):
    return lax.broadcasted_iota(jnp.int32, shape, dim)


def gelu2(x):
    return x + x * jnp.tanh(x * (GELU_C + (GELU_C * 0.044715) * (x * x)))


def dot(a, b):
    return lax.dot_general(a, b, (((1,), (0,)), ((), ())), preferred_element_type=F32)


def dot_t(a, b):
    return lax.dot_general(a, b, (((1,), (1,)), ((), ())), preferred_element_type=F32)


def split2(x):
    high = x.astype(BF)
    return high, (x - high.astype(F32)).astype(BF)


def split3(x):
    high, rest = x.astype(BF), x
    rest = rest - high.astype(F32)
    mid = rest.astype(BF)
    low = (rest - mid.astype(F32)).astype(BF)
    return jnp.concatenate([high.astype(F32), mid.astype(F32), low.astype(F32)], axis=0).astype(BF)


def join3(x):
    rows = x.shape[0] // 3
    return x[:rows] + x[rows : 2 * rows] + x[2 * rows :]


def centre(x):
    return x - jnp.mean(x, axis=-1, keepdims=True)


def inverse_spread(centered):
    return lax.rsqrt(jnp.mean(centered * centered, axis=-1, keepdims=True) + EPS)


def start_all(pairs, sems):
    copies = [pltpu.make_async_copy(src, dst, sems.at[i]) for i, (src, dst) in enumerate(pairs)]
    for copy in copies:
        copy.start()
    return copies


def route_kernel(
    n, half, relative, esc_hbm, own_hbm, feat_hbm, down_hbm, up_hbm, fw_hbm, ow_hbm,
    index_ref, rows_ref, down_ref, segment_ref, both_ref, esc_ref, own_ref, feat_ref, sems,
):
    copies = start_all(
        [(esc_hbm, esc_ref), (own_hbm, own_ref), (feat_hbm, feat_ref), (down_hbm.at[0], down_ref),
         (fw_hbm, both_ref.at[: fw_hbm.shape[0]]), (ow_hbm, both_ref.at[fw_hbm.shape[0] :]),
         (up_hbm.at[0], segment_ref.at[: up_hbm.shape[1]])], sems)
    segment_ref[up_hbm.shape[1] :, :] = jnp.zeros((EXTRA, up_hbm.shape[2]), BF)
    core = lax.axis_index("member")
    count = esc_hbm.shape[1]
    dealt = count // 2
    copies[0].wait()
    copies[1].wait()
    esc = esc_ref[...]
    own = own_ref[...]
    ii = iota((count, count), 0)
    jj = iota((count, count), 1)
    own_col = jnp.sum(jnp.where(ii == jj, own, 0).astype(F32), axis=1, keepdims=True).astype(jnp.int32)
    before = jnp.sum((own_col < own).astype(F32), axis=0, keepdims=True).astype(jnp.int32)
    rank = jnp.sum(((own_col == own) & (ii < jj)).astype(F32), axis=0, keepdims=True).astype(jnp.int32)
    position = before + rank
    side = position & 1
    slot = rank >> 1
    apart = own ^ lax.axis_index("rows")
    pair = apart if relative else (own - (own & 1)) + (apart & 1)
    place = pair * half + slot
    dense = (position >> 1) + jnp.where(side == core, 0, dealt)
    source = jnp.sum(jnp.where(dense == ii, esc, 0).astype(F32), axis=1, keepdims=True).astype(jnp.int32)
    chosen = (source == iota((count, feat_ref.shape[0]), 1)).astype(F32).astype(BF)
    line = pair >> 1
    line = line * (n // 2 + 1) + (side ^ core) * (n // 2) ** 2 if relative else line + (side ^ core) * (n // 2)
    for i, row in enumerate((line, (apart & 1) * half + slot, esc, place, dense)):
        index_ref[i : i + 1, :] = row
    copies[2].wait()
    rows_ref[...] = dot(chosen, feat_ref[...]).astype(BF)
    for copy in copies[3:]:
        copy.wait()


def predict_kernel(
    rows_ref, w_ref, bias_ref, out_ref, upb_ref, head_ref, down_ref, raw_ref,
    near_ref, far_ref, segment_ref,
):
    depth = raw_ref.shape[0] - EXTRA
    here = w_ref.shape[0]
    core = lax.axis_index("member")
    dealt = near_ref.shape[0]
    lane = iota((8, 1), 0)
    preds = None
    for m in range(here):
        act = gelu2(dot(rows_ref[...], w_ref[m]) + bias_ref[m : m + 1]).astype(BF)
        on_lane = jnp.where(lane == core * here + m, 0.5 * out_ref[m : m + 1].astype(F32), 0.0).astype(BF)
        pred = dot_t(act, on_lane)
        preds = pred if preds is None else preds + pred
    preds = preds.astype(BF)
    near_ref[...] = preds[:dealt]
    far_ref[...] = preds[dealt:]
    head = split3(head_ref[...]).astype(F32)
    head = jnp.concatenate([head, jnp.zeros((LANES - 3, head.shape[1]), F32)], axis=0).astype(BF)
    down = jnp.sum(dot_t(down_ref[...], head).T[:8], axis=0, keepdims=True)
    extra = [split3(x).astype(F32) for x in (down, upb_ref[...], head_ref[...])]
    extra.append(jnp.zeros((EXTRA - 9, down.shape[1]), F32))
    segment_ref[depth:, :] = jnp.concatenate(extra, axis=0).astype(BF)


def constants_kernel(
    cls_ref, gain_ref, scale_ref, shift_ref, fbias_ref, fgain_ref, q0_ref, q1_ref, index_ref,
    table_ref, where_ref, place_ref,
):
    count = index_ref.shape[1]
    diag = iota((count, count), 0) == iota((count, count), 1)
    cols = [
        jnp.sum(jnp.where(diag, index_ref[i : i + 1, :], 0).astype(F32), axis=1, keepdims=True) for i in range(5)]
    for i in range(3):
        where_ref[:, i : i + 1] = cols[i].astype(jnp.int32)
    dealt = place_ref.shape[1]
    placed = cols[4].astype(jnp.int32) == iota((count, dealt), 1)
    place_ref[...] = jnp.sum(jnp.where(placed, cols[3], 0.0), axis=0, keepdims=True).astype(jnp.int32)
    gain = gain_ref[...]
    cls = cls_ref[...]
    centered = centre(cls)
    ncls = (centered * inverse_spread(centered) * gain).astype(BF)
    table_ref[...] = jnp.zeros_like(table_ref)
    members = scale_ref.shape[0]
    table_ref[SCALE : SCALE + members, :] = centre(scale_ref[...])
    table_ref[SHIFT : SHIFT + members, :] = centre(shift_ref[...])
    table_ref[GAIN : GAIN + 1, :] = gain
    table_ref[FBIAS : FBIAS + 1, :] = fbias_ref[...]
    table_ref[CLS : CLS + 1, :] = cls
    table_ref[FGAIN : FGAIN + 1, :] = fgain_ref[...]
    lhs = jnp.broadcast_to(ncls.astype(F32), (8, ncls.shape[1])).astype(BF)
    local = q0_ref.shape[2]
    heads = local // HD
    row = iota((8, local), 0)
    col = iota((8, local), 1) // HD
    kmap = None
    for i, ref in enumerate((q0_ref, q1_ref)):
        query = dot(lhs, ref[0]) * (1.0 / math.sqrt(HD))
        spread = jnp.where(row == col + i * heads, query, 0.0)
        part = join3(dot_t(split3(spread), ref[1]))
        kmap = part if kmap is None else kmap + part
        table_ref[VCLS : VCLS + 1, i * local : (i + 1) * local] = dot(lhs, ref[2])[0:1]
    table_ref[KMAP : KMAP + 8, :] = kmap
    logits = jnp.sum(kmap * ncls.astype(F32), axis=-1, keepdims=True)
    eye = iota((8, LANES), 0) == iota((8, LANES), 1)
    table_ref[LCLS : LCLS + 1, :LANES] = jnp.sum(jnp.where(eye, logits, 0.0), axis=0, keepdims=True)


def attend_kernel(
    members, rows_ref, near_ref, far_ref, place_ref, table_ref, fw0_ref, fw1_ref, q0_ref, q1_ref, *sent_refs
):
    core = lax.axis_index("member")
    total = near_ref.shape[0]
    fwidth = rows_ref.shape[1]
    rows = rows_ref[:total]
    local = q0_ref.shape[2]
    gain = table_ref[GAIN : GAIN + 1, :]
    low, high = rows[:, : fwidth // 2].astype(F32), rows[:, fwidth // 2 :].astype(F32)
    first = jnp.where(core == 0, low, high).astype(BF)
    second = jnp.where(core == 0, high, low).astype(BF)
    token = dot(first, fw0_ref[: fwidth // 2]) + dot(second, fw1_ref[: fwidth // 2]) + table_ref[FBIAS : FBIAS + 1, :]
    centered = centre(token)
    tokens = [(centered * inverse_spread(centered) * gain).astype(BF)]
    preds = near_ref[...].astype(F32) + far_ref[...].astype(F32)
    for m in range(members):
        centered = preds[:, m : m + 1] * table_ref[SCALE + m : SCALE + m + 1, :] + table_ref[SHIFT + m : SHIFT + m + 1, :]
        tokens.append((centered * inverse_spread(centered) * gain).astype(BF))
    normed = jnp.concatenate(tokens, axis=0)
    count = len(tokens)

    kmap = jnp.concatenate([table_ref[KMAP : KMAP + 8, :], jnp.zeros((LANES - 8, table_ref.shape[1]), F32)], axis=0)
    logits = dot_t(normed, jnp.concatenate(split2(kmap), axis=0))
    logits = logits[:, :LANES] + logits[:, LANES:]
    expo = jnp.exp(logits)
    expo_cls = jnp.exp(table_ref[LCLS : LCLS + 1, :LANES])
    norm = expo_cls
    for t in range(count):
        norm = norm + expo[t * total : (t + 1) * total]
    inverse = 1.0 / norm
    weights = jnp.concatenate(
        [expo[t * total : (t + 1) * total] * inverse for t in range(count)] + [expo_cls * inverse], axis=0)
    expand = (iota((2 * LANES, 2 * local), 0) & (LANES - 1)) == iota((2 * LANES, 2 * local), 1) // HD
    spread = dot(jnp.concatenate(split2(weights), axis=1), expand.astype(F32).astype(BF))
    parts = []
    for i, ref in enumerate((q0_ref, q1_ref)):
        at = slice(i * local, (i + 1) * local)
        value = dot(normed, ref[2])
        mixed = spread[count * total :, at] * table_ref[VCLS : VCLS + 1, at]
        for t in range(count):
            rng = slice(t * total, (t + 1) * total)
            mixed = mixed + spread[rng, at] * value[rng]
        parts.append(mixed)
    mixed = jnp.concatenate(parts, axis=1).astype(BF)
    size = sent_refs[0].shape[0]
    scatter = (place_ref[...] == iota((size * len(sent_refs), total), 0)).astype(F32).astype(BF)
    sent = dot(scatter, mixed).astype(BF)
    for k, sent_ref in enumerate(sent_refs):
        sent_ref[...] = sent[k * size : (k + 1) * size]


def ensemble_kernel(first, count, tile, feat_ref, w_ref, bias_ref, out_ref, after_ref, *refs):
    held = (len(refs) - 1) // 2
    copies = start_all(list(zip(refs[:held], refs[held + 1 :])), refs[-1]) if held else []
    pred_ref = refs[held]
    for t in range(count):
        rows = feat_ref[(first + t) * tile : (first + t + 1) * tile]
        total = None
        for m in range(w_ref.shape[0]):
            hidden = gelu2(dot(rows, w_ref[m]) + bias_ref[m : m + 1]).astype(BF)
            weights = jnp.broadcast_to(out_ref[m : m + 1].astype(F32), (8, out_ref.shape[1])).astype(BF)
            pred = dot_t(weights, hidden)[0:1]
            total = pred if total is None else total + pred
        per = tile // LANES
        for i in range(per):
            pred_ref[t * per + i : t * per + i + 1, :] = total[:, i * LANES : (i + 1) * LANES]
    for copy in copies:
        copy.wait()


def unpack(ref):
    depth = ref.shape[0] - EXTRA
    extra = ref[depth:, :].astype(F32)
    return ref[:depth, :], *(jnp.sum(extra[i : i + 3], axis=0, keepdims=True) for i in (DOWN, BIAS, HEAD))


def hidden_terms(normed, up, down, bias):
    return jnp.maximum(dot(normed, up) + bias, 0.0).astype(BF).astype(F32) * down


def states(mixed, table_ref, both0_ref, both1_ref):
    local = mixed.shape[1] // 2
    ow0, ow1 = (ref[ref.shape[0] - local :] for ref in (both0_ref, both1_ref))
    state = table_ref[CLS : CLS + 1, :] + dot(mixed[:, :local], ow0) + dot(mixed[:, local:], ow1)
    centered = centre(state)
    return state, (centered * inverse_spread(centered) * table_ref[FGAIN : FGAIN + 1, :]).astype(BF)


def arrived(got_refs, half, e):
    if len(got_refs) == 1:
        rows = got_refs[0].shape[0] // 2
        return got_refs[0][e * rows : (e + 1) * rows]
    return jnp.concatenate([ref[e * half : (e + 1) * half] for ref in got_refs], axis=0)


def arrive_kernel(blocks, half, *refs):
    table_ref, both0_ref, both1_ref, state_ref, normed_ref = refs[blocks:]
    state_ref[...], normed_ref[...] = states(arrived(refs[:blocks][::-1], half, 1), table_ref, both0_ref, both1_ref)


def near_score_kernel(blocks, half, *refs):
    table_ref, both0_ref, both1_ref, up0_ref, up1_ref, score_ref = refs[blocks:]
    state, normed = states(arrived(refs[:blocks][::-1], half, 0), table_ref, both0_ref, both1_ref)
    up, down, bias, head = unpack(up0_ref)
    terms = state * head + hidden_terms(normed, up, down, bias)
    up, down, bias, _ = unpack(up1_ref)
    terms = terms + hidden_terms(normed, up, down, bias)
    score_ref[...] = jnp.sum(terms, axis=-1, keepdims=True)


def far_score_kernel(blocks, half, near_ref, state_ref, mine_ref, other_ref, up2_ref, out_ref):
    rows = near_ref.shape[0]
    up, down, bias, head = unpack(up2_ref)
    terms = hidden_terms(jnp.concatenate([mine_ref[...], other_ref[...]], axis=0), up, down, bias)
    scores = [
        near_ref[...],
        jnp.sum(terms[:rows] + state_ref[...] * head, axis=-1, keepdims=True),
        jnp.sum(terms[rows:], axis=-1, keepdims=True),
    ]
    if blocks == 1:
        eye = iota((rows, rows), 0) == iota((rows, rows), 1)
        for e, score in enumerate(scores):
            out_ref[:, e * rows : (e + 1) * rows] = jnp.sum(jnp.where(eye, score, 0.0), axis=0, keepdims=True)
    else:
        row, lane = iota((half, LANES), 0), iota((half, LANES), 1)
        for k in range(blocks):
            line = jnp.zeros((half, LANES), F32)
            for e, score in enumerate(scores):
                line = jnp.where(lane == row + e * half, score[k * half : (k + 1) * half], line)
            out_ref[k : k + 1, :] = jnp.sum(line, axis=0, keepdims=True)


def expand_kernel(lines, where_ref, after_ref, line_ref, lane_ref):
    rows = lane_ref.shape[1]
    hit = where_ref[:, 2:3] == iota((where_ref.shape[0], rows), 1)

    def by_row(i):
        return jnp.sum(jnp.where(hit, where_ref[:, i : i + 1] + 1, 0).astype(F32), axis=0, keepdims=True).astype(jnp.int32)

    line = (by_row(0) - 1 == iota((lines, rows), 0)).astype(F32)
    line_ref[...] = jnp.concatenate([line] * 3, axis=0).astype(BF)
    lane_ref[...] = by_row(1) - 1


def finish_kernel(members, half, lines, line_ref, lane_ref, near_ref, far_ref, out_ref):
    near, far = near_ref[...], far_ref[...]
    ensemble = (near[lines:] + far[lines:]) * (0.5 / members)
    ensemble = jnp.concatenate([ensemble[i : i + 1] for i in range(ensemble.shape[0])], axis=1)
    lanes = iota((lines, LANES), 1)
    last = (lanes >= half) & (lanes < 2 * half)

    def whole(mine, others):
        return mine[:lines] + jnp.where(last, pltpu.roll(others[:lines], LANES - half, 1), 0.0)

    table = split3(jnp.concatenate([whole(near, far), whole(far, near)], axis=0))
    by_lane = lax.dot_general(table, line_ref[...], (((0,), (0,)), ((), ())), preferred_element_type=F32)
    lane = lane_ref[...]
    replaced = jnp.sum(jnp.where(lane == iota(by_lane.shape, 0), by_lane, 0.0), axis=0, keepdims=True)
    out_ref[...] = jnp.where(lane >= 0, replaced, ensemble)


def cost(flops, size, trans=0):
    return pl.CostEstimate(flops=flops, bytes_accessed=size, transcendentals=trans)


def params(mib):
    return pltpu.CompilerParams(vmem_limit_bytes=mib * 2**20)


def in_hbm(arrays):
    return [pltpu.with_memory_space_constraint(x, pltpu.HBM) for x in arrays]


def shape(dims, dtype):
    return jax.ShapeDtypeStruct(dims, dtype)


def per_device(
    features, escalated, owner_ids, member_in, member_bias, member_out, feat_weight, feat_bias,
    pred_scale, pred_shift, cls_token, attn_gain, qkv_weight, out_weight, ffn_gain, up_weight,
    up_bias, down_weight, owner_heads,
):
    n = lax.axis_size("rows")
    rows, fwidth = features.shape
    count = escalated.shape[1]
    half = max(1, count // n)
    slots = n * half
    here, _, hidden = member_in.shape
    members = pred_scale.shape[0]
    width = cls_token.shape[0]

    def swap(x):
        return lax.ppermute(x, "member", [(0, 1), (1, 0)])

    row = lambda x: x.reshape(1, -1)
    cls_token, attn_gain, ffn_gain, feat_bias = map(row, (cls_token, attn_gain, ffn_gain, feat_bias))
    owners = owner_ids.reshape(1, count)

    pairs = n // 2
    relative = pairs <= 8
    blocks = pairs if relative else 1
    other_qkv = swap(qkv_weight)

    dealt = count // 2
    ins = (escalated, owners, features, down_weight, up_weight, feat_weight, out_weight)
    index, mine, down, segment, own_both = pl.pallas_call(
        functools.partial(route_kernel, n, half, relative),
        out_shape=[shape((8, count), jnp.int32), shape((count, fwidth), BF), shape(down_weight.shape[1:], BF),
                   shape((up_weight.shape[1] + EXTRA, up_weight.shape[2]), BF),
                   shape((feat_weight.shape[0] + out_weight.shape[0], width), BF)],
        in_specs=[HBM] * len(ins),
        out_specs=[VMEM] * 5,
        scratch_shapes=[pltpu.VMEM(x.shape, x.dtype) for x in ins[:3]] + [pltpu.SemaphoreType.DMA((7,))],
        compiler_params=params(24),
        cost_estimate=cost(2 * count * rows * fwidth, 3 * 10**6),
        name="route",
    )(*in_hbm(ins))
    near, far, segment = pl.pallas_call(
        predict_kernel,
        out_shape=[shape((dealt, 8), BF), shape((dealt, 8), BF), shape(segment.shape, BF)],
        in_specs=[VMEM] * 8,
        out_specs=[VMEM] * 3,
        input_output_aliases={7: 2},
        compiler_params=params(24),
        cost_estimate=cost(2 * here * count * fwidth * hidden, 3 * 10**6, here * count * hidden),
        name="predict",
    )(mine, member_in, member_bias, member_out, up_bias, owner_heads, down, segment)
    far = swap(far)
    other_both = swap(own_both)
    next_segment = lax.ppermute(segment, "rows", [(i, i ^ 1) for i in range(n)])
    other_segment = swap(segment)

    ins = (cls_token, attn_gain, pred_scale, pred_shift, feat_bias, ffn_gain, qkv_weight, other_qkv, index)
    table, where, place = pl.pallas_call(
        constants_kernel,
        out_shape=[shape((TABLE, width), F32), shape((count, 3), jnp.int32), shape((1, dealt), jnp.int32)],
        in_specs=[VMEM] * len(ins),
        out_specs=[VMEM] * 3,
        compiler_params=params(16),
        cost_estimate=cost(10**8, 2 * 10**6),
        name="constants",
    )(*ins)

    local = qkv_weight.shape[2]
    sent = pl.pallas_call(
        functools.partial(attend_kernel, members),
        out_shape=[shape((slots // blocks, 2 * local), BF)] * blocks,
        in_specs=[VMEM] * 9,
        out_specs=[VMEM] * blocks,
        compiler_params=params(24),
        cost_estimate=cost(10**9, 2 * 10**6),
        name="attend",
    )(mine, near, far, place, table, own_both, other_both, qkv_weight, other_qkv)

    def across(x, k):
        return lax.ppermute(x, "rows", [(i, i ^ (2 * k)) for i in range(n)])

    def exchange(x):
        groups = [[2 * q + b for q in range(pairs)] for b in range(2)]
        return lax.all_to_all(x, "rows", split_axis=0, concat_axis=0, axis_index_groups=groups, tiled=True)

    if relative:
        got = [sent[0]] + [across(sent[k], k) for k in range(1, pairs)]
    else:
        got = exchange(sent[0].reshape(pairs, 2, half, 2 * local))
        got = [got.transpose(1, 0, 2, 3).reshape(slots, 2 * local)]

    tile = min(rows, 256)
    tiles = rows // tile

    def ensemble(first, number, after, held=()):
        return pl.pallas_call(
            functools.partial(ensemble_kernel, first, number, tile),
            out_shape=[shape((number * tile // LANES, LANES), F32)] + [shape(x.shape, x.dtype) for x in held],
            in_specs=[VMEM] * 4 + [ANY] * (1 + len(held)),
            out_specs=[VMEM] * (1 + len(held)),
            scratch_shapes=[pltpu.SemaphoreType.DMA((len(held),))] if held else [],
            compiler_params=params(24),
            cost_estimate=cost(2 * here * number * tile * fwidth * hidden, 10**6, here * number * tile * hidden),
            name="ensemble",
        )(features, member_in, member_bias, member_out, after, *held)

    early = (tiles + 1) // 2
    preds, table, both0, both1, up0, up1 = ensemble(
        0, early, sent[0], (table, own_both, other_both, segment, other_segment))
    preds = [preds]

    state, next_rows = pl.pallas_call(
        functools.partial(arrive_kernel, blocks, half),
        out_shape=[shape((slots // 2, width), F32), shape((slots // 2, width), BF)],
        in_specs=[VMEM] * (blocks + 3),
        out_specs=[VMEM] * 2,
        compiler_params=params(24),
        cost_estimate=cost(2 * 10**8, 2 * 10**6),
        name="arrive",
    )(*got[::-1], table, both0, both1)
    other_rows = swap(next_rows)
    near_scores = pl.pallas_call(
        functools.partial(near_score_kernel, blocks, half),
        out_shape=shape((slots // 2, 1), F32),
        in_specs=[VMEM] * (blocks + 5),
        out_specs=VMEM,
        compiler_params=params(24),
        cost_estimate=cost(5 * 10**8, 2 * 10**6),
        name="near_score",
    )(*got[::-1], table, both0, both1, up0, up1)
    scores = pl.pallas_call(
        functools.partial(far_score_kernel, blocks, half),
        out_shape=shape((blocks, LANES if relative else 3 * slots // 2), F32),
        in_specs=[VMEM] * 5,
        out_specs=VMEM,
        compiler_params=params(24),
        cost_estimate=cost(2 * 10**8, 10**6),
        name="far_score",
    )(near_scores, state, next_rows, other_rows, next_segment)
    for first in range(early, tiles):
        preds += ensemble(first, 1, scores)
    back = scores
    if relative:
        step = 1
        while step < pairs:
            back = jnp.concatenate([back, across(back, step)], axis=0)
            step *= 2
    else:
        back = exchange(back.reshape(3, pairs, half).transpose(1, 0, 2)).reshape(pairs, 3 * half)
        back = jnp.pad(back, ((0, 0), (0, LANES - 3 * half)))
    lines = back.shape[0]
    near_lines = jnp.concatenate([back, *preds], axis=0)
    line_of, lane_of = pl.pallas_call(
        functools.partial(expand_kernel, 2 * lines),
        out_shape=[shape((6 * lines, rows), BF), shape((1, rows), jnp.int32)],
        in_specs=[VMEM, ANY],
        out_specs=[VMEM] * 2,
        compiler_params=params(16),
        cost_estimate=cost(10**8, 10**6),
        name="expand",
    )(where, preds[-1])

    final = pl.pallas_call(
        functools.partial(finish_kernel, members, half, lines),
        out_shape=shape((1, rows), F32),
        in_specs=[VMEM] * 4,
        out_specs=VMEM,
        compiler_params=params(8),
        cost_estimate=cost(10**6, 10**6),
        name="finish",
    )(line_of, lane_of, near_lines, swap(near_lines))
    return final.reshape(rows)


def solution(mesh):
    placed = (
        P(("groups", "rows"), None),
        P(("groups", "rows"), None),
        P(("groups", "rows"), None, None),
        P("member", None, None),
        P("member", None),
        P("member", None),
        P("member", None),
        P(),
        P(),
        P(),
        P(),
        P(),
        P(None, None, "member"),
        P("member", None),
        P(),
        P("rows", None, "member"),
        P("rows", "member"),
        P("rows", "member", None),
        P("rows", None),
    )
    return jax.shard_map(
        per_device, mesh=mesh, in_specs=placed, out_specs=P(("groups", "rows")), check_vma=False
    )
```

```python
import functools
import math

import jax
import jax.numpy as jnp
from jax import lax
from jax.experimental import pallas as pl
from jax.experimental.pallas import tpu as pltpu
from jax.sharding import PartitionSpec as P

HD = 64
EPS = 1e-05
LANES = 128
BF = jnp.bfloat16
F32 = jnp.float32
VMEM = pl.BlockSpec(memory_space=pltpu.VMEM)
HBM = pl.BlockSpec(memory_space=pltpu.HBM)
ANY = pl.BlockSpec(memory_space=pl.ANY)
GELU_C = math.sqrt(2.0 / math.pi)

KMAP, VCLS, LCLS, SCALE, SHIFT, GAIN, FBIAS, CLS, FGAIN = 0, 8, 9, 16, 24, 32, 33, 34, 35
TABLE = 40
DOWN, BIAS, HEAD, PREDS, EXTRA = 0, 3, 6, 9, 16


def iota(shape, dim):
    return lax.broadcasted_iota(jnp.int32, shape, dim)


def gelu2(x):
    return x + x * jnp.tanh(x * (GELU_C + (GELU_C * 0.044715) * (x * x)))


def dot(a, b):
    return lax.dot_general(a, b, (((1,), (0,)), ((), ())), preferred_element_type=F32)


def dot_t(a, b):
    return lax.dot_general(a, b, (((1,), (1,)), ((), ())), preferred_element_type=F32)


def split2(x):
    high = x.astype(BF)
    return high, (x - high.astype(F32)).astype(BF)


def split3(x):
    high, rest = x.astype(BF), x
    rest = rest - high.astype(F32)
    mid = rest.astype(BF)
    low = (rest - mid.astype(F32)).astype(BF)
    return jnp.concatenate([high.astype(F32), mid.astype(F32), low.astype(F32)], axis=0).astype(BF)


def join3(x):
    rows = x.shape[0] // 3
    return x[:rows] + x[rows : 2 * rows] + x[2 * rows :]


def centre(x):
    return x - jnp.mean(x, axis=-1, keepdims=True)


def inverse_spread(centered):
    return lax.rsqrt(jnp.mean(centered * centered, axis=-1, keepdims=True) + EPS)


def start_all(pairs, sems):
    copies = [pltpu.make_async_copy(src, dst, sems.at[i]) for i, (src, dst) in enumerate(pairs)]
    for copy in copies:
        copy.start()
    return copies


def route_kernel(
    n, half, relative, esc_hbm, own_hbm, feat_hbm, down_hbm, up_hbm, fw_hbm, ow_hbm,
    index_ref, rows_ref, down_ref, segment_ref, both_ref, esc_ref, own_ref, feat_ref, sems,
):
    copies = start_all(
        [(esc_hbm, esc_ref), (own_hbm, own_ref), (feat_hbm, feat_ref), (down_hbm.at[0], down_ref),
         (fw_hbm, both_ref.at[: fw_hbm.shape[0]]), (ow_hbm, both_ref.at[fw_hbm.shape[0] :]),
         (up_hbm.at[0], segment_ref.at[: up_hbm.shape[1]])], sems)
    segment_ref[up_hbm.shape[1] :, :] = jnp.zeros((EXTRA, up_hbm.shape[2]), BF)
    core = lax.axis_index("member")
    count = esc_hbm.shape[1]
    dealt = count // 2
    copies[0].wait()
    copies[1].wait()
    esc = esc_ref[...]
    own = own_ref[...]
    ii = iota((count, count), 0)
    jj = iota((count, count), 1)
    own_col = jnp.sum(jnp.where(ii == jj, own, 0).astype(F32), axis=1, keepdims=True).astype(jnp.int32)
    before = jnp.sum((own_col < own).astype(F32), axis=0, keepdims=True).astype(jnp.int32)
    rank = jnp.sum(((own_col == own) & (ii < jj)).astype(F32), axis=0, keepdims=True).astype(jnp.int32)
    position = before + rank
    side = position & 1
    slot = rank >> 1
    apart = own ^ lax.axis_index("rows")
    pair = apart if relative else (own - (own & 1)) + (apart & 1)
    place = pair * half + slot
    dense = (position >> 1) + jnp.where(side == core, 0, dealt)
    source = jnp.sum(jnp.where(dense == ii, esc, 0).astype(F32), axis=1, keepdims=True).astype(jnp.int32)
    chosen = (source == iota((count, feat_ref.shape[0]), 1)).astype(F32).astype(BF)
    line = pair >> 1
    line = line * (n // 2 + 1) + (side ^ core) * (n // 2) ** 2 if relative else line + (side ^ core) * (n // 2)
    for i, row in enumerate((line, (apart & 1) * half + slot, esc, place, dense)):
        index_ref[i : i + 1, :] = row
    copies[2].wait()
    rows_ref[...] = dot(chosen, feat_ref[...]).astype(BF)
    for copy in copies[3:]:
        copy.wait()


def predict_kernel(
    rows_ref, w_ref, bias_ref, out_ref, upb_ref, head_ref, down_ref, raw_ref,
    near_ref, segment_ref,
):
    depth = raw_ref.shape[0] - EXTRA
    here = w_ref.shape[0]
    core = lax.axis_index("member")
    dealt = near_ref.shape[1]
    row = iota((8, 1), 0)
    preds = None
    for m in range(here):
        act = gelu2(dot(rows_ref[...], w_ref[m]) + bias_ref[m : m + 1]).astype(BF)
        on_row = jnp.where(row == core * here + m, 0.5 * out_ref[m : m + 1].astype(F32), 0.0).astype(BF)
        pred = dot_t(on_row, act)
        preds = pred if preds is None else preds + pred
    preds = preds.astype(BF).astype(F32)
    near_ref[...] = preds[:, :dealt]
    head = split3(head_ref[...]).astype(F32)
    head = jnp.concatenate([head, jnp.zeros((LANES - 3, head.shape[1]), F32)], axis=0).astype(BF)
    down = jnp.sum(dot_t(down_ref[...], head).T[:8], axis=0, keepdims=True)
    extra = [split3(x).astype(F32) for x in (down, upb_ref[...], head_ref[...])]
    members = EXTRA - PREDS
    far = jnp.concatenate([preds[:members, dealt:], jnp.zeros((members, down.shape[1] - dealt), F32)], axis=1)
    extra.append(far)
    segment_ref[depth:, :] = jnp.concatenate(extra, axis=0).astype(BF)


def constants_kernel(
    cls_ref, gain_ref, scale_ref, shift_ref, fbias_ref, fgain_ref, q0_ref, q1_ref, index_ref,
    table_ref, where_ref, place_ref,
):
    count = index_ref.shape[1]
    diag = iota((count, count), 0) == iota((count, count), 1)
    cols = [
        jnp.sum(jnp.where(diag, index_ref[i : i + 1, :], 0).astype(F32), axis=1, keepdims=True) for i in range(5)]
    for i in range(3):
        where_ref[:, i : i + 1] = cols[i].astype(jnp.int32)
    dealt = place_ref.shape[1]
    placed = cols[4].astype(jnp.int32) == iota((count, dealt), 1)
    place_ref[...] = jnp.sum(jnp.where(placed, cols[3], 0.0), axis=0, keepdims=True).astype(jnp.int32)
    gain = gain_ref[...]
    cls = cls_ref[...]
    centered = centre(cls)
    ncls = (centered * inverse_spread(centered) * gain).astype(BF)
    table_ref[...] = jnp.zeros_like(table_ref)
    members = scale_ref.shape[0]
    table_ref[SCALE : SCALE + members, :] = centre(scale_ref[...])
    table_ref[SHIFT : SHIFT + members, :] = centre(shift_ref[...])
    table_ref[GAIN : GAIN + 1, :] = gain
    table_ref[FBIAS : FBIAS + 1, :] = fbias_ref[...]
    table_ref[CLS : CLS + 1, :] = cls
    table_ref[FGAIN : FGAIN + 1, :] = fgain_ref[...]
    lhs = jnp.broadcast_to(ncls.astype(F32), (8, ncls.shape[1])).astype(BF)
    local = q0_ref.shape[2]
    heads = local // HD
    row = iota((8, local), 0)
    col = iota((8, local), 1) // HD
    kmap = None
    for i, ref in enumerate((q0_ref, q1_ref)):
        query = dot(lhs, ref[0]) * (1.0 / math.sqrt(HD))
        spread = jnp.where(row == col + i * heads, query, 0.0)
        part = join3(dot_t(split3(spread), ref[1]))
        kmap = part if kmap is None else kmap + part
        table_ref[VCLS : VCLS + 1, i * local : (i + 1) * local] = dot(lhs, ref[2])[0:1]
    table_ref[KMAP : KMAP + 8, :] = kmap
    logits = jnp.sum(kmap * ncls.astype(F32), axis=-1, keepdims=True)
    eye = iota((8, LANES), 0) == iota((8, LANES), 1)
    table_ref[LCLS : LCLS + 1, :LANES] = jnp.sum(jnp.where(eye, logits, 0.0), axis=0, keepdims=True)


def attend_kernel(
    members, rows_ref, near_ref, other_ref, place_ref, table_ref, fw0_ref, fw1_ref, q0_ref, q1_ref, *sent_refs
):
    core = lax.axis_index("member")
    total = near_ref.shape[1]
    fwidth = rows_ref.shape[1]
    rows = rows_ref[:total]
    local = q0_ref.shape[2]
    gain = table_ref[GAIN : GAIN + 1, :]
    low, high = rows[:, : fwidth // 2].astype(F32), rows[:, fwidth // 2 :].astype(F32)
    first = jnp.where(core == 0, low, high).astype(BF)
    second = jnp.where(core == 0, high, low).astype(BF)
    token = dot(first, fw0_ref[: fwidth // 2]) + dot(second, fw1_ref[: fwidth // 2]) + table_ref[FBIAS : FBIAS + 1, :]
    centered = centre(token)
    tokens = [(centered * inverse_spread(centered) * gain).astype(BF)]
    first = other_ref.shape[0] - EXTRA + PREDS
    far = other_ref[first : first + EXTRA - PREDS, :total].astype(F32)
    preds = (near_ref[...] + jnp.concatenate([far, jnp.zeros((8 - far.shape[0], total), F32)], axis=0)).T
    for m in range(members):
        centered = preds[:, m : m + 1] * table_ref[SCALE + m : SCALE + m + 1, :] + table_ref[SHIFT + m : SHIFT + m + 1, :]
        tokens.append((centered * inverse_spread(centered) * gain).astype(BF))
    normed = jnp.concatenate(tokens, axis=0)
    count = len(tokens)

    kmap = jnp.concatenate([table_ref[KMAP : KMAP + 8, :], jnp.zeros((LANES - 8, table_ref.shape[1]), F32)], axis=0)
    logits = dot_t(normed, jnp.concatenate(split2(kmap), axis=0))
    logits = logits[:, :LANES] + logits[:, LANES:]
    expo = jnp.exp(logits)
    expo_cls = jnp.exp(table_ref[LCLS : LCLS + 1, :LANES])
    norm = expo_cls
    for t in range(count):
        norm = norm + expo[t * total : (t + 1) * total]
    inverse = 1.0 / norm
    weights = jnp.concatenate(
        [expo[t * total : (t + 1) * total] * inverse for t in range(count)] + [expo_cls * inverse], axis=0)
    expand = (iota((2 * LANES, 2 * local), 0) & (LANES - 1)) == iota((2 * LANES, 2 * local), 1) // HD
    spread = dot(jnp.concatenate(split2(weights), axis=1), expand.astype(F32).astype(BF))
    parts = []
    for i, ref in enumerate((q0_ref, q1_ref)):
        at = slice(i * local, (i + 1) * local)
        value = dot(normed, ref[2])
        mixed = spread[count * total :, at] * table_ref[VCLS : VCLS + 1, at]
        for t in range(count):
            rng = slice(t * total, (t + 1) * total)
            mixed = mixed + spread[rng, at] * value[rng]
        parts.append(mixed)
    mixed = jnp.concatenate(parts, axis=1).astype(BF)
    size = sent_refs[0].shape[0]
    scatter = (place_ref[...] == iota((size * len(sent_refs), total), 0)).astype(F32).astype(BF)
    sent = dot(scatter, mixed).astype(BF)
    for k, sent_ref in enumerate(sent_refs):
        sent_ref[...] = sent[k * size : (k + 1) * size]


def ensemble_kernel(first, count, tile, feat_ref, w_ref, bias_ref, out_ref, after_ref, *refs):
    held = (len(refs) - 1) // 2
    copies = start_all(list(zip(refs[:held], refs[held + 1 :])), refs[-1]) if held else []
    pred_ref = refs[held]
    for t in range(count):
        rows = feat_ref[(first + t) * tile : (first + t + 1) * tile]
        total = None
        for m in range(w_ref.shape[0]):
            hidden = gelu2(dot(rows, w_ref[m]) + bias_ref[m : m + 1]).astype(BF)
            weights = jnp.broadcast_to(out_ref[m : m + 1].astype(F32), (8, out_ref.shape[1])).astype(BF)
            pred = dot_t(weights, hidden)[0:1]
            total = pred if total is None else total + pred
        per = tile // LANES
        for i in range(per):
            pred_ref[t * per + i : t * per + i + 1, :] = total[:, i * LANES : (i + 1) * LANES]
    for copy in copies:
        copy.wait()


def unpack(ref):
    depth = ref.shape[0] - EXTRA
    extra = ref[depth:, :].astype(F32)
    return ref[:depth, :], *(jnp.sum(extra[i : i + 3], axis=0, keepdims=True) for i in (DOWN, BIAS, HEAD))


def hidden_terms(normed, up, down, bias):
    return jnp.maximum(dot(normed, up) + bias, 0.0).astype(BF).astype(F32) * down


def states(mixed, table_ref, both0_ref, both1_ref):
    local = mixed.shape[1] // 2
    ow0, ow1 = (ref[ref.shape[0] - local :] for ref in (both0_ref, both1_ref))
    state = table_ref[CLS : CLS + 1, :] + dot(mixed[:, :local], ow0) + dot(mixed[:, local:], ow1)
    centered = centre(state)
    return state, (centered * inverse_spread(centered) * table_ref[FGAIN : FGAIN + 1, :]).astype(BF)


def arrived(got_refs, half, e):
    if len(got_refs) == 1:
        rows = got_refs[0].shape[0] // 2
        return got_refs[0][e * rows : (e + 1) * rows]
    return jnp.concatenate([ref[e * half : (e + 1) * half] for ref in got_refs], axis=0)


def arrive_kernel(blocks, half, *refs):
    table_ref, both0_ref, both1_ref, state_ref, normed_ref = refs[blocks:]
    state_ref[...], normed_ref[...] = states(arrived(refs[:blocks][::-1], half, 1), table_ref, both0_ref, both1_ref)


def near_score_kernel(blocks, half, *refs):
    table_ref, both0_ref, both1_ref, up0_ref, up1_ref, score_ref = refs[blocks:]
    state, normed = states(arrived(refs[:blocks][::-1], half, 0), table_ref, both0_ref, both1_ref)
    up, down, bias, head = unpack(up0_ref)
    terms = state * head + hidden_terms(normed, up, down, bias)
    up, down, bias, _ = unpack(up1_ref)
    terms = terms + hidden_terms(normed, up, down, bias)
    score_ref[...] = jnp.sum(terms, axis=-1, keepdims=True)


def far_score_kernel(blocks, half, near_ref, state_ref, mine_ref, other_ref, up2_ref, out_ref):
    rows = near_ref.shape[0]
    up, down, bias, head = unpack(up2_ref)
    terms = hidden_terms(jnp.concatenate([mine_ref[...], other_ref[...]], axis=0), up, down, bias)
    scores = [
        near_ref[...],
        jnp.sum(terms[:rows] + state_ref[...] * head, axis=-1, keepdims=True),
        jnp.sum(terms[rows:], axis=-1, keepdims=True),
    ]
    if blocks == 1:
        eye = iota((rows, rows), 0) == iota((rows, rows), 1)
        for e, score in enumerate(scores):
            out_ref[:, e * rows : (e + 1) * rows] = jnp.sum(jnp.where(eye, score, 0.0), axis=0, keepdims=True)
    else:
        row, lane = iota((half, LANES), 0), iota((half, LANES), 1)
        for k in range(blocks):
            line = jnp.zeros((half, LANES), F32)
            for e, score in enumerate(scores):
                line = jnp.where(lane == row + e * half, score[k * half : (k + 1) * half], line)
            out_ref[k : k + 1, :] = jnp.sum(line, axis=0, keepdims=True)


def expand_kernel(lines, where_ref, after_ref, line_ref, lane_ref):
    rows = lane_ref.shape[1]
    hit = where_ref[:, 2:3] == iota((where_ref.shape[0], rows), 1)

    def by_row(i):
        return jnp.sum(jnp.where(hit, where_ref[:, i : i + 1] + 1, 0).astype(F32), axis=0, keepdims=True).astype(jnp.int32)

    line = (by_row(0) - 1 == iota((lines, rows), 0)).astype(F32)
    line_ref[...] = jnp.concatenate([line] * 3, axis=0).astype(BF)
    lane_ref[...] = by_row(1) - 1


def finish_kernel(members, half, lines, line_ref, lane_ref, near_ref, far_ref, out_ref):
    near, far = near_ref[...], far_ref[...]
    ensemble = (near[lines:] + far[lines:]) * (0.5 / members)
    ensemble = jnp.concatenate([ensemble[i : i + 1] for i in range(ensemble.shape[0])], axis=1)
    lanes = iota((lines, LANES), 1)
    last = (lanes >= half) & (lanes < 2 * half)

    def whole(mine, others):
        return mine[:lines] + jnp.where(last, pltpu.roll(others[:lines], LANES - half, 1), 0.0)

    table = split3(jnp.concatenate([whole(near, far), whole(far, near)], axis=0))
    by_lane = lax.dot_general(table, line_ref[...], (((0,), (0,)), ((), ())), preferred_element_type=F32)
    lane = lane_ref[...]
    replaced = jnp.sum(jnp.where(lane == iota(by_lane.shape, 0), by_lane, 0.0), axis=0, keepdims=True)
    out_ref[...] = jnp.where(lane >= 0, replaced, ensemble)


def cost(flops, size, trans=0):
    return pl.CostEstimate(flops=flops, bytes_accessed=size, transcendentals=trans)


def params(mib):
    return pltpu.CompilerParams(vmem_limit_bytes=mib * 2**20)


def in_hbm(arrays):
    return [pltpu.with_memory_space_constraint(x, pltpu.HBM) for x in arrays]


def shape(dims, dtype):
    return jax.ShapeDtypeStruct(dims, dtype)


def per_device(
    features, escalated, owner_ids, member_in, member_bias, member_out, feat_weight, feat_bias,
    pred_scale, pred_shift, cls_token, attn_gain, qkv_weight, out_weight, ffn_gain, up_weight,
    up_bias, down_weight, owner_heads,
):
    n = lax.axis_size("rows")
    rows, fwidth = features.shape
    count = escalated.shape[1]
    half = max(1, count // n)
    slots = n * half
    here, _, hidden = member_in.shape
    members = pred_scale.shape[0]
    width = cls_token.shape[0]

    def swap(x):
        return lax.ppermute(x, "member", [(0, 1), (1, 0)])

    row = lambda x: x.reshape(1, -1)
    cls_token, attn_gain, ffn_gain, feat_bias = map(row, (cls_token, attn_gain, ffn_gain, feat_bias))
    owners = owner_ids.reshape(1, count)

    pairs = n // 2
    relative = pairs <= 8
    blocks = pairs if relative else 1
    other_qkv = swap(qkv_weight)

    dealt = count // 2
    ins = (escalated, owners, features, down_weight, up_weight, feat_weight, out_weight)
    index, mine, down, segment, own_both = pl.pallas_call(
        functools.partial(route_kernel, n, half, relative),
        out_shape=[shape((8, count), jnp.int32), shape((count, fwidth), BF), shape(down_weight.shape[1:], BF),
                   shape((up_weight.shape[1] + EXTRA, up_weight.shape[2]), BF),
                   shape((feat_weight.shape[0] + out_weight.shape[0], width), BF)],
        in_specs=[HBM] * len(ins),
        out_specs=[VMEM] * 5,
        scratch_shapes=[pltpu.VMEM(x.shape, x.dtype) for x in ins[:3]] + [pltpu.SemaphoreType.DMA((7,))],
        compiler_params=params(24),
        cost_estimate=cost(2 * count * rows * fwidth, 3 * 10**6),
        name="route",
    )(*in_hbm(ins))
    near, segment = pl.pallas_call(
        predict_kernel,
        out_shape=[shape((8, dealt), F32), shape(segment.shape, BF)],
        in_specs=[VMEM] * 8,
        out_specs=[VMEM] * 2,
        input_output_aliases={7: 1},
        compiler_params=params(24),
        cost_estimate=cost(2 * here * count * fwidth * hidden, 3 * 10**6, here * count * hidden),
        name="predict",
    )(mine, member_in, member_bias, member_out, up_bias, owner_heads, down, segment)
    other_both = swap(own_both)
    next_segment = lax.ppermute(segment, "rows", [(i, i ^ 1) for i in range(n)])
    other_segment = swap(segment)

    ins = (cls_token, attn_gain, pred_scale, pred_shift, feat_bias, ffn_gain, qkv_weight, other_qkv, index)
    table, where, place = pl.pallas_call(
        constants_kernel,
        out_shape=[shape((TABLE, width), F32), shape((count, 3), jnp.int32), shape((1, dealt), jnp.int32)],
        in_specs=[VMEM] * len(ins),
        out_specs=[VMEM] * 3,
        compiler_params=params(16),
        cost_estimate=cost(10**8, 2 * 10**6),
        name="constants",
    )(*ins)

    local = qkv_weight.shape[2]
    sent = pl.pallas_call(
        functools.partial(attend_kernel, members),
        out_shape=[shape((slots // blocks, 2 * local), BF)] * blocks,
        in_specs=[VMEM] * 9,
        out_specs=[VMEM] * blocks,
        compiler_params=params(24),
        cost_estimate=cost(10**9, 2 * 10**6),
        name="attend",
    )(mine, near, other_segment, place, table, own_both, other_both, qkv_weight, other_qkv)

    def across(x, k):
        return lax.ppermute(x, "rows", [(i, i ^ (2 * k)) for i in range(n)])

    def exchange(x):
        groups = [[2 * q + b for q in range(pairs)] for b in range(2)]
        return lax.all_to_all(x, "rows", split_axis=0, concat_axis=0, axis_index_groups=groups, tiled=True)

    if relative:
        got = [sent[0]] + [across(sent[k], k) for k in range(1, pairs)]
    else:
        got = exchange(sent[0].reshape(pairs, 2, half, 2 * local))
        got = [got.transpose(1, 0, 2, 3).reshape(slots, 2 * local)]

    tile = min(rows, 256)
    tiles = rows // tile

    def ensemble(first, number, after, held=()):
        return pl.pallas_call(
            functools.partial(ensemble_kernel, first, number, tile),
            out_shape=[shape((number * tile // LANES, LANES), F32)] + [shape(x.shape, x.dtype) for x in held],
            in_specs=[VMEM] * 4 + [ANY] * (1 + len(held)),
            out_specs=[VMEM] * (1 + len(held)),
            scratch_shapes=[pltpu.SemaphoreType.DMA((len(held),))] if held else [],
            compiler_params=params(24),
            cost_estimate=cost(2 * here * number * tile * fwidth * hidden, 10**6, here * number * tile * hidden),
            name="ensemble",
        )(features, member_in, member_bias, member_out, after, *held)

    early = (tiles + 1) // 2
    preds, table, both0, both1, up0, up1 = ensemble(
        0, early, sent[0], (table, own_both, other_both, segment, other_segment))
    preds = [preds]

    state, next_rows = pl.pallas_call(
        functools.partial(arrive_kernel, blocks, half),
        out_shape=[shape((slots // 2, width), F32), shape((slots // 2, width), BF)],
        in_specs=[VMEM] * (blocks + 3),
        out_specs=[VMEM] * 2,
        compiler_params=params(24),
        cost_estimate=cost(2 * 10**8, 2 * 10**6),
        name="arrive",
    )(*got[::-1], table, both0, both1)
    other_rows = swap(next_rows)
    near_scores = pl.pallas_call(
        functools.partial(near_score_kernel, blocks, half),
        out_shape=shape((slots // 2, 1), F32),
        in_specs=[VMEM] * (blocks + 5),
        out_specs=VMEM,
        compiler_params=params(24),
        cost_estimate=cost(5 * 10**8, 2 * 10**6),
        name="near_score",
    )(*got[::-1], table, both0, both1, up0, up1)
    scores = pl.pallas_call(
        functools.partial(far_score_kernel, blocks, half),
        out_shape=shape((blocks, LANES if relative else 3 * slots // 2), F32),
        in_specs=[VMEM] * 5,
        out_specs=VMEM,
        compiler_params=params(24),
        cost_estimate=cost(2 * 10**8, 10**6),
        name="far_score",
    )(near_scores, state, next_rows, other_rows, next_segment)
    for first in range(early, tiles):
        preds += ensemble(first, 1, scores)
    back = scores
    if relative:
        step = 1
        while step < pairs:
            back = jnp.concatenate([back, across(back, step)], axis=0)
            step *= 2
    else:
        back = exchange(back.reshape(3, pairs, half).transpose(1, 0, 2)).reshape(pairs, 3 * half)
        back = jnp.pad(back, ((0, 0), (0, LANES - 3 * half)))
    lines = back.shape[0]
    near_lines = jnp.concatenate([back, *preds], axis=0)
    line_of, lane_of = pl.pallas_call(
        functools.partial(expand_kernel, 2 * lines),
        out_shape=[shape((6 * lines, rows), BF), shape((1, rows), jnp.int32)],
        in_specs=[VMEM, ANY],
        out_specs=[VMEM] * 2,
        compiler_params=params(16),
        cost_estimate=cost(10**8, 10**6),
        name="expand",
    )(where, preds[-1])

    final = pl.pallas_call(
        functools.partial(finish_kernel, members, half, lines),
        out_shape=shape((1, rows), F32),
        in_specs=[VMEM] * 4,
        out_specs=VMEM,
        compiler_params=params(8),
        cost_estimate=cost(10**6, 10**6),
        name="finish",
    )(line_of, lane_of, near_lines, swap(near_lines))
    return final.reshape(rows)


def solution(mesh):
    placed = (
        P(("groups", "rows"), None),
        P(("groups", "rows"), None),
        P(("groups", "rows"), None, None),
        P("member", None, None),
        P("member", None),
        P("member", None),
        P("member", None),
        P(),
        P(),
        P(),
        P(),
        P(),
        P(None, None, "member"),
        P("member", None),
        P(),
        P("rows", None, "member"),
        P("rows", "member"),
        P("rows", "member", None),
        P("rows", None),
    )
    return jax.shard_map(
        per_device, mesh=mesh, in_specs=placed, out_specs=P(("groups", "rows")), check_vma=False
    )
```

```python
import functools
import math

import jax
import jax.numpy as jnp
from jax import lax
from jax.experimental import pallas as pl
from jax.experimental.pallas import tpu as pltpu
from jax.sharding import PartitionSpec as P

HD = 64
EPS = 1e-05
LANES = 128
BF = jnp.bfloat16
F32 = jnp.float32
VMEM = pl.BlockSpec(memory_space=pltpu.VMEM)
HBM = pl.BlockSpec(memory_space=pltpu.HBM)
ANY = pl.BlockSpec(memory_space=pl.ANY)
GELU_C = math.sqrt(2.0 / math.pi)

KMAP, VCLS, LCLS, SCALE, SHIFT, GAIN, FBIAS, CLS, FGAIN = 0, 8, 9, 16, 24, 32, 33, 34, 35
TABLE = 40
DOWN, BIAS, HEAD, PREDS, EXTRA = 0, 3, 6, 9, 16


def iota(shape, dim):
    return lax.broadcasted_iota(jnp.int32, shape, dim)


def gelu2(x):
    return x + x * jnp.tanh(x * (GELU_C + (GELU_C * 0.044715) * (x * x)))


def dot(a, b):
    return lax.dot_general(a, b, (((1,), (0,)), ((), ())), preferred_element_type=F32)


def dot_t(a, b):
    return lax.dot_general(a, b, (((1,), (1,)), ((), ())), preferred_element_type=F32)


def split2(x):
    high = x.astype(BF)
    return high, (x - high.astype(F32)).astype(BF)


def split3(x):
    high, rest = x.astype(BF), x
    rest = rest - high.astype(F32)
    mid = rest.astype(BF)
    low = (rest - mid.astype(F32)).astype(BF)
    return jnp.concatenate([high.astype(F32), mid.astype(F32), low.astype(F32)], axis=0).astype(BF)


def join3(x):
    rows = x.shape[0] // 3
    return x[:rows] + x[rows : 2 * rows] + x[2 * rows :]


def centre(x):
    return x - jnp.mean(x, axis=-1, keepdims=True)


def inverse_spread(centered):
    return lax.rsqrt(jnp.mean(centered * centered, axis=-1, keepdims=True) + EPS)


def start_all(pairs, sems):
    copies = [pltpu.make_async_copy(src, dst, sems.at[i]) for i, (src, dst) in enumerate(pairs)]
    for copy in copies:
        copy.start()
    return copies


def route_kernel(
    n, half, relative, esc_hbm, own_hbm, feat_hbm, down_hbm, up_hbm, fw_hbm, ow_hbm,
    index_ref, rows_ref, down_ref, segment_ref, both_ref, esc_ref, own_ref, feat_ref, sems,
):
    copies = start_all(
        [(esc_hbm, esc_ref), (own_hbm, own_ref), (feat_hbm, feat_ref), (down_hbm.at[0], down_ref),
         (fw_hbm, both_ref.at[: fw_hbm.shape[0]]), (ow_hbm, both_ref.at[fw_hbm.shape[0] :]),
         (up_hbm.at[0], segment_ref.at[: up_hbm.shape[1]])], sems)
    segment_ref[up_hbm.shape[1] :, :] = jnp.zeros((EXTRA, up_hbm.shape[2]), BF)
    core = lax.axis_index("member")
    count = esc_hbm.shape[1]
    dealt = count // 2
    copies[0].wait()
    copies[1].wait()
    esc = esc_ref[...]
    own = own_ref[...]
    ii = iota((count, count), 0)
    jj = iota((count, count), 1)
    own_col = jnp.sum(jnp.where(ii == jj, own, 0).astype(F32), axis=1, keepdims=True).astype(jnp.int32)
    before = jnp.sum((own_col < own).astype(F32), axis=0, keepdims=True).astype(jnp.int32)
    rank = jnp.sum(((own_col == own) & (ii < jj)).astype(F32), axis=0, keepdims=True).astype(jnp.int32)
    position = before + rank
    side = position & 1
    slot = rank >> 1
    apart = own ^ lax.axis_index("rows")
    pair = apart if relative else (own - (own & 1)) + (apart & 1)
    place = pair * half + slot
    dense = (position >> 1) + jnp.where(side == core, 0, dealt)
    source = jnp.sum(jnp.where(dense == ii, esc, 0).astype(F32), axis=1, keepdims=True).astype(jnp.int32)
    chosen = (source == iota((count, feat_ref.shape[0]), 1)).astype(F32).astype(BF)
    line = pair >> 1
    line = line * (n // 2 + 1) + (side ^ core) * (n // 2) ** 2 if relative else line + (side ^ core) * (n // 2)
    for i, row in enumerate((line, (apart & 1) * half + slot, esc, place, dense)):
        index_ref[i : i + 1, :] = row
    copies[2].wait()
    rows_ref[...] = dot(chosen, feat_ref[...]).astype(BF)
    for copy in copies[3:]:
        copy.wait()


def predict_kernel(
    rows_ref, w_ref, bias_ref, out_ref, upb_ref, head_ref, down_ref, raw_ref,
    near_ref, segment_ref,
):
    depth = raw_ref.shape[0] - EXTRA
    here = w_ref.shape[0]
    core = lax.axis_index("member")
    dealt = near_ref.shape[1]
    row = iota((8, 1), 0)
    preds = None
    for m in range(here):
        act = gelu2(dot(rows_ref[...], w_ref[m]) + bias_ref[m : m + 1]).astype(BF)
        on_row = jnp.where(row == core * here + m, 0.5 * out_ref[m : m + 1].astype(F32), 0.0).astype(BF)
        pred = dot_t(on_row, act)
        preds = pred if preds is None else preds + pred
    preds = preds.astype(BF).astype(F32)
    near_ref[...] = preds[:, :dealt]
    head = split3(head_ref[...]).astype(F32)
    head = jnp.concatenate([head, jnp.zeros((LANES - 3, head.shape[1]), F32)], axis=0).astype(BF)
    down = jnp.sum(dot_t(down_ref[...], head).T[:8], axis=0, keepdims=True)
    extra = [split3(x).astype(F32) for x in (down, upb_ref[...], head_ref[...])]
    members = EXTRA - PREDS
    far = jnp.concatenate([preds[:members, dealt:], jnp.zeros((members, down.shape[1] - dealt), F32)], axis=1)
    extra.append(far)
    segment_ref[depth:, :] = jnp.concatenate(extra, axis=0).astype(BF)


def constants_kernel(
    cls_ref, gain_ref, scale_ref, shift_ref, fbias_ref, fgain_ref, q0_ref, q1_ref, index_ref,
    table_ref, where_ref, place_ref,
):
    count = index_ref.shape[1]
    diag = iota((count, count), 0) == iota((count, count), 1)
    cols = [
        jnp.sum(jnp.where(diag, index_ref[i : i + 1, :], 0).astype(F32), axis=1, keepdims=True) for i in range(5)]
    for i in range(3):
        where_ref[:, i : i + 1] = cols[i].astype(jnp.int32)
    dealt = place_ref.shape[1]
    placed = cols[4].astype(jnp.int32) == iota((count, dealt), 1)
    place_ref[...] = jnp.sum(jnp.where(placed, cols[3], 0.0), axis=0, keepdims=True).astype(jnp.int32)
    gain = gain_ref[...]
    cls = cls_ref[...]
    centered = centre(cls)
    ncls = (centered * inverse_spread(centered) * gain).astype(BF)
    table_ref[...] = jnp.zeros_like(table_ref)
    members = scale_ref.shape[0]
    table_ref[SCALE : SCALE + members, :] = centre(scale_ref[...])
    table_ref[SHIFT : SHIFT + members, :] = centre(shift_ref[...])
    table_ref[GAIN : GAIN + 1, :] = gain
    table_ref[FBIAS : FBIAS + 1, :] = fbias_ref[...]
    table_ref[CLS : CLS + 1, :] = cls
    table_ref[FGAIN : FGAIN + 1, :] = fgain_ref[...]
    lhs = jnp.broadcast_to(ncls.astype(F32), (8, ncls.shape[1])).astype(BF)
    local = q0_ref.shape[2]
    heads = local // HD
    row = iota((8, local), 0)
    col = iota((8, local), 1) // HD
    kmap = None
    for i, ref in enumerate((q0_ref, q1_ref)):
        query = dot(lhs, ref[0]) * (1.0 / math.sqrt(HD))
        spread = jnp.where(row == col + i * heads, query, 0.0)
        part = join3(dot_t(split3(spread), ref[1]))
        kmap = part if kmap is None else kmap + part
        table_ref[VCLS : VCLS + 1, i * local : (i + 1) * local] = dot(lhs, ref[2])[0:1]
    table_ref[KMAP : KMAP + 8, :] = kmap
    logits = jnp.sum(kmap * ncls.astype(F32), axis=-1, keepdims=True)
    eye = iota((8, LANES), 0) == iota((8, LANES), 1)
    table_ref[LCLS : LCLS + 1, :LANES] = jnp.sum(jnp.where(eye, logits, 0.0), axis=0, keepdims=True)


def attend_kernel(
    members, rows_ref, near_ref, other_ref, place_ref, table_ref, fw0_ref, fw1_ref, q0_ref, q1_ref, *sent_refs
):
    core = lax.axis_index("member")
    total = near_ref.shape[1]
    fwidth = rows_ref.shape[1]
    rows = rows_ref[:total]
    local = q0_ref.shape[2]
    gain = table_ref[GAIN : GAIN + 1, :]
    low, high = rows[:, : fwidth // 2].astype(F32), rows[:, fwidth // 2 :].astype(F32)
    first = jnp.where(core == 0, low, high).astype(BF)
    second = jnp.where(core == 0, high, low).astype(BF)
    token = dot(first, fw0_ref[: fwidth // 2]) + dot(second, fw1_ref[: fwidth // 2]) + table_ref[FBIAS : FBIAS + 1, :]
    centered = centre(token)
    tokens = [(centered * inverse_spread(centered) * gain).astype(BF)]
    first = other_ref.shape[0] - EXTRA + PREDS
    far = other_ref[first : first + EXTRA - PREDS, :total].astype(F32)
    preds = (near_ref[...] + jnp.concatenate([far, jnp.zeros((8 - far.shape[0], total), F32)], axis=0)).T
    scale, shift = table_ref[SCALE : SCALE + 8, :], table_ref[SHIFT : SHIFT + 8, :]
    square = jnp.mean(scale * scale, axis=-1, keepdims=True)
    ratio = jnp.mean(scale * shift, axis=-1, keepdims=True) / jnp.maximum(square, 1e-30)
    rest = shift - ratio * scale
    rest = jnp.mean(rest * rest, axis=-1, keepdims=True) + EPS
    scale, shift = scale * gain, shift * gain
    for m in range(members):
        at = slice(m, m + 1)
        pred = preds[:, at]
        moved = pred + ratio[at]
        inverse = lax.rsqrt(square[at] * moved * moved + rest[at])
        tokens.append(((pred * inverse) * scale[at] + inverse * shift[at]).astype(BF))
    normed = jnp.concatenate(tokens, axis=0)
    count = len(tokens)

    kmap = jnp.concatenate([table_ref[KMAP : KMAP + 8, :], jnp.zeros((LANES - 8, table_ref.shape[1]), F32)], axis=0)
    logits = dot_t(normed, jnp.concatenate(split2(kmap), axis=0))
    logits = logits[:, :LANES] + logits[:, LANES:]
    expo = jnp.exp(logits)
    expo_cls = jnp.exp(table_ref[LCLS : LCLS + 1, :LANES])
    norm = expo_cls
    for t in range(count):
        norm = norm + expo[t * total : (t + 1) * total]
    inverse = 1.0 / norm
    weights = jnp.concatenate(
        [expo[t * total : (t + 1) * total] * inverse for t in range(count)] + [expo_cls * inverse], axis=0)
    expand = (iota((2 * LANES, 2 * local), 0) & (LANES - 1)) == iota((2 * LANES, 2 * local), 1) // HD
    spread = dot(jnp.concatenate(split2(weights), axis=1), expand.astype(F32).astype(BF))
    parts = []
    for i, ref in enumerate((q0_ref, q1_ref)):
        at = slice(i * local, (i + 1) * local)
        value = dot(normed, ref[2])
        mixed = spread[count * total :, at] * table_ref[VCLS : VCLS + 1, at]
        for t in range(count):
            rng = slice(t * total, (t + 1) * total)
            mixed = mixed + spread[rng, at] * value[rng]
        parts.append(mixed)
    mixed = jnp.concatenate(parts, axis=1).astype(BF)
    size = sent_refs[0].shape[0]
    scatter = (place_ref[...] == iota((size * len(sent_refs), total), 0)).astype(F32).astype(BF)
    sent = dot(scatter, mixed).astype(BF)
    for k, sent_ref in enumerate(sent_refs):
        sent_ref[...] = sent[k * size : (k + 1) * size]


def ensemble_kernel(first, count, tile, feat_ref, w_ref, bias_ref, out_ref, after_ref, *refs):
    held = (len(refs) - 1) // 2
    copies = start_all(list(zip(refs[:held], refs[held + 1 :])), refs[-1]) if held else []
    pred_ref = refs[held]
    for t in range(count):
        rows = feat_ref[(first + t) * tile : (first + t + 1) * tile]
        total = None
        for m in range(w_ref.shape[0]):
            hidden = gelu2(dot(rows, w_ref[m]) + bias_ref[m : m + 1]).astype(BF)
            weights = jnp.broadcast_to(out_ref[m : m + 1].astype(F32), (8, out_ref.shape[1])).astype(BF)
            pred = dot_t(weights, hidden)[0:1]
            total = pred if total is None else total + pred
        per = tile // LANES
        for i in range(per):
            pred_ref[t * per + i : t * per + i + 1, :] = total[:, i * LANES : (i + 1) * LANES]
    for copy in copies:
        copy.wait()


def unpack(ref):
    depth = ref.shape[0] - EXTRA
    extra = ref[depth:, :].astype(F32)
    return ref[:depth, :], *(jnp.sum(extra[i : i + 3], axis=0, keepdims=True) for i in (DOWN, BIAS, HEAD))


def hidden_terms(normed, up, down, bias):
    return jnp.maximum(dot(normed, up) + bias, 0.0).astype(BF).astype(F32) * down


def states(mixed, table_ref, both0_ref, both1_ref):
    local = mixed.shape[1] // 2
    ow0, ow1 = (ref[ref.shape[0] - local :] for ref in (both0_ref, both1_ref))
    state = table_ref[CLS : CLS + 1, :] + dot(mixed[:, :local], ow0) + dot(mixed[:, local:], ow1)
    centered = centre(state)
    return state, (centered * inverse_spread(centered) * table_ref[FGAIN : FGAIN + 1, :]).astype(BF)


def arrived(got_refs, half, e):
    if len(got_refs) == 1:
        rows = got_refs[0].shape[0] // 2
        return got_refs[0][e * rows : (e + 1) * rows]
    return jnp.concatenate([ref[e * half : (e + 1) * half] for ref in got_refs], axis=0)


def arrive_kernel(blocks, half, *refs):
    table_ref, both0_ref, both1_ref, state_ref, normed_ref = refs[blocks:]
    state_ref[...], normed_ref[...] = states(arrived(refs[:blocks][::-1], half, 1), table_ref, both0_ref, both1_ref)


def near_score_kernel(blocks, half, *refs):
    table_ref, both0_ref, both1_ref, up0_ref, up1_ref, score_ref = refs[blocks:]
    state, normed = states(arrived(refs[:blocks][::-1], half, 0), table_ref, both0_ref, both1_ref)
    up, down, bias, head = unpack(up0_ref)
    terms = state * head + hidden_terms(normed, up, down, bias)
    up, down, bias, _ = unpack(up1_ref)
    terms = terms + hidden_terms(normed, up, down, bias)
    score_ref[...] = jnp.sum(terms, axis=-1, keepdims=True)


def far_score_kernel(blocks, half, near_ref, state_ref, mine_ref, other_ref, up2_ref, out_ref):
    rows = near_ref.shape[0]
    up, down, bias, head = unpack(up2_ref)
    terms = hidden_terms(jnp.concatenate([mine_ref[...], other_ref[...]], axis=0), up, down, bias)
    scores = [
        near_ref[...],
        jnp.sum(terms[:rows] + state_ref[...] * head, axis=-1, keepdims=True),
        jnp.sum(terms[rows:], axis=-1, keepdims=True),
    ]
    if blocks == 1:
        eye = iota((rows, rows), 0) == iota((rows, rows), 1)
        for e, score in enumerate(scores):
            out_ref[:, e * rows : (e + 1) * rows] = jnp.sum(jnp.where(eye, score, 0.0), axis=0, keepdims=True)
    else:
        row, lane = iota((half, LANES), 0), iota((half, LANES), 1)
        for k in range(blocks):
            line = jnp.zeros((half, LANES), F32)
            for e, score in enumerate(scores):
                line = jnp.where(lane == row + e * half, score[k * half : (k + 1) * half], line)
            out_ref[k : k + 1, :] = jnp.sum(line, axis=0, keepdims=True)


def expand_kernel(lines, where_ref, after_ref, line_ref, lane_ref):
    rows = lane_ref.shape[1]
    hit = where_ref[:, 2:3] == iota((where_ref.shape[0], rows), 1)

    def by_row(i):
        return jnp.sum(jnp.where(hit, where_ref[:, i : i + 1] + 1, 0).astype(F32), axis=0, keepdims=True).astype(jnp.int32)

    line = (by_row(0) - 1 == iota((lines, rows), 0)).astype(F32)
    line_ref[...] = jnp.concatenate([line] * 3, axis=0).astype(BF)
    lane_ref[...] = by_row(1) - 1


def finish_kernel(members, half, lines, line_ref, lane_ref, near_ref, far_ref, out_ref):
    near, far = near_ref[...], far_ref[...]
    ensemble = (near[lines:] + far[lines:]) * (0.5 / members)
    ensemble = jnp.concatenate([ensemble[i : i + 1] for i in range(ensemble.shape[0])], axis=1)
    lanes = iota((lines, LANES), 1)
    last = (lanes >= half) & (lanes < 2 * half)

    def whole(mine, others):
        return mine[:lines] + jnp.where(last, pltpu.roll(others[:lines], LANES - half, 1), 0.0)

    table = split3(jnp.concatenate([whole(near, far), whole(far, near)], axis=0))
    by_lane = lax.dot_general(table, line_ref[...], (((0,), (0,)), ((), ())), preferred_element_type=F32)
    lane = lane_ref[...]
    replaced = jnp.sum(jnp.where(lane == iota(by_lane.shape, 0), by_lane, 0.0), axis=0, keepdims=True)
    out_ref[...] = jnp.where(lane >= 0, replaced, ensemble)


def cost(flops, size, trans=0):
    return pl.CostEstimate(flops=flops, bytes_accessed=size, transcendentals=trans)


def params(mib):
    return pltpu.CompilerParams(vmem_limit_bytes=mib * 2**20)


def in_hbm(arrays):
    return [pltpu.with_memory_space_constraint(x, pltpu.HBM) for x in arrays]


def shape(dims, dtype):
    return jax.ShapeDtypeStruct(dims, dtype)


def per_device(
    features, escalated, owner_ids, member_in, member_bias, member_out, feat_weight, feat_bias,
    pred_scale, pred_shift, cls_token, attn_gain, qkv_weight, out_weight, ffn_gain, up_weight,
    up_bias, down_weight, owner_heads,
):
    n = lax.axis_size("rows")
    rows, fwidth = features.shape
    count = escalated.shape[1]
    half = max(1, count // n)
    slots = n * half
    here, _, hidden = member_in.shape
    members = pred_scale.shape[0]
    width = cls_token.shape[0]

    def swap(x):
        return lax.ppermute(x, "member", [(0, 1), (1, 0)])

    row = lambda x: x.reshape(1, -1)
    cls_token, attn_gain, ffn_gain, feat_bias = map(row, (cls_token, attn_gain, ffn_gain, feat_bias))
    owners = owner_ids.reshape(1, count)

    pairs = n // 2
    relative = pairs <= 8
    blocks = pairs if relative else 1
    other_qkv = swap(qkv_weight)

    dealt = count // 2
    ins = (escalated, owners, features, down_weight, up_weight, feat_weight, out_weight)
    index, mine, down, segment, own_both = pl.pallas_call(
        functools.partial(route_kernel, n, half, relative),
        out_shape=[shape((8, count), jnp.int32), shape((count, fwidth), BF), shape(down_weight.shape[1:], BF),
                   shape((up_weight.shape[1] + EXTRA, up_weight.shape[2]), BF),
                   shape((feat_weight.shape[0] + out_weight.shape[0], width), BF)],
        in_specs=[HBM] * len(ins),
        out_specs=[VMEM] * 5,
        scratch_shapes=[pltpu.VMEM(x.shape, x.dtype) for x in ins[:3]] + [pltpu.SemaphoreType.DMA((7,))],
        compiler_params=params(24),
        cost_estimate=cost(2 * count * rows * fwidth, 3 * 10**6),
        name="route",
    )(*in_hbm(ins))
    near, segment = pl.pallas_call(
        predict_kernel,
        out_shape=[shape((8, dealt), F32), shape(segment.shape, BF)],
        in_specs=[VMEM] * 8,
        out_specs=[VMEM] * 2,
        input_output_aliases={7: 1},
        compiler_params=params(24),
        cost_estimate=cost(2 * here * count * fwidth * hidden, 3 * 10**6, here * count * hidden),
        name="predict",
    )(mine, member_in, member_bias, member_out, up_bias, owner_heads, down, segment)
    other_both = swap(own_both)
    next_segment = lax.ppermute(segment, "rows", [(i, i ^ 1) for i in range(n)])
    other_segment = swap(segment)

    ins = (cls_token, attn_gain, pred_scale, pred_shift, feat_bias, ffn_gain, qkv_weight, other_qkv, index)
    table, where, place = pl.pallas_call(
        constants_kernel,
        out_shape=[shape((TABLE, width), F32), shape((count, 3), jnp.int32), shape((1, dealt), jnp.int32)],
        in_specs=[VMEM] * len(ins),
        out_specs=[VMEM] * 3,
        compiler_params=params(16),
        cost_estimate=cost(10**8, 2 * 10**6),
        name="constants",
    )(*ins)

    local = qkv_weight.shape[2]
    sent = pl.pallas_call(
        functools.partial(attend_kernel, members),
        out_shape=[shape((slots // blocks, 2 * local), BF)] * blocks,
        in_specs=[VMEM] * 9,
        out_specs=[VMEM] * blocks,
        compiler_params=params(24),
        cost_estimate=cost(10**9, 2 * 10**6),
        name="attend",
    )(mine, near, other_segment, place, table, own_both, other_both, qkv_weight, other_qkv)

    def across(x, k):
        return lax.ppermute(x, "rows", [(i, i ^ (2 * k)) for i in range(n)])

    def exchange(x):
        groups = [[2 * q + b for q in range(pairs)] for b in range(2)]
        return lax.all_to_all(x, "rows", split_axis=0, concat_axis=0, axis_index_groups=groups, tiled=True)

    if relative:
        got = [sent[0]] + [across(sent[k], k) for k in range(1, pairs)]
    else:
        got = exchange(sent[0].reshape(pairs, 2, half, 2 * local))
        got = [got.transpose(1, 0, 2, 3).reshape(slots, 2 * local)]

    tile = min(rows, 256)
    tiles = rows // tile

    def ensemble(first, number, after, held=()):
        return pl.pallas_call(
            functools.partial(ensemble_kernel, first, number, tile),
            out_shape=[shape((number * tile // LANES, LANES), F32)] + [shape(x.shape, x.dtype) for x in held],
            in_specs=[VMEM] * 4 + [ANY] * (1 + len(held)),
            out_specs=[VMEM] * (1 + len(held)),
            scratch_shapes=[pltpu.SemaphoreType.DMA((len(held),))] if held else [],
            compiler_params=params(24),
            cost_estimate=cost(2 * here * number * tile * fwidth * hidden, 10**6, here * number * tile * hidden),
            name="ensemble",
        )(features, member_in, member_bias, member_out, after, *held)

    early = (tiles + 1) // 2
    preds, table, both0, both1, up0, up1 = ensemble(
        0, early, sent[0], (table, own_both, other_both, segment, other_segment))
    preds = [preds]

    state, next_rows = pl.pallas_call(
        functools.partial(arrive_kernel, blocks, half),
        out_shape=[shape((slots // 2, width), F32), shape((slots // 2, width), BF)],
        in_specs=[VMEM] * (blocks + 3),
        out_specs=[VMEM] * 2,
        compiler_params=params(24),
        cost_estimate=cost(2 * 10**8, 2 * 10**6),
        name="arrive",
    )(*got[::-1], table, both0, both1)
    other_rows = swap(next_rows)
    near_scores = pl.pallas_call(
        functools.partial(near_score_kernel, blocks, half),
        out_shape=shape((slots // 2, 1), F32),
        in_specs=[VMEM] * (blocks + 5),
        out_specs=VMEM,
        compiler_params=params(24),
        cost_estimate=cost(5 * 10**8, 2 * 10**6),
        name="near_score",
    )(*got[::-1], table, both0, both1, up0, up1)
    scores = pl.pallas_call(
        functools.partial(far_score_kernel, blocks, half),
        out_shape=shape((blocks, LANES if relative else 3 * slots // 2), F32),
        in_specs=[VMEM] * 5,
        out_specs=VMEM,
        compiler_params=params(24),
        cost_estimate=cost(2 * 10**8, 10**6),
        name="far_score",
    )(near_scores, state, next_rows, other_rows, next_segment)
    for first in range(early, tiles):
        preds += ensemble(first, 1, scores)
    back = scores
    if relative:
        step = 1
        while step < pairs:
            back = jnp.concatenate([back, across(back, step)], axis=0)
            step *= 2
    else:
        back = exchange(back.reshape(3, pairs, half).transpose(1, 0, 2)).reshape(pairs, 3 * half)
        back = jnp.pad(back, ((0, 0), (0, LANES - 3 * half)))
    lines = back.shape[0]
    near_lines = jnp.concatenate([back, *preds], axis=0)
    line_of, lane_of = pl.pallas_call(
        functools.partial(expand_kernel, 2 * lines),
        out_shape=[shape((6 * lines, rows), BF), shape((1, rows), jnp.int32)],
        in_specs=[VMEM, ANY],
        out_specs=[VMEM] * 2,
        compiler_params=params(16),
        cost_estimate=cost(10**8, 10**6),
        name="expand",
    )(where, preds[-1])

    final = pl.pallas_call(
        functools.partial(finish_kernel, members, half, lines),
        out_shape=shape((1, rows), F32),
        in_specs=[VMEM] * 4,
        out_specs=VMEM,
        compiler_params=params(8),
        cost_estimate=cost(10**6, 10**6),
        name="finish",
    )(line_of, lane_of, near_lines, swap(near_lines))
    return final.reshape(rows)


def solution(mesh):
    placed = (
        P(("groups", "rows"), None),
        P(("groups", "rows"), None),
        P(("groups", "rows"), None, None),
        P("member", None, None),
        P("member", None),
        P("member", None),
        P("member", None),
        P(),
        P(),
        P(),
        P(),
        P(),
        P(None, None, "member"),
        P("member", None),
        P(),
        P("rows", None, "member"),
        P("rows", "member"),
        P("rows", "member", None),
        P("rows", None),
    )
    return jax.shard_map(
        per_device, mesh=mesh, in_specs=placed, out_specs=P(("groups", "rows")), check_vma=False
    )
```

```python
import functools
import math

import jax
import jax.numpy as jnp
from jax import lax
from jax.experimental import pallas as pl
from jax.experimental.pallas import tpu as pltpu
from jax.sharding import PartitionSpec as P

HD = 64
EPS = 1e-05
LANES = 128
BF = jnp.bfloat16
F32 = jnp.float32
VMEM = pl.BlockSpec(memory_space=pltpu.VMEM)
HBM = pl.BlockSpec(memory_space=pltpu.HBM)
ANY = pl.BlockSpec(memory_space=pl.ANY)
GELU_C = math.sqrt(2.0 / math.pi)

KMAP, VCLS, LCLS, SCALE, SHIFT, GAIN, FBIAS, CLS, FGAIN = 0, 8, 9, 16, 24, 32, 33, 34, 35
TABLE = 40
DOWN, BIAS, HEAD, PREDS, EXTRA = 0, 3, 6, 9, 16


def iota(shape, dim):
    return lax.broadcasted_iota(jnp.int32, shape, dim)


def gelu2(x):
    return x + x * jnp.tanh(x * (GELU_C + (GELU_C * 0.044715) * (x * x)))


def dot(a, b):
    return lax.dot_general(a, b, (((1,), (0,)), ((), ())), preferred_element_type=F32)


def dot_t(a, b):
    return lax.dot_general(a, b, (((1,), (1,)), ((), ())), preferred_element_type=F32)


def split2(x):
    high = x.astype(BF)
    return high, (x - high.astype(F32)).astype(BF)


def split3(x):
    high, rest = x.astype(BF), x
    rest = rest - high.astype(F32)
    mid = rest.astype(BF)
    low = (rest - mid.astype(F32)).astype(BF)
    return jnp.concatenate([high.astype(F32), mid.astype(F32), low.astype(F32)], axis=0).astype(BF)


def join3(x):
    rows = x.shape[0] // 3
    return x[:rows] + x[rows : 2 * rows] + x[2 * rows :]


def centre(x):
    return x - jnp.mean(x, axis=-1, keepdims=True)


def inverse_spread(centered):
    return lax.rsqrt(jnp.mean(centered * centered, axis=-1, keepdims=True) + EPS)


def start_all(pairs, sems):
    copies = [pltpu.make_async_copy(src, dst, sems.at[i]) for i, (src, dst) in enumerate(pairs)]
    for copy in copies:
        copy.start()
    return copies


def route_kernel(
    n, half, relative, esc_hbm, own_hbm, feat_hbm, down_hbm, up_hbm, fw_hbm, ow_hbm,
    index_ref, rows_ref, down_ref, segment_ref, bundle_ref, esc_ref, own_ref, feat_ref, sems,
):
    depth = up_hbm.shape[1]
    copies = start_all(
        [(esc_hbm, esc_ref), (own_hbm, own_ref), (feat_hbm, feat_ref), (down_hbm.at[0], down_ref),
         (up_hbm.at[0], segment_ref.at[:depth]), (up_hbm.at[0], bundle_ref.at[:depth]),
         (fw_hbm, bundle_ref.at[pl.ds(depth + EXTRA, fw_hbm.shape[0])]),
         (ow_hbm, bundle_ref.at[pl.ds(depth + EXTRA + fw_hbm.shape[0], ow_hbm.shape[0])])], sems)
    for ref in (segment_ref, bundle_ref):
        ref[depth : depth + EXTRA, :] = jnp.zeros((EXTRA, up_hbm.shape[2]), BF)
    core = lax.axis_index("member")
    count = esc_hbm.shape[1]
    dealt = count // 2
    copies[0].wait()
    copies[1].wait()
    esc = esc_ref[...]
    own = own_ref[...]
    ii = iota((count, count), 0)
    jj = iota((count, count), 1)
    own_col = jnp.sum(jnp.where(ii == jj, own, 0).astype(F32), axis=1, keepdims=True).astype(jnp.int32)
    before = jnp.sum((own_col < own).astype(F32), axis=0, keepdims=True).astype(jnp.int32)
    rank = jnp.sum(((own_col == own) & (ii < jj)).astype(F32), axis=0, keepdims=True).astype(jnp.int32)
    position = before + rank
    side = position & 1
    slot = rank >> 1
    apart = own ^ lax.axis_index("rows")
    pair = apart if relative else (own - (own & 1)) + (apart & 1)
    place = pair * half + slot
    dense = (position >> 1) + jnp.where(side == core, 0, dealt)
    source = jnp.sum(jnp.where(dense == ii, esc, 0).astype(F32), axis=1, keepdims=True).astype(jnp.int32)
    chosen = (source == iota((count, feat_ref.shape[0]), 1)).astype(F32).astype(BF)
    line = pair >> 1
    line = line * (n // 2 + 1) + (side ^ core) * (n // 2) ** 2 if relative else line + (side ^ core) * (n // 2)
    for i, row in enumerate((line, (apart & 1) * half + slot, esc, place, dense)):
        index_ref[i : i + 1, :] = row
    copies[2].wait()
    rows_ref[...] = dot(chosen, feat_ref[...]).astype(BF)
    for copy in copies[3:]:
        copy.wait()


def predict_kernel(
    rows_ref, w_ref, bias_ref, out_ref, upb_ref, head_ref, down_ref, raw_ref, raw_bundle_ref, after_ref,
    near_ref, segment_ref, bundle_ref,
):
    depth = raw_ref.shape[0] - EXTRA
    here = w_ref.shape[0]
    core = lax.axis_index("member")
    dealt = near_ref.shape[1]
    row = iota((8, 1), 0)
    preds = None
    for m in range(here):
        act = gelu2(dot(rows_ref[...], w_ref[m]) + bias_ref[m : m + 1]).astype(BF)
        on_row = jnp.where(row == core * here + m, 0.5 * out_ref[m : m + 1].astype(F32), 0.0).astype(BF)
        pred = dot_t(on_row, act)
        preds = pred if preds is None else preds + pred
    preds = preds.astype(BF).astype(F32)
    near_ref[...] = preds[:, :dealt]
    head = split3(head_ref[...]).astype(F32)
    head = jnp.concatenate([head, jnp.zeros((LANES - 3, head.shape[1]), F32)], axis=0).astype(BF)
    down = jnp.sum(dot_t(down_ref[...], head).T[:8], axis=0, keepdims=True)
    extra = [split3(x).astype(F32) for x in (down, upb_ref[...], head_ref[...])]
    members = EXTRA - PREDS
    far = jnp.concatenate([preds[:members, dealt:], jnp.zeros((members, down.shape[1] - dealt), F32)], axis=1)
    extra.append(far)
    for ref in (segment_ref, bundle_ref):
        ref[depth : depth + EXTRA, :] = jnp.concatenate(extra, axis=0).astype(BF)


def constants_kernel(
    cls_ref, gain_ref, scale_ref, shift_ref, fbias_ref, fgain_ref, q0_ref, q1_ref, index_ref,
    table_ref, where_ref, place_ref,
):
    count = index_ref.shape[1]
    diag = iota((count, count), 0) == iota((count, count), 1)
    cols = [
        jnp.sum(jnp.where(diag, index_ref[i : i + 1, :], 0).astype(F32), axis=1, keepdims=True) for i in range(5)]
    for i in range(3):
        where_ref[:, i : i + 1] = cols[i].astype(jnp.int32)
    dealt = place_ref.shape[1]
    placed = cols[4].astype(jnp.int32) == iota((count, dealt), 1)
    place_ref[...] = jnp.sum(jnp.where(placed, cols[3], 0.0), axis=0, keepdims=True).astype(jnp.int32)
    gain = gain_ref[...]
    cls = cls_ref[...]
    centered = centre(cls)
    ncls = (centered * inverse_spread(centered) * gain).astype(BF)
    table_ref[...] = jnp.zeros_like(table_ref)
    members = scale_ref.shape[0]
    table_ref[SCALE : SCALE + members, :] = centre(scale_ref[...])
    table_ref[SHIFT : SHIFT + members, :] = centre(shift_ref[...])
    table_ref[GAIN : GAIN + 1, :] = gain
    table_ref[FBIAS : FBIAS + 1, :] = fbias_ref[...]
    table_ref[CLS : CLS + 1, :] = cls
    table_ref[FGAIN : FGAIN + 1, :] = fgain_ref[...]
    lhs = jnp.broadcast_to(ncls.astype(F32), (8, ncls.shape[1])).astype(BF)
    local = q0_ref.shape[2]
    heads = local // HD
    row = iota((8, local), 0)
    col = iota((8, local), 1) // HD
    kmap = None
    for i, ref in enumerate((q0_ref, q1_ref)):
        query = dot(lhs, ref[0]) * (1.0 / math.sqrt(HD))
        spread = jnp.where(row == col + i * heads, query, 0.0)
        part = join3(dot_t(split3(spread), ref[1]))
        kmap = part if kmap is None else kmap + part
        table_ref[VCLS : VCLS + 1, i * local : (i + 1) * local] = dot(lhs, ref[2])[0:1]
    table_ref[KMAP : KMAP + 8, :] = kmap
    logits = jnp.sum(kmap * ncls.astype(F32), axis=-1, keepdims=True)
    eye = iota((8, LANES), 0) == iota((8, LANES), 1)
    table_ref[LCLS : LCLS + 1, :LANES] = jnp.sum(jnp.where(eye, logits, 0.0), axis=0, keepdims=True)


def feature_half(bundle_ref, rows):
    first = bundle_ref.shape[1] + EXTRA
    return bundle_ref[first : first + rows]


def attend_kernel(
    members, rows_ref, near_ref, other_ref, place_ref, table_ref, fw0_ref, fw1_ref, q0_ref, q1_ref, *sent_refs
):
    core = lax.axis_index("member")
    total = near_ref.shape[1]
    fwidth = rows_ref.shape[1]
    rows = rows_ref[:total]
    local = q0_ref.shape[2]
    gain = table_ref[GAIN : GAIN + 1, :]
    low, high = rows[:, : fwidth // 2].astype(F32), rows[:, fwidth // 2 :].astype(F32)
    first = jnp.where(core == 0, low, high).astype(BF)
    second = jnp.where(core == 0, high, low).astype(BF)
    token = dot(first, feature_half(fw0_ref, fwidth // 2)) + dot(second, feature_half(fw1_ref, fwidth // 2)) + table_ref[FBIAS : FBIAS + 1, :]
    centered = centre(token)
    tokens = [(centered * inverse_spread(centered) * gain).astype(BF)]
    first = table_ref.shape[1] + PREDS
    far = other_ref[first : first + EXTRA - PREDS, :total].astype(F32)
    preds = (near_ref[...] + jnp.concatenate([far, jnp.zeros((8 - far.shape[0], total), F32)], axis=0)).T
    for m in range(members):
        centered = preds[:, m : m + 1] * table_ref[SCALE + m : SCALE + m + 1, :] + table_ref[SHIFT + m : SHIFT + m + 1, :]
        tokens.append((centered * inverse_spread(centered) * gain).astype(BF))
    normed = jnp.concatenate(tokens, axis=0)
    count = len(tokens)

    kmap = jnp.concatenate([table_ref[KMAP : KMAP + 8, :], jnp.zeros((LANES - 8, table_ref.shape[1]), F32)], axis=0)
    logits = dot_t(normed, jnp.concatenate(split2(kmap), axis=0))
    logits = logits[:, :LANES] + logits[:, LANES:]
    expo = jnp.exp(logits)
    expo_cls = jnp.exp(table_ref[LCLS : LCLS + 1, :LANES])
    norm = expo_cls
    for t in range(count):
        norm = norm + expo[t * total : (t + 1) * total]
    inverse = 1.0 / norm
    weights = jnp.concatenate(
        [expo[t * total : (t + 1) * total] * inverse for t in range(count)] + [expo_cls * inverse], axis=0)
    expand = (iota((2 * LANES, 2 * local), 0) & (LANES - 1)) == iota((2 * LANES, 2 * local), 1) // HD
    spread = dot(jnp.concatenate(split2(weights), axis=1), expand.astype(F32).astype(BF))
    parts = []
    for i, ref in enumerate((q0_ref, q1_ref)):
        at = slice(i * local, (i + 1) * local)
        value = dot(normed, ref[2])
        mixed = spread[count * total :, at] * table_ref[VCLS : VCLS + 1, at]
        for t in range(count):
            rng = slice(t * total, (t + 1) * total)
            mixed = mixed + spread[rng, at] * value[rng]
        parts.append(mixed)
    mixed = jnp.concatenate(parts, axis=1).astype(BF)
    size = sent_refs[0].shape[0]
    scatter = (place_ref[...] == iota((size * len(sent_refs), total), 0)).astype(F32).astype(BF)
    sent = dot(scatter, mixed).astype(BF)
    for k, sent_ref in enumerate(sent_refs):
        sent_ref[...] = sent[k * size : (k + 1) * size]


def ensemble_kernel(first, count, tile, feat_ref, w_ref, bias_ref, out_ref, after_ref, *refs):
    held = (len(refs) - 1) // 2
    copies = start_all(list(zip(refs[:held], refs[held + 1 :])), refs[-1]) if held else []
    pred_ref = refs[held]
    for t in range(count):
        rows = feat_ref[(first + t) * tile : (first + t + 1) * tile]
        total = None
        for m in range(w_ref.shape[0]):
            hidden = gelu2(dot(rows, w_ref[m]) + bias_ref[m : m + 1]).astype(BF)
            weights = jnp.broadcast_to(out_ref[m : m + 1].astype(F32), (8, out_ref.shape[1])).astype(BF)
            pred = dot_t(weights, hidden)[0:1]
            total = pred if total is None else total + pred
        per = tile // LANES
        for i in range(per):
            pred_ref[t * per + i : t * per + i + 1, :] = total[:, i * LANES : (i + 1) * LANES]
    for copy in copies:
        copy.wait()


def unpack(ref, depth):
    extra = ref[depth : depth + EXTRA, :].astype(F32)
    return ref[:depth, :], *(jnp.sum(extra[i : i + 3], axis=0, keepdims=True) for i in (DOWN, BIAS, HEAD))


def hidden_terms(normed, up, down, bias):
    return jnp.maximum(dot(normed, up) + bias, 0.0).astype(BF).astype(F32) * down


def states(mixed, table_ref, both0_ref, both1_ref):
    local = mixed.shape[1] // 2
    ow0, ow1 = (ref[ref.shape[0] - local :] for ref in (both0_ref, both1_ref))
    state = table_ref[CLS : CLS + 1, :] + dot(mixed[:, :local], ow0) + dot(mixed[:, local:], ow1)
    centered = centre(state)
    return state, (centered * inverse_spread(centered) * table_ref[FGAIN : FGAIN + 1, :]).astype(BF)


def arrived(got_refs, half, e):
    if len(got_refs) == 1:
        rows = got_refs[0].shape[0] // 2
        return got_refs[0][e * rows : (e + 1) * rows]
    return jnp.concatenate([ref[e * half : (e + 1) * half] for ref in got_refs], axis=0)


def arrive_kernel(blocks, half, *refs):
    table_ref, both0_ref, both1_ref, state_ref, normed_ref = refs[blocks:]
    state_ref[...], normed_ref[...] = states(arrived(refs[:blocks][::-1], half, 1), table_ref, both0_ref, both1_ref)


def near_score_kernel(blocks, half, *refs):
    table_ref, both0_ref, both1_ref, score_ref = refs[blocks:]
    state, normed = states(arrived(refs[:blocks][::-1], half, 0), table_ref, both0_ref, both1_ref)
    up, down, bias, head = unpack(both0_ref, normed.shape[1])
    terms = state * head + hidden_terms(normed, up, down, bias)
    up, down, bias, _ = unpack(both1_ref, normed.shape[1])
    terms = terms + hidden_terms(normed, up, down, bias)
    score_ref[...] = jnp.sum(terms, axis=-1, keepdims=True)


def far_score_kernel(blocks, half, near_ref, state_ref, mine_ref, other_ref, up2_ref, out_ref):
    rows = near_ref.shape[0]
    up, down, bias, head = unpack(up2_ref, mine_ref.shape[1])
    terms = hidden_terms(jnp.concatenate([mine_ref[...], other_ref[...]], axis=0), up, down, bias)
    scores = [
        near_ref[...],
        jnp.sum(terms[:rows] + state_ref[...] * head, axis=-1, keepdims=True),
        jnp.sum(terms[rows:], axis=-1, keepdims=True),
    ]
    if blocks == 1:
        eye = iota((rows, rows), 0) == iota((rows, rows), 1)
        for e, score in enumerate(scores):
            out_ref[:, e * rows : (e + 1) * rows] = jnp.sum(jnp.where(eye, score, 0.0), axis=0, keepdims=True)
    else:
        row, lane = iota((half, LANES), 0), iota((half, LANES), 1)
        for k in range(blocks):
            line = jnp.zeros((half, LANES), F32)
            for e, score in enumerate(scores):
                line = jnp.where(lane == row + e * half, score[k * half : (k + 1) * half], line)
            out_ref[k : k + 1, :] = jnp.sum(line, axis=0, keepdims=True)


def expand_kernel(lines, where_ref, after_ref, line_ref, lane_ref):
    rows = lane_ref.shape[1]
    hit = where_ref[:, 2:3] == iota((where_ref.shape[0], rows), 1)

    def by_row(i):
        return jnp.sum(jnp.where(hit, where_ref[:, i : i + 1] + 1, 0).astype(F32), axis=0, keepdims=True).astype(jnp.int32)

    line = (by_row(0) - 1 == iota((lines, rows), 0)).astype(F32)
    line_ref[...] = jnp.concatenate([line] * 3, axis=0).astype(BF)
    lane_ref[...] = by_row(1) - 1


def finish_kernel(members, half, lines, line_ref, lane_ref, near_ref, far_ref, out_ref):
    near, far = near_ref[...], far_ref[...]
    ensemble = (near[lines:] + far[lines:]) * (0.5 / members)
    ensemble = jnp.concatenate([ensemble[i : i + 1] for i in range(ensemble.shape[0])], axis=1)
    lanes = iota((lines, LANES), 1)
    last = (lanes >= half) & (lanes < 2 * half)

    def whole(mine, others):
        return mine[:lines] + jnp.where(last, pltpu.roll(others[:lines], LANES - half, 1), 0.0)

    table = split3(jnp.concatenate([whole(near, far), whole(far, near)], axis=0))
    by_lane = lax.dot_general(table, line_ref[...], (((0,), (0,)), ((), ())), preferred_element_type=F32)
    lane = lane_ref[...]
    replaced = jnp.sum(jnp.where(lane == iota(by_lane.shape, 0), by_lane, 0.0), axis=0, keepdims=True)
    out_ref[...] = jnp.where(lane >= 0, replaced, ensemble)


def cost(flops, size, trans=0):
    return pl.CostEstimate(flops=flops, bytes_accessed=size, transcendentals=trans)


def params(mib):
    return pltpu.CompilerParams(vmem_limit_bytes=mib * 2**20)


def in_hbm(arrays):
    return [pltpu.with_memory_space_constraint(x, pltpu.HBM) for x in arrays]


def shape(dims, dtype):
    return jax.ShapeDtypeStruct(dims, dtype)


def per_device(
    features, escalated, owner_ids, member_in, member_bias, member_out, feat_weight, feat_bias,
    pred_scale, pred_shift, cls_token, attn_gain, qkv_weight, out_weight, ffn_gain, up_weight,
    up_bias, down_weight, owner_heads,
):
    n = lax.axis_size("rows")
    rows, fwidth = features.shape
    count = escalated.shape[1]
    half = max(1, count // n)
    slots = n * half
    here, _, hidden = member_in.shape
    members = pred_scale.shape[0]
    width = cls_token.shape[0]

    def swap(x):
        return lax.ppermute(x, "member", [(0, 1), (1, 0)])

    row = lambda x: x.reshape(1, -1)
    cls_token, attn_gain, ffn_gain, feat_bias = map(row, (cls_token, attn_gain, ffn_gain, feat_bias))
    owners = owner_ids.reshape(1, count)

    pairs = n // 2
    relative = pairs <= 8
    blocks = pairs if relative else 1
    other_qkv = swap(qkv_weight)

    dealt = count // 2
    ins = (escalated, owners, features, down_weight, up_weight, feat_weight, out_weight)
    index, mine, down, segment, bundle = pl.pallas_call(
        functools.partial(route_kernel, n, half, relative),
        out_shape=[shape((8, count), jnp.int32), shape((count, fwidth), BF), shape(down_weight.shape[1:], BF),
                   shape((up_weight.shape[1] + EXTRA, up_weight.shape[2]), BF),
                   shape((up_weight.shape[1] + EXTRA + feat_weight.shape[0] + out_weight.shape[0], width), BF)],
        in_specs=[HBM] * len(ins),
        out_specs=[VMEM] * 5,
        scratch_shapes=[pltpu.VMEM(x.shape, x.dtype) for x in ins[:3]] + [pltpu.SemaphoreType.DMA((8,))],
        compiler_params=params(24),
        cost_estimate=cost(2 * count * rows * fwidth, 3 * 10**6),
        name="route",
    )(*in_hbm(ins))
    near, segment, bundle = pl.pallas_call(
        predict_kernel,
        out_shape=[shape((8, dealt), F32), shape(segment.shape, BF), shape(bundle.shape, BF)],
        in_specs=[VMEM] * 9 + [ANY],
        out_specs=[VMEM] * 3,
        input_output_aliases={7: 1, 8: 2},
        compiler_params=params(24),
        cost_estimate=cost(2 * here * count * fwidth * hidden, 3 * 10**6, here * count * hidden),
        name="predict",
    )(mine, member_in, member_bias, member_out, up_bias, owner_heads, down, segment, bundle, other_qkv)
    other_bundle = swap(bundle)
    next_segment = lax.ppermute(segment, "rows", [(i, i ^ 1) for i in range(n)])

    ins = (cls_token, attn_gain, pred_scale, pred_shift, feat_bias, ffn_gain, qkv_weight, other_qkv, index)
    table, where, place = pl.pallas_call(
        constants_kernel,
        out_shape=[shape((TABLE, width), F32), shape((count, 3), jnp.int32), shape((1, dealt), jnp.int32)],
        in_specs=[VMEM] * len(ins),
        out_specs=[VMEM] * 3,
        compiler_params=params(16),
        cost_estimate=cost(10**8, 2 * 10**6),
        name="constants",
    )(*ins)

    local = qkv_weight.shape[2]
    sent = pl.pallas_call(
        functools.partial(attend_kernel, members),
        out_shape=[shape((slots // blocks, 2 * local), BF)] * blocks,
        in_specs=[VMEM] * 9,
        out_specs=[VMEM] * blocks,
        compiler_params=params(24),
        cost_estimate=cost(10**9, 2 * 10**6),
        name="attend",
    )(mine, near, other_bundle, place, table, bundle, other_bundle, qkv_weight, other_qkv)

    def across(x, k):
        return lax.ppermute(x, "rows", [(i, i ^ (2 * k)) for i in range(n)])

    def exchange(x):
        groups = [[2 * q + b for q in range(pairs)] for b in range(2)]
        return lax.all_to_all(x, "rows", split_axis=0, concat_axis=0, axis_index_groups=groups, tiled=True)

    if relative:
        got = [sent[0]] + [across(sent[k], k) for k in range(1, pairs)]
    else:
        got = exchange(sent[0].reshape(pairs, 2, half, 2 * local))
        got = [got.transpose(1, 0, 2, 3).reshape(slots, 2 * local)]

    tile = min(rows, 256)
    tiles = rows // tile

    def ensemble(first, number, after, held=()):
        return pl.pallas_call(
            functools.partial(ensemble_kernel, first, number, tile),
            out_shape=[shape((number * tile // LANES, LANES), F32)] + [shape(x.shape, x.dtype) for x in held],
            in_specs=[VMEM] * 4 + [ANY] * (1 + len(held)),
            out_specs=[VMEM] * (1 + len(held)),
            scratch_shapes=[pltpu.SemaphoreType.DMA((len(held),))] if held else [],
            compiler_params=params(24),
            cost_estimate=cost(2 * here * number * tile * fwidth * hidden, 10**6, here * number * tile * hidden),
            name="ensemble",
        )(features, member_in, member_bias, member_out, after, *held)

    early = (tiles + 1) // 2
    preds, table, bundle, other_bundle = ensemble(0, early, sent[0], (table, bundle, other_bundle))
    preds = [preds]

    state, next_rows = pl.pallas_call(
        functools.partial(arrive_kernel, blocks, half),
        out_shape=[shape((slots // 2, width), F32), shape((slots // 2, width), BF)],
        in_specs=[VMEM] * (blocks + 3),
        out_specs=[VMEM] * 2,
        compiler_params=params(24),
        cost_estimate=cost(2 * 10**8, 2 * 10**6),
        name="arrive",
    )(*got[::-1], table, bundle, other_bundle)
    other_rows = swap(next_rows)
    near_scores = pl.pallas_call(
        functools.partial(near_score_kernel, blocks, half),
        out_shape=shape((slots // 2, 1), F32),
        in_specs=[VMEM] * (blocks + 3),
        out_specs=VMEM,
        compiler_params=params(24),
        cost_estimate=cost(5 * 10**8, 2 * 10**6),
        name="near_score",
    )(*got[::-1], table, bundle, other_bundle)
    scores = pl.pallas_call(
        functools.partial(far_score_kernel, blocks, half),
        out_shape=shape((blocks, LANES if relative else 3 * slots // 2), F32),
        in_specs=[VMEM] * 5,
        out_specs=VMEM,
        compiler_params=params(24),
        cost_estimate=cost(2 * 10**8, 10**6),
        name="far_score",
    )(near_scores, state, next_rows, other_rows, next_segment)
    for first in range(early, tiles):
        preds += ensemble(first, 1, scores)
    back = scores
    if relative:
        step = 1
        while step < pairs:
            back = jnp.concatenate([back, across(back, step)], axis=0)
            step *= 2
    else:
        back = exchange(back.reshape(3, pairs, half).transpose(1, 0, 2)).reshape(pairs, 3 * half)
        back = jnp.pad(back, ((0, 0), (0, LANES - 3 * half)))
    lines = back.shape[0]
    near_lines = jnp.concatenate([back, *preds], axis=0)
    line_of, lane_of = pl.pallas_call(
        functools.partial(expand_kernel, 2 * lines),
        out_shape=[shape((6 * lines, rows), BF), shape((1, rows), jnp.int32)],
        in_specs=[VMEM, ANY],
        out_specs=[VMEM] * 2,
        compiler_params=params(16),
        cost_estimate=cost(10**8, 10**6),
        name="expand",
    )(where, preds[-1])

    final = pl.pallas_call(
        functools.partial(finish_kernel, members, half, lines),
        out_shape=shape((1, rows), F32),
        in_specs=[VMEM] * 4,
        out_specs=VMEM,
        compiler_params=params(8),
        cost_estimate=cost(10**6, 10**6),
        name="finish",
    )(line_of, lane_of, near_lines, swap(near_lines))
    return final.reshape(rows)


def solution(mesh):
    placed = (
        P(("groups", "rows"), None),
        P(("groups", "rows"), None),
        P(("groups", "rows"), None, None),
        P("member", None, None),
        P("member", None),
        P("member", None),
        P("member", None),
        P(),
        P(),
        P(),
        P(),
        P(),
        P(None, None, "member"),
        P("member", None),
        P(),
        P("rows", None, "member"),
        P("rows", "member"),
        P("rows", "member", None),
        P("rows", None),
    )
    return jax.shard_map(
        per_device, mesh=mesh, in_specs=placed, out_specs=P(("groups", "rows")), check_vma=False
    )
```

```python
import functools
import math

import jax
import jax.numpy as jnp
from jax import lax
from jax.experimental import pallas as pl
from jax.experimental.pallas import tpu as pltpu
from jax.sharding import PartitionSpec as P

HD = 64
EPS = 1e-05
LANES = 128
BF = jnp.bfloat16
F32 = jnp.float32
VMEM = pl.BlockSpec(memory_space=pltpu.VMEM)
HBM = pl.BlockSpec(memory_space=pltpu.HBM)
ANY = pl.BlockSpec(memory_space=pl.ANY)
GELU_C = math.sqrt(2.0 / math.pi)

KMAP, VCLS, LCLS, SCALE, SHIFT, GAIN, FBIAS, CLS, FGAIN = 0, 8, 9, 16, 24, 32, 33, 34, 35
TABLE = 40
DOWN, BIAS, HEAD, PREDS, EXTRA = 0, 3, 6, 9, 16


def iota(shape, dim):
    return lax.broadcasted_iota(jnp.int32, shape, dim)


def gelu2(x):
    return x + x * jnp.tanh(x * (GELU_C + (GELU_C * 0.044715) * (x * x)))


def dot(a, b):
    return lax.dot_general(a, b, (((1,), (0,)), ((), ())), preferred_element_type=F32)


def dot_t(a, b):
    return lax.dot_general(a, b, (((1,), (1,)), ((), ())), preferred_element_type=F32)


def split2(x):
    high = x.astype(BF)
    return high, (x - high.astype(F32)).astype(BF)


def split3(x):
    high, rest = x.astype(BF), x
    rest = rest - high.astype(F32)
    mid = rest.astype(BF)
    low = (rest - mid.astype(F32)).astype(BF)
    return jnp.concatenate([high.astype(F32), mid.astype(F32), low.astype(F32)], axis=0).astype(BF)


def join3(x):
    rows = x.shape[0] // 3
    return x[:rows] + x[rows : 2 * rows] + x[2 * rows :]


def centre(x):
    return x - jnp.mean(x, axis=-1, keepdims=True)


def inverse_spread(centered):
    return lax.rsqrt(jnp.mean(centered * centered, axis=-1, keepdims=True) + EPS)


def start_all(pairs, sems):
    copies = [pltpu.make_async_copy(src, dst, sems.at[i]) for i, (src, dst) in enumerate(pairs)]
    for copy in copies:
        copy.start()
    return copies


def route_kernel(
    n, half, relative, esc_hbm, own_hbm, feat_hbm, down_hbm, up_hbm, fw_hbm, ow_hbm,
    index_ref, rows_ref, down_ref, segment_ref, both_ref, esc_ref, own_ref, feat_ref, sems,
):
    copies = start_all(
        [(esc_hbm, esc_ref), (own_hbm, own_ref), (feat_hbm, feat_ref), (down_hbm.at[0], down_ref),
         (fw_hbm, both_ref.at[: fw_hbm.shape[0]]), (ow_hbm, both_ref.at[fw_hbm.shape[0] :]),
         (up_hbm.at[0], segment_ref.at[: up_hbm.shape[1]])], sems)
    segment_ref[up_hbm.shape[1] :, :] = jnp.zeros((EXTRA, up_hbm.shape[2]), BF)
    core = lax.axis_index("member")
    count = esc_hbm.shape[1]
    dealt = count // 2
    copies[0].wait()
    copies[1].wait()
    esc = esc_ref[...]
    own = own_ref[...]
    ii = iota((count, count), 0)
    jj = iota((count, count), 1)
    own_col = jnp.sum(jnp.where(ii == jj, own, 0).astype(F32), axis=1, keepdims=True).astype(jnp.int32)
    before = jnp.sum((own_col < own).astype(F32), axis=0, keepdims=True).astype(jnp.int32)
    rank = jnp.sum(((own_col == own) & (ii < jj)).astype(F32), axis=0, keepdims=True).astype(jnp.int32)
    position = before + rank
    side = position & 1
    slot = rank >> 1
    apart = own ^ lax.axis_index("rows")
    pair = apart if relative else (own - (own & 1)) + (apart & 1)
    place = pair * half + slot
    dense = (position >> 1) + jnp.where(side == core, 0, dealt)
    source = jnp.sum(jnp.where(dense == ii, esc, 0).astype(F32), axis=1, keepdims=True).astype(jnp.int32)
    chosen = (source == iota((count, feat_ref.shape[0]), 1)).astype(F32).astype(BF)
    line = pair >> 1
    line = line * (n // 2 + 1) + (side ^ core) * (n // 2) ** 2 if relative else line + (side ^ core) * (n // 2)
    for i, row in enumerate((line, (apart & 1) * half + slot, esc, place, dense)):
        index_ref[i : i + 1, :] = row
    copies[2].wait()
    rows_ref[...] = dot(chosen, feat_ref[...]).astype(BF)
    for copy in copies[3:]:
        copy.wait()


def predict_kernel(
    rows_ref, w_ref, bias_ref, out_ref, upb_ref, head_ref, down_ref, raw_ref,
    near_ref, segment_ref,
):
    depth = raw_ref.shape[0] - EXTRA
    here = w_ref.shape[0]
    core = lax.axis_index("member")
    dealt = near_ref.shape[1]
    row = iota((8, 1), 0)
    preds = None
    for m in range(here):
        act = gelu2(dot(rows_ref[...], w_ref[m]) + bias_ref[m : m + 1]).astype(BF)
        on_row = jnp.where(row == core * here + m, 0.5 * out_ref[m : m + 1].astype(F32), 0.0).astype(BF)
        pred = dot_t(on_row, act)
        preds = pred if preds is None else preds + pred
    preds = preds.astype(BF).astype(F32)
    near_ref[...] = preds[:, :dealt]
    head = split3(head_ref[...]).astype(F32)
    head = jnp.concatenate([head, jnp.zeros((LANES - 3, head.shape[1]), F32)], axis=0).astype(BF)
    down = jnp.sum(dot_t(down_ref[...], head).T[:8], axis=0, keepdims=True)
    extra = [split3(x).astype(F32) for x in (down, upb_ref[...], head_ref[...])]
    members = EXTRA - PREDS
    far = jnp.concatenate([preds[:members, dealt:], jnp.zeros((members, down.shape[1] - dealt), F32)], axis=1)
    extra.append(far)
    segment_ref[depth:, :] = jnp.concatenate(extra, axis=0).astype(BF)


def constants_kernel(
    cls_ref, gain_ref, scale_ref, shift_ref, fbias_ref, fgain_ref, q0_ref, q1_ref, index_ref, after_ref,
    table_ref, where_ref, place_ref,
):
    count = index_ref.shape[1]
    diag = iota((count, count), 0) == iota((count, count), 1)
    cols = [
        jnp.sum(jnp.where(diag, index_ref[i : i + 1, :], 0).astype(F32), axis=1, keepdims=True) for i in range(5)]
    for i in range(3):
        where_ref[:, i : i + 1] = cols[i].astype(jnp.int32)
    dealt = place_ref.shape[1]
    placed = cols[4].astype(jnp.int32) == iota((count, dealt), 1)
    place_ref[...] = jnp.sum(jnp.where(placed, cols[3], 0.0), axis=0, keepdims=True).astype(jnp.int32)
    gain = gain_ref[...]
    cls = cls_ref[...]
    centered = centre(cls)
    ncls = (centered * inverse_spread(centered) * gain).astype(BF)
    table_ref[...] = jnp.zeros_like(table_ref)
    members = scale_ref.shape[0]
    table_ref[SCALE : SCALE + members, :] = centre(scale_ref[...])
    table_ref[SHIFT : SHIFT + members, :] = centre(shift_ref[...])
    table_ref[GAIN : GAIN + 1, :] = gain
    table_ref[FBIAS : FBIAS + 1, :] = fbias_ref[...]
    table_ref[CLS : CLS + 1, :] = cls
    table_ref[FGAIN : FGAIN + 1, :] = fgain_ref[...]
    lhs = jnp.broadcast_to(ncls.astype(F32), (8, ncls.shape[1])).astype(BF)
    local = q0_ref.shape[2]
    heads = local // HD
    row = iota((8, local), 0)
    col = iota((8, local), 1) // HD
    kmap = None
    for i, ref in enumerate((q0_ref, q1_ref)):
        query = dot(lhs, ref[0]) * (1.0 / math.sqrt(HD))
        spread = jnp.where(row == col + i * heads, query, 0.0)
        part = join3(dot_t(split3(spread), ref[1]))
        kmap = part if kmap is None else kmap + part
        table_ref[VCLS : VCLS + 1, i * local : (i + 1) * local] = dot(lhs, ref[2])[0:1]
    table_ref[KMAP : KMAP + 8, :] = kmap
    logits = jnp.sum(kmap * ncls.astype(F32), axis=-1, keepdims=True)
    eye = iota((8, LANES), 0) == iota((8, LANES), 1)
    table_ref[LCLS : LCLS + 1, :LANES] = jnp.sum(jnp.where(eye, logits, 0.0), axis=0, keepdims=True)


def attend_kernel(
    members, rows_ref, near_ref, other_ref, place_ref, table_ref, fw0_ref, fw1_ref, q0_ref, q1_ref, *sent_refs
):
    core = lax.axis_index("member")
    total = near_ref.shape[1]
    fwidth = rows_ref.shape[1]
    rows = rows_ref[:total]
    local = q0_ref.shape[2]
    gain = table_ref[GAIN : GAIN + 1, :]
    low, high = rows[:, : fwidth // 2].astype(F32), rows[:, fwidth // 2 :].astype(F32)
    first = jnp.where(core == 0, low, high).astype(BF)
    second = jnp.where(core == 0, high, low).astype(BF)
    token = dot(first, fw0_ref[: fwidth // 2]) + dot(second, fw1_ref[: fwidth // 2]) + table_ref[FBIAS : FBIAS + 1, :]
    centered = centre(token)
    tokens = [(centered * inverse_spread(centered) * gain).astype(BF)]
    first = other_ref.shape[0] - EXTRA + PREDS
    far = other_ref[first : first + EXTRA - PREDS, :total].astype(F32)
    preds = (near_ref[...] + jnp.concatenate([far, jnp.zeros((8 - far.shape[0], total), F32)], axis=0)).T
    for m in range(members):
        centered = preds[:, m : m + 1] * table_ref[SCALE + m : SCALE + m + 1, :] + table_ref[SHIFT + m : SHIFT + m + 1, :]
        tokens.append((centered * inverse_spread(centered) * gain).astype(BF))
    normed = jnp.concatenate(tokens, axis=0)
    count = len(tokens)

    kmap = jnp.concatenate([table_ref[KMAP : KMAP + 8, :], jnp.zeros((LANES - 8, table_ref.shape[1]), F32)], axis=0)
    logits = dot_t(normed, jnp.concatenate(split2(kmap), axis=0))
    logits = logits[:, :LANES] + logits[:, LANES:]
    expo = jnp.exp(logits)
    expo_cls = jnp.exp(table_ref[LCLS : LCLS + 1, :LANES])
    norm = expo_cls
    for t in range(count):
        norm = norm + expo[t * total : (t + 1) * total]
    inverse = 1.0 / norm
    weights = jnp.concatenate(
        [expo[t * total : (t + 1) * total] * inverse for t in range(count)] + [expo_cls * inverse], axis=0)
    expand = (iota((2 * LANES, 2 * local), 0) & (LANES - 1)) == iota((2 * LANES, 2 * local), 1) // HD
    spread = dot(jnp.concatenate(split2(weights), axis=1), expand.astype(F32).astype(BF))
    parts = []
    for i, ref in enumerate((q0_ref, q1_ref)):
        at = slice(i * local, (i + 1) * local)
        value = dot(normed, ref[2])
        mixed = spread[count * total :, at] * table_ref[VCLS : VCLS + 1, at]
        for t in range(count):
            rng = slice(t * total, (t + 1) * total)
            mixed = mixed + spread[rng, at] * value[rng]
        parts.append(mixed)
    mixed = jnp.concatenate(parts, axis=1).astype(BF)
    size = sent_refs[0].shape[0]
    scatter = (place_ref[...] == iota((size * len(sent_refs), total), 0)).astype(F32).astype(BF)
    sent = dot(scatter, mixed).astype(BF)
    for k, sent_ref in enumerate(sent_refs):
        sent_ref[...] = sent[k * size : (k + 1) * size]


def ensemble_kernel(first, count, tile, feat_ref, w_ref, bias_ref, out_ref, after_ref, *refs):
    held = (len(refs) - 1) // 2
    copies = start_all(list(zip(refs[:held], refs[held + 1 :])), refs[-1]) if held else []
    pred_ref = refs[held]
    for t in range(count):
        rows = feat_ref[(first + t) * tile : (first + t + 1) * tile]
        total = None
        for m in range(w_ref.shape[0]):
            hidden = gelu2(dot(rows, w_ref[m]) + bias_ref[m : m + 1]).astype(BF)
            weights = jnp.broadcast_to(out_ref[m : m + 1].astype(F32), (8, out_ref.shape[1])).astype(BF)
            pred = dot_t(weights, hidden)[0:1]
            total = pred if total is None else total + pred
        per = tile // LANES
        for i in range(per):
            pred_ref[t * per + i : t * per + i + 1, :] = total[:, i * LANES : (i + 1) * LANES]
    for copy in copies:
        copy.wait()


def unpack(ref):
    depth = ref.shape[0] - EXTRA
    extra = ref[depth:, :].astype(F32)
    return ref[:depth, :], *(jnp.sum(extra[i : i + 3], axis=0, keepdims=True) for i in (DOWN, BIAS, HEAD))


def hidden_terms(normed, up, down, bias):
    return jnp.maximum(dot(normed, up) + bias, 0.0).astype(BF).astype(F32) * down


def states(mixed, table_ref, both0_ref, both1_ref):
    local = mixed.shape[1] // 2
    ow0, ow1 = (ref[ref.shape[0] - local :] for ref in (both0_ref, both1_ref))
    state = table_ref[CLS : CLS + 1, :] + dot(mixed[:, :local], ow0) + dot(mixed[:, local:], ow1)
    centered = centre(state)
    return state, (centered * inverse_spread(centered) * table_ref[FGAIN : FGAIN + 1, :]).astype(BF)


def arrived(got_refs, half, e):
    if len(got_refs) == 1:
        rows = got_refs[0].shape[0] // 2
        return got_refs[0][e * rows : (e + 1) * rows]
    return jnp.concatenate([ref[e * half : (e + 1) * half] for ref in got_refs], axis=0)


def arrive_kernel(blocks, half, *refs):
    table_ref, both0_ref, both1_ref, state_ref, normed_ref = refs[blocks:]
    state_ref[...], normed_ref[...] = states(arrived(refs[:blocks][::-1], half, 1), table_ref, both0_ref, both1_ref)


def near_score_kernel(blocks, half, *refs):
    table_ref, both0_ref, both1_ref, up0_ref, up1_ref, score_ref = refs[blocks:]
    state, normed = states(arrived(refs[:blocks][::-1], half, 0), table_ref, both0_ref, both1_ref)
    up, down, bias, head = unpack(up0_ref)
    terms = state * head + hidden_terms(normed, up, down, bias)
    up, down, bias, _ = unpack(up1_ref)
    terms = terms + hidden_terms(normed, up, down, bias)
    score_ref[...] = jnp.sum(terms, axis=-1, keepdims=True)


def far_score_kernel(blocks, half, near_ref, state_ref, mine_ref, other_ref, up2_ref, out_ref):
    rows = near_ref.shape[0]
    up, down, bias, head = unpack(up2_ref)
    terms = hidden_terms(jnp.concatenate([mine_ref[...], other_ref[...]], axis=0), up, down, bias)
    scores = [
        near_ref[...],
        jnp.sum(terms[:rows] + state_ref[...] * head, axis=-1, keepdims=True),
        jnp.sum(terms[rows:], axis=-1, keepdims=True),
    ]
    if blocks == 1:
        eye = iota((rows, rows), 0) == iota((rows, rows), 1)
        for e, score in enumerate(scores):
            out_ref[:, e * rows : (e + 1) * rows] = jnp.sum(jnp.where(eye, score, 0.0), axis=0, keepdims=True)
    else:
        row, lane = iota((half, LANES), 0), iota((half, LANES), 1)
        for k in range(blocks):
            line = jnp.zeros((half, LANES), F32)
            for e, score in enumerate(scores):
                line = jnp.where(lane == row + e * half, score[k * half : (k + 1) * half], line)
            out_ref[k : k + 1, :] = jnp.sum(line, axis=0, keepdims=True)


def expand_kernel(lines, where_ref, after_ref, line_ref, lane_ref):
    rows = lane_ref.shape[1]
    hit = where_ref[:, 2:3] == iota((where_ref.shape[0], rows), 1)

    def by_row(i):
        return jnp.sum(jnp.where(hit, where_ref[:, i : i + 1] + 1, 0).astype(F32), axis=0, keepdims=True).astype(jnp.int32)

    line = (by_row(0) - 1 == iota((lines, rows), 0)).astype(F32)
    line_ref[...] = jnp.concatenate([line] * 3, axis=0).astype(BF)
    lane_ref[...] = by_row(1) - 1


def finish_kernel(members, half, lines, line_ref, lane_ref, near_ref, far_ref, out_ref):
    near, far = near_ref[...], far_ref[...]
    ensemble = (near[lines:] + far[lines:]) * (0.5 / members)
    ensemble = jnp.concatenate([ensemble[i : i + 1] for i in range(ensemble.shape[0])], axis=1)
    lanes = iota((lines, LANES), 1)
    last = (lanes >= half) & (lanes < 2 * half)

    def whole(mine, others):
        return mine[:lines] + jnp.where(last, pltpu.roll(others[:lines], LANES - half, 1), 0.0)

    table = split3(jnp.concatenate([whole(near, far), whole(far, near)], axis=0))
    by_lane = lax.dot_general(table, line_ref[...], (((0,), (0,)), ((), ())), preferred_element_type=F32)
    lane = lane_ref[...]
    replaced = jnp.sum(jnp.where(lane == iota(by_lane.shape, 0), by_lane, 0.0), axis=0, keepdims=True)
    out_ref[...] = jnp.where(lane >= 0, replaced, ensemble)


def cost(flops, size, trans=0):
    return pl.CostEstimate(flops=flops, bytes_accessed=size, transcendentals=trans)


def params(mib):
    return pltpu.CompilerParams(vmem_limit_bytes=mib * 2**20)


def in_hbm(arrays):
    return [pltpu.with_memory_space_constraint(x, pltpu.HBM) for x in arrays]


def shape(dims, dtype):
    return jax.ShapeDtypeStruct(dims, dtype)


def per_device(
    features, escalated, owner_ids, member_in, member_bias, member_out, feat_weight, feat_bias,
    pred_scale, pred_shift, cls_token, attn_gain, qkv_weight, out_weight, ffn_gain, up_weight,
    up_bias, down_weight, owner_heads,
):
    n = lax.axis_size("rows")
    rows, fwidth = features.shape
    count = escalated.shape[1]
    half = max(1, count // n)
    slots = n * half
    here, _, hidden = member_in.shape
    members = pred_scale.shape[0]
    width = cls_token.shape[0]

    def swap(x):
        return lax.ppermute(x, "member", [(0, 1), (1, 0)])

    row = lambda x: x.reshape(1, -1)
    cls_token, attn_gain, ffn_gain, feat_bias = map(row, (cls_token, attn_gain, ffn_gain, feat_bias))
    owners = owner_ids.reshape(1, count)

    pairs = n // 2
    relative = pairs <= 8
    blocks = pairs if relative else 1
    other_qkv = swap(qkv_weight)

    dealt = count // 2
    ins = (escalated, owners, features, down_weight, up_weight, feat_weight, out_weight)
    index, mine, down, segment, own_both = pl.pallas_call(
        functools.partial(route_kernel, n, half, relative),
        out_shape=[shape((8, count), jnp.int32), shape((count, fwidth), BF), shape(down_weight.shape[1:], BF),
                   shape((up_weight.shape[1] + EXTRA, up_weight.shape[2]), BF),
                   shape((feat_weight.shape[0] + out_weight.shape[0], width), BF)],
        in_specs=[HBM] * len(ins),
        out_specs=[VMEM] * 5,
        scratch_shapes=[pltpu.VMEM(x.shape, x.dtype) for x in ins[:3]] + [pltpu.SemaphoreType.DMA((7,))],
        compiler_params=params(24),
        cost_estimate=cost(2 * count * rows * fwidth, 3 * 10**6),
        name="route",
    )(*in_hbm(ins))
    near, segment = pl.pallas_call(
        predict_kernel,
        out_shape=[shape((8, dealt), F32), shape(segment.shape, BF)],
        in_specs=[VMEM] * 8,
        out_specs=[VMEM] * 2,
        input_output_aliases={7: 1},
        compiler_params=params(24),
        cost_estimate=cost(2 * here * count * fwidth * hidden, 3 * 10**6, here * count * hidden),
        name="predict",
    )(mine, member_in, member_bias, member_out, up_bias, owner_heads, down, segment)
    other_both = swap(own_both)
    next_segment = lax.ppermute(segment, "rows", [(i, i ^ 1) for i in range(n)])
    other_segment = swap(segment)

    ins = (cls_token, attn_gain, pred_scale, pred_shift, feat_bias, ffn_gain, qkv_weight, other_qkv, index)
    table, where, place = pl.pallas_call(
        constants_kernel,
        out_shape=[shape((TABLE, width), F32), shape((count, 3), jnp.int32), shape((1, dealt), jnp.int32)],
        in_specs=[VMEM] * len(ins) + [ANY],
        out_specs=[VMEM] * 3,
        compiler_params=params(16),
        cost_estimate=cost(10**8, 2 * 10**6),
        name="constants",
    )(*ins, other_both)

    local = qkv_weight.shape[2]
    sent = pl.pallas_call(
        functools.partial(attend_kernel, members),
        out_shape=[shape((slots // blocks, 2 * local), BF)] * blocks,
        in_specs=[VMEM] * 9,
        out_specs=[VMEM] * blocks,
        compiler_params=params(24),
        cost_estimate=cost(10**9, 2 * 10**6),
        name="attend",
    )(mine, near, other_segment, place, table, own_both, other_both, qkv_weight, other_qkv)

    def across(x, k):
        return lax.ppermute(x, "rows", [(i, i ^ (2 * k)) for i in range(n)])

    def exchange(x):
        groups = [[2 * q + b for q in range(pairs)] for b in range(2)]
        return lax.all_to_all(x, "rows", split_axis=0, concat_axis=0, axis_index_groups=groups, tiled=True)

    if relative:
        got = [sent[0]] + [across(sent[k], k) for k in range(1, pairs)]
    else:
        got = exchange(sent[0].reshape(pairs, 2, half, 2 * local))
        got = [got.transpose(1, 0, 2, 3).reshape(slots, 2 * local)]

    tile = min(rows, 256)
    tiles = rows // tile

    def ensemble(first, number, after, held=()):
        return pl.pallas_call(
            functools.partial(ensemble_kernel, first, number, tile),
            out_shape=[shape((number * tile // LANES, LANES), F32)] + [shape(x.shape, x.dtype) for x in held],
            in_specs=[VMEM] * 4 + [ANY] * (1 + len(held)),
            out_specs=[VMEM] * (1 + len(held)),
            scratch_shapes=[pltpu.SemaphoreType.DMA((len(held),))] if held else [],
            compiler_params=params(24),
            cost_estimate=cost(2 * here * number * tile * fwidth * hidden, 10**6, here * number * tile * hidden),
            name="ensemble",
        )(features, member_in, member_bias, member_out, after, *held)

    early = (tiles + 1) // 2
    preds, table, both0, both1, up0, up1 = ensemble(
        0, early, sent[0], (table, own_both, other_both, segment, other_segment))
    preds = [preds]

    state, next_rows = pl.pallas_call(
        functools.partial(arrive_kernel, blocks, half),
        out_shape=[shape((slots // 2, width), F32), shape((slots // 2, width), BF)],
        in_specs=[VMEM] * (blocks + 3),
        out_specs=[VMEM] * 2,
        compiler_params=params(24),
        cost_estimate=cost(2 * 10**8, 2 * 10**6),
        name="arrive",
    )(*got[::-1], table, both0, both1)
    other_rows = swap(next_rows)
    near_scores = pl.pallas_call(
        functools.partial(near_score_kernel, blocks, half),
        out_shape=shape((slots // 2, 1), F32),
        in_specs=[VMEM] * (blocks + 5),
        out_specs=VMEM,
        compiler_params=params(24),
        cost_estimate=cost(5 * 10**8, 2 * 10**6),
        name="near_score",
    )(*got[::-1], table, both0, both1, up0, up1)
    scores = pl.pallas_call(
        functools.partial(far_score_kernel, blocks, half),
        out_shape=shape((blocks, LANES if relative else 3 * slots // 2), F32),
        in_specs=[VMEM] * 5,
        out_specs=VMEM,
        compiler_params=params(24),
        cost_estimate=cost(2 * 10**8, 10**6),
        name="far_score",
    )(near_scores, state, next_rows, other_rows, next_segment)
    for first in range(early, tiles):
        preds += ensemble(first, 1, scores)
    back = scores
    if relative:
        step = 1
        while step < pairs:
            back = jnp.concatenate([back, across(back, step)], axis=0)
            step *= 2
    else:
        back = exchange(back.reshape(3, pairs, half).transpose(1, 0, 2)).reshape(pairs, 3 * half)
        back = jnp.pad(back, ((0, 0), (0, LANES - 3 * half)))
    lines = back.shape[0]
    near_lines = jnp.concatenate([back, *preds], axis=0)
    line_of, lane_of = pl.pallas_call(
        functools.partial(expand_kernel, 2 * lines),
        out_shape=[shape((6 * lines, rows), BF), shape((1, rows), jnp.int32)],
        in_specs=[VMEM, ANY],
        out_specs=[VMEM] * 2,
        compiler_params=params(16),
        cost_estimate=cost(10**8, 10**6),
        name="expand",
    )(where, preds[-1])

    final = pl.pallas_call(
        functools.partial(finish_kernel, members, half, lines),
        out_shape=shape((1, rows), F32),
        in_specs=[VMEM] * 4,
        out_specs=VMEM,
        compiler_params=params(8),
        cost_estimate=cost(10**6, 10**6),
        name="finish",
    )(line_of, lane_of, near_lines, swap(near_lines))
    return final.reshape(rows)


def solution(mesh):
    placed = (
        P(("groups", "rows"), None),
        P(("groups", "rows"), None),
        P(("groups", "rows"), None, None),
        P("member", None, None),
        P("member", None),
        P("member", None),
        P("member", None),
        P(),
        P(),
        P(),
        P(),
        P(),
        P(None, None, "member"),
        P("member", None),
        P(),
        P("rows", None, "member"),
        P("rows", "member"),
        P("rows", "member", None),
        P("rows", None),
    )
    return jax.shard_map(
        per_device, mesh=mesh, in_specs=placed, out_specs=P(("groups", "rows")), check_vma=False
    )
```
